32 devices in a mesh: wide: 8 (over z, y), narrow: 4 (over x, core).
Axes of the slice: x: 2, y: 2, z: 4, core: 2. Of those that a mesh axis runs over, the one named last changes fastest.
Arguments:
- x_lo: bfloat16 [64, 10, 10, 1024], P(('wide', 'narrow')), may hold values from -6 to 6
- x_mid: bfloat16 [64, 14, 14, 1024], P(('wide', 'narrow')), may hold values from -6 to 6
- x_hi: bfloat16 [64, 18, 18, 1024], P(('wide', 'narrow')), may hold values from -6 to 6
- cot_lo: bfloat16 [64, 5, 5, 2048], P(('wide', 'narrow')), may hold values from -6 to 6
- cot_mid: bfloat16 [64, 7, 7, 2048], P(('wide', 'narrow')), may hold values from -6 to 6
- cot_hi: bfloat16 [64, 9, 9, 2048], P(('wide', 'narrow')), may hold values from -6 to 6
- live_counts: int32 [32, 3], P(('wide', 'narrow')), may hold values from 1 to 2, as said below
- slim_master: float32 [12288, 512], P(('wide', 'narrow'))
- broad_master: float32 [2048, 2048], P(('wide', 'narrow'))
- slim_rowstat: float32 [12288], P(('wide', 'narrow')), as said below
- broad_rowstat: float32 [2048], P(('wide', 'narrow')), as said below
- slim_colstat: float32 [4, 512], replicated, as said below
- broad_colstat: float32 [3, 2048], replicated, as said below
- norm_params: float32 [2, 8192], replicated
- norm_moments: float32 [2, 8192], replicated, as said below
Outputs:
- y_lo: bfloat16 [64, 5, 5, 2048], P(('wide', 'narrow'))
- y_mid: bfloat16 [64, 7, 7, 2048], P(('wide', 'narrow'))
- y_hi: bfloat16 [64, 9, 9, 2048], P(('wide', 'narrow'))
- dx_lo: float32 [64, 10, 10, 1024], P(('wide', 'narrow'))
- dx_mid: float32 [64, 14, 14, 1024], P(('wide', 'narrow'))
- dx_hi: float32 [64, 18, 18, 1024], P(('wide', 'narrow'))
- slim_grad: float32 [12288, 512], P(('wide', 'narrow'))
- broad_grad: float32 [2048, 2048], P(('wide', 'narrow'))
- slim_rows_new: float32 [12288], P(('wide', 'narrow'))
- broad_rows_new: float32 [2048], P(('wide', 'narrow'))
- slim_cols_new: float32 [4, 512], replicated
- broad_cols_new: float32 [3, 2048], replicated
- slim_new: float32 [12288, 512], P(('wide', 'narrow'))
- broad_new: float32 [2048, 2048], P(('wide', 'narrow'))
- slim_copy: bfloat16 [12288, 512], P(('wide', 'narrow'))
- broad_copy: bfloat16 [2048, 2048], P(('wide', 'narrow'))
- norm_grad: float32 [2, 8192], replicated
- norm_moments_new: float32 [2, 8192], replicated
- norm_new: float32 [2, 8192], replicated
The draws below stay inside these ranges and needn't reach their ends.
Inputs may be any that keep to these rules, and one draw needn't show every extreme that they name: Each device uses its first live_counts slots of each resolution; in each column some device has all 2 slots in use. `slim_rowstat`: positive. `broad_rowstat`: positive. `slim_colstat`: positive. `broad_colstat`: positive. `norm_moments`: positive.
All inputs are finite; a program needn't handle non-finite values.
Results may differ from the reference program's by a relative error of at most 0.04.
Values may be sent and summed in bfloat16 or wider, within the bound.
No kernel may reach another device: no remote copies, remote signals or barrier semaphores. Data moves between devices by JAX's collectives and lax.ppermute only.
A program may use at most 256 MiB of HBM per device.

```python
import jax
import jax.numpy as jnp
from jax import lax

C_IN = 1024
MID = 512
C_OUT = 2048
GL = 10
GM = 14
GH = 18
IMGS = 2
STEP = 10
SLIM_ROWS = 12288
BROAD_ROWS = 2048
NORM_CH = 8192
IMAGES = 64
N_WIDE = 8
N_NARROW = 4
DEVICES = 32


def state_ratio():
    decay_rate = 1.0 - STEP ** (-0.8)
    return (1.0 - decay_rate) / decay_rate


def pixel_scale():
    return 0.2 * DEVICES * IMGS * (GL * GL + GM * GM + GH * GH)


def draw_live_counts(key, part):
    key = jax.random.fold_in(key, 1)
    key_one, key_two = jax.random.split(key)
    counts_now = jax.random.randint(key_one, (DEVICES, 3), 1, IMGS + 1)
    picked = jax.random.randint(key_two, (3,), 0, DEVICES)
    return counts_now.at[picked, jnp.arange(3)].set(IMGS).astype(jnp.int32)


def draw_slim_master(key, part):
    key = jax.random.fold_in(key, 2)
    row_index = jnp.arange(SLIM_ROWS)
    row_scale = jnp.where(row_index < C_IN, C_IN ** (-0.5), jnp.where(row_index < C_IN + 9 * MID, (9 * MID) ** (-0.5), jnp.where(row_index < C_IN + 9 * MID + C_OUT, C_OUT ** (-0.5), (9 * MID) ** (-0.5))))
    return jax.random.normal(key, (SLIM_ROWS, MID), jnp.float32) * row_scale[:, None]


def draw_broad_master(key, part):
    key = jax.random.fold_in(key, 3)
    row_index = jnp.arange(BROAD_ROWS)
    row_scale = jnp.where(row_index < MID, MID ** (-0.5), jnp.where(row_index < MID + C_IN, C_IN ** (-0.5), MID ** (-0.5)))
    return jax.random.normal(key, (BROAD_ROWS, C_OUT), jnp.float32) * row_scale[:, None]


def draw_slim_rowstat(key, part):
    key = jax.random.fold_in(key, 4)
    row_index = jnp.arange(SLIM_ROWS)
    level_vec = jnp.where(row_index < C_IN, 1.0, 0.25) * pixel_scale()
    return level_vec * state_ratio() * jax.random.uniform(key, (SLIM_ROWS,), jnp.float32, 1.0, 4.0)


def draw_broad_rowstat(key, part):
    key = jax.random.fold_in(key, 5)
    return 0.25 * pixel_scale() * state_ratio() * jax.random.uniform(key, (BROAD_ROWS,), jnp.float32, 1.0, 4.0)


def draw_slim_colstat(key, part):
    key = jax.random.fold_in(key, 6)
    level_vec = jnp.array([1.0, 0.25, 0.25, 0.25], jnp.float32) * pixel_scale()
    return level_vec[:, None] * state_ratio() * jax.random.uniform(key, (4, MID), jnp.float32, 1.0, 4.0)


def draw_broad_colstat(key, part):
    key = jax.random.fold_in(key, 7)
    return 0.25 * pixel_scale() * state_ratio() * jax.random.uniform(key, (3, C_OUT), jnp.float32, 1.0, 4.0)


def draw_norm_params(key, part):
    key = jax.random.fold_in(key, 8)
    key_one, key_two = jax.random.split(key)
    position = jnp.arange(NORM_CH).astype(jnp.float32) / NORM_CH
    gain_row = (0.5 + position) * jax.random.uniform(key_one, (NORM_CH,), jnp.float32, 0.8, 1.2)
    shift_row = 0.3 * jax.random.normal(key_two, (NORM_CH,), jnp.float32)
    return jnp.stack([gain_row, shift_row])


def draw_norm_moments(key, part):
    key = jax.random.fold_in(key, 9)
    channel = jnp.arange(NORM_CH)
    level_vec = jnp.where(channel < MID, 1.0, 0.25) * pixel_scale()
    return level_vec[None, :] * state_ratio() * jax.random.uniform(key, (2, NORM_CH), jnp.float32, 1.0, 4.0)


def block_scale(own_key, shape, shards, smallest, high):
    level, own = 1.0, jax.random.fold_in(own_key, 6)
    for dim, parts in shards:
        steps = jnp.exp(jax.random.uniform(jax.random.fold_in(own, dim), (parts,), jnp.float32, smallest / len(shards), high / len(shards)))
        level = level * jnp.repeat(steps, shape[dim] // parts).reshape([-1 if axis == dim else 1 for axis in range(len(shape))])
    return level


def normal_values(stream_key, shape, spread, most, cuts=(), dtype=jnp.bfloat16):
    factor_of = block_scale(stream_key, shape, cuts, -0.22, 0.18) if cuts else 1.0
    drawn = jax.random.normal(stream_key, shape, jnp.float32) * spread * factor_of
    return jnp.minimum(jnp.maximum(drawn, -most), most).astype(dtype)


def setup_inputs(seed: int = 0) -> dict:
    splits = jax.random.split(jax.random.key(seed), 16)
    x_lo = normal_values(splits[0], (IMAGES, GL, GL, C_IN), 1.0, 6.0, ((0, 32),))
    x_mid = normal_values(splits[1], (IMAGES, GM, GM, C_IN), 1.0, 6.0, ((0, 32),))
    x_hi = normal_values(splits[2], (IMAGES, GH, GH, C_IN), 1.0, 6.0, ((0, 32),))
    cot_lo = normal_values(splits[3], (IMAGES, GL // 2, GL // 2, C_OUT), 1.0, 6.0, ((0, 32),))
    cot_mid = normal_values(splits[4], (IMAGES, GM // 2, GM // 2, C_OUT), 1.0, 6.0, ((0, 32),))
    cot_hi = normal_values(splits[5], (IMAGES, GH // 2, GH // 2, C_OUT), 1.0, 6.0, ((0, 32),))
    live_counts = draw_live_counts(jax.random.fold_in(splits[15], 71), 0)
    slim_master = draw_slim_master(jax.random.fold_in(splits[15], 71), 0)
    broad_master = draw_broad_master(jax.random.fold_in(splits[15], 71), 0)
    slim_rowstat = draw_slim_rowstat(jax.random.fold_in(splits[15], 71), 0)
    broad_rowstat = draw_broad_rowstat(jax.random.fold_in(splits[15], 71), 0)
    slim_colstat = draw_slim_colstat(jax.random.fold_in(splits[15], 71), 0)
    broad_colstat = draw_broad_colstat(jax.random.fold_in(splits[15], 71), 0)
    norm_params = draw_norm_params(jax.random.fold_in(splits[15], 71), 0)
    norm_moments = draw_norm_moments(jax.random.fold_in(splits[15], 71), 0)
    return dict(x_lo=x_lo, x_mid=x_mid, x_hi=x_hi, cot_lo=cot_lo, cot_mid=cot_mid, cot_hi=cot_hi, live_counts=live_counts, slim_master=slim_master, broad_master=broad_master, slim_rowstat=slim_rowstat, broad_rowstat=broad_rowstat, slim_colstat=slim_colstat, broad_colstat=broad_colstat, norm_params=norm_params, norm_moments=norm_moments)


EPS_NORM = 1e-05
EPS_ONE = 1e-30
EPS_TWO = 0.001
STEP_RATE = 0.3
CLIP_LIMIT = 1.0

@jax.custom_vjp
def low(v):
    return lax.optimization_barrier(v.astype(jnp.bfloat16)).astype(jnp.float32)

@jax.custom_vjp
def low_back(v):
    return v

def low_keep(v):
    return (low(v), None)

def low_pass(kept, grad):
    return (grad,)

def back_keep(v):
    return (v, None)

def back_low(kept, grad):
    return (low(grad),)
low.defvjp(low_keep, low_pass)
low_back.defvjp(back_keep, back_low)

def product(first_op, second_op):
    return jnp.dot(first_op, second_op, precision=lax.Precision.HIGHEST, preferred_element_type=jnp.float32)

def split_flat(flat, images, grid_sizes):
    pieces = []
    offset = 0
    for extent in grid_sizes:
        length = images * extent * extent
        pieces.append(flat[offset:offset + length].reshape(images, extent, extent, flat.shape[1]))
        offset += length
    return pieces

def patches(flat, images, grid_sizes, stride):
    pieces = []
    for block_view in split_flat(flat, images, grid_sizes):
        extent = block_view.shape[1]
        reach = stride * (extent // stride - 1) + 1
        padded = jnp.pad(block_view, ((0, 0), (1, 1), (1, 1), (0, 0)))
        tap_list = [padded[:, row_tap:row_tap + reach:stride, col_tap:col_tap + reach:stride, :] for row_tap in range(3) for col_tap in range(3)]
        joined = jnp.concatenate(tap_list, axis=3)
        pieces.append(joined.reshape(-1, joined.shape[3]))
    return jnp.concatenate(pieces, 0)

def subsample(flat, images, grid_sizes):
    pieces = [block_view[:, ::2, ::2, :].reshape(-1, flat.shape[1]) for block_view in split_flat(flat, images, grid_sizes)]
    return jnp.concatenate(pieces, 0)

def normalize(values, mask_in):
    weighted = values * mask_in[:, None]
    count_all = jnp.sum(mask_in)
    mean_val = lax.optimization_barrier(jnp.sum(weighted, 0)) / count_all
    var_val = lax.optimization_barrier(jnp.sum(weighted * values, 0)) / count_all - mean_val * mean_val
    return (values - mean_val) * lax.rsqrt(var_val + EPS_NORM)

def forward(slim_master, broad_master, norm_params, x_flat, mask_in, mask_out, images, grid_sizes):
    width_in = x_flat.shape[1]
    width_mid = slim_master.shape[1]
    width_out = broad_master.shape[1]
    slim_low = low(slim_master)
    broad_low = low(broad_master)
    bound_two = width_in + 9 * width_mid
    bound_three = bound_two + width_out
    w_one = slim_low[:width_in]
    w_two = slim_low[width_in:bound_two]
    w_four = slim_low[bound_two:bound_three]
    w_five = slim_low[bound_three:]
    w_three = broad_low[:width_mid]
    w_side = broad_low[width_mid:width_mid + width_in]
    w_six = broad_low[width_mid + width_in:]
    widths = (width_mid, width_mid, width_out, width_out, width_mid, width_mid, width_out)
    starts = [sum(widths[:level]) for level in range(8)]
    gain_list = [norm_params[0, starts[level]:starts[level + 1]] for level in range(7)]
    shifts = [norm_params[1, starts[level]:starts[level + 1]] for level in range(7)]
    grids_out = tuple((extent // 2 for extent in grid_sizes))
    z_one = low_back(product(x_flat, w_one))
    act_one = low(jax.nn.silu(gain_list[0] * normalize(z_one, mask_in) + shifts[0]))
    z_two = low_back(product(patches(act_one, images, grid_sizes, 2), w_two))
    act_two = low(jax.nn.silu(gain_list[1] * normalize(z_two, mask_out) + shifts[1]))
    z_three = low_back(product(act_two, w_three))
    z_side = low_back(product(subsample(x_flat, images, grid_sizes), w_side))
    hidden = jax.nn.silu(gain_list[2] * normalize(z_three, mask_out) + shifts[2] + gain_list[3] * normalize(z_side, mask_out) + shifts[3])
    z_four = low_back(product(low(hidden), w_four))
    act_four = low(jax.nn.silu(gain_list[4] * normalize(z_four, mask_out) + shifts[4]))
    z_five = low_back(product(patches(act_four, images, grids_out, 1), w_five))
    act_five = low(jax.nn.silu(gain_list[5] * normalize(z_five, mask_out) + shifts[5]))
    z_six = low_back(product(act_five, w_six))
    return jax.nn.silu(gain_list[6] * normalize(z_six, mask_out) + shifts[6] + hidden)

def factored(gradient, master, rowstat, colstat, bounds, decay_rate):
    rows_out = []
    cols_out = []
    masters_out = []
    for level in range(len(bounds) - 1):
        grad_part = gradient[bounds[level]:bounds[level + 1]]
        weight_part = master[bounds[level]:bounds[level + 1]]
        grad_sq = grad_part * grad_part + EPS_ONE
        rows_new = decay_rate * rowstat[bounds[level]:bounds[level + 1]] + (1.0 - decay_rate) * lax.optimization_barrier(jnp.mean(grad_sq, 1))
        cols_new = decay_rate * colstat[level] + (1.0 - decay_rate) * lax.optimization_barrier(jnp.mean(grad_sq, 0))
        second = rows_new[:, None] * cols_new[None, :] / jnp.mean(rows_new)
        update = grad_part * lax.rsqrt(second)
        update_rms = jnp.sqrt(jnp.mean(update * update))
        weight_rms = jnp.sqrt(jnp.mean(weight_part * weight_part))
        masters_out.append(weight_part - STEP_RATE * jnp.maximum(EPS_TWO, weight_rms) / jnp.maximum(1.0, update_rms / CLIP_LIMIT) * update)
        rows_out.append(rows_new)
        cols_out.append(cols_new)
    return (jnp.concatenate(rows_out), jnp.stack(cols_out), jnp.concatenate(masters_out, 0))

def reference(x_lo, x_mid, x_hi, cot_lo, cot_mid, cot_hi, live_counts, slim_master, broad_master, slim_rowstat, broad_rowstat, slim_colstat, broad_colstat, norm_params, norm_moments):
    images = N_NARROW * IMGS
    grid_sizes = (GL, GM, GH)
    grids_out = (GL // 2, GM // 2, GH // 2)

    def grouped(array):
        return array.reshape((N_WIDE, images) + array.shape[1:])
    inputs = (grouped(x_lo), grouped(x_mid), grouped(x_hi), grouped(cot_lo), grouped(cot_mid), grouped(cot_hi), live_counts.reshape(N_WIDE, N_NARROW, 3))

    def group_step(carry, group_in):
        acc_slim, acc_broad, acc_norm = carry
        xs_list = group_in[0:3]
        cots_list = group_in[3:6]
        counts_now = group_in[6]
        alive_list = [(jnp.arange(IMGS)[None, :] < counts_now[:, level][:, None]).reshape(-1).astype(jnp.float32) for level in range(3)]
        mask_in = jnp.concatenate([jnp.repeat(alive_list[level], grid_sizes[level] * grid_sizes[level]) for level in range(3)])
        mask_out = jnp.concatenate([jnp.repeat(alive_list[level], grids_out[level] * grids_out[level]) for level in range(3)])
        x_flat = jnp.concatenate([value.astype(jnp.float32).reshape(-1, C_IN) for value in xs_list], 0)
        cot_flat = jnp.concatenate([value.astype(jnp.float32).reshape(-1, C_OUT) for value in cots_list], 0) * mask_out[:, None]

        def local_forward(slim_arg, broad_arg, norm_arg, x_arg):
            return forward(slim_arg, broad_arg, norm_arg, x_arg, mask_in, mask_out, images, grid_sizes)
        result, pull = jax.vjp(local_forward, slim_master, broad_master, norm_params, x_flat)
        grad_slim, grad_broad, grad_norm, grad_x = pull(cot_flat)
        y_parts = split_flat(result.astype(jnp.bfloat16), images, grids_out)
        dx_parts = split_flat(grad_x, images, grid_sizes)
        return ((acc_slim + grad_slim, acc_broad + grad_broad, acc_norm + grad_norm), (y_parts[0], y_parts[1], y_parts[2], dx_parts[0], dx_parts[1], dx_parts[2]))
    start = (jnp.zeros(slim_master.shape, jnp.float32), jnp.zeros(broad_master.shape, jnp.float32), jnp.zeros(norm_params.shape, jnp.float32))
    totals, stacked = lax.scan(group_step, start, inputs)
    slim_grad, broad_grad, norm_grad = totals
    y_lo = stacked[0].reshape(IMAGES, GL // 2, GL // 2, C_OUT)
    y_mid = stacked[1].reshape(IMAGES, GM // 2, GM // 2, C_OUT)
    y_hi = stacked[2].reshape(IMAGES, GH // 2, GH // 2, C_OUT)
    dx_lo = stacked[3].reshape(IMAGES, GL, GL, C_IN)
    dx_mid = stacked[4].reshape(IMAGES, GM, GM, C_IN)
    dx_hi = stacked[5].reshape(IMAGES, GH, GH, C_IN)
    decay_rate = 1.0 - STEP ** (-0.8)
    slim_bounds = (0, C_IN, C_IN + 9 * MID, C_IN + 9 * MID + C_OUT, C_IN + 18 * MID + C_OUT)
    broad_bounds = (0, MID, MID + C_IN, 2 * MID + C_IN)
    slim_rows_new, slim_cols_new, slim_new = factored(slim_grad, slim_master, slim_rowstat, slim_colstat, slim_bounds, decay_rate)
    broad_rows_new, broad_cols_new, broad_new = factored(broad_grad, broad_master, broad_rowstat, broad_colstat, broad_bounds, decay_rate)
    norm_moments_new = decay_rate * norm_moments + (1.0 - decay_rate) * (norm_grad * norm_grad + EPS_ONE)
    norm_update = norm_grad * lax.rsqrt(norm_moments_new)
    update_rms = jnp.sqrt(lax.optimization_barrier(jnp.mean(norm_update * norm_update, 1)))
    weight_rms = jnp.sqrt(lax.optimization_barrier(jnp.mean(norm_params * norm_params, 1)))
    norm_new = norm_params - (STEP_RATE * jnp.maximum(EPS_TWO, weight_rms) / jnp.maximum(1.0, update_rms / CLIP_LIMIT))[:, None] * norm_update
    return (y_lo, y_mid, y_hi, dx_lo, dx_mid, dx_hi, slim_grad, broad_grad, slim_rows_new, broad_rows_new, slim_cols_new, broad_cols_new, slim_new, broad_new, slim_new.astype(jnp.bfloat16), broad_new.astype(jnp.bfloat16), norm_grad, norm_moments_new, norm_new)
```

```python
import jax
import jax.numpy as jnp
import numpy as np
from jax import lax
from jax.experimental import pallas as pl
from jax.experimental.pallas import tpu as pltpu
from jax.sharding import PartitionSpec as P

STEP = 10
EPS_NORM = 1e-05
EPS_ONE = 1e-30
EPS_TWO = 0.001
STEP_RATE = 0.3
DECAY = 1.0 - STEP ** (-0.8)
AXES = ("wide", "narrow")
BF16 = jnp.bfloat16
F32 = jnp.float32
VMEM_LIMIT = 48 * 1024 * 1024


def shape_of(dims, dtype):
    return jax.ShapeDtypeStruct(dims, dtype)


def whole(dims):
    return pl.BlockSpec(dims, lambda *step: (0,) * len(dims))


def block(dims, place):
    return pl.BlockSpec(dims, place)


def kernel_call(body, name, grid, in_specs, out_specs, out_shape, flops, scratch=(), aliases=None):
    return pl.pallas_call(
        body,
        grid=grid,
        in_specs=in_specs,
        out_specs=out_specs,
        out_shape=out_shape,
        scratch_shapes=list(scratch),
        input_output_aliases=aliases or {},
        cost_estimate=pl.CostEstimate(flops=flops, bytes_accessed=flops // 200, transcendentals=0),
        compiler_params=pltpu.CompilerParams(vmem_limit_bytes=VMEM_LIMIT),
        name=name,
    )


def dot_nn(first, second):
    return jnp.dot(first, second, preferred_element_type=F32)


def dot_nt(first, second):
    return lax.dot_general(first, second, (((1,), (1,)), ((), ())), preferred_element_type=F32)


def dot_tn(first, second):
    return lax.dot_general(first, second, (((0,), (0,)), ((), ())), preferred_element_type=F32)


def sigmoid(value):
    return 1.0 / (1.0 + jnp.exp(-value))


def slope(value):
    gate = sigmoid(value)
    return gate * (1.0 + value * (1.0 - gate))


def tree_sum(values):
    values = list(values)
    while len(values) > 1:
        values = [values[i] + values[i + 1] for i in range(0, len(values), 2)]
    return values[0]


def moments(parts, recip):
    total = tree_sum([part[...] for part in parts]) * recip
    mean = total[0:1]
    return mean, lax.rsqrt(total[1:2] - mean * mean + EPS_NORM)


def column_sum(value):
    return jnp.sum(value, axis=0, keepdims=True)


def stat_rows(value, mask):
    kept = value * mask
    return jnp.concatenate([column_sum(kept), column_sum(kept * value)], 0)


def grid_rows(images, sides):
    return sum(images * side * side for side in sides)


def class_table(images, sides_out, padded):
    table = -np.ones((4, padded), np.int32)
    base_in, base_out = 0, 0
    for side in sides_out:
        extent = 2 * side
        for image in range(images):
            for row in range(side):
                for col in range(side):
                    for kind in range(4):
                        row_in, col_in = 2 * row + kind // 2, 2 * col + kind % 2
                        table[kind, base_out + row * side + col] = (
                            base_in + row_in * extent + col_in
                        )
            base_in += extent * extent
            base_out += side * side
    return table


def shift_table(images, sides_out, padded):
    table = -np.ones((9, padded), np.int32)
    base = 0
    for side in sides_out:
        for _ in range(images):
            for row in range(side):
                for col in range(side):
                    for which in range(9):
                        row_to, col_to = row + which // 3 - 1, col + which % 3 - 1
                        if 0 <= row_to < side and 0 <= col_to < side:
                            table[which, base + row * side + col] = base + row_to * side + col_to
            base += side * side
    return table


def one_hot(table, width):
    return (jnp.asarray(table)[..., None] == jnp.arange(width, dtype=jnp.int32)).astype(BF16)


def first_kernel(x_ref, w_ref, mask_ref, z_ref, stat_ref):
    z = dot_nn(x_ref[0], w_ref[...])
    z_ref[0] = z
    rows = stat_rows(z, mask_ref[...])

    @pl.when(pl.program_id(0) == 0)
    def _():
        stat_ref[...] = rows

    @pl.when(pl.program_id(0) > 0)
    def _():
        stat_ref[...] += rows


def side_kernel(x_ref, w_ref, mask_ref, z_ref, stat_ref):
    z = dot_nn(x_ref[0], w_ref[...])
    z_ref[...] = z
    stat_ref[...] = stat_rows(z, mask_ref[...])


def tap_forward(tap, stride):
    if stride == 1:
        return 0, tap
    row_tap, col_tap = tap // 3, tap % 3
    kind = jnp.where(row_tap == 1, 0, 2) + jnp.where(col_tap == 1, 0, 1)
    shift = jnp.where(row_tap == 0, 0, 3) + jnp.where(col_tap == 0, 0, 1)
    return kind, shift


def tap_backward(tap, stride):
    if stride == 1:
        return 0, 8 - tap
    row_tap, col_tap = tap // 3, tap % 3
    kind = jnp.where(row_tap == 1, 0, 2) + jnp.where(col_tap == 1, 0, 1)
    shift = jnp.where(row_tap == 0, 6, 3) + jnp.where(col_tap == 0, 2, 1)
    return kind, shift


def conv_kernel(count, kinds, stride):
    def body(*refs):
        z_ref = refs[0]
        parts = refs[1 : 1 + count]
        affine_ref, recip_ref, mask_ref, shift_ref, w_ref, act_ref, out_ref, stat_ref = refs[
            1 + count :
        ]
        tap = pl.program_id(0)

        @pl.when(tap == 0)
        def _():
            mean, inv = moments(parts, recip_ref[...])
            for kind in range(kinds):
                pre = affine_ref[0:1] * ((z_ref[kind] - mean) * inv) + affine_ref[1:2]
                act_ref[kind] = (pre * sigmoid(pre)).astype(BF16)

        kind, shift = tap_forward(tap, stride)
        patch = dot_nn(shift_ref[shift], act_ref[kind]).astype(BF16)
        term = dot_nn(patch, w_ref[...])

        @pl.when(tap == 0)
        def _():
            out_ref[...] = term

        @pl.when(tap > 0)
        def _():
            out_ref[...] += term

        @pl.when(tap == 8)
        def _():
            stat_ref[...] = stat_rows(out_ref[...], mask_ref[...])

    return body


def widen_kernel(count, carry):
    def body(*refs):
        z_ref = refs[0]
        parts = refs[1 : 1 + count]
        rest = refs[1 + count :]
        if carry:
            affine_ref, recip_ref, mask_ref, w_ref, side_ref, act_ref, out_ref, stat_ref = rest
        else:
            affine_ref, recip_ref, mask_ref, w_ref, act_ref, out_ref, stat_ref = rest

        @pl.when(pl.program_id(0) == 0)
        def _():
            mean, inv = moments(parts, recip_ref[...])
            pre = affine_ref[0:1] * ((z_ref[...] - mean) * inv) + affine_ref[1:2]
            act_ref[...] = (pre * sigmoid(pre)).astype(BF16)

        z = dot_nn(act_ref[...], w_ref[...])
        out_ref[...] = z
        if carry:
            stat_ref[...] = jnp.concatenate([stat_rows(z, mask_ref[...]), side_ref[...]], 0)
        else:
            stat_ref[...] = stat_rows(z, mask_ref[...])

    return body


def pair_moments(parts, recip):
    total = tree_sum([part[...] for part in parts]) * recip
    mean, mean_side = total[0:1], total[2:3]
    inv = lax.rsqrt(total[1:2] - mean * mean + EPS_NORM)
    inv_side = lax.rsqrt(total[3:4] - mean_side * mean_side + EPS_NORM)
    return mean, inv, mean_side, inv_side


def mix_kernel(count):
    def body(*refs):
        z_ref, side_ref = refs[:2]
        parts = refs[2 : 2 + count]
        (affine_ref, affine_side_ref, recip_ref, mask_ref, w_ref) = refs[2 + count : 7 + count]
        hidden_ref, low_ref, out_ref, stat_ref = refs[7 + count :]
        mean, inv, mean_side, inv_side = pair_moments(parts, recip_ref[...])
        pre = (
            affine_ref[0:1] * ((z_ref[...] - mean) * inv)
            + affine_ref[1:2]
            + affine_side_ref[0:1] * ((side_ref[...] - mean_side) * inv_side)
            + affine_side_ref[1:2]
        )
        hidden = pre * sigmoid(pre)
        hidden_ref[...] = hidden
        low = hidden.astype(BF16)
        low_ref[...] = low
        term = dot_nn(low, w_ref[...])

        @pl.when(pl.program_id(0) == 0)
        def _():
            out_ref[...] = term

        @pl.when(pl.program_id(0) > 0)
        def _():
            out_ref[...] += term

        @pl.when(pl.program_id(0) == pl.num_programs(0) - 1)
        def _():
            stat_ref[...] = stat_rows(out_ref[...], mask_ref[...])

    return body


def output_kernel(count):
    def body(*refs):
        z_ref = refs[0]
        parts = refs[1 : 1 + count]
        affine_ref, recip_ref, mask_ref, hidden_ref, cot_ref, y_ref, grad_ref, stat_ref = refs[
            1 + count :
        ]
        mean, inv = moments(parts, recip_ref[...])
        normed = (z_ref[...] - mean) * inv
        pre = affine_ref[0:1] * normed + affine_ref[1:2] + hidden_ref[...]
        gate = sigmoid(pre)
        y_ref[...] = (pre * gate).astype(BF16)
        grad = cot_ref[...].astype(F32) * mask_ref[...] * (gate * (1.0 + pre * (1.0 - gate)))
        grad_ref[...] = grad
        stat_ref[...] = jnp.concatenate([column_sum(grad), column_sum(grad * normed)], 0)

    return body


def norm_back(grad, normed, sums, recip, mask, scale):
    return scale * (grad - mask * (sums[0:1] * recip + normed * (sums[1:2] * recip)))


def back_linear_kernel(count):
    def body(*refs):
        grad_ref, z_ref = refs[:2]
        parts = refs[2 : 2 + count]
        sums = refs[2 + count : 2 + 2 * count]
        affine_ref, recip_ref, mask_ref, w_ref, below_ref = refs[2 + 2 * count : 7 + 2 * count]
        below_parts = refs[7 + 2 * count : 7 + 3 * count]
        below_affine_ref, dz_ref, out_ref, stat_ref = refs[7 + 3 * count :]
        recip = recip_ref[...]
        mean, inv = moments(parts, recip)
        total = tree_sum([part[...] for part in sums])
        normed = (z_ref[...] - mean) * inv
        dz = norm_back(grad_ref[...], normed, total, recip, mask_ref[...], affine_ref[0:1] * inv)
        dz = dz.astype(BF16)
        dz_ref[...] = dz
        term = dot_nt(dz, w_ref[...])

        @pl.when(pl.program_id(0) == 0)
        def _():
            out_ref[...] = term

        @pl.when(pl.program_id(0) > 0)
        def _():
            out_ref[...] += term

        @pl.when(pl.program_id(0) == pl.num_programs(0) - 1)
        def _():
            finish_below(out_ref, below_ref, below_parts, below_affine_ref, recip, stat_ref)

    return body


def finish_below(out_ref, below_ref, below_parts, below_affine_ref, recip, stat_ref):
    mean, inv = moments(below_parts, recip)
    normed = (below_ref[...] - mean) * inv
    pre = below_affine_ref[0:1] * normed + below_affine_ref[1:2]
    grad = out_ref[...] * slope(pre)
    out_ref[...] = grad
    stat_ref[...] = jnp.concatenate([column_sum(grad), column_sum(grad * normed)], 0)


def back_conv_kernel(count, kinds, stride):
    def body(*refs):
        grad_ref, z_ref = refs[:2]
        parts = refs[2 : 2 + count]
        sums = refs[2 + count : 2 + 2 * count]
        affine_ref, recip_ref, mask_ref, shift_ref, w_ref, below_ref = refs[
            2 + 2 * count : 8 + 2 * count
        ]
        below_parts = refs[8 + 2 * count : 8 + 3 * count]
        below_affine_ref, below_recip_ref, dz_ref, out_ref, stat_ref = refs[8 + 3 * count :]
        tap = pl.program_id(0)

        @pl.when(tap == 0)
        def _():
            recip = recip_ref[...]
            mean, inv = moments(parts, recip)
            total = tree_sum([part[...] for part in sums])
            normed = (z_ref[...] - mean) * inv
            dz = norm_back(
                grad_ref[...], normed, total, recip, mask_ref[...], affine_ref[0:1] * inv
            )
            dz_ref[...] = dz.astype(BF16)
            out_ref[...] = jnp.zeros_like(out_ref)

        kind, shift = tap_backward(tap, stride)
        patch = dot_nn(shift_ref[shift], dz_ref[...]).astype(BF16)
        out_ref[kind] += dot_nt(patch, w_ref[...])

        @pl.when(tap == 8)
        def _():
            mean, inv = moments(below_parts, below_recip_ref[...])
            rows = None
            for which in range(kinds):
                normed = (below_ref[which] - mean) * inv
                pre = below_affine_ref[0:1] * normed + below_affine_ref[1:2]
                grad = out_ref[which] * slope(pre)
                out_ref[which] = grad
                part = jnp.concatenate([column_sum(grad), column_sum(grad * normed)], 0)
                rows = part if rows is None else rows + part
            stat_ref[...] = rows

    return body


def back_mix_kernel(count):
    def body(*refs):
        grad_ref, z_ref = refs[:2]
        parts = refs[2 : 2 + count]
        sums = refs[2 + count : 2 + 2 * count]
        affine_ref, recip_ref, mask_ref, w_ref, above_ref, mid_ref, side_ref = refs[
            2 + 2 * count : 9 + 2 * count
        ]
        pair_parts = refs[9 + 2 * count : 9 + 3 * count]
        affine_mid_ref, affine_side_ref, dz_ref, out_ref, stat_ref = refs[9 + 3 * count :]
        recip = recip_ref[...]

        @pl.when(pl.program_id(0) == 0)
        def _():
            mean, inv = moments(parts, recip)
            total = tree_sum([part[...] for part in sums])
            normed = (z_ref[...] - mean) * inv
            dz = norm_back(
                grad_ref[...], normed, total, recip, mask_ref[...], affine_ref[0:1] * inv
            )
            dz_ref[...] = dz.astype(BF16)

        mean, inv, mean_side, inv_side = pair_moments(pair_parts, recip)
        normed = (mid_ref[...] - mean) * inv
        normed_side = (side_ref[...] - mean_side) * inv_side
        pre = (
            affine_mid_ref[0:1] * normed
            + affine_mid_ref[1:2]
            + affine_side_ref[0:1] * normed_side
            + affine_side_ref[1:2]
        )
        grad = (above_ref[...] + dot_nt(dz_ref[...], w_ref[...])) * slope(pre)
        out_ref[...] = grad
        stat_ref[...] = jnp.concatenate(
            [column_sum(grad), column_sum(grad * normed), column_sum(grad * normed_side)], 0
        )

    return body


def back_pair_kernel(count):
    def body(*refs):
        grad_ref, mid_ref, side_ref = refs[:3]
        pair_parts = refs[3 : 3 + count]
        sums = refs[3 + count : 3 + 2 * count]
        affine_mid_ref, affine_side_ref, recip_ref, mask_ref, w_ref, below_ref = refs[
            3 + 2 * count : 9 + 2 * count
        ]
        below_parts = refs[9 + 2 * count : 9 + 3 * count]
        below_affine_ref, dz_ref, dz_side_ref, out_ref, stat_ref = refs[9 + 3 * count :]
        recip = recip_ref[...]
        mean, inv, mean_side, inv_side = pair_moments(pair_parts, recip)
        total = tree_sum([part[...] for part in sums])
        normed = (mid_ref[...] - mean) * inv
        normed_side = (side_ref[...] - mean_side) * inv_side
        grad = grad_ref[...]
        mask = mask_ref[...]
        dz = norm_back(grad, normed, total[0:2], recip, mask, affine_mid_ref[0:1] * inv)
        dz = dz.astype(BF16)
        dz_ref[...] = dz
        total_side = jnp.concatenate([total[0:1], total[2:3]], 0)
        dz_side_ref[...] = norm_back(
            grad, normed_side, total_side, recip, mask, affine_side_ref[0:1] * inv_side
        ).astype(BF16)
        term = dot_nt(dz, w_ref[...])

        @pl.when(pl.program_id(0) == 0)
        def _():
            out_ref[...] = term

        @pl.when(pl.program_id(0) > 0)
        def _():
            out_ref[...] += term

        @pl.when(pl.program_id(0) == pl.num_programs(0) - 1)
        def _():
            finish_below(out_ref, below_ref, below_parts, below_affine_ref, recip, stat_ref)

    return body


def back_first_kernel(count):
    def body(*refs):
        grad_ref, z_ref = refs[:2]
        parts = refs[2 : 2 + count]
        sums = refs[2 + count : 2 + 2 * count]
        affine_ref, recip_ref, mask_ref, x_ref, _, dz_ref, grad_w_ref, total_ref = refs[
            2 + 2 * count :
        ]
        recip = recip_ref[...]
        mean, inv = moments(parts, recip)
        total = tree_sum([part[...] for part in sums])
        normed = (z_ref[0] - mean) * inv
        dz = norm_back(grad_ref[0], normed, total, recip, mask_ref[...], affine_ref[0:1] * inv)
        dz = dz.astype(BF16)
        dz_ref[0] = dz
        term = dot_tn(x_ref[0], dz)

        @pl.when(pl.program_id(0) == 0)
        def _():
            total_ref[...] = term

        @pl.when(pl.program_id(0) > 0)
        def _():
            total_ref[...] += term

        @pl.when(pl.program_id(0) == pl.num_programs(0) - 1)
        def _():
            grad_w_ref[...] = total_ref[...].astype(BF16)

    return body


def weight_grad_kernel(act_ref, dz_ref, *rest):
    rest[-1][...] = dot_tn(act_ref[...], dz_ref[...]).astype(BF16)


def conv_grad_kernel(stride):
    def body(act_ref, shift_ref, dz_ref, *rest):
        kind, shift = tap_forward(pl.program_id(0), stride)
        patch = dot_nn(shift_ref[shift], act_ref[kind]).astype(BF16)
        rest[-1][...] = dot_tn(patch, dz_ref[...]).astype(BF16)

    return body


def level_masks(first_row, rows, bounds):
    index = first_row + lax.broadcasted_iota(jnp.int32, (rows, 1), 0)
    return [
        ((index >= bounds[level]) & (index < bounds[level + 1])).astype(F32)
        for level in range(len(bounds) - 1)
    ]


def tally_kernel(bounds):
    levels = len(bounds) - 1

    def body(first_ref, grad_ref, master_ref, old_ref, rows_ref, sums_ref):
        grad = grad_ref[...]
        master = master_ref[...]
        square = grad * grad
        raised = square + EPS_ONE
        rows_new = DECAY * old_ref[...] + (1.0 - DECAY) * jnp.mean(raised, 1, keepdims=True)
        rows_ref[...] = rows_new
        ratio = square / rows_new
        weight = jnp.sum(master * master, 1, keepdims=True)
        masks = level_masks(first_ref[0], grad.shape[0], bounds)
        spread = jnp.zeros((1, grad.shape[1]), F32)
        for level in range(levels):
            mask = masks[level]
            sums_ref[level : level + 1] = column_sum(raised * mask)
            sums_ref[levels + level : levels + level + 1] = column_sum(ratio * mask)
            low = 2 * levels + level
            sums_ref[low : low + 1] = spread + column_sum(rows_new * mask)
            low = 3 * levels + level
            sums_ref[low : low + 1] = spread + column_sum(weight * mask)

    return body


def renew_kernel(bounds):
    levels = len(bounds) - 1

    def body(first_ref, grad_ref, master_ref, rows_ref, sums_ref, old_ref, cols_ref, new_ref, low_ref):
        grad = grad_ref[...]
        columns = grad.shape[1]
        masks = level_masks(first_ref[0], grad.shape[0], bounds)
        factor = None
        for level in range(levels):
            height = float(bounds[level + 1] - bounds[level])
            cells = height * columns
            col_sum = sums_ref[level : level + 1]
            ratio_sum = sums_ref[levels + level : levels + level + 1]
            row_mean = sums_ref[2 * levels + level : 2 * levels + level + 1] / height
            weight_sum = sums_ref[3 * levels + level : 3 * levels + level + 1]
            cols_new = DECAY * old_ref[level : level + 1] + (1.0 - DECAY) * (col_sum / height)
            cols_ref[level : level + 1] = cols_new
            relative = cols_new / row_mean
            update_sq = jnp.sum(ratio_sum / relative, axis=1, keepdims=True)
            update_rms = jnp.sqrt(update_sq / cells)
            weight_rms = jnp.sqrt(weight_sum / cells)
            step = STEP_RATE * jnp.maximum(EPS_TWO, weight_rms) / jnp.maximum(1.0, update_rms)
            part = masks[level] * (step * lax.rsqrt(relative))
            factor = part if factor is None else factor + part
        new = master_ref[...] - grad * lax.rsqrt(rows_ref[...]) * factor
        new_ref[...] = new
        low_ref[...] = new.astype(BF16)

    return body


class Exchange:
    def __init__(self, n_wide, n_narrow):
        self.n_narrow = n_narrow
        self.total = n_wide * n_narrow
        self.bits = self.total.bit_length() - 1
        self.narrow_bits = n_narrow.bit_length() - 1
        self.index = lax.axis_index(AXES)

    def bit(self, level):
        return (self.index >> level) & 1

    def swap(self, value, level):
        pairs = [(device, device ^ (1 << level)) for device in range(self.total)]
        return lax.ppermute(value, AXES, pairs)

    def group_parts(self, value):
        return [value] + [
            lax.ppermute(value, "narrow", [(i, i ^ k) for i in range(self.n_narrow)])
            for k in range(1, self.n_narrow)
        ]

    def total_sum(self, value, first=0):
        for level in range(first, self.bits):
            value = value + self.swap(value, level)
        return value

    def scatter(self, part, prefix):
        open_bits = self.bits - len(prefix)
        rows = part.shape[0] >> open_bits
        current = part
        for level in range(open_bits):
            view = current.reshape((1 << (open_bits - level - 1), 2, rows, part.shape[1]))
            mine = self.bit(level)
            sent = lax.dynamic_index_in_dim(view, 1 - mine, 1, keepdims=False)
            kept = lax.dynamic_index_in_dim(view, mine, 1, keepdims=False)
            came = self.swap(sent, level)
            current = self.add(kept, came, level)
        current = current.reshape(rows, part.shape[1])
        for level in range(open_bits, self.bits):
            want = prefix[level - open_bits]
            pairs = []
            for device in range(self.total):
                settled = all(
                    (device >> other) & 1 == prefix[other - open_bits]
                    for other in range(open_bits, level)
                )
                if settled and (device >> level) & 1 != want:
                    pairs.append((device, device ^ (1 << level)))
            came = lax.ppermute(current, AXES, pairs)
            current = self.add(current, came, level)
        return current

    def add(self, kept, came, level):
        total = kept.astype(F32) + came.astype(F32)
        return total if level == self.bits - 1 else total.astype(BF16)


def make_body(mesh):
    n_wide, n_narrow = mesh.shape["wide"], mesh.shape["narrow"]

    def body(
        x_lo,
        x_mid,
        x_hi,
        cot_lo,
        cot_mid,
        cot_hi,
        live_counts,
        slim_master,
        broad_master,
        slim_rowstat,
        broad_rowstat,
        slim_colstat,
        broad_colstat,
        norm_params,
        norm_moments,
    ):
        link = Exchange(n_wide, n_narrow)
        count = n_narrow
        images = x_lo.shape[0]
        sides = tuple(value.shape[1] // 2 for value in (x_lo, x_mid, x_hi))
        c_in, mid, c_out = x_lo.shape[3], slim_master.shape[1], broad_master.shape[1]
        cells = grid_rows(images, sides)
        cells_in = 4 * cells
        rows = -(-cells // 16) * 16
        chunks = c_out // mid
        bounds_slim = (0, c_in, c_in + 9 * mid, c_in + 9 * mid + c_out, c_in + 18 * mid + c_out)
        bounds_broad = (0, mid, mid + c_in, 2 * mid + c_in)
        at_two, at_four, at_five = (bounds_slim[level] // mid for level in (1, 2, 3))
        at_six = bounds_broad[2] // mid
        widths = (mid, mid, c_out, c_out, mid, mid, c_out)
        norm_at = [sum(widths[:level]) // mid for level in range(7)]

        slim = lax.all_gather(slim_master.astype(BF16), AXES, axis=0, tiled=True)
        broad = lax.all_gather(broad_master.astype(BF16), AXES, axis=0, tiled=True)

        kinds = class_table(images, sides, rows)
        shifts = one_hot(shift_table(images, sides, rows), rows)
        x_flat = jnp.concatenate([value.reshape(-1, c_in) for value in (x_lo, x_mid, x_hi)], 0)
        x_kinds = jnp.dot(one_hot(kinds.reshape(-1), cells_in), x_flat, preferred_element_type=F32)
        x_kinds = x_kinds.astype(BF16).reshape(4, rows, c_in)
        cot = jnp.concatenate(
            [value.reshape(-1, c_out) for value in (cot_lo, cot_mid, cot_hi)]
            + [jnp.zeros((rows - cells, c_out), BF16)],
            0,
        )
        alive = [
            (jnp.arange(images) < live_counts[0, level]).astype(F32) for level in range(3)
        ]
        mask = jnp.concatenate(
            [jnp.repeat(alive[level], side * side) for level, side in enumerate(sides)]
            + [jnp.zeros((rows - cells,), F32)]
        )
        cell_count = lax.psum(jnp.sum(mask), "narrow")
        mask = mask[:, None]
        recip = (1.0 / cell_count).reshape(1, 1)
        recip_in = (0.25 / cell_count).reshape(1, 1)

        narrow_all = whole((rows, mid))
        kinds_all = whole((4, rows, mid))
        stat_all = whole((2, mid))
        mask_all = whole((rows, 1))
        one_all = whole((1, 1))
        shifts_all = whole((9, rows, rows))
        chunk = block((rows, mid), lambda j: (0, j))

        def stat_chunk(height):
            return block((height, mid), lambda j: (0, j))

        def affine(level):
            return block((2, mid), lambda j: (0, norm_at[level]))

        def affine_chunk(level):
            return block((2, mid), lambda j: (0, norm_at[level] + j))

        def slim_block(at):
            return block((mid, mid), lambda j: (at + j, 0))

        def broad_block(at):
            return block((mid, mid), lambda j: (at, j))

        narrow_f32 = shape_of((rows, mid), F32)
        wide_f32 = shape_of((rows, c_out), F32)
        narrow_low = shape_of((rows, mid), BF16)
        wide_low = shape_of((rows, c_out), BF16)
        stat_narrow = shape_of((2, mid), F32)
        stat_wide = shape_of((2, c_out), F32)
        flops_conv = 2 * rows * 9 * mid * (mid + rows)
        flops_wide = 2 * rows * mid * c_out

        z_one, stat = kernel_call(
            first_kernel,
            "first",
            (4,),
            [
                block((1, rows, c_in), lambda j: (j, 0, 0)),
                whole((c_in, mid)),
                mask_all,
            ],
            [block((1, rows, mid), lambda j: (j, 0, 0)), stat_all],
            [shape_of((4, rows, mid), F32), stat_narrow],
            2 * 4 * rows * c_in * mid,
        )(x_kinds, slim, mask)
        parts_one = link.group_parts(stat)
        z_side, stat_side = kernel_call(
            side_kernel,
            "side",
            (chunks,),
            [
                block((1, rows, c_in), lambda j: (0, 0, 0)),
                block((c_in, mid), lambda j: (0, j)),
                mask_all,
            ],
            [chunk, stat_chunk(2)],
            [wide_f32, stat_wide],
            2 * rows * c_in * c_out,
        )(x_kinds, broad[mid : mid + c_in], mask)
        act_one, z_two, stat = kernel_call(
            conv_kernel(count, 4, 2),
            "conv_two",
            (9,),
            [kinds_all]
            + [stat_all] * count
            + [affine(0), one_all, mask_all, shifts_all, slim_block(at_two)],
            [kinds_all, narrow_all, stat_all],
            [shape_of((4, rows, mid), BF16), narrow_f32, stat_narrow],
            flops_conv,
        )(z_one, *parts_one, norm_params, recip_in, mask, shifts, slim)
        parts_two = link.group_parts(stat)
        act_two, z_three, stat = kernel_call(
            widen_kernel(count, True),
            "widen_three",
            (chunks,),
            [narrow_all]
            + [stat_all] * count
            + [affine(1), one_all, mask_all, broad_block(0), stat_chunk(2)],
            [narrow_all, chunk, stat_chunk(4)],
            [narrow_low, wide_f32, shape_of((4, c_out), F32)],
            flops_wide,
        )(z_two, *parts_two, norm_params, recip, mask, broad, stat_side)
        parts_pair = link.group_parts(stat)
        hidden, hidden_low, z_four, stat = kernel_call(
            mix_kernel(count),
            "mix",
            (chunks,),
            [chunk, chunk]
            + [stat_chunk(4)] * count
            + [affine_chunk(2), affine_chunk(3), one_all, mask_all, slim_block(at_four)],
            [chunk, chunk, narrow_all, stat_all],
            [wide_f32, wide_low, narrow_f32, stat_narrow],
            flops_wide,
        )(z_three, z_side, *parts_pair, norm_params, norm_params, recip, mask, slim)
        parts_four = link.group_parts(stat)
        one_kind = whole((1, rows, mid))
        act_four, z_five, stat = kernel_call(
            conv_kernel(count, 1, 1),
            "conv_five",
            (9,),
            [one_kind]
            + [stat_all] * count
            + [affine(4), one_all, mask_all, shifts_all, slim_block(at_five)],
            [one_kind, narrow_all, stat_all],
            [shape_of((1, rows, mid), BF16), narrow_f32, stat_narrow],
            flops_conv,
        )(z_four[None], *parts_four, norm_params, recip, mask, shifts, slim)
        parts_five = link.group_parts(stat)
        act_five, z_six, stat = kernel_call(
            widen_kernel(count, False),
            "widen_six",
            (chunks,),
            [narrow_all]
            + [stat_all] * count
            + [affine(5), one_all, mask_all, broad_block(at_six)],
            [narrow_all, chunk, stat_chunk(2)],
            [narrow_low, wide_f32, stat_wide],
            flops_wide,
        )(z_five, *parts_five, norm_params, recip, mask, broad)
        parts_six = link.group_parts(stat)
        y, grad_out, stat = kernel_call(
            output_kernel(count),
            "output",
            (chunks,),
            [chunk]
            + [stat_chunk(2)] * count
            + [affine_chunk(6), one_all, mask_all, chunk, chunk],
            [chunk, chunk, stat_chunk(2)],
            [wide_low, wide_f32, stat_wide],
            flops_wide // 8,
        )(z_six, *parts_six, norm_params, recip, mask, hidden, cot)
        sums_six = link.group_parts(stat)

        dz_six, grad_five, stat = kernel_call(
            back_linear_kernel(count),
            "back_six",
            (chunks,),
            [chunk, chunk]
            + [stat_chunk(2)] * (2 * count)
            + [affine_chunk(6), one_all, mask_all, broad_block(at_six), narrow_all]
            + [stat_all] * count
            + [affine(5)],
            [chunk, narrow_all, stat_all],
            [wide_low, narrow_f32, stat_narrow],
            flops_wide,
        )(
            grad_out,
            z_six,
            *parts_six,
            *sums_six,
            norm_params,
            recip,
            mask,
            broad,
            z_five,
            *parts_five,
            norm_params,
        )
        sums_five = link.group_parts(stat)

        def weight_grad(act, dz, steps, act_at, out_shape, out_at, base, name):
            high, across = steps
            height = act.shape[0]
            specs = [
                block((height, mid), lambda i, j: (0, act_at + i)),
                block((height, mid), lambda i, j: (0, j)),
            ]
            args = [act, dz]
            if base is not None:
                specs.append(pl.BlockSpec(memory_space=pl.ANY))
                args.append(base)
            return kernel_call(
                weight_grad_kernel,
                name,
                (high, across),
                specs,
                block((mid, mid), lambda i, j: (out_at + i, j)),
                shape_of(out_shape, BF16),
                2 * height * mid * mid * high * across,
                aliases={2: 0} if base is not None else None,
            )(*args)

        def conv_grad(act, dz, stride, out_at, base, name):
            kinds_here = act.shape[0]
            return kernel_call(
                conv_grad_kernel(stride),
                name,
                (9,),
                [
                    whole((kinds_here, rows, mid)),
                    shifts_all,
                    narrow_all,
                    pl.BlockSpec(memory_space=pl.ANY),
                ],
                block((mid, mid), lambda t: (out_at + t, 0)),
                shape_of(base.shape, BF16),
                flops_conv,
                aliases={3: 0},
            )(act, shifts, dz, base)

        half = bounds_slim[-1] // 2
        quarter = bounds_broad[-1] // 4
        term_six = weight_grad(act_five, dz_six, (1, chunks), 0, (mid, c_out), 0, None, "grad_six")
        broad_three = link.scatter(term_six, (1, 1))

        dz_five, grad_four, stat = kernel_call(
            back_conv_kernel(count, 1, 1),
            "back_five",
            (9,),
            [narrow_all, narrow_all]
            + [stat_all] * (2 * count)
            + [affine(5), one_all, mask_all, shifts_all, slim_block(at_five), one_kind]
            + [stat_all] * count
            + [affine(4), one_all],
            [narrow_all, one_kind, stat_all],
            [narrow_low, shape_of((1, rows, mid), F32), stat_narrow],
            flops_conv,
        )(
            grad_five,
            z_five,
            *parts_five,
            *sums_five,
            norm_params,
            recip,
            mask,
            shifts,
            slim,
            z_four[None],
            *parts_four,
            norm_params,
            recip,
        )
        grad_four = grad_four[0]
        sums_four = link.group_parts(stat)
        dz_four, grad_mid, stat = kernel_call(
            back_mix_kernel(count),
            "back_four",
            (chunks,),
            [narrow_all, narrow_all]
            + [stat_all] * (2 * count)
            + [affine(4), one_all, mask_all, slim_block(at_four), chunk, chunk, chunk]
            + [stat_chunk(4)] * count
            + [affine_chunk(2), affine_chunk(3)],
            [narrow_all, chunk, stat_chunk(3)],
            [narrow_low, wide_f32, shape_of((3, c_out), F32)],
            flops_wide,
        )(
            grad_four,
            z_four,
            *parts_four,
            *sums_four,
            norm_params,
            recip,
            mask,
            slim,
            grad_out,
            z_three,
            z_side,
            *parts_pair,
            norm_params,
            norm_params,
        )
        sums_pair = link.group_parts(stat)
        low_four = half // mid - at_four
        slim_high = weight_grad(
            hidden_low,
            dz_four,
            (chunks - low_four, 1),
            low_four,
            (half, mid),
            0,
            None,
            "grad_four",
        )
        slim_high = conv_grad(
            act_four, dz_five, 1, at_five - half // mid, slim_high, "grad_five"
        )
        slim_high = link.scatter(slim_high, (1,))

        dz_three, dz_side, grad_two, stat = kernel_call(
            back_pair_kernel(count),
            "back_three",
            (chunks,),
            [chunk, chunk, chunk]
            + [stat_chunk(4)] * count
            + [stat_chunk(3)] * count
            + [affine_chunk(2), affine_chunk(3), one_all, mask_all, broad_block(0), narrow_all]
            + [stat_all] * count
            + [affine(1)],
            [chunk, chunk, narrow_all, stat_all],
            [wide_low, wide_low, narrow_f32, stat_narrow],
            flops_wide,
        )(
            grad_mid,
            z_three,
            z_side,
            *parts_pair,
            *sums_pair,
            norm_params,
            norm_params,
            recip,
            mask,
            broad,
            z_two,
            *parts_two,
            norm_params,
        )
        sums_two = link.group_parts(stat)
        x_sub = x_kinds[0]
        broad_low = weight_grad(
            act_two, dz_three, (1, chunks), 0, (2 * quarter, c_out), 0, None, "grad_three"
        )
        broad_low = weight_grad(
            x_sub, dz_side, (1, chunks), 0, (2 * quarter, c_out), 1, broad_low, "grad_side_low"
        )
        broad_low = link.scatter(broad_low, (0,))
        broad_two = weight_grad(
            x_sub, dz_side, (1, chunks), 1, (quarter, c_out), 0, None, "grad_side_high"
        )
        broad_two = link.scatter(broad_two, (0, 1))

        dz_two, grad_one, stat = kernel_call(
            back_conv_kernel(count, 4, 2),
            "back_two",
            (9,),
            [narrow_all, narrow_all]
            + [stat_all] * (2 * count)
            + [affine(1), one_all, mask_all, shifts_all, slim_block(at_two), kinds_all]
            + [stat_all] * count
            + [affine(0), one_all],
            [narrow_all, kinds_all, stat_all],
            [narrow_low, shape_of((4, rows, mid), F32), stat_narrow],
            flops_conv,
        )(
            grad_two,
            z_two,
            *parts_two,
            *sums_two,
            norm_params,
            recip,
            mask,
            shifts,
            slim,
            z_one,
            *parts_one,
            norm_params,
            recip_in,
        )
        sums_one = link.group_parts(stat)
        slim_low = weight_grad(
            hidden_low, dz_four, (low_four, 1), 0, (half, mid), at_four, None, "grad_four_low"
        )
        slim_low = conv_grad(act_one, dz_two, 2, at_two, slim_low, "grad_two")
        dz_one, slim_low = kernel_call(
            back_first_kernel(count),
            "back_one",
            (4,),
            [block((1, rows, mid), lambda j: (j, 0, 0))] * 2
            + [stat_all] * (2 * count)
            + [
                affine(0),
                one_all,
                mask_all,
                block((1, rows, c_in), lambda j: (j, 0, 0)),
                pl.BlockSpec(memory_space=pl.ANY),
            ],
            [block((1, rows, mid), lambda j: (j, 0, 0)), whole((c_in, mid))],
            [shape_of((4, rows, mid), BF16), shape_of((half, mid), BF16)],
            2 * 4 * rows * c_in * mid,
            scratch=[pltpu.VMEM((c_in, mid), F32)],
            aliases={2 + 2 * count + 4: 1},
        )(grad_one, z_one, *parts_one, *sums_one, norm_params, recip_in, mask, x_kinds, slim_low)
        slim_low = link.scatter(slim_low, (0,))

        back_rows = -np.ones((cells_in,), np.int32)
        side_rows = -np.ones((cells_in,), np.int32)
        for kind in range(4):
            for row in range(cells):
                back_rows[kinds[kind, row]] = kind * rows + row
        side_rows[kinds[0, :cells]] = np.arange(cells)
        dz_natural = jnp.dot(
            one_hot(back_rows, 4 * rows),
            dz_one.reshape(4 * rows, mid),
            preferred_element_type=F32,
        ).astype(BF16)
        side_natural = jnp.dot(
            one_hot(side_rows, rows), dz_side, preferred_element_type=F32
        ).astype(BF16)
        grad_x = dot_nt(dz_natural, slim[:c_in]) + dot_nt(side_natural, broad[mid : mid + c_in])

        def split(flat, extents):
            pieces = []
            offset = 0
            for extent in extents:
                length = images * extent * extent
                pieces.append(
                    flat[offset : offset + length].reshape(images, extent, extent, flat.shape[1])
                )
                offset += length
            return pieces

        y_parts = split(y, sides)
        dx_parts = split(grad_x, tuple(2 * side for side in sides))

        top = link.bit(link.bits - 1)
        second = link.bit(link.bits - 2)
        slim_grad = jnp.where(top == 1, slim_high, slim_low)
        broad_grad = jnp.where(
            top == 0, broad_low, jnp.where(second == 1, broad_three, broad_two)
        )

        def optimize(grad, master, rowstat, colstat, bounds, name):
            height, columns = grad.shape
            levels = len(bounds) - 1
            first = (link.index * height).astype(jnp.int32).reshape(1)
            scalar = pl.BlockSpec(memory_space=pltpu.SMEM)
            matrix, column = whole((height, columns)), whole((height, 1))
            sums_all, cols_all = whole((4 * levels, columns)), whole((levels, columns))
            rows_new, sums = kernel_call(
                tally_kernel(bounds),
                name + "_tally",
                (1,),
                [scalar, matrix, matrix, column],
                [column, sums_all],
                [shape_of((height, 1), F32), shape_of((4 * levels, columns), F32)],
                20 * height * columns,
            )(first, grad, master, rowstat.reshape(height, 1))
            sums = link.total_sum(sums)
            cols_new, new, low = kernel_call(
                renew_kernel(bounds),
                name + "_renew",
                (1,),
                [scalar, matrix, matrix, column, sums_all, cols_all],
                [cols_all, matrix, matrix],
                [
                    shape_of((levels, columns), F32),
                    shape_of((height, columns), F32),
                    shape_of((height, columns), BF16),
                ],
                20 * height * columns,
            )(first, grad, master, rows_new, sums, colstat)
            return rows_new.reshape(height), cols_new, new, low

        broad_rows_new, broad_cols_new, broad_new, broad_copy = optimize(
            broad_grad, broad_master, broad_rowstat, broad_colstat, bounds_broad, "broad"
        )
        slim_rows_new, slim_cols_new, slim_new, slim_copy = optimize(
            slim_grad, slim_master, slim_rowstat, slim_colstat, bounds_slim, "slim"
        )

        pair = tree_sum(sums_pair)
        norm_sums = [
            tree_sum(sums_one),
            tree_sum(sums_two),
            pair[0:2],
            pair[0:3:2],
            tree_sum(sums_four),
            tree_sum(sums_five),
            tree_sum(sums_six),
        ]
        norm_grad = jnp.concatenate(norm_sums, 1)[::-1]
        norm_grad = link.total_sum(norm_grad, link.narrow_bits)
        norm_moments_new = DECAY * norm_moments + (1.0 - DECAY) * (
            norm_grad * norm_grad + EPS_ONE
        )
        norm_update = norm_grad * lax.rsqrt(norm_moments_new)
        update_rms = jnp.sqrt(jnp.mean(norm_update * norm_update, 1))
        weight_rms = jnp.sqrt(jnp.mean(norm_params * norm_params, 1))
        step = STEP_RATE * jnp.maximum(EPS_TWO, weight_rms) / jnp.maximum(1.0, update_rms)
        norm_new = norm_params - step[:, None] * norm_update
        return (
            *y_parts,
            *dx_parts,
            slim_grad,
            broad_grad,
            slim_rows_new,
            broad_rows_new,
            slim_cols_new,
            broad_cols_new,
            slim_new,
            broad_new,
            slim_copy,
            broad_copy,
            norm_grad,
            norm_moments_new,
            norm_new,
        )

    return body


def solution(mesh):
    split = P(AXES)
    return jax.shard_map(
        make_body(mesh),
        mesh=mesh,
        in_specs=(split,) * 11 + (P(),) * 4,
        out_specs=(split,) * 10 + (P(),) * 2 + (split,) * 4 + (P(),) * 3,
        check_vma=False,
    )
```

```python
import jax
import jax.numpy as jnp
import numpy as np
from jax import lax
from jax.experimental import pallas as pl
from jax.experimental.pallas import tpu as pltpu
from jax.sharding import PartitionSpec as P

STEP = 10
EPS_NORM = 1e-05
EPS_ONE = 1e-30
EPS_TWO = 0.001
STEP_RATE = 0.3
DECAY = 1.0 - STEP ** (-0.8)
AXES = ("wide", "narrow")
BF16 = jnp.bfloat16
F32 = jnp.float32
VMEM_LIMIT = 48 * 1024 * 1024


def shape_of(dims, dtype):
    return jax.ShapeDtypeStruct(dims, dtype)


def whole(dims):
    return pl.BlockSpec(dims, lambda *step: (0,) * len(dims))


def block(dims, place):
    return pl.BlockSpec(dims, place)


class Kernels:
    def __init__(self):
        self.last = None

    def __call__(
        self,
        body,
        name,
        grid,
        in_specs,
        out_specs,
        out_shape,
        flops,
        scratch=(),
        aliases=None,
        after=(),
        scalars=0,
    ):
        after = [value for value in (*after, self.last) if value is not None]
        taken = scalars + len(in_specs)

        def trimmed(*refs):
            body(*refs[:taken], *refs[taken + len(after) :])

        call = pl.pallas_call(
            trimmed,
            grid_spec=pltpu.PrefetchScalarGridSpec(
                num_scalar_prefetch=scalars,
                grid=grid,
                in_specs=list(in_specs) + [pl.BlockSpec(memory_space=pl.ANY)] * len(after),
                out_specs=out_specs,
                scratch_shapes=list(scratch),
            ),
            out_shape=out_shape,
            input_output_aliases=aliases or {},
            cost_estimate=pl.CostEstimate(
                flops=flops, bytes_accessed=flops // 200, transcendentals=0
            ),
            compiler_params=pltpu.CompilerParams(vmem_limit_bytes=VMEM_LIMIT),
            name=name,
        )

        def run(*args):
            out = call(*args, *after)
            self.last = out[0] if isinstance(out, (list, tuple)) else out
            return out

        return run


def dot_nn(first, second):
    return jnp.dot(first, second, preferred_element_type=F32)


def dot_nt(first, second):
    return lax.dot_general(first, second, (((1,), (1,)), ((), ())), preferred_element_type=F32)


def dot_tn(first, second):
    return lax.dot_general(first, second, (((0,), (0,)), ((), ())), preferred_element_type=F32)


def sigmoid(value):
    return 1.0 / (1.0 + jnp.exp(-value))


def slope(value):
    gate = sigmoid(value)
    return gate * (1.0 + value * (1.0 - gate))


def tree_sum(values):
    values = list(values)
    while len(values) > 1:
        values = [values[i] + values[i + 1] for i in range(0, len(values), 2)]
    return values[0]


def moments(parts, recip):
    total = tree_sum([part[...] for part in parts]) * recip
    mean = total[0:1]
    return mean, lax.rsqrt(total[1:2] - mean * mean + EPS_NORM)


def column_sum(value):
    return jnp.sum(value, axis=0, keepdims=True)


def stat_rows(value, mask):
    kept = value * mask
    return jnp.concatenate([column_sum(kept), column_sum(kept * value)], 0)


def grid_rows(images, sides):
    return sum(images * side * side for side in sides)


def class_table(images, sides_out, padded):
    table = -np.ones((4, padded), np.int32)
    base_in, base_out = 0, 0
    for side in sides_out:
        extent = 2 * side
        for row in range(side):
            for col in range(side):
                for image in range(images):
                    for kind in range(4):
                        cell = (2 * row + kind // 2) * extent + 2 * col + kind % 2
                        table[kind, base_out + (row * side + col) * images + image] = (
                            base_in + cell * images + image
                        )
        base_in += images * extent * extent
        base_out += images * side * side
    return table


def shift_table(images, sides_out, padded):
    table = -np.ones((9, padded), np.int32)
    base = 0
    for side in sides_out:
        for row in range(side):
            for col in range(side):
                for which in range(9):
                    row_to, col_to = row + which // 3 - 1, col + which % 3 - 1
                    if 0 <= row_to < side and 0 <= col_to < side:
                        for image in range(images):
                            table[which, base + (row * side + col) * images + image] = (
                                base + (row_to * side + col_to) * images + image
                            )
        base += images * side * side
    return table


def one_hot(table, width):
    return (jnp.asarray(table)[..., None] == jnp.arange(width, dtype=jnp.int32)).astype(BF16)


def first_kernel(x_ref, w_ref, mask_ref, z_ref, stat_ref):
    z = dot_nn(x_ref[0], w_ref[...])
    z_ref[0] = z
    rows = stat_rows(z, mask_ref[...])

    @pl.when(pl.program_id(0) == 0)
    def _():
        stat_ref[...] = rows

    @pl.when(pl.program_id(0) > 0)
    def _():
        stat_ref[...] += rows


def side_kernel(x_ref, w_ref, mask_ref, z_ref, stat_ref):
    term = dot_nn(x_ref[0], w_ref[...])

    @pl.when(pl.program_id(1) == 0)
    def _():
        z_ref[...] = term

    @pl.when(pl.program_id(1) > 0)
    def _():
        z_ref[...] += term

    @pl.when(pl.program_id(1) == pl.num_programs(1) - 1)
    def _():
        stat_ref[...] = stat_rows(z_ref[...], mask_ref[...])


def tap_forward(tap, stride):
    if stride == 1:
        return 0, tap
    row_tap, col_tap = tap // 3, tap % 3
    kind = jnp.where(row_tap == 1, 0, 2) + jnp.where(col_tap == 1, 0, 1)
    shift = jnp.where(row_tap == 0, 0, 3) + jnp.where(col_tap == 0, 0, 1)
    return kind, shift


def tap_backward(tap, stride):
    if stride == 1:
        return 0, 8 - tap
    row_tap, col_tap = tap // 3, tap % 3
    kind = jnp.where(row_tap == 1, 0, 2) + jnp.where(col_tap == 1, 0, 1)
    shift = jnp.where(row_tap == 0, 6, 3) + jnp.where(col_tap == 0, 2, 1)
    return kind, shift


def conv_kernel(count, kinds, stride):
    def body(*refs):
        z_ref = refs[0]
        parts = refs[1 : 1 + count]
        affine_ref, recip_ref, mask_ref, shift_ref, w_ref, act_ref, out_ref, stat_ref = refs[
            1 + count :
        ]
        tap = pl.program_id(0)

        @pl.when(tap == 0)
        def _():
            mean, inv = moments(parts, recip_ref[...])
            for kind in range(kinds):
                pre = affine_ref[0:1] * ((z_ref[kind] - mean) * inv) + affine_ref[1:2]
                act_ref[kind] = (pre * sigmoid(pre)).astype(BF16)

        kind, shift = tap_forward(tap, stride)
        patch = dot_nn(shift_ref[shift], act_ref[kind]).astype(BF16)
        term = dot_nn(patch, w_ref[...])

        @pl.when(tap == 0)
        def _():
            out_ref[...] = term

        @pl.when(tap > 0)
        def _():
            out_ref[...] += term

        @pl.when(tap == 8)
        def _():
            stat_ref[...] = stat_rows(out_ref[...], mask_ref[...])

    return body


def widen_kernel(count, carry):
    def body(*refs):
        z_ref = refs[0]
        parts = refs[1 : 1 + count]
        rest = refs[1 + count :]
        if carry:
            affine_ref, recip_ref, mask_ref, w_ref, side_ref, act_ref, out_ref, stat_ref = rest
        else:
            affine_ref, recip_ref, mask_ref, w_ref, act_ref, out_ref, stat_ref = rest

        @pl.when(pl.program_id(0) == 0)
        def _():
            mean, inv = moments(parts, recip_ref[...])
            pre = affine_ref[0:1] * ((z_ref[...] - mean) * inv) + affine_ref[1:2]
            act_ref[...] = (pre * sigmoid(pre)).astype(BF16)

        z = dot_nn(act_ref[...], w_ref[...])
        out_ref[...] = z
        if carry:
            stat_ref[...] = jnp.concatenate([stat_rows(z, mask_ref[...]), side_ref[...]], 0)
        else:
            stat_ref[...] = stat_rows(z, mask_ref[...])

    return body


def pair_moments(parts, recip):
    total = tree_sum([part[...] for part in parts]) * recip
    mean, mean_side = total[0:1], total[2:3]
    inv = lax.rsqrt(total[1:2] - mean * mean + EPS_NORM)
    inv_side = lax.rsqrt(total[3:4] - mean_side * mean_side + EPS_NORM)
    return mean, inv, mean_side, inv_side


def mix_kernel(count):
    def body(*refs):
        z_ref, side_ref = refs[:2]
        parts = refs[2 : 2 + count]
        (affine_ref, affine_side_ref, recip_ref, mask_ref, w_ref) = refs[2 + count : 7 + count]
        hidden_ref, low_ref, out_ref, stat_ref = refs[7 + count :]
        mean, inv, mean_side, inv_side = pair_moments(parts, recip_ref[...])
        pre = (
            affine_ref[0:1] * ((z_ref[...] - mean) * inv)
            + affine_ref[1:2]
            + affine_side_ref[0:1] * ((side_ref[...] - mean_side) * inv_side)
            + affine_side_ref[1:2]
        )
        hidden = pre * sigmoid(pre)
        hidden_ref[...] = hidden
        low = hidden.astype(BF16)
        low_ref[...] = low
        term = dot_nn(low, w_ref[...])

        @pl.when(pl.program_id(0) == 0)
        def _():
            out_ref[...] = term

        @pl.when(pl.program_id(0) > 0)
        def _():
            out_ref[...] += term

        @pl.when(pl.program_id(0) == pl.num_programs(0) - 1)
        def _():
            stat_ref[...] = stat_rows(out_ref[...], mask_ref[...])

    return body


def cell_rows(images, sides):
    base = 0
    for level, side in enumerate(sides):
        for row in range(side):
            for col in range(side):
                yield level, row, col, base + (row * side + col) * images
        base += images * side * side


def output_kernel(count, images, sides):
    def body(*refs):
        z_ref = refs[0]
        parts = refs[1 : 1 + count]
        affine_ref, recip_ref, mask_ref, hidden_ref = refs[1 + count : 5 + count]
        cot_refs = refs[5 + count : 8 + count]
        y_refs = refs[8 + count : 11 + count]
        grad_ref, stat_ref, flat_ref = refs[11 + count :]
        used = grid_rows(images, sides)
        if flat_ref.shape[0] > used:
            flat_ref[used:] = jnp.zeros((flat_ref.shape[0] - used, flat_ref.shape[1]), F32)
        for level, row, col, at in cell_rows(images, sides):
            flat_ref[at : at + images] = cot_refs[level][row, col].astype(F32)
        mean, inv = moments(parts, recip_ref[...])
        normed = (z_ref[...] - mean) * inv
        pre = affine_ref[0:1] * normed + affine_ref[1:2] + hidden_ref[...]
        gate = sigmoid(pre)
        grad = flat_ref[...] * mask_ref[...] * (gate * (1.0 + pre * (1.0 - gate)))
        grad_ref[...] = grad
        stat_ref[...] = jnp.concatenate([column_sum(grad * normed), column_sum(grad)], 0)
        flat_ref[...] = pre * gate
        for level, row, col, at in cell_rows(images, sides):
            y_refs[level][row, col] = flat_ref[at : at + images].astype(BF16)

    return body


def input_grad_kernel(images, sides):
    def body(dz_ref, w_ref, side_ref, w_side_ref, *rest):
        out_refs, flat_ref = rest[:3], rest[3]
        for kind in range(4):
            value = dot_nt(dz_ref[kind], w_ref[...])
            if kind == 0:
                value += dot_nt(side_ref[...], w_side_ref[...])
            flat_ref[...] = value
            for level, row, col, at in cell_rows(images, sides):
                out_refs[level][2 * row + kind // 2, 2 * col + kind % 2] = flat_ref[
                    at : at + images
                ]

    return body


def norm_back(grad, normed, sums, recip, mask, scale):
    return scale * (grad - mask * (sums[1:2] * recip + normed * (sums[0:1] * recip)))


def back_linear_kernel(count):
    def body(*refs):
        grad_ref, z_ref = refs[:2]
        parts = refs[2 : 2 + count]
        sums = refs[2 + count : 2 + 2 * count]
        affine_ref, recip_ref, mask_ref, w_ref, below_ref = refs[2 + 2 * count : 7 + 2 * count]
        below_parts = refs[7 + 2 * count : 7 + 3 * count]
        below_affine_ref, dz_ref, out_ref, stat_ref = refs[7 + 3 * count :]
        recip = recip_ref[...]
        mean, inv = moments(parts, recip)
        total = tree_sum([part[...] for part in sums])
        normed = (z_ref[...] - mean) * inv
        dz = norm_back(grad_ref[...], normed, total, recip, mask_ref[...], affine_ref[0:1] * inv)
        dz = dz.astype(BF16)
        dz_ref[...] = dz
        term = dot_nt(dz, w_ref[...])

        @pl.when(pl.program_id(0) == 0)
        def _():
            out_ref[...] = term

        @pl.when(pl.program_id(0) > 0)
        def _():
            out_ref[...] += term

        @pl.when(pl.program_id(0) == pl.num_programs(0) - 1)
        def _():
            finish_below(out_ref, below_ref, below_parts, below_affine_ref, recip, stat_ref)

    return body


def finish_below(out_ref, below_ref, below_parts, below_affine_ref, recip, stat_ref):
    mean, inv = moments(below_parts, recip)
    normed = (below_ref[...] - mean) * inv
    pre = below_affine_ref[0:1] * normed + below_affine_ref[1:2]
    grad = out_ref[...] * slope(pre)
    out_ref[...] = grad
    stat_ref[...] = jnp.concatenate([column_sum(grad * normed), column_sum(grad)], 0)


def back_conv_kernel(count, kinds, stride):
    def body(*refs):
        grad_ref, z_ref = refs[:2]
        parts = refs[2 : 2 + count]
        sums = refs[2 + count : 2 + 2 * count]
        affine_ref, recip_ref, mask_ref, shift_ref, w_ref, below_ref = refs[
            2 + 2 * count : 8 + 2 * count
        ]
        below_parts = refs[8 + 2 * count : 8 + 3 * count]
        below_affine_ref, below_recip_ref, dz_ref, out_ref, stat_ref = refs[8 + 3 * count :]
        tap = pl.program_id(0)

        @pl.when(tap == 0)
        def _():
            recip = recip_ref[...]
            mean, inv = moments(parts, recip)
            total = tree_sum([part[...] for part in sums])
            normed = (z_ref[...] - mean) * inv
            dz = norm_back(
                grad_ref[...], normed, total, recip, mask_ref[...], affine_ref[0:1] * inv
            )
            dz_ref[...] = dz.astype(BF16)
            out_ref[...] = jnp.zeros_like(out_ref)

        kind, shift = tap_backward(tap, stride)
        patch = dot_nn(shift_ref[shift], dz_ref[...]).astype(BF16)
        out_ref[kind] += dot_nt(patch, w_ref[...])

        @pl.when(tap == 8)
        def _():
            mean, inv = moments(below_parts, below_recip_ref[...])
            rows = None
            for which in range(kinds):
                normed = (below_ref[which] - mean) * inv
                pre = below_affine_ref[0:1] * normed + below_affine_ref[1:2]
                grad = out_ref[which] * slope(pre)
                out_ref[which] = grad
                part = jnp.concatenate([column_sum(grad * normed), column_sum(grad)], 0)
                rows = part if rows is None else rows + part
            stat_ref[...] = rows

    return body


def back_mix_kernel(count):
    def body(*refs):
        grad_ref, z_ref = refs[:2]
        parts = refs[2 : 2 + count]
        sums = refs[2 + count : 2 + 2 * count]
        affine_ref, recip_ref, mask_ref, w_ref, above_ref, mid_ref, side_ref = refs[
            2 + 2 * count : 9 + 2 * count
        ]
        pair_parts = refs[9 + 2 * count : 9 + 3 * count]
        affine_mid_ref, affine_side_ref, dz_ref, out_ref, stat_ref = refs[9 + 3 * count :]
        recip = recip_ref[...]

        @pl.when(pl.program_id(0) == 0)
        def _():
            mean, inv = moments(parts, recip)
            total = tree_sum([part[...] for part in sums])
            normed = (z_ref[...] - mean) * inv
            dz = norm_back(
                grad_ref[...], normed, total, recip, mask_ref[...], affine_ref[0:1] * inv
            )
            dz_ref[...] = dz.astype(BF16)

        mean, inv, mean_side, inv_side = pair_moments(pair_parts, recip)
        normed = (mid_ref[...] - mean) * inv
        normed_side = (side_ref[...] - mean_side) * inv_side
        pre = (
            affine_mid_ref[0:1] * normed
            + affine_mid_ref[1:2]
            + affine_side_ref[0:1] * normed_side
            + affine_side_ref[1:2]
        )
        grad = (above_ref[...] + dot_nt(dz_ref[...], w_ref[...])) * slope(pre)
        out_ref[...] = grad
        stat_ref[...] = jnp.concatenate(
            [column_sum(grad * normed), column_sum(grad), column_sum(grad * normed_side)], 0
        )

    return body


def back_pair_kernel(count):
    def body(*refs):
        grad_ref, mid_ref, side_ref = refs[:3]
        pair_parts = refs[3 : 3 + count]
        sums = refs[3 + count : 3 + 2 * count]
        affine_mid_ref, affine_side_ref, recip_ref, mask_ref, w_ref, below_ref = refs[
            3 + 2 * count : 9 + 2 * count
        ]
        below_parts = refs[9 + 2 * count : 9 + 3 * count]
        below_affine_ref, dz_ref, dz_side_ref, out_ref, stat_ref = refs[9 + 3 * count :]
        recip = recip_ref[...]
        mean, inv, mean_side, inv_side = pair_moments(pair_parts, recip)
        total = tree_sum([part[...] for part in sums])
        normed = (mid_ref[...] - mean) * inv
        normed_side = (side_ref[...] - mean_side) * inv_side
        grad = grad_ref[...]
        mask = mask_ref[...]
        dz = norm_back(grad, normed, total[0:2], recip, mask, affine_mid_ref[0:1] * inv)
        dz = dz.astype(BF16)
        dz_ref[...] = dz
        total_side = jnp.concatenate([total[2:3], total[1:2]], 0)
        dz_side_ref[...] = norm_back(
            grad, normed_side, total_side, recip, mask, affine_side_ref[0:1] * inv_side
        ).astype(BF16)
        term = dot_nt(dz, w_ref[...])

        @pl.when(pl.program_id(0) == 0)
        def _():
            out_ref[...] = term

        @pl.when(pl.program_id(0) > 0)
        def _():
            out_ref[...] += term

        @pl.when(pl.program_id(0) == pl.num_programs(0) - 1)
        def _():
            finish_below(out_ref, below_ref, below_parts, below_affine_ref, recip, stat_ref)

    return body


def back_first_kernel(count):
    def body(*refs):
        grad_ref, z_ref = refs[:2]
        parts = refs[2 : 2 + count]
        sums = refs[2 + count : 2 + 2 * count]
        affine_ref, recip_ref, mask_ref, x_ref, _, dz_ref, grad_w_ref, total_ref = refs[
            2 + 2 * count :
        ]
        recip = recip_ref[...]
        mean, inv = moments(parts, recip)
        total = tree_sum([part[...] for part in sums])
        normed = (z_ref[0] - mean) * inv
        dz = norm_back(grad_ref[0], normed, total, recip, mask_ref[...], affine_ref[0:1] * inv)
        dz = dz.astype(BF16)
        dz_ref[0] = dz
        term = dot_tn(x_ref[0], dz)

        @pl.when(pl.program_id(0) == 0)
        def _():
            total_ref[...] = term

        @pl.when(pl.program_id(0) > 0)
        def _():
            total_ref[...] += term

        @pl.when(pl.program_id(0) == pl.num_programs(0) - 1)
        def _():
            grad_w_ref[...] = total_ref[...].astype(BF16)

    return body


def weight_grad_kernel(act_ref, dz_ref, *rest):
    rest[-1][...] = dot_tn(act_ref[...], dz_ref[...]).astype(BF16)


def conv_grad_kernel(stride, first):
    def body(act_ref, shift_ref, dz_ref, *rest):
        kind, shift = tap_forward(pl.program_id(0) + first, stride)
        patch = dot_nn(shift_ref[shift], act_ref[kind]).astype(BF16)
        rest[-1][...] = dot_tn(patch, dz_ref[...]).astype(BF16)

    return body


def pack_kernel(count, spans):
    def body(*refs):
        out_ref = refs[-1]
        for which, (start, stop, rows) in enumerate(spans):
            parts = refs[which * count : (which + 1) * count]
            total = tree_sum([part[...] for part in parts])
            for slot, row in enumerate(rows):
                out_ref[slot : slot + 1, start:stop] = total[row : row + 1]

    return body


def merge_kernel(split, has_kept, last):
    def add(kept_ref, came_ref):
        total = kept_ref[...].astype(F32) + came_ref[...].astype(F32)
        return total if last else total.astype(BF16)

    def body(index_ref, *refs):
        if not has_kept:
            refs[1][...] = refs[0][...]
        elif split:
            refs[4][...] = add(refs[0], refs[1])
            refs[5][...] = add(refs[2], refs[3])
        else:
            refs[2][...] = add(refs[0], refs[1])

    return body


def level_masks(first_row, rows, bounds):
    index = first_row + lax.broadcasted_iota(jnp.int32, (rows, 1), 0)
    return [
        ((index >= bounds[level]) & (index < bounds[level + 1])).astype(F32)
        for level in range(len(bounds) - 1)
    ]


def tally_kernel(bounds):
    levels = len(bounds) - 1

    def body(first_ref, grad_ref, master_ref, old_ref, rows_ref, sums_ref):
        grad = grad_ref[...]
        master = master_ref[...]
        square = grad * grad
        raised = square + EPS_ONE
        rows_new = DECAY * old_ref[...] + (1.0 - DECAY) * jnp.mean(raised, 1, keepdims=True)
        rows_ref[...] = rows_new
        ratio = square / rows_new
        weight = jnp.sum(master * master, 1, keepdims=True)
        masks = level_masks(first_ref[0], grad.shape[0], bounds)
        spread = jnp.zeros((1, grad.shape[1]), F32)
        for level in range(levels):
            mask = masks[level]
            sums_ref[level : level + 1] = column_sum(raised * mask)
            sums_ref[levels + level : levels + level + 1] = column_sum(ratio * mask)
            low = 2 * levels + level
            sums_ref[low : low + 1] = spread + column_sum(rows_new * mask)
            low = 3 * levels + level
            sums_ref[low : low + 1] = spread + column_sum(weight * mask)

    return body


def renew_kernel(bounds):
    levels = len(bounds) - 1

    def body(first_ref, grad_ref, master_ref, rows_ref, sums_ref, old_ref, cols_ref, new_ref, low_ref):
        grad = grad_ref[...]
        columns = grad.shape[1]
        masks = level_masks(first_ref[0], grad.shape[0], bounds)
        factor = None
        for level in range(levels):
            height = float(bounds[level + 1] - bounds[level])
            cells = height * columns
            col_sum = sums_ref[level : level + 1]
            ratio_sum = sums_ref[levels + level : levels + level + 1]
            row_mean = sums_ref[2 * levels + level : 2 * levels + level + 1] / height
            weight_sum = sums_ref[3 * levels + level : 3 * levels + level + 1]
            cols_new = DECAY * old_ref[level : level + 1] + (1.0 - DECAY) * (col_sum / height)
            cols_ref[level : level + 1] = cols_new
            relative = cols_new / row_mean
            update_sq = jnp.sum(ratio_sum / relative, axis=1, keepdims=True)
            update_rms = jnp.sqrt(update_sq / cells)
            weight_rms = jnp.sqrt(weight_sum / cells)
            step = STEP_RATE * jnp.maximum(EPS_TWO, weight_rms) / jnp.maximum(1.0, update_rms)
            part = masks[level] * (step * lax.rsqrt(relative))
            factor = part if factor is None else factor + part
        new = master_ref[...] - grad * lax.rsqrt(rows_ref[...]) * factor
        new_ref[...] = new
        low_ref[...] = new.astype(BF16)

    return body


class Exchange:
    def __init__(self, n_wide, n_narrow):
        self.n_narrow = n_narrow
        self.total = n_wide * n_narrow
        self.bits = self.total.bit_length() - 1
        self.narrow_bits = n_narrow.bit_length() - 1
        self.index = lax.axis_index(AXES)

    def bit(self, level):
        return (self.index >> level) & 1

    def swap(self, value, level):
        pairs = [(device, device ^ (1 << level)) for device in range(self.total)]
        return lax.ppermute(value, AXES, pairs)

    def group_parts(self, value):
        return [value] + [
            lax.ppermute(value, "narrow", [(i, i ^ k) for i in range(self.n_narrow)])
            for k in range(1, self.n_narrow)
        ]

    def total_sum(self, value, first=0):
        for level in range(first, self.bits):
            value = value + self.swap(value, level)
        return value


def insert_bit(unit, place, bit):
    return ((unit >> place) << (place + 1)) | (bit << place) | (unit & ((1 << place) - 1))


class Scatter:
    def __init__(self, link, kernels, part, name, prefix=(), swap=False):
        self.link = link
        self.kernels = kernels
        self.name = name
        self.prefix = prefix
        self.open_bits = link.bits - len(prefix)
        units = 1 << self.open_bits
        self.kept = part.reshape(units, part.shape[0] // units, part.shape[1])
        self.left = list(range(self.open_bits))
        self.levels = list(range(self.open_bits))
        if swap:
            self.levels[1], self.levels[2] = self.levels[2], self.levels[1]
        self.levels += list(range(self.open_bits, link.bits))
        self.at = 0
        self.came = None
        self.chosen = None
        self.send_half(None)

    def place(self, level):
        return self.left.index(level)

    def unit_spec(self, source):
        dims = (1,) + self.kept.shape[1:]
        return block(dims, lambda unit, index: (source(unit, index[0]), 0, 0))

    def kept_source(self, source):
        if self.chosen is None:
            return source
        place, level = self.chosen
        return lambda unit, index: insert_bit(
            source(unit, index), place, (index >> level) & 1
        )

    def run(self, body, specs, outs, number, args, dtype):
        spec = self.unit_spec(lambda unit, index: unit)
        shape = shape_of((number,) + self.kept.shape[1:], dtype)
        out = self.kernels(
            body,
            self.name + "_" + str(self.at),
            (number,),
            specs,
            [spec] * outs,
            [shape] * outs,
            4 * number * self.kept.shape[1] * self.kept.shape[2] * 200,
            scalars=1,
        )(self.link.index.astype(jnp.int32).reshape(1), *args)
        return out

    def send_half(self, came):
        level = self.levels[self.at] if self.at < len(self.levels) else None
        total_units = 1 << len(self.left)
        if level is not None and level < self.open_bits:
            place = self.place(level)

            def keep(unit, index):
                return insert_bit(unit, place, (index >> level) & 1)

            def send(unit, index):
                return insert_bit(unit, place, 1 - ((index >> level) & 1))

            half = total_units // 2
            if came is None:
                (sent,) = self.run(
                    merge_kernel(True, False, False),
                    [self.unit_spec(send)],
                    1,
                    half,
                    [self.kept],
                    BF16,
                )
                self.chosen = (place, level)
            else:
                kept_keep = self.unit_spec(self.kept_source(keep))
                kept_send = self.unit_spec(self.kept_source(send))
                kept, sent = self.run(
                    merge_kernel(True, True, False),
                    [kept_keep, self.unit_spec(keep), kept_send, self.unit_spec(send)],
                    2,
                    half,
                    [self.kept, came, self.kept, came],
                    BF16,
                )
                self.kept, self.chosen = kept, None
            self.left.remove(level)
            self.came = self.link.swap(sent, level)
        else:
            same = lambda unit, index: unit
            (self.kept,) = self.run(
                merge_kernel(False, True, level is None),
                [self.unit_spec(self.kept_source(same)), self.unit_spec(same)],
                1,
                total_units,
                [self.kept, came],
                F32 if level is None else BF16,
            )
            self.chosen = None
            if level is None:
                return
            pairs = []
            for device in range(self.link.total):
                settled = all(
                    (device >> other) & 1 == self.prefix[other - self.open_bits]
                    for other in range(self.open_bits, level)
                )
                if settled and (device >> level) & 1 != self.prefix[level - self.open_bits]:
                    pairs.append((device, device ^ (1 << level)))
            self.came = lax.ppermute(self.kept, AXES, pairs)

    def step(self, number=1):
        for _ in range(number):
            if self.at < len(self.levels):
                self.at += 1
                self.send_half(self.came)

    def finish(self):
        self.step(len(self.levels))
        return self.kept.reshape(self.kept.shape[1:])


def make_body(mesh):
    n_wide, n_narrow = mesh.shape["wide"], mesh.shape["narrow"]

    def body(
        x_lo,
        x_mid,
        x_hi,
        cot_lo,
        cot_mid,
        cot_hi,
        live_counts,
        slim_master,
        broad_master,
        slim_rowstat,
        broad_rowstat,
        slim_colstat,
        broad_colstat,
        norm_params,
        norm_moments,
    ):
        link = Exchange(n_wide, n_narrow)
        kernel_call = Kernels()
        count = n_narrow
        images = x_lo.shape[0]
        sides = tuple(value.shape[1] // 2 for value in (x_lo, x_mid, x_hi))
        c_in, mid, c_out = x_lo.shape[3], slim_master.shape[1], broad_master.shape[1]
        cells = grid_rows(images, sides)
        cells_in = 4 * cells
        rows = -(-cells // 16) * 16
        chunks = c_out // mid
        bounds_slim = (0, c_in, c_in + 9 * mid, c_in + 9 * mid + c_out, c_in + 18 * mid + c_out)
        bounds_broad = (0, mid, mid + c_in, 2 * mid + c_in)
        at_two, at_four, at_five = (bounds_slim[level] // mid for level in (1, 2, 3))
        at_six = bounds_broad[2] // mid
        widths = (mid, mid, c_out, c_out, mid, mid, c_out)
        norm_at = [sum(widths[:level]) // mid for level in range(7)]

        slim = lax.all_gather(slim_master.astype(BF16), AXES, axis=0, tiled=True)
        broad = lax.all_gather(broad_master.astype(BF16), AXES, axis=0, tiled=True)

        kinds = class_table(images, sides, rows)
        shifts = one_hot(shift_table(images, sides, rows), rows)

        def by_cell(value):
            return jnp.transpose(value, (1, 2, 0, 3))

        x_flat = jnp.concatenate(
            [by_cell(value).reshape(-1, c_in) for value in (x_lo, x_mid, x_hi)], 0
        )
        x_kinds = jnp.dot(one_hot(kinds.reshape(-1), cells_in), x_flat, preferred_element_type=F32)
        x_kinds = x_kinds.astype(BF16).reshape(4, rows, c_in)
        alive = [
            (jnp.arange(images) < live_counts[0, level]).astype(F32) for level in range(3)
        ]
        mask = jnp.concatenate(
            [jnp.tile(alive[level], side * side) for level, side in enumerate(sides)]
            + [jnp.zeros((rows - cells,), F32)]
        )
        cell_count = tree_sum(link.group_parts(jnp.sum(mask).reshape(1, 1)))
        mask = mask[:, None]
        recip = 1.0 / cell_count
        recip_in = 0.25 / cell_count

        narrow_all = whole((rows, mid))
        kinds_all = whole((4, rows, mid))
        stat_all = whole((2, mid))
        mask_all = whole((rows, 1))
        one_all = whole((1, 1))
        shifts_all = whole((9, rows, rows))
        chunk = block((rows, mid), lambda j: (0, j))

        def stat_chunk(height):
            return block((height, mid), lambda j: (0, j))

        def affine(level):
            return block((2, mid), lambda j: (0, norm_at[level]))

        def affine_chunk(level):
            return block((2, mid), lambda j: (0, norm_at[level] + j))

        def slim_block(at):
            return block((mid, mid), lambda j: (at + j, 0))

        def broad_block(at):
            return block((mid, mid), lambda j: (at, j))

        narrow_f32 = shape_of((rows, mid), F32)
        wide_f32 = shape_of((rows, c_out), F32)
        narrow_low = shape_of((rows, mid), BF16)
        wide_low = shape_of((rows, c_out), BF16)
        stat_narrow = shape_of((2, mid), F32)
        stat_wide = shape_of((2, c_out), F32)
        flops_conv = 2 * rows * 9 * mid * (mid + rows)
        flops_wide = 2 * rows * mid * c_out

        z_one, stat = kernel_call(
            first_kernel,
            "first",
            (4,),
            [
                block((1, rows, c_in), lambda j: (j, 0, 0)),
                whole((c_in, mid)),
                mask_all,
            ],
            [block((1, rows, mid), lambda j: (j, 0, 0)), stat_all],
            [shape_of((4, rows, mid), F32), stat_narrow],
            2 * 4 * rows * c_in * mid,
            after=[recip],
        )(x_kinds, slim, mask)
        parts_one = link.group_parts(stat)
        act_one, z_two, stat = kernel_call(
            conv_kernel(count, 4, 2),
            "conv_two",
            (9,),
            [kinds_all]
            + [stat_all] * count
            + [affine(0), one_all, mask_all, shifts_all, slim_block(at_two)],
            [kinds_all, narrow_all, stat_all],
            [shape_of((4, rows, mid), BF16), narrow_f32, stat_narrow],
            flops_conv,
        )(z_one, *parts_one, norm_params, recip_in, mask, shifts, slim)
        parts_two = link.group_parts(stat)
        z_side, stat_side = kernel_call(
            side_kernel,
            "side",
            (chunks, c_in // mid),
            [
                block((1, rows, mid), lambda j, k: (0, 0, k)),
                block((mid, mid), lambda j, k: (1 + k, j)),
                whole((rows, 1)),
            ],
            [
                block((rows, mid), lambda j, k: (0, j)),
                block((2, mid), lambda j, k: (0, j)),
            ],
            [wide_f32, stat_wide],
            2 * rows * c_in * c_out,
        )(x_kinds, broad, mask)
        act_two, z_three, stat = kernel_call(
            widen_kernel(count, True),
            "widen_three",
            (chunks,),
            [narrow_all]
            + [stat_all] * count
            + [affine(1), one_all, mask_all, broad_block(0), stat_chunk(2)],
            [narrow_all, chunk, stat_chunk(4)],
            [narrow_low, wide_f32, shape_of((4, c_out), F32)],
            flops_wide,
        )(z_two, *parts_two, norm_params, recip, mask, broad, stat_side)
        parts_pair = link.group_parts(stat)
        hidden, hidden_low, z_four, stat = kernel_call(
            mix_kernel(count),
            "mix",
            (chunks,),
            [chunk, chunk]
            + [stat_chunk(4)] * count
            + [affine_chunk(2), affine_chunk(3), one_all, mask_all, slim_block(at_four)],
            [chunk, chunk, narrow_all, stat_all],
            [wide_f32, wide_low, narrow_f32, stat_narrow],
            flops_wide,
        )(z_three, z_side, *parts_pair, norm_params, norm_params, recip, mask, slim)
        parts_four = link.group_parts(stat)
        one_kind = whole((1, rows, mid))
        act_four, z_five, stat = kernel_call(
            conv_kernel(count, 1, 1),
            "conv_five",
            (9,),
            [one_kind]
            + [stat_all] * count
            + [affine(4), one_all, mask_all, shifts_all, slim_block(at_five)],
            [one_kind, narrow_all, stat_all],
            [shape_of((1, rows, mid), BF16), narrow_f32, stat_narrow],
            flops_conv,
        )(z_four[None], *parts_four, norm_params, recip, mask, shifts, slim)
        parts_five = link.group_parts(stat)
        act_five, z_six, stat = kernel_call(
            widen_kernel(count, False),
            "widen_six",
            (chunks,),
            [narrow_all]
            + [stat_all] * count
            + [affine(5), one_all, mask_all, broad_block(at_six)],
            [narrow_all, chunk, stat_chunk(2)],
            [narrow_low, wide_f32, stat_wide],
            flops_wide,
        )(z_five, *parts_five, norm_params, recip, mask, broad)
        parts_six = link.group_parts(stat)
        grids = [
            block((side, side, images, mid), lambda j: (0, 0, 0, j)) for side in sides
        ]
        *y_grids, grad_out, stat = kernel_call(
            output_kernel(count, images, sides),
            "output",
            (chunks,),
            [chunk]
            + [stat_chunk(2)] * count
            + [affine_chunk(6), one_all, mask_all, chunk]
            + grids,
            grids + [chunk, stat_chunk(2)],
            [shape_of((side, side, images, c_out), BF16) for side in sides]
            + [wide_f32, stat_wide],
            flops_wide // 8,
            scratch=[pltpu.VMEM((rows, mid), F32)],
        )(
            z_six,
            *parts_six,
            norm_params,
            recip,
            mask,
            hidden,
            *[by_cell(value) for value in (cot_lo, cot_mid, cot_hi)],
        )
        sums_six = link.group_parts(stat)

        dz_six, grad_five, stat = kernel_call(
            back_linear_kernel(count),
            "back_six",
            (chunks,),
            [chunk, chunk]
            + [stat_chunk(2)] * (2 * count)
            + [affine_chunk(6), one_all, mask_all, broad_block(at_six), narrow_all]
            + [stat_all] * count
            + [affine(5)],
            [chunk, narrow_all, stat_all],
            [wide_low, narrow_f32, stat_narrow],
            flops_wide,
        )(
            grad_out,
            z_six,
            *parts_six,
            *sums_six,
            norm_params,
            recip,
            mask,
            broad,
            z_five,
            *parts_five,
            norm_params,
        )
        sums_five = link.group_parts(stat)

        def weight_grad(act, dz, steps, act_at, out_shape, out_at, base, name):
            high, across = steps
            height = act.shape[0]
            specs = [
                block((height, mid), lambda i, j: (0, act_at + i)),
                block((height, mid), lambda i, j: (0, j)),
            ]
            args = [act, dz]
            if base is not None:
                specs.append(pl.BlockSpec(memory_space=pl.ANY))
                args.append(base)
            return kernel_call(
                weight_grad_kernel,
                name,
                (high, across),
                specs,
                block((mid, mid), lambda i, j: (out_at + i, j)),
                shape_of(out_shape, BF16),
                2 * height * mid * mid * high * across,
                aliases={2: 0} if base is not None else None,
            )(*args)

        def conv_grad(act, dz, stride, taps, out_shape, out_at, base, name):
            first, number = taps
            kinds_here = act.shape[0]
            specs = [whole((kinds_here, rows, mid)), shifts_all, narrow_all]
            args = [act, shifts, dz]
            if base is not None:
                specs.append(pl.BlockSpec(memory_space=pl.ANY))
                args.append(base)
            return kernel_call(
                conv_grad_kernel(stride, first),
                name,
                (number,),
                specs,
                block((mid, mid), lambda t: (out_at + t, 0)),
                shape_of(out_shape, BF16),
                flops_conv * number // 9,
                aliases={3: 0} if base is not None else None,
            )(*args)

        slim_part = (bounds_slim[-1] // 4, mid)
        broad_part = (bounds_broad[-1] // 4, c_out)
        per_part = slim_part[0] // mid
        term_six = weight_grad(act_five, dz_six, (1, chunks), 0, broad_part, 0, None, "grad_six")
        chain_six = Scatter(link, kernel_call, term_six, "sum_six", (1, 1))

        dz_five, grad_four, stat = kernel_call(
            back_conv_kernel(count, 1, 1),
            "back_five",
            (9,),
            [narrow_all, narrow_all]
            + [stat_all] * (2 * count)
            + [affine(5), one_all, mask_all, shifts_all, slim_block(at_five), one_kind]
            + [stat_all] * count
            + [affine(4), one_all],
            [narrow_all, one_kind, stat_all],
            [narrow_low, shape_of((1, rows, mid), F32), stat_narrow],
            flops_conv,
        )(
            grad_five,
            z_five,
            *parts_five,
            *sums_five,
            norm_params,
            recip,
            mask,
            shifts,
            slim,
            z_four[None],
            *parts_four,
            norm_params,
            recip,
        )
        grad_four = grad_four[0]
        sums_four = link.group_parts(stat)
        low_four = 2 * per_part - at_four
        upper_part = (2 * slim_part[0], mid)
        term = conv_grad(
            act_four, dz_five, 1, (0, 9), upper_part, chunks - low_four, None, "grad_five"
        )
        chain_six.step()
        dz_four, grad_mid, stat = kernel_call(
            back_mix_kernel(count),
            "back_four",
            (chunks,),
            [narrow_all, narrow_all]
            + [stat_all] * (2 * count)
            + [affine(4), one_all, mask_all, slim_block(at_four), chunk, chunk, chunk]
            + [stat_chunk(4)] * count
            + [affine_chunk(2), affine_chunk(3)],
            [narrow_all, chunk, stat_chunk(3)],
            [narrow_low, wide_f32, shape_of((3, c_out), F32)],
            flops_wide,
        )(
            grad_four,
            z_four,
            *parts_four,
            *sums_four,
            norm_params,
            recip,
            mask,
            slim,
            grad_out,
            z_three,
            z_side,
            *parts_pair,
            norm_params,
            norm_params,
        )
        sums_pair = link.group_parts(stat)
        term = weight_grad(
            hidden_low,
            dz_four,
            (chunks - low_four, 1),
            low_four,
            upper_part,
            0,
            term,
            "grad_four",
        )
        chain_upper = Scatter(link, kernel_call, term, "sum_upper", (1,), True)
        dz_three, dz_side, grad_two, stat = kernel_call(
            back_pair_kernel(count),
            "back_three",
            (chunks,),
            [chunk, chunk, chunk]
            + [stat_chunk(4)] * count
            + [stat_chunk(3)] * count
            + [affine_chunk(2), affine_chunk(3), one_all, mask_all, broad_block(0), narrow_all]
            + [stat_all] * count
            + [affine(1)],
            [chunk, chunk, narrow_all, stat_all],
            [wide_low, wide_low, narrow_f32, stat_narrow],
            flops_wide,
        )(
            grad_mid,
            z_three,
            z_side,
            *parts_pair,
            *sums_pair,
            norm_params,
            norm_params,
            recip,
            mask,
            broad,
            z_two,
            *parts_two,
            norm_params,
        )
        sums_two = link.group_parts(stat)
        chain_six.step()
        chain_upper.step()
        x_sub = x_kinds[0]
        two_parts = (2 * broad_part[0], c_out)
        term = weight_grad(
            act_two, dz_three, (1, chunks), 0, two_parts, 0, None, "grad_three"
        )
        term = weight_grad(
            x_sub, dz_side, (1, chunks), 0, two_parts, 1, term, "grad_side_low"
        )
        chain_three = Scatter(link, kernel_call, term, "sum_three", (0,))
        term = weight_grad(
            x_sub, dz_side, (1, chunks), 1, broad_part, 0, None, "grad_side_high"
        )
        chain_side = Scatter(link, kernel_call, term, "sum_side", (0, 1), True)
        chain_six.step()

        dz_two, grad_one, stat = kernel_call(
            back_conv_kernel(count, 4, 2),
            "back_two",
            (9,),
            [narrow_all, narrow_all]
            + [stat_all] * (2 * count)
            + [affine(1), one_all, mask_all, shifts_all, slim_block(at_two), kinds_all]
            + [stat_all] * count
            + [affine(0), one_all],
            [narrow_all, kinds_all, stat_all],
            [narrow_low, shape_of((4, rows, mid), F32), stat_narrow],
            flops_conv,
        )(
            grad_two,
            z_two,
            *parts_two,
            *sums_two,
            norm_params,
            recip,
            mask,
            shifts,
            slim,
            z_one,
            *parts_one,
            norm_params,
            recip_in,
        )
        sums_one = link.group_parts(stat)
        chain_three.step()
        chain_side.step()
        chain_six.step()
        term = conv_grad(
            act_one, dz_two, 2, (per_part - at_two, 9 - per_part + at_two), slim_part, 0, None,
            "grad_two_high",
        )
        term = weight_grad(
            hidden_low, dz_four, (low_four, 1), 0, slim_part, per_part - low_four, term,
            "grad_four_low",
        )
        chain_two = Scatter(link, kernel_call, term, "sum_two", (1, 0), True)
        half_part = (slim_part[0] // 2, mid)
        per_half = per_part // 2
        taps_low = per_half - at_two
        term = conv_grad(
            act_one, dz_two, 2, (taps_low, per_half), half_part, 0, None, "grad_two_mid"
        )
        chain_mid = Scatter(link, kernel_call, term, "sum_mid", (1, 0, 0))
        slim_low = conv_grad(
            act_one, dz_two, 2, (0, taps_low), half_part, at_two, None, "grad_two_low"
        )
        dz_one, slim_low = kernel_call(
            back_first_kernel(count),
            "back_one",
            (4,),
            [block((1, rows, mid), lambda j: (j, 0, 0))] * 2
            + [stat_all] * (2 * count)
            + [
                affine(0),
                one_all,
                mask_all,
                block((1, rows, c_in), lambda j: (j, 0, 0)),
                pl.BlockSpec(memory_space=pl.ANY),
            ],
            [block((1, rows, mid), lambda j: (j, 0, 0)), whole((c_in, mid))],
            [shape_of((4, rows, mid), BF16), shape_of(half_part, BF16)],
            2 * 4 * rows * c_in * mid,
            scratch=[pltpu.VMEM((c_in, mid), F32)],
            aliases={2 + 2 * count + 4: 1},
        )(grad_one, z_one, *parts_one, *sums_one, norm_params, recip_in, mask, x_kinds, slim_low)
        chain_one = Scatter(link, kernel_call, slim_low, "sum_one", (0, 0, 0))
        chain_six.step()
        chain_upper.step()
        chain_two.step()
        chain_mid.step()
        chain_one.step()

        extents = tuple(2 * side for side in sides)
        dx_grids = kernel_call(
            input_grad_kernel(images, sides),
            "input_grad",
            (c_in // mid,),
            [
                kinds_all,
                slim_block(0),
                whole((rows, c_out)),
                block((mid, c_out), lambda j: (1 + j, 0)),
            ],
            [
                block((extent, extent, images, mid), lambda j: (0, 0, 0, j))
                for extent in extents
            ],
            [shape_of((extent, extent, images, c_in), F32) for extent in extents],
            2 * 4 * rows * c_in * mid + 2 * rows * c_in * c_out,
            scratch=[pltpu.VMEM((rows, mid), F32)],
        )(dz_one, slim, dz_side, broad)

        def by_image(value):
            return jnp.transpose(value, (2, 0, 1, 3))

        y_parts = [by_image(value) for value in y_grids]
        dx_parts = [by_image(value) for value in dx_grids]

        top = link.bit(link.bits - 1)
        second = link.bit(link.bits - 2)
        third = link.bit(link.bits - 3)

        def choose(bit, upper, lower):
            return jnp.where(bit == 1, upper, lower)

        spans = [
            (mid * at, mid * at + width, rows_of)
            for at, width, rows_of in zip(
                norm_at, widths, ((0, 1),) * 2 + ((0, 1), (2, 1)) + ((0, 1),) * 3
            )
        ]
        sum_sets = [sums_one, sums_two, sums_pair, sums_pair, sums_four, sums_five, sums_six]
        flat_sets = [part for parts in sum_sets for part in parts]
        norm_grad = kernel_call(
            pack_kernel(count, spans),
            "pack",
            (1,),
            [whole(part.shape) for part in flat_sets],
            whole(norm_params.shape),
            shape_of(norm_params.shape, F32),
            1000000,
        )(*flat_sets)
        norm_grad = link.total_sum(norm_grad, link.narrow_bits)

        chain_side.step()
        chain_three.step()
        chain_upper.step()
        chain_mid.step()
        chain_one.step()
        chain_two.step()
        chain_side.step()
        chain_three.step()
        chain_mid.step()
        chain_one.step()
        chain_upper.step()
        chain_two.step()
        chain_side.step()
        chain_three.step()
        broad_six, broad_three, broad_side = (
            chain_six.finish(),
            chain_three.finish(),
            chain_side.finish(),
        )
        broad_grad = choose(top, choose(second, broad_six, broad_side), broad_three)
        slim_high = chain_upper.finish()
        slim_mid = chain_two.finish()
        slim_low = choose(third, chain_mid.finish(), chain_one.finish())
        slim_grad = choose(top, slim_high, choose(second, slim_mid, slim_low))

        def optimize(grad, master, rowstat, colstat, bounds, name, after):
            height, columns = grad.shape
            levels = len(bounds) - 1
            first = (link.index * height).astype(jnp.int32).reshape(1)
            scalar = pl.BlockSpec(memory_space=pltpu.SMEM)
            matrix, column = whole((height, columns)), whole((height, 1))
            sums_all, cols_all = whole((4 * levels, columns)), whole((levels, columns))
            rows_new, sums = kernel_call(
                tally_kernel(bounds),
                name + "_tally",
                (1,),
                [scalar, matrix, matrix, column],
                [column, sums_all],
                [shape_of((height, 1), F32), shape_of((4 * levels, columns), F32)],
                20 * height * columns,
                after=after,
            )(first, grad, master, rowstat.reshape(height, 1))
            sums = link.total_sum(sums)
            cols_new, new, low = kernel_call(
                renew_kernel(bounds),
                name + "_renew",
                (1,),
                [scalar, matrix, matrix, column, sums_all, cols_all],
                [cols_all, matrix, matrix],
                [
                    shape_of((levels, columns), F32),
                    shape_of((height, columns), F32),
                    shape_of((height, columns), BF16),
                ],
                20 * height * columns,
            )(first, grad, master, rows_new, sums, colstat)
            return (rows_new.reshape(height), cols_new, new, low), sums

        (broad_rows_new, broad_cols_new, broad_new, broad_copy), sums = optimize(
            broad_grad, broad_master, broad_rowstat, broad_colstat, bounds_broad, "broad", []
        )
        (slim_rows_new, slim_cols_new, slim_new, slim_copy), _ = optimize(
            slim_grad,
            slim_master,
            slim_rowstat,
            slim_colstat,
            bounds_slim,
            "slim",
            [sums, norm_grad, dx_grids[2]],
        )
        norm_moments_new = DECAY * norm_moments + (1.0 - DECAY) * (
            norm_grad * norm_grad + EPS_ONE
        )
        norm_update = norm_grad * lax.rsqrt(norm_moments_new)
        update_rms = jnp.sqrt(jnp.mean(norm_update * norm_update, 1))
        weight_rms = jnp.sqrt(jnp.mean(norm_params * norm_params, 1))
        step = STEP_RATE * jnp.maximum(EPS_TWO, weight_rms) / jnp.maximum(1.0, update_rms)
        norm_new = norm_params - step[:, None] * norm_update
        return (
            *y_parts,
            *dx_parts,
            slim_grad,
            broad_grad,
            slim_rows_new,
            broad_rows_new,
            slim_cols_new,
            broad_cols_new,
            slim_new,
            broad_new,
            slim_copy,
            broad_copy,
            norm_grad,
            norm_moments_new,
            norm_new,
        )

    return body


def solution(mesh):
    split = P(AXES)
    return jax.shard_map(
        make_body(mesh),
        mesh=mesh,
        in_specs=(split,) * 11 + (P(),) * 4,
        out_specs=(split,) * 10 + (P(),) * 2 + (split,) * 4 + (P(),) * 3,
        check_vma=False,
    )
```

```python
import jax
import jax.numpy as jnp
import numpy as np
from jax import lax
from jax.experimental import pallas as pl
from jax.experimental.pallas import tpu as pltpu
from jax.sharding import PartitionSpec as P

STEP = 10
EPS_NORM = 1e-05
EPS_ONE = 1e-30
EPS_TWO = 0.001
STEP_RATE = 0.3
DECAY = 1.0 - STEP ** (-0.8)
AXES = ("wide", "narrow")
BF16 = jnp.bfloat16
F32 = jnp.float32
VMEM_LIMIT = 48 * 1024 * 1024


def shape_of(dims, dtype):
    return jax.ShapeDtypeStruct(dims, dtype)


def whole(dims):
    return pl.BlockSpec(dims, lambda *step: (0,) * len(dims))


def block(dims, place):
    return pl.BlockSpec(dims, place)


LENGTHS = dict(
    first=3.9,
    conv_two=10.8,
    side=7.2,
    widen_three=3.8,
    mix=5.3,
    conv_five=8.9,
    widen_six=3.9,
    output=6.8,
    back_six=5.1,
    grad_six=2.1,
    back_five=10,
    grad_five_high=5.5,
    grad_five_low=3.2,
    back_four=6.5,
    grad_four=1.5,
    back_three=6,
    grad_three=3,
    grad_side_low=2.1,
    grad_side_high=2.1,
    back_two=13.7,
    grad_two_high=4.8,
    grad_four_low=0.5,
    grad_two_low=4.8,
    back_one=6.3,
    input_grad=6.7,
    sum_six_0=1,
    sum_five_0=1.8,
    sum_four_0=2.1,
    sum_three_0=4.5,
    sum_side_0=1.5,
    sum_two_0=2.2,
    sum_one_0=2,
    sum_five_1=2.2,
    sum_four_1=2.7,
    sum_three_1=3.6,
    sum_side_1=2,
    sum_two_1=2.2,
)


def length(name):
    return LENGTHS.get(name, 1)


class Kernels:
    def __init__(self):
        self.last = None

    def __call__(
        self,
        body,
        name,
        grid,
        in_specs,
        out_specs,
        out_shape,
        flops,
        scratch=(),
        aliases=None,
        after=(),
        scalars=0,
    ):
        after = [value for value in (*after, self.last) if value is not None]
        if aliases:
            after = []
        taken = scalars + len(in_specs)

        def trimmed(*refs):
            body(*refs[:taken], *refs[taken + len(after) :])

        call = pl.pallas_call(
            trimmed,
            grid_spec=pltpu.PrefetchScalarGridSpec(
                num_scalar_prefetch=scalars,
                grid=grid,
                in_specs=list(in_specs) + [pl.BlockSpec(memory_space=pl.ANY)] * len(after),
                out_specs=out_specs,
                scratch_shapes=list(scratch),
            ),
            out_shape=out_shape,
            input_output_aliases=aliases or {},
            cost_estimate=pl.CostEstimate(
                flops=int(length(name) * 1.15e9),
                bytes_accessed=int(length(name) * 3.6e6),
                transcendentals=0,
            ),
            compiler_params=pltpu.CompilerParams(vmem_limit_bytes=VMEM_LIMIT),
            name=name,
        )

        def run(*args):
            out = call(*args, *after)
            self.last = out[0] if isinstance(out, (list, tuple)) else out
            return out

        return run


def dot_nn(first, second):
    return jnp.dot(first, second, preferred_element_type=F32)


def dot_nt(first, second):
    return lax.dot_general(first, second, (((1,), (1,)), ((), ())), preferred_element_type=F32)


def dot_tn(first, second):
    return lax.dot_general(first, second, (((0,), (0,)), ((), ())), preferred_element_type=F32)


def sigmoid(value):
    return 1.0 / (1.0 + jnp.exp(-value))


def slope(value):
    gate = sigmoid(value)
    return gate * (1.0 + value * (1.0 - gate))


def tree_sum(values):
    values = list(values)
    while len(values) > 1:
        values = [values[i] + values[i + 1] for i in range(0, len(values), 2)]
    return values[0]


def moments(parts, recip):
    total = tree_sum([part[...] for part in parts]) * recip
    mean = total[0:1]
    return mean, lax.rsqrt(total[1:2] - mean * mean + EPS_NORM)


def column_sum(value):
    return jnp.sum(value, axis=0, keepdims=True)


def stat_rows(value, mask):
    kept = value * mask
    return jnp.concatenate([column_sum(kept), column_sum(kept * value)], 0)


def grid_rows(images, sides):
    return sum(images * side * side for side in sides)


def class_table(images, sides_out, padded):
    table = -np.ones((4, padded), np.int32)
    base_in, base_out = 0, 0
    for side in sides_out:
        extent = 2 * side
        for row in range(side):
            for col in range(side):
                for image in range(images):
                    for kind in range(4):
                        cell = (2 * row + kind // 2) * extent + 2 * col + kind % 2
                        table[kind, base_out + (row * side + col) * images + image] = (
                            base_in + cell * images + image
                        )
        base_in += images * extent * extent
        base_out += images * side * side
    return table


def shift_table(images, sides_out, padded):
    table = -np.ones((9, padded), np.int32)
    base = 0
    for side in sides_out:
        for row in range(side):
            for col in range(side):
                for which in range(9):
                    row_to, col_to = row + which // 3 - 1, col + which % 3 - 1
                    if 0 <= row_to < side and 0 <= col_to < side:
                        for image in range(images):
                            table[which, base + (row * side + col) * images + image] = (
                                base + (row_to * side + col_to) * images + image
                            )
        base += images * side * side
    return table


def one_hot(table, width):
    return (jnp.asarray(table)[..., None] == jnp.arange(width, dtype=jnp.int32)).astype(BF16)


def first_kernel(x_ref, w_ref, mask_ref, z_ref, stat_ref):
    z = dot_nn(x_ref[0], w_ref[...])
    z_ref[0] = z
    rows = stat_rows(z, mask_ref[...])

    @pl.when(pl.program_id(0) == 0)
    def _():
        stat_ref[...] = rows

    @pl.when(pl.program_id(0) > 0)
    def _():
        stat_ref[...] += rows


def side_kernel(x_ref, w_ref, mask_ref, z_ref, stat_ref):
    term = dot_nn(x_ref[0], w_ref[...])

    @pl.when(pl.program_id(1) == 0)
    def _():
        z_ref[...] = term

    @pl.when(pl.program_id(1) > 0)
    def _():
        z_ref[...] += term

    @pl.when(pl.program_id(1) == pl.num_programs(1) - 1)
    def _():
        stat_ref[...] = stat_rows(z_ref[...], mask_ref[...])


def tap_forward(tap, stride):
    if stride == 1:
        return 0, tap
    row_tap, col_tap = tap // 3, tap % 3
    kind = jnp.where(row_tap == 1, 0, 2) + jnp.where(col_tap == 1, 0, 1)
    shift = jnp.where(row_tap == 0, 0, 3) + jnp.where(col_tap == 0, 0, 1)
    return kind, shift


def tap_backward(tap, stride):
    if stride == 1:
        return 0, 8 - tap
    row_tap, col_tap = tap // 3, tap % 3
    kind = jnp.where(row_tap == 1, 0, 2) + jnp.where(col_tap == 1, 0, 1)
    shift = jnp.where(row_tap == 0, 6, 3) + jnp.where(col_tap == 0, 2, 1)
    return kind, shift


def conv_kernel(count, kinds, stride):
    def body(*refs):
        z_ref = refs[0]
        parts = refs[1 : 1 + count]
        affine_ref, recip_ref, mask_ref, shift_ref, w_ref, act_ref, out_ref, stat_ref = refs[
            1 + count :
        ]
        tap = pl.program_id(0)

        @pl.when(tap == 0)
        def _():
            mean, inv = moments(parts, recip_ref[...])
            for kind in range(kinds):
                pre = affine_ref[0:1] * ((z_ref[kind] - mean) * inv) + affine_ref[1:2]
                act_ref[kind] = (pre * sigmoid(pre)).astype(BF16)

        kind, shift = tap_forward(tap, stride)
        patch = dot_nn(shift_ref[shift], act_ref[kind]).astype(BF16)
        term = dot_nn(patch, w_ref[...])

        @pl.when(tap == 0)
        def _():
            out_ref[...] = term

        @pl.when(tap > 0)
        def _():
            out_ref[...] += term

        @pl.when(tap == 8)
        def _():
            stat_ref[...] = stat_rows(out_ref[...], mask_ref[...])

    return body


def widen_kernel(count, carry):
    def body(*refs):
        z_ref = refs[0]
        parts = refs[1 : 1 + count]
        rest = refs[1 + count :]
        if carry:
            affine_ref, recip_ref, mask_ref, w_ref, side_ref, act_ref, out_ref, stat_ref = rest
        else:
            affine_ref, recip_ref, mask_ref, w_ref, act_ref, out_ref, stat_ref = rest

        @pl.when(pl.program_id(0) == 0)
        def _():
            mean, inv = moments(parts, recip_ref[...])
            pre = affine_ref[0:1] * ((z_ref[...] - mean) * inv) + affine_ref[1:2]
            act_ref[...] = (pre * sigmoid(pre)).astype(BF16)

        z = dot_nn(act_ref[...], w_ref[...])
        out_ref[...] = z
        if carry:
            stat_ref[...] = jnp.concatenate([stat_rows(z, mask_ref[...]), side_ref[...]], 0)
        else:
            stat_ref[...] = stat_rows(z, mask_ref[...])

    return body


def pair_moments(parts, recip):
    total = tree_sum([part[...] for part in parts]) * recip
    mean, mean_side = total[0:1], total[2:3]
    inv = lax.rsqrt(total[1:2] - mean * mean + EPS_NORM)
    inv_side = lax.rsqrt(total[3:4] - mean_side * mean_side + EPS_NORM)
    return mean, inv, mean_side, inv_side


def mix_kernel(count):
    def body(*refs):
        z_ref, side_ref = refs[:2]
        parts = refs[2 : 2 + count]
        (affine_ref, affine_side_ref, recip_ref, mask_ref, w_ref) = refs[2 + count : 7 + count]
        hidden_ref, low_ref, out_ref, stat_ref = refs[7 + count :]
        mean, inv, mean_side, inv_side = pair_moments(parts, recip_ref[...])
        pre = (
            affine_ref[0:1] * ((z_ref[...] - mean) * inv)
            + affine_ref[1:2]
            + affine_side_ref[0:1] * ((side_ref[...] - mean_side) * inv_side)
            + affine_side_ref[1:2]
        )
        hidden = pre * sigmoid(pre)
        hidden_ref[...] = hidden
        low = hidden.astype(BF16)
        low_ref[...] = low
        term = dot_nn(low, w_ref[...])

        @pl.when(pl.program_id(0) == 0)
        def _():
            out_ref[...] = term

        @pl.when(pl.program_id(0) > 0)
        def _():
            out_ref[...] += term

        @pl.when(pl.program_id(0) == pl.num_programs(0) - 1)
        def _():
            stat_ref[...] = stat_rows(out_ref[...], mask_ref[...])

    return body


def cell_rows(images, sides):
    base = 0
    for level, side in enumerate(sides):
        for row in range(side):
            for col in range(side):
                yield level, row, col, base + (row * side + col) * images
        base += images * side * side


def output_kernel(count, images, sides):
    def body(*refs):
        z_ref = refs[0]
        parts = refs[1 : 1 + count]
        affine_ref, recip_ref, mask_ref, hidden_ref = refs[1 + count : 5 + count]
        cot_refs = refs[5 + count : 8 + count]
        y_refs = refs[8 + count : 11 + count]
        grad_ref, stat_ref, flat_ref = refs[11 + count :]
        used = grid_rows(images, sides)
        if flat_ref.shape[0] > used:
            flat_ref[used:] = jnp.zeros((flat_ref.shape[0] - used, flat_ref.shape[1]), F32)
        for level, row, col, at in cell_rows(images, sides):
            flat_ref[at : at + images] = cot_refs[level][row, col].astype(F32)
        mean, inv = moments(parts, recip_ref[...])
        normed = (z_ref[...] - mean) * inv
        pre = affine_ref[0:1] * normed + affine_ref[1:2] + hidden_ref[...]
        gate = sigmoid(pre)
        grad = flat_ref[...] * mask_ref[...] * (gate * (1.0 + pre * (1.0 - gate)))
        grad_ref[...] = grad
        stat_ref[...] = jnp.concatenate([column_sum(grad * normed), column_sum(grad)], 0)
        flat_ref[...] = pre * gate
        for level, row, col, at in cell_rows(images, sides):
            y_refs[level][row, col] = flat_ref[at : at + images].astype(BF16)

    return body


def input_grad_kernel(images, sides):
    def body(dz_ref, w_ref, side_ref, w_side_ref, *rest):
        out_refs, flat_ref = rest[:3], rest[3]
        for kind in range(4):
            value = dot_nt(dz_ref[kind], w_ref[...])
            if kind == 0:
                value += dot_nt(side_ref[...], w_side_ref[...])
            flat_ref[...] = value
            for level, row, col, at in cell_rows(images, sides):
                out_refs[level][2 * row + kind // 2, 2 * col + kind % 2] = flat_ref[
                    at : at + images
                ]

    return body


def norm_back(grad, normed, sums, recip, mask, scale):
    return scale * (grad - mask * (sums[1:2] * recip + normed * (sums[0:1] * recip)))


def back_linear_kernel(count):
    def body(*refs):
        grad_ref, z_ref = refs[:2]
        parts = refs[2 : 2 + count]
        sums = refs[2 + count : 2 + 2 * count]
        affine_ref, recip_ref, mask_ref, w_ref, below_ref = refs[2 + 2 * count : 7 + 2 * count]
        below_parts = refs[7 + 2 * count : 7 + 3 * count]
        below_affine_ref, dz_ref, out_ref, stat_ref = refs[7 + 3 * count :]
        recip = recip_ref[...]
        mean, inv = moments(parts, recip)
        total = tree_sum([part[...] for part in sums])
        normed = (z_ref[...] - mean) * inv
        dz = norm_back(grad_ref[...], normed, total, recip, mask_ref[...], affine_ref[0:1] * inv)
        dz = dz.astype(BF16)
        dz_ref[...] = dz
        term = dot_nt(dz, w_ref[...])

        @pl.when(pl.program_id(0) == 0)
        def _():
            out_ref[...] = term

        @pl.when(pl.program_id(0) > 0)
        def _():
            out_ref[...] += term

        @pl.when(pl.program_id(0) == pl.num_programs(0) - 1)
        def _():
            finish_below(out_ref, below_ref, below_parts, below_affine_ref, recip, stat_ref)

    return body


def finish_below(out_ref, below_ref, below_parts, below_affine_ref, recip, stat_ref):
    mean, inv = moments(below_parts, recip)
    normed = (below_ref[...] - mean) * inv
    pre = below_affine_ref[0:1] * normed + below_affine_ref[1:2]
    grad = out_ref[...] * slope(pre)
    out_ref[...] = grad
    stat_ref[...] = jnp.concatenate([column_sum(grad * normed), column_sum(grad)], 0)


def back_conv_kernel(count, kinds, stride):
    def body(*refs):
        grad_ref, z_ref = refs[:2]
        parts = refs[2 : 2 + count]
        sums = refs[2 + count : 2 + 2 * count]
        affine_ref, recip_ref, mask_ref, shift_ref, w_ref, below_ref = refs[
            2 + 2 * count : 8 + 2 * count
        ]
        below_parts = refs[8 + 2 * count : 8 + 3 * count]
        below_affine_ref, below_recip_ref, dz_ref, out_ref, stat_ref = refs[8 + 3 * count :]
        tap = pl.program_id(0)

        @pl.when(tap == 0)
        def _():
            recip = recip_ref[...]
            mean, inv = moments(parts, recip)
            total = tree_sum([part[...] for part in sums])
            normed = (z_ref[...] - mean) * inv
            dz = norm_back(
                grad_ref[...], normed, total, recip, mask_ref[...], affine_ref[0:1] * inv
            )
            dz_ref[...] = dz.astype(BF16)
            out_ref[...] = jnp.zeros_like(out_ref)

        kind, shift = tap_backward(tap, stride)
        patch = dot_nn(shift_ref[shift], dz_ref[...]).astype(BF16)
        out_ref[kind] += dot_nt(patch, w_ref[...])

        @pl.when(tap == 8)
        def _():
            mean, inv = moments(below_parts, below_recip_ref[...])
            rows = None
            for which in range(kinds):
                normed = (below_ref[which] - mean) * inv
                pre = below_affine_ref[0:1] * normed + below_affine_ref[1:2]
                grad = out_ref[which] * slope(pre)
                out_ref[which] = grad
                part = jnp.concatenate([column_sum(grad * normed), column_sum(grad)], 0)
                rows = part if rows is None else rows + part
            stat_ref[...] = rows

    return body


def back_mix_kernel(count):
    def body(*refs):
        grad_ref, z_ref = refs[:2]
        parts = refs[2 : 2 + count]
        sums = refs[2 + count : 2 + 2 * count]
        affine_ref, recip_ref, mask_ref, w_ref, above_ref, mid_ref, side_ref = refs[
            2 + 2 * count : 9 + 2 * count
        ]
        pair_parts = refs[9 + 2 * count : 9 + 3 * count]
        affine_mid_ref, affine_side_ref, dz_ref, out_ref, stat_ref = refs[9 + 3 * count :]
        recip = recip_ref[...]

        @pl.when(pl.program_id(0) == 0)
        def _():
            mean, inv = moments(parts, recip)
            total = tree_sum([part[...] for part in sums])
            normed = (z_ref[...] - mean) * inv
            dz = norm_back(
                grad_ref[...], normed, total, recip, mask_ref[...], affine_ref[0:1] * inv
            )
            dz_ref[...] = dz.astype(BF16)

        mean, inv, mean_side, inv_side = pair_moments(pair_parts, recip)
        normed = (mid_ref[...] - mean) * inv
        normed_side = (side_ref[...] - mean_side) * inv_side
        pre = (
            affine_mid_ref[0:1] * normed
            + affine_mid_ref[1:2]
            + affine_side_ref[0:1] * normed_side
            + affine_side_ref[1:2]
        )
        grad = (above_ref[...] + dot_nt(dz_ref[...], w_ref[...])) * slope(pre)
        out_ref[...] = grad
        stat_ref[...] = jnp.concatenate(
            [column_sum(grad * normed), column_sum(grad), column_sum(grad * normed_side)], 0
        )

    return body


def back_pair_kernel(count):
    def body(*refs):
        grad_ref, mid_ref, side_ref = refs[:3]
        pair_parts = refs[3 : 3 + count]
        sums = refs[3 + count : 3 + 2 * count]
        affine_mid_ref, affine_side_ref, recip_ref, mask_ref, w_ref, below_ref = refs[
            3 + 2 * count : 9 + 2 * count
        ]
        below_parts = refs[9 + 2 * count : 9 + 3 * count]
        below_affine_ref, dz_ref, dz_side_ref, out_ref, stat_ref = refs[9 + 3 * count :]
        recip = recip_ref[...]
        mean, inv, mean_side, inv_side = pair_moments(pair_parts, recip)
        total = tree_sum([part[...] for part in sums])
        normed = (mid_ref[...] - mean) * inv
        normed_side = (side_ref[...] - mean_side) * inv_side
        grad = grad_ref[...]
        mask = mask_ref[...]
        dz = norm_back(grad, normed, total[0:2], recip, mask, affine_mid_ref[0:1] * inv)
        dz = dz.astype(BF16)
        dz_ref[...] = dz
        total_side = jnp.concatenate([total[2:3], total[1:2]], 0)
        dz_side_ref[...] = norm_back(
            grad, normed_side, total_side, recip, mask, affine_side_ref[0:1] * inv_side
        ).astype(BF16)
        term = dot_nt(dz, w_ref[...])

        @pl.when(pl.program_id(0) == 0)
        def _():
            out_ref[...] = term

        @pl.when(pl.program_id(0) > 0)
        def _():
            out_ref[...] += term

        @pl.when(pl.program_id(0) == pl.num_programs(0) - 1)
        def _():
            finish_below(out_ref, below_ref, below_parts, below_affine_ref, recip, stat_ref)

    return body


def back_first_kernel(count):
    def body(*refs):
        grad_ref, z_ref = refs[:2]
        parts = refs[2 : 2 + count]
        sums = refs[2 + count : 2 + 2 * count]
        affine_ref, recip_ref, mask_ref, x_ref, _, dz_ref, grad_w_ref, total_ref = refs[
            2 + 2 * count :
        ]
        recip = recip_ref[...]
        mean, inv = moments(parts, recip)
        total = tree_sum([part[...] for part in sums])
        normed = (z_ref[0] - mean) * inv
        dz = norm_back(grad_ref[0], normed, total, recip, mask_ref[...], affine_ref[0:1] * inv)
        dz = dz.astype(BF16)
        dz_ref[0] = dz
        term = dot_tn(x_ref[0], dz)

        @pl.when(pl.program_id(0) == 0)
        def _():
            total_ref[...] = term

        @pl.when(pl.program_id(0) > 0)
        def _():
            total_ref[...] += term

        @pl.when(pl.program_id(0) == pl.num_programs(0) - 1)
        def _():
            grad_w_ref[...] = total_ref[...].astype(BF16)

    return body


def weight_grad_kernel(act_ref, dz_ref, *rest):
    rest[-1][...] = dot_tn(act_ref[...], dz_ref[...]).astype(BF16)


def conv_grad_kernel(stride, first):
    def body(act_ref, shift_ref, dz_ref, *rest):
        kind, shift = tap_forward(pl.program_id(0) + first, stride)
        patch = dot_nn(shift_ref[shift], act_ref[kind]).astype(BF16)
        rest[-1][...] = dot_tn(patch, dz_ref[...]).astype(BF16)

    return body


def pack_kernel(count, spans, piece):
    def body(*refs):
        out_ref = refs[-1]
        columns = out_ref.shape[1]
        high = out_ref.shape[0] // 2
        for which, (start, width, rows) in enumerate(spans):
            parts = refs[which * count : (which + 1) * count]
            total = tree_sum([part[...] for part in parts])
            for offset in range(0, width, piece):
                line, at = (start + offset) // columns, (start + offset) % columns
                for slot, row in enumerate(rows):
                    here = slot * high + line
                    out_ref[here : here + 1, at : at + piece] = total[
                        row : row + 1, offset : offset + piece
                    ]

    return body


def merge_kernel(split, has_kept, last):
    def add(kept_ref, came_ref):
        total = kept_ref[...].astype(F32) + came_ref[...].astype(F32)
        return total if last else total.astype(BF16)

    def body(index_ref, *refs):
        if not has_kept:
            refs[1][...] = refs[0][...]
        elif split:
            refs[4][...] = add(refs[0], refs[1])
            refs[5][...] = add(refs[2], refs[3])
        else:
            refs[2][...] = add(refs[0], refs[1])

    return body


def level_masks(first_row, rows, bounds):
    index = first_row + lax.broadcasted_iota(jnp.int32, (rows, 1), 0)
    return [
        ((index >= bounds[level]) & (index < bounds[level + 1])).astype(F32)
        for level in range(len(bounds) - 1)
    ]


def tally_kernel(bounds, extra):
    levels = len(bounds) - 1

    def body(first_ref, grad_ref, master_ref, old_ref, *rest):
        rows_ref, sums_ref = rest[-2:]
        if extra:
            sums_ref[4 * levels :] = rest[0][...]
        grad = grad_ref[...]
        master = master_ref[...]
        square = grad * grad
        raised = square + EPS_ONE
        rows_new = DECAY * old_ref[...] + (1.0 - DECAY) * jnp.mean(raised, 1, keepdims=True)
        rows_ref[...] = rows_new
        ratio = square / rows_new
        weight = jnp.sum(master * master, 1, keepdims=True)
        masks = level_masks(first_ref[0], grad.shape[0], bounds)
        spread = jnp.zeros((1, grad.shape[1]), F32)
        for level in range(levels):
            mask = masks[level]
            sums_ref[level : level + 1] = column_sum(raised * mask)
            sums_ref[levels + level : levels + level + 1] = column_sum(ratio * mask)
            low = 2 * levels + level
            sums_ref[low : low + 1] = spread + column_sum(rows_new * mask)
            low = 3 * levels + level
            sums_ref[low : low + 1] = spread + column_sum(weight * mask)

    return body


def renew_kernel(bounds):
    levels = len(bounds) - 1

    def body(first_ref, grad_ref, master_ref, rows_ref, sums_ref, old_ref, cols_ref, new_ref, low_ref):
        grad = grad_ref[...]
        columns = grad.shape[1]
        masks = level_masks(first_ref[0], grad.shape[0], bounds)
        factor = None
        for level in range(levels):
            height = float(bounds[level + 1] - bounds[level])
            cells = height * columns
            col_sum = sums_ref[level : level + 1]
            ratio_sum = sums_ref[levels + level : levels + level + 1]
            row_mean = sums_ref[2 * levels + level : 2 * levels + level + 1] / height
            weight_sum = sums_ref[3 * levels + level : 3 * levels + level + 1]
            cols_new = DECAY * old_ref[level : level + 1] + (1.0 - DECAY) * (col_sum / height)
            cols_ref[level : level + 1] = cols_new
            relative = cols_new / row_mean
            update_sq = jnp.sum(ratio_sum / relative, axis=1, keepdims=True)
            update_rms = jnp.sqrt(update_sq / cells)
            weight_rms = jnp.sqrt(weight_sum / cells)
            step = STEP_RATE * jnp.maximum(EPS_TWO, weight_rms) / jnp.maximum(1.0, update_rms)
            part = masks[level] * (step * lax.rsqrt(relative))
            factor = part if factor is None else factor + part
        new = master_ref[...] - grad * lax.rsqrt(rows_ref[...]) * factor
        new_ref[...] = new
        low_ref[...] = new.astype(BF16)

    return body


class Exchange:
    def __init__(self, n_wide, n_narrow):
        self.n_narrow = n_narrow
        self.total = n_wide * n_narrow
        self.bits = self.total.bit_length() - 1
        self.narrow_bits = n_narrow.bit_length() - 1
        self.index = lax.axis_index(AXES)

    def bit(self, level):
        return (self.index >> level) & 1

    def swap(self, value, level):
        pairs = [(device, device ^ (1 << level)) for device in range(self.total)]
        return lax.ppermute(value, AXES, pairs)

    def group_parts(self, value):
        return [value] + [
            lax.ppermute(value, "narrow", [(i, i ^ k) for i in range(self.n_narrow)])
            for k in range(1, self.n_narrow)
        ]

    def total_sums(self, value, first=0):
        sums = []
        for level in range(first, self.bits):
            value = value + self.swap(value, level)
            sums.append(value)
        return sums


def insert_bit(unit, place, bit):
    return ((unit >> place) << (place + 1)) | (bit << place) | (unit & ((1 << place) - 1))


class Scatter:
    def __init__(self, link, kernels, part, name, prefix=(), first="narrow"):
        self.link = link
        self.kernels = kernels
        self.name = name
        self.prefix = prefix
        self.open_bits = link.bits - len(prefix)
        units = 1 << self.open_bits
        self.kept = part.reshape(units, part.shape[0] // units, part.shape[1])
        self.left = list(range(self.open_bits))
        inner = list(range(1, link.narrow_bits))
        outer = list(range(link.narrow_bits, link.bits))
        orders = {
            "narrow": inner + outer,
            "wide": outer[:1] + inner + outer[1:],
            "all_wide": outer + inner,
        }
        self.levels = [0] + orders[first]
        self.at = 0
        self.came = None
        self.chosen = None
        self.after = []
        self.send_half(None)

    def place(self, level):
        return self.left.index(level)

    def unit_spec(self, source):
        dims = (1,) + self.kept.shape[1:]
        return block(dims, lambda unit, index: (source(unit, index[0]), 0, 0))

    def kept_source(self, source):
        if self.chosen is None:
            return source
        place, level = self.chosen
        return lambda unit, index: insert_bit(
            source(unit, index), place, (index >> level) & 1
        )

    def run(self, body, specs, outs, number, args, dtype):
        spec = self.unit_spec(lambda unit, index: unit)
        shape = shape_of((number,) + self.kept.shape[1:], dtype)
        out = self.kernels(
            body,
            self.name + "_" + str(self.at),
            (number,),
            specs,
            [spec] * outs,
            [shape] * outs,
            4 * number * self.kept.shape[1] * self.kept.shape[2] * 200,
            scalars=1,
            after=self.after,
        )(self.link.index.astype(jnp.int32).reshape(1), *args)
        return out

    def send_half(self, came):
        level = self.levels[self.at] if self.at < len(self.levels) else None
        total_units = 1 << len(self.left)
        if level is not None and level < self.open_bits:
            place = self.place(level)

            def keep(unit, index):
                return insert_bit(unit, place, (index >> level) & 1)

            def send(unit, index):
                return insert_bit(unit, place, 1 - ((index >> level) & 1))

            half = total_units // 2
            if came is None:
                (sent,) = self.run(
                    merge_kernel(True, False, False),
                    [self.unit_spec(send)],
                    1,
                    half,
                    [self.kept],
                    BF16,
                )
                self.chosen = (place, level)
            else:
                kept_keep = self.unit_spec(self.kept_source(keep))
                kept_send = self.unit_spec(self.kept_source(send))
                kept, sent = self.run(
                    merge_kernel(True, True, False),
                    [kept_keep, self.unit_spec(keep), kept_send, self.unit_spec(send)],
                    2,
                    half,
                    [self.kept, came, self.kept, came],
                    BF16,
                )
                self.kept, self.chosen = kept, None
            self.left.remove(level)
            with jax.named_scope(self.name + "_bit" + str(level)):
                self.came = self.link.swap(sent, level)
        else:
            same = lambda unit, index: unit
            (self.kept,) = self.run(
                merge_kernel(False, True, level is None),
                [self.unit_spec(self.kept_source(same)), self.unit_spec(same)],
                1,
                total_units,
                [self.kept, came],
                F32 if level is None else BF16,
            )
            self.chosen = None
            if level is None:
                return
            pairs = []
            for device in range(self.link.total):
                settled = all(
                    (device >> other) & 1 == self.prefix[other - self.open_bits]
                    for other in range(self.open_bits, level)
                )
                if settled and (device >> level) & 1 != self.prefix[level - self.open_bits]:
                    pairs.append((device, device ^ (1 << level)))
            with jax.named_scope(self.name + "_bit" + str(level)):
                self.came = lax.ppermute(self.kept, AXES, pairs)

    def step(self, after=()):
        if self.at < len(self.levels):
            self.at += 1
            self.after = list(after)
            self.send_half(self.came)

    def finish(self):
        while self.at < len(self.levels):
            self.step()
        return self.kept.reshape(self.kept.shape[1:])


def make_body(mesh):
    n_wide, n_narrow = mesh.shape["wide"], mesh.shape["narrow"]

    def body(
        x_lo,
        x_mid,
        x_hi,
        cot_lo,
        cot_mid,
        cot_hi,
        live_counts,
        slim_master,
        broad_master,
        slim_rowstat,
        broad_rowstat,
        slim_colstat,
        broad_colstat,
        norm_params,
        norm_moments,
    ):
        link = Exchange(n_wide, n_narrow)
        kernel_call = Kernels()
        count = n_narrow
        images = x_lo.shape[0]
        sides = tuple(value.shape[1] // 2 for value in (x_lo, x_mid, x_hi))
        c_in, mid, c_out = x_lo.shape[3], slim_master.shape[1], broad_master.shape[1]
        cells = grid_rows(images, sides)
        cells_in = 4 * cells
        rows = -(-cells // 16) * 16
        chunks = c_out // mid
        bounds_slim = (0, c_in, c_in + 9 * mid, c_in + 9 * mid + c_out, c_in + 18 * mid + c_out)
        bounds_broad = (0, mid, mid + c_in, 2 * mid + c_in)
        at_two, at_four, at_five = (bounds_slim[level] // mid for level in (1, 2, 3))
        at_six = bounds_broad[2] // mid
        widths = (mid, mid, c_out, c_out, mid, mid, c_out)
        norm_at = [sum(widths[:level]) // mid for level in range(7)]

        slim = lax.all_gather(slim_master.astype(BF16), AXES, axis=0, tiled=True)
        broad = lax.all_gather(broad_master.astype(BF16), AXES, axis=0, tiled=True)

        kinds = class_table(images, sides, rows)
        shifts = one_hot(shift_table(images, sides, rows), rows)

        def by_cell(value):
            return jnp.transpose(value, (1, 2, 0, 3))

        x_flat = jnp.concatenate(
            [by_cell(value).reshape(-1, c_in) for value in (x_lo, x_mid, x_hi)], 0
        )
        x_kinds = jnp.dot(one_hot(kinds.reshape(-1), cells_in), x_flat, preferred_element_type=F32)
        x_kinds = x_kinds.astype(BF16).reshape(4, rows, c_in)
        alive = [
            (jnp.arange(images) < live_counts[0, level]).astype(F32) for level in range(3)
        ]
        mask = jnp.concatenate(
            [jnp.tile(alive[level], side * side) for level, side in enumerate(sides)]
            + [jnp.zeros((rows - cells,), F32)]
        )
        cell_count = tree_sum(link.group_parts(jnp.sum(mask).reshape(1, 1)))
        mask = mask[:, None]
        recip = 1.0 / cell_count
        recip_in = 0.25 / cell_count

        narrow_all = whole((rows, mid))
        kinds_all = whole((4, rows, mid))
        stat_all = whole((2, mid))
        mask_all = whole((rows, 1))
        one_all = whole((1, 1))
        shifts_all = whole((9, rows, rows))
        chunk = block((rows, mid), lambda j: (0, j))

        def stat_chunk(height):
            return block((height, mid), lambda j: (0, j))

        def affine(level):
            return block((2, mid), lambda j: (0, norm_at[level]))

        def affine_chunk(level):
            return block((2, mid), lambda j: (0, norm_at[level] + j))

        def slim_block(at):
            return block((mid, mid), lambda j: (at + j, 0))

        def broad_block(at):
            return block((mid, mid), lambda j: (at, j))

        narrow_f32 = shape_of((rows, mid), F32)
        wide_f32 = shape_of((rows, c_out), F32)
        narrow_low = shape_of((rows, mid), BF16)
        wide_low = shape_of((rows, c_out), BF16)
        stat_narrow = shape_of((2, mid), F32)
        stat_wide = shape_of((2, c_out), F32)
        flops_conv = 2 * rows * 9 * mid * (mid + rows)
        flops_wide = 2 * rows * mid * c_out

        z_one, stat = kernel_call(
            first_kernel,
            "first",
            (4,),
            [
                block((1, rows, c_in), lambda j: (j, 0, 0)),
                whole((c_in, mid)),
                mask_all,
            ],
            [block((1, rows, mid), lambda j: (j, 0, 0)), stat_all],
            [shape_of((4, rows, mid), F32), stat_narrow],
            2 * 4 * rows * c_in * mid,
            after=[recip],
        )(x_kinds, slim, mask)
        parts_one = link.group_parts(stat)
        act_one, z_two, stat = kernel_call(
            conv_kernel(count, 4, 2),
            "conv_two",
            (9,),
            [kinds_all]
            + [stat_all] * count
            + [affine(0), one_all, mask_all, shifts_all, slim_block(at_two)],
            [kinds_all, narrow_all, stat_all],
            [shape_of((4, rows, mid), BF16), narrow_f32, stat_narrow],
            flops_conv,
        )(z_one, *parts_one, norm_params, recip_in, mask, shifts, slim)
        parts_two = link.group_parts(stat)
        z_side, stat_side = kernel_call(
            side_kernel,
            "side",
            (chunks, c_in // mid),
            [
                block((1, rows, mid), lambda j, k: (0, 0, k)),
                block((mid, mid), lambda j, k: (1 + k, j)),
                whole((rows, 1)),
            ],
            [
                block((rows, mid), lambda j, k: (0, j)),
                block((2, mid), lambda j, k: (0, j)),
            ],
            [wide_f32, stat_wide],
            2 * rows * c_in * c_out,
        )(x_kinds, broad, mask)
        act_two, z_three, stat = kernel_call(
            widen_kernel(count, True),
            "widen_three",
            (chunks,),
            [narrow_all]
            + [stat_all] * count
            + [affine(1), one_all, mask_all, broad_block(0), stat_chunk(2)],
            [narrow_all, chunk, stat_chunk(4)],
            [narrow_low, wide_f32, shape_of((4, c_out), F32)],
            flops_wide,
        )(z_two, *parts_two, norm_params, recip, mask, broad, stat_side)
        parts_pair = link.group_parts(stat)
        hidden, hidden_low, z_four, stat = kernel_call(
            mix_kernel(count),
            "mix",
            (chunks,),
            [chunk, chunk]
            + [stat_chunk(4)] * count
            + [affine_chunk(2), affine_chunk(3), one_all, mask_all, slim_block(at_four)],
            [chunk, chunk, narrow_all, stat_all],
            [wide_f32, wide_low, narrow_f32, stat_narrow],
            flops_wide,
        )(z_three, z_side, *parts_pair, norm_params, norm_params, recip, mask, slim)
        parts_four = link.group_parts(stat)
        one_kind = whole((1, rows, mid))
        act_four, z_five, stat = kernel_call(
            conv_kernel(count, 1, 1),
            "conv_five",
            (9,),
            [one_kind]
            + [stat_all] * count
            + [affine(4), one_all, mask_all, shifts_all, slim_block(at_five)],
            [one_kind, narrow_all, stat_all],
            [shape_of((1, rows, mid), BF16), narrow_f32, stat_narrow],
            flops_conv,
        )(z_four[None], *parts_four, norm_params, recip, mask, shifts, slim)
        parts_five = link.group_parts(stat)
        act_five, z_six, stat = kernel_call(
            widen_kernel(count, False),
            "widen_six",
            (chunks,),
            [narrow_all]
            + [stat_all] * count
            + [affine(5), one_all, mask_all, broad_block(at_six)],
            [narrow_all, chunk, stat_chunk(2)],
            [narrow_low, wide_f32, stat_wide],
            flops_wide,
        )(z_five, *parts_five, norm_params, recip, mask, broad)
        parts_six = link.group_parts(stat)
        grids = [
            block((side, side, images, mid), lambda j: (0, 0, 0, j)) for side in sides
        ]
        *y_grids, grad_out, stat = kernel_call(
            output_kernel(count, images, sides),
            "output",
            (chunks,),
            [chunk]
            + [stat_chunk(2)] * count
            + [affine_chunk(6), one_all, mask_all, chunk]
            + grids,
            grids + [chunk, stat_chunk(2)],
            [shape_of((side, side, images, c_out), BF16) for side in sides]
            + [wide_f32, stat_wide],
            flops_wide // 8,
            scratch=[pltpu.VMEM((rows, mid), F32)],
        )(
            z_six,
            *parts_six,
            norm_params,
            recip,
            mask,
            hidden,
            *[by_cell(value) for value in (cot_lo, cot_mid, cot_hi)],
        )
        sums_six = link.group_parts(stat)

        dz_six, grad_five, stat = kernel_call(
            back_linear_kernel(count),
            "back_six",
            (chunks,),
            [chunk, chunk]
            + [stat_chunk(2)] * (2 * count)
            + [affine_chunk(6), one_all, mask_all, broad_block(at_six), narrow_all]
            + [stat_all] * count
            + [affine(5)],
            [chunk, narrow_all, stat_all],
            [wide_low, narrow_f32, stat_narrow],
            flops_wide,
        )(
            grad_out,
            z_six,
            *parts_six,
            *sums_six,
            norm_params,
            recip,
            mask,
            broad,
            z_five,
            *parts_five,
            norm_params,
        )
        sums_five = link.group_parts(stat)

        def weight_grad(act, dz, steps, act_at, out_shape, out_at, base, name):
            high, across = steps
            height = act.shape[0]
            specs = [
                block((height, mid), lambda i, j: (0, act_at + i)),
                block((height, mid), lambda i, j: (0, j)),
            ]
            args = [act, dz]
            if base is not None:
                specs.append(pl.BlockSpec(memory_space=pl.ANY))
                args.append(base)
            return kernel_call(
                weight_grad_kernel,
                name,
                (high, across),
                specs,
                block((mid, mid), lambda i, j: (out_at + i, j)),
                shape_of(out_shape, BF16),
                2 * height * mid * mid * high * across,
                aliases={2: 0} if base is not None else None,
            )(*args)

        def conv_grad(act, dz, stride, taps, out_shape, out_at, base, name):
            first, number = taps
            kinds_here = act.shape[0]
            specs = [whole((kinds_here, rows, mid)), shifts_all, narrow_all]
            args = [act, shifts, dz]
            if base is not None:
                specs.append(pl.BlockSpec(memory_space=pl.ANY))
                args.append(base)
            return kernel_call(
                conv_grad_kernel(stride, first),
                name,
                (number,),
                specs,
                block((mid, mid), lambda t: (out_at + t, 0)),
                shape_of(out_shape, BF16),
                flops_conv * number // 9,
                aliases={3: 0} if base is not None else None,
            )(*args)

        slim_part = (bounds_slim[-1] // 4, mid)
        broad_part = (bounds_broad[-1] // 4, c_out)
        per_part = slim_part[0] // mid
        term_six = weight_grad(act_five, dz_six, (1, chunks), 0, broad_part, 0, None, "grad_six")
        chain_six = Scatter(link, kernel_call, term_six, "sum_six", (1, 1), "all_wide")

        dz_five, grad_four, stat = kernel_call(
            back_conv_kernel(count, 1, 1),
            "back_five",
            (9,),
            [narrow_all, narrow_all]
            + [stat_all] * (2 * count)
            + [affine(5), one_all, mask_all, shifts_all, slim_block(at_five), one_kind]
            + [stat_all] * count
            + [affine(4), one_all],
            [narrow_all, one_kind, stat_all],
            [narrow_low, shape_of((1, rows, mid), F32), stat_narrow],
            flops_conv,
        )(
            grad_five,
            z_five,
            *parts_five,
            *sums_five,
            norm_params,
            recip,
            mask,
            shifts,
            slim,
            z_four[None],
            *parts_four,
            norm_params,
            recip,
        )
        grad_four = grad_four[0]
        sums_four = link.group_parts(stat)
        low_four = 2 * per_part - at_four
        low_five = 3 * per_part - at_five
        chain_six.step()
        term = conv_grad(
            act_four, dz_five, 1, (low_five, 9 - low_five), slim_part, 0, None, "grad_five_high"
        )
        chain_five = Scatter(link, kernel_call, term, "sum_five", (1, 1), "all_wide")
        term_four = conv_grad(
            act_four, dz_five, 1, (0, low_five), slim_part, chunks - low_four, None, "grad_five_low"
        )
        dz_four, grad_mid, stat = kernel_call(
            back_mix_kernel(count),
            "back_four",
            (chunks,),
            [narrow_all, narrow_all]
            + [stat_all] * (2 * count)
            + [affine(4), one_all, mask_all, slim_block(at_four), chunk, chunk, chunk]
            + [stat_chunk(4)] * count
            + [affine_chunk(2), affine_chunk(3)],
            [narrow_all, chunk, stat_chunk(3)],
            [narrow_low, wide_f32, shape_of((3, c_out), F32)],
            flops_wide,
        )(
            grad_four,
            z_four,
            *parts_four,
            *sums_four,
            norm_params,
            recip,
            mask,
            slim,
            grad_out,
            z_three,
            z_side,
            *parts_pair,
            norm_params,
            norm_params,
        )
        sums_pair = link.group_parts(stat)
        chain_five.step()
        chain_six.step()
        term_four = weight_grad(
            hidden_low,
            dz_four,
            (chunks - low_four, 1),
            low_four,
            slim_part,
            0,
            term_four,
            "grad_four",
        )
        chain_four = Scatter(link, kernel_call, term_four, "sum_four", (0, 1), "all_wide")
        dz_three, dz_side, grad_two, stat = kernel_call(
            back_pair_kernel(count),
            "back_three",
            (chunks,),
            [chunk, chunk, chunk]
            + [stat_chunk(4)] * count
            + [stat_chunk(3)] * count
            + [affine_chunk(2), affine_chunk(3), one_all, mask_all, broad_block(0), narrow_all]
            + [stat_all] * count
            + [affine(1)],
            [chunk, chunk, narrow_all, stat_all],
            [wide_low, wide_low, narrow_f32, stat_narrow],
            flops_wide,
        )(
            grad_mid,
            z_three,
            z_side,
            *parts_pair,
            *sums_pair,
            norm_params,
            norm_params,
            recip,
            mask,
            broad,
            z_two,
            *parts_two,
            norm_params,
        )
        sums_two = link.group_parts(stat)
        chain_four.step()
        x_sub = x_kinds[0]
        two_parts = (2 * broad_part[0], c_out)
        term_three = weight_grad(
            act_two, dz_three, (1, chunks), 0, two_parts, 0, None, "grad_three"
        )
        term = weight_grad(
            x_sub, dz_side, (1, chunks), 0, two_parts, 1, term_three, "grad_side_low"
        )
        chain_six.step()
        chain_three = Scatter(link, kernel_call, term, "sum_three", (0,), "all_wide")
        chain_five.step()
        term = weight_grad(
            x_sub, dz_side, (1, chunks), 1, broad_part, 0, None, "grad_side_high"
        )
        chain_side = Scatter(link, kernel_call, term, "sum_side", (0, 1), "narrow")

        dz_two, grad_one, stat = kernel_call(
            back_conv_kernel(count, 4, 2),
            "back_two",
            (9,),
            [narrow_all, narrow_all]
            + [stat_all] * (2 * count)
            + [affine(1), one_all, mask_all, shifts_all, slim_block(at_two), kinds_all]
            + [stat_all] * count
            + [affine(0), one_all],
            [narrow_all, kinds_all, stat_all],
            [narrow_low, shape_of((4, rows, mid), F32), stat_narrow],
            flops_conv,
        )(
            grad_two,
            z_two,
            *parts_two,
            *sums_two,
            norm_params,
            recip,
            mask,
            shifts,
            slim,
            z_one,
            *parts_one,
            norm_params,
            recip_in,
        )
        sums_one = link.group_parts(stat)
        chain_three.step()
        chain_four.step()
        chain_five.step()
        term = conv_grad(
            act_one, dz_two, 2, (per_part - at_two, 9 - per_part + at_two), slim_part, 0, None,
            "grad_two_high",
        )
        term = weight_grad(
            hidden_low, dz_four, (low_four, 1), 0, slim_part, per_part - low_four, term,
            "grad_four_low",
        )
        chain_two = Scatter(link, kernel_call, term, "sum_two", (1, 0), "narrow")
        slim_low = conv_grad(
            act_one, dz_two, 2, (0, per_part - at_two), slim_part, at_two, None, "grad_two_low"
        )
        dz_one, slim_low = kernel_call(
            back_first_kernel(count),
            "back_one",
            (4,),
            [block((1, rows, mid), lambda j: (j, 0, 0))] * 2
            + [stat_all] * (2 * count)
            + [
                affine(0),
                one_all,
                mask_all,
                block((1, rows, c_in), lambda j: (j, 0, 0)),
                pl.BlockSpec(memory_space=pl.ANY),
            ],
            [block((1, rows, mid), lambda j: (j, 0, 0)), whole((c_in, mid))],
            [shape_of((4, rows, mid), BF16), shape_of(slim_part, BF16)],
            2 * 4 * rows * c_in * mid,
            scratch=[pltpu.VMEM((c_in, mid), F32)],
            aliases={2 + 2 * count + 4: 1},
        )(grad_one, z_one, *parts_one, *sums_one, norm_params, recip_in, mask, x_kinds, slim_low)
        chain_one = Scatter(link, kernel_call, slim_low, "sum_one", (0, 0), "wide")
        chain_side.step()
        chain_two.step()
        chain_six.step()

        extents = tuple(2 * side for side in sides)
        dx_grids = kernel_call(
            input_grad_kernel(images, sides),
            "input_grad",
            (c_in // mid,),
            [
                kinds_all,
                slim_block(0),
                whole((rows, c_out)),
                block((mid, c_out), lambda j: (1 + j, 0)),
            ],
            [
                block((extent, extent, images, mid), lambda j: (0, 0, 0, j))
                for extent in extents
            ],
            [shape_of((extent, extent, images, c_in), F32) for extent in extents],
            2 * 4 * rows * c_in * mid + 2 * rows * c_in * c_out,
            scratch=[pltpu.VMEM((rows, mid), F32)],
        )(dz_one, slim, dz_side, broad)

        def by_image(value):
            return jnp.transpose(value, (2, 0, 1, 3))

        y_parts = [by_image(value) for value in y_grids]
        dx_parts = [by_image(value) for value in dx_grids]

        top = link.bit(link.bits - 1)
        second = link.bit(link.bits - 2)

        def choose(bit, upper, lower):
            return jnp.where(bit == 1, upper, lower)

        def tally(grad, master, rowstat, bounds, name, after, extra=None):
            height, columns = grad.shape
            levels = len(bounds) - 1
            first = (link.index * height).astype(jnp.int32).reshape(1)
            matrix, column = whole((height, columns)), whole((height, 1))
            extras = [] if extra is None else [extra]
            sum_dims = (4 * levels + sum(value.shape[0] for value in extras), columns)
            rows_new, sums = kernel_call(
                tally_kernel(bounds, bool(extras)),
                name,
                (1,),
                [pl.BlockSpec(memory_space=pltpu.SMEM), matrix, matrix, column]
                + [whole(value.shape) for value in extras],
                [column, whole(sum_dims)],
                [shape_of((height, 1), F32), shape_of(sum_dims, F32)],
                20 * height * columns,
                after=after,
            )(first, grad, master, rowstat.reshape(height, 1), *extras)
            return rows_new, link.total_sums(sums)

        def renew(grad, master, rows_new, sums, colstat, bounds, name):
            height, columns = grad.shape
            levels = len(bounds) - 1
            first = (link.index * height).astype(jnp.int32).reshape(1)
            matrix, column = whole((height, columns)), whole((height, 1))
            sums_all, cols_all = whole((4 * levels, columns)), whole((levels, columns))
            return kernel_call(
                renew_kernel(bounds),
                name,
                (1,),
                [
                    pl.BlockSpec(memory_space=pltpu.SMEM),
                    matrix,
                    matrix,
                    column,
                    sums_all,
                    cols_all,
                ],
                [cols_all, matrix, matrix],
                [
                    shape_of((levels, columns), F32),
                    shape_of((height, columns), F32),
                    shape_of((height, columns), BF16),
                ],
                20 * height * columns,
            )(first, grad, master, rows_new, sums, colstat)

        spans = [
            (mid * at, width, rows_of)
            for at, width, rows_of in zip(
                norm_at, widths, ((0, 1),) * 2 + ((0, 1), (2, 1)) + ((0, 1),) * 3
            )
        ]
        sum_sets = [sums_one, sums_two, sums_pair, sums_pair, sums_four, sums_five, sums_six]
        flat_sets = [part for parts in sum_sets for part in parts]
        norm_rows = norm_params.size // c_out
        norm_sums = kernel_call(
            pack_kernel(count, spans, mid),
            "pack",
            (1,),
            [whole(part.shape) for part in flat_sets],
            whole((norm_rows, c_out)),
            shape_of((norm_rows, c_out), F32),
            1000000,
        )(*flat_sets)

        chain_one.step()
        chain_three.step()
        chain_four.step()
        chain_five.step()
        chain_side.step()
        chain_two.step()
        chain_one.step()
        chain_three.step()
        chain_side.step()
        chain_four.step()
        broad_six = chain_six.finish()
        chain_two.step()
        chain_one.step()
        chain_side.step()
        slim_five = chain_five.finish()
        chain_three.step()
        chain_two.step()
        chain_one.step()
        broad_side = chain_side.finish()
        broad_three = chain_three.finish()
        broad_grad = choose(top, choose(second, broad_six, broad_side), broad_three)
        broad_rows_new, broad_sums = tally(
            broad_grad, broad_master, broad_rowstat, bounds_broad, "broad_tally", [], norm_sums
        )
        slim_four = chain_four.finish()
        slim_two = chain_two.finish()
        slim_one = chain_one.finish()
        slim_high = choose(second, slim_five, slim_four)
        slim_low = choose(second, slim_two, slim_one)
        slim_grad = choose(top, slim_high, slim_low)

        slim_rows_new, slim_sums = tally(
            slim_grad, slim_master, slim_rowstat, bounds_slim, "slim_tally", []
        )
        broad_cols_new, broad_new, broad_copy = renew(
            broad_grad,
            broad_master,
            broad_rows_new,
            broad_sums[-1][:-norm_rows],
            broad_colstat,
            bounds_broad,
            "broad_renew",
        )
        slim_cols_new, slim_new, slim_copy = renew(
            slim_grad,
            slim_master,
            slim_rows_new,
            slim_sums[-1],
            slim_colstat,
            bounds_slim,
            "slim_renew",
        )
        norm_grad = broad_sums[-1][-norm_rows:].reshape(norm_params.shape) * (1.0 / n_narrow)
        norm_moments_new = DECAY * norm_moments + (1.0 - DECAY) * (
            norm_grad * norm_grad + EPS_ONE
        )
        norm_update = norm_grad * lax.rsqrt(norm_moments_new)
        update_rms = jnp.sqrt(jnp.mean(norm_update * norm_update, 1))
        weight_rms = jnp.sqrt(jnp.mean(norm_params * norm_params, 1))
        step = STEP_RATE * jnp.maximum(EPS_TWO, weight_rms) / jnp.maximum(1.0, update_rms)
        norm_new = norm_params - step[:, None] * norm_update
        return (
            *y_parts,
            *dx_parts,
            slim_grad,
            broad_grad,
            slim_rows_new.reshape(-1),
            broad_rows_new.reshape(-1),
            slim_cols_new,
            broad_cols_new,
            slim_new,
            broad_new,
            slim_copy,
            broad_copy,
            norm_grad,
            norm_moments_new,
            norm_new,
        )

    return body


def solution(mesh):
    split = P(AXES)
    return jax.shard_map(
        make_body(mesh),
        mesh=mesh,
        in_specs=(split,) * 11 + (P(),) * 4,
        out_specs=(split,) * 10 + (P(),) * 2 + (split,) * 4 + (P(),) * 3,
        check_vma=False,
    )
```

```python
import jax
import jax.numpy as jnp
import numpy as np
from jax import lax
from jax.experimental import pallas as pl
from jax.experimental.pallas import tpu as pltpu
from jax.sharding import PartitionSpec as P

STEP = 10
EPS_NORM = 1e-05
EPS_ONE = 1e-30
EPS_TWO = 0.001
STEP_RATE = 0.3
DECAY = 1.0 - STEP ** (-0.8)
AXES = ("wide", "narrow")
BF16 = jnp.bfloat16
F32 = jnp.float32
LATE_STEPS = 2
VMEM_LIMIT = 48 * 1024 * 1024


def shape_of(dims, dtype):
    return jax.ShapeDtypeStruct(dims, dtype)


def whole(dims):
    return pl.BlockSpec(dims, lambda *step: (0,) * len(dims))


def block(dims, place):
    return pl.BlockSpec(dims, place)


LENGTHS = dict(
    first=3.9,
    conv_two=10.8,
    side=7.2,
    widen_three=3.8,
    mix=5.3,
    conv_five=8.9,
    widen_six=3.9,
    output=6.8,
    back_six=5.1,
    grad_six=2.1,
    back_five=10,
    grad_five_high=5.5,
    grad_five_low=3.2,
    back_four=6.5,
    grad_four=1.5,
    back_three=6,
    grad_three=3,
    grad_side_low=2.1,
    grad_side_high=2.1,
    back_two=13.7,
    grad_two_high=4.8,
    grad_four_low=0.5,
    grad_two_low=4.8,
    back_one=6.3,
    input_grad=6.7,
    sum_six_0=1,
    sum_five_0=1.8,
    sum_four_0=2.1,
    sum_three_0=4.5,
    sum_side_0=1.5,
    sum_two_0=2.2,
    sum_one_0=2,
    sum_five_1=2.2,
    sum_four_1=2.7,
    sum_three_1=3.6,
    sum_side_1=2,
    sum_two_1=2.2,
)


def length(name):
    return LENGTHS.get(name, 1)


class Kernels:
    def __init__(self):
        self.last = None

    def __call__(
        self,
        body,
        name,
        grid,
        in_specs,
        out_specs,
        out_shape,
        flops,
        scratch=(),
        aliases=None,
        after=(),
        scalars=0,
    ):
        taken = scalars + len(in_specs)

        def run(*args):
            waits = [
                value
                for value in (*after, self.last)
                if value is not None and not any(value is arg for arg in args)
            ]

            def trimmed(*refs):
                body(*refs[:taken], *refs[taken + len(waits) :])

            out = pl.pallas_call(
                trimmed,
                grid_spec=pltpu.PrefetchScalarGridSpec(
                    num_scalar_prefetch=scalars,
                    grid=grid,
                    in_specs=list(in_specs) + [pl.BlockSpec(memory_space=pl.ANY)] * len(waits),
                    out_specs=out_specs,
                    scratch_shapes=list(scratch),
                ),
                out_shape=out_shape,
                input_output_aliases=aliases or {},
                cost_estimate=pl.CostEstimate(
                    flops=int(length(name) * 1.15e9),
                    bytes_accessed=int(length(name) * 3.6e6),
                    transcendentals=0,
                ),
                compiler_params=pltpu.CompilerParams(vmem_limit_bytes=VMEM_LIMIT),
                name=name,
            )(*args, *waits)
            self.last = out[0] if isinstance(out, (list, tuple)) else out
            return out

        return run


def dot_nn(first, second):
    return jnp.dot(first, second, preferred_element_type=F32)


def dot_nt(first, second):
    return lax.dot_general(first, second, (((1,), (1,)), ((), ())), preferred_element_type=F32)


def dot_tn(first, second):
    return lax.dot_general(first, second, (((0,), (0,)), ((), ())), preferred_element_type=F32)


def sigmoid(value):
    return 1.0 / (1.0 + jnp.exp(-value))


def slope(value):
    gate = sigmoid(value)
    return gate * (1.0 + value * (1.0 - gate))


def tree_sum(values):
    values = list(values)
    while len(values) > 1:
        values = [values[i] + values[i + 1] for i in range(0, len(values), 2)]
    return values[0]


def moments(parts, recip):
    total = tree_sum([part[...] for part in parts]) * recip
    mean = total[0:1]
    return mean, lax.rsqrt(total[1:2] - mean * mean + EPS_NORM)


def column_sum(value):
    return jnp.sum(value, axis=0, keepdims=True)


def stat_rows(value, mask):
    kept = value * mask
    return jnp.concatenate([column_sum(kept), column_sum(kept * value)], 0)


def grid_rows(images, sides):
    return sum(images * side * side for side in sides)


def class_table(images, sides_out, padded):
    table = -np.ones((4, padded), np.int32)
    base_in, base_out = 0, 0
    for side in sides_out:
        extent = 2 * side
        for row in range(side):
            for col in range(side):
                for image in range(images):
                    for kind in range(4):
                        cell = (2 * row + kind // 2) * extent + 2 * col + kind % 2
                        table[kind, base_out + (row * side + col) * images + image] = (
                            base_in + cell * images + image
                        )
        base_in += images * extent * extent
        base_out += images * side * side
    return table


def shift_table(images, sides_out, padded):
    table = -np.ones((9, padded), np.int32)
    base = 0
    for side in sides_out:
        for row in range(side):
            for col in range(side):
                for which in range(9):
                    row_to, col_to = row + which // 3 - 1, col + which % 3 - 1
                    if 0 <= row_to < side and 0 <= col_to < side:
                        for image in range(images):
                            table[which, base + (row * side + col) * images + image] = (
                                base + (row_to * side + col_to) * images + image
                            )
        base += images * side * side
    return table


def one_hot(table, width):
    return (jnp.asarray(table)[..., None] == jnp.arange(width, dtype=jnp.int32)).astype(BF16)


def first_kernel(x_ref, w_ref, mask_ref, z_ref, stat_ref):
    z = dot_nn(x_ref[0], w_ref[...])
    z_ref[0] = z
    rows = stat_rows(z, mask_ref[...])

    @pl.when(pl.program_id(0) == 0)
    def _():
        stat_ref[...] = rows

    @pl.when(pl.program_id(0) > 0)
    def _():
        stat_ref[...] += rows


def side_kernel(x_ref, w_ref, mask_ref, z_ref, stat_ref):
    term = dot_nn(x_ref[0], w_ref[...])

    @pl.when(pl.program_id(1) == 0)
    def _():
        z_ref[...] = term

    @pl.when(pl.program_id(1) > 0)
    def _():
        z_ref[...] += term

    @pl.when(pl.program_id(1) == pl.num_programs(1) - 1)
    def _():
        stat_ref[...] = stat_rows(z_ref[...], mask_ref[...])


def tap_forward(tap, stride):
    if stride == 1:
        return 0, tap
    row_tap, col_tap = tap // 3, tap % 3
    kind = jnp.where(row_tap == 1, 0, 2) + jnp.where(col_tap == 1, 0, 1)
    shift = jnp.where(row_tap == 0, 0, 3) + jnp.where(col_tap == 0, 0, 1)
    return kind, shift


def tap_backward(tap, stride):
    if stride == 1:
        return 0, 8 - tap
    row_tap, col_tap = tap // 3, tap % 3
    kind = jnp.where(row_tap == 1, 0, 2) + jnp.where(col_tap == 1, 0, 1)
    shift = jnp.where(row_tap == 0, 6, 3) + jnp.where(col_tap == 0, 2, 1)
    return kind, shift


def conv_kernel(count, kinds, stride):
    def body(*refs):
        z_ref = refs[0]
        parts = refs[1 : 1 + count]
        affine_ref, recip_ref, mask_ref, shift_ref, w_ref, act_ref, out_ref, stat_ref = refs[
            1 + count :
        ]
        tap = pl.program_id(0)

        @pl.when(tap == 0)
        def _():
            mean, inv = moments(parts, recip_ref[...])
            for kind in range(kinds):
                pre = affine_ref[0:1] * ((z_ref[kind] - mean) * inv) + affine_ref[1:2]
                act_ref[kind] = (pre * sigmoid(pre)).astype(BF16)

        kind, shift = tap_forward(tap, stride)
        patch = dot_nn(shift_ref[shift], act_ref[kind]).astype(BF16)
        term = dot_nn(patch, w_ref[...])

        @pl.when(tap == 0)
        def _():
            out_ref[...] = term

        @pl.when(tap > 0)
        def _():
            out_ref[...] += term

        @pl.when(tap == 8)
        def _():
            stat_ref[...] = stat_rows(out_ref[...], mask_ref[...])

    return body


def widen_kernel(count, carry):
    def body(*refs):
        z_ref = refs[0]
        parts = refs[1 : 1 + count]
        rest = refs[1 + count :]
        if carry:
            affine_ref, recip_ref, mask_ref, w_ref, side_ref, act_ref, out_ref, stat_ref = rest
        else:
            affine_ref, recip_ref, mask_ref, w_ref, act_ref, out_ref, stat_ref = rest

        @pl.when(pl.program_id(0) == 0)
        def _():
            mean, inv = moments(parts, recip_ref[...])
            pre = affine_ref[0:1] * ((z_ref[...] - mean) * inv) + affine_ref[1:2]
            act_ref[...] = (pre * sigmoid(pre)).astype(BF16)

        z = dot_nn(act_ref[...], w_ref[...])
        out_ref[...] = z
        if carry:
            stat_ref[...] = jnp.concatenate([stat_rows(z, mask_ref[...]), side_ref[...]], 0)
        else:
            stat_ref[...] = stat_rows(z, mask_ref[...])

    return body


def pair_moments(parts, recip):
    total = tree_sum([part[...] for part in parts]) * recip
    mean, mean_side = total[0:1], total[2:3]
    inv = lax.rsqrt(total[1:2] - mean * mean + EPS_NORM)
    inv_side = lax.rsqrt(total[3:4] - mean_side * mean_side + EPS_NORM)
    return mean, inv, mean_side, inv_side


def mix_kernel(count):
    def body(*refs):
        z_ref, side_ref = refs[:2]
        parts = refs[2 : 2 + count]
        (affine_ref, affine_side_ref, recip_ref, mask_ref, w_ref) = refs[2 + count : 7 + count]
        hidden_ref, low_ref, out_ref, stat_ref = refs[7 + count :]
        mean, inv, mean_side, inv_side = pair_moments(parts, recip_ref[...])
        pre = (
            affine_ref[0:1] * ((z_ref[...] - mean) * inv)
            + affine_ref[1:2]
            + affine_side_ref[0:1] * ((side_ref[...] - mean_side) * inv_side)
            + affine_side_ref[1:2]
        )
        hidden = pre * sigmoid(pre)
        hidden_ref[...] = hidden
        low = hidden.astype(BF16)
        low_ref[...] = low
        term = dot_nn(low, w_ref[...])

        @pl.when(pl.program_id(0) == 0)
        def _():
            out_ref[...] = term

        @pl.when(pl.program_id(0) > 0)
        def _():
            out_ref[...] += term

        @pl.when(pl.program_id(0) == pl.num_programs(0) - 1)
        def _():
            stat_ref[...] = stat_rows(out_ref[...], mask_ref[...])

    return body


def cell_rows(images, sides):
    base = 0
    for level, side in enumerate(sides):
        for row in range(side):
            for col in range(side):
                yield level, row, col, base + (row * side + col) * images
        base += images * side * side


def output_kernel(count, images, sides):
    def body(*refs):
        z_ref = refs[0]
        parts = refs[1 : 1 + count]
        affine_ref, recip_ref, mask_ref, hidden_ref = refs[1 + count : 5 + count]
        cot_refs = refs[5 + count : 8 + count]
        y_refs = refs[8 + count : 11 + count]
        grad_ref, stat_ref, flat_ref = refs[11 + count :]
        used = grid_rows(images, sides)
        if flat_ref.shape[0] > used:
            flat_ref[used:] = jnp.zeros((flat_ref.shape[0] - used, flat_ref.shape[1]), F32)
        for level, row, col, at in cell_rows(images, sides):
            flat_ref[at : at + images] = cot_refs[level][row, col].astype(F32)
        mean, inv = moments(parts, recip_ref[...])
        normed = (z_ref[...] - mean) * inv
        pre = affine_ref[0:1] * normed + affine_ref[1:2] + hidden_ref[...]
        gate = sigmoid(pre)
        grad = flat_ref[...] * mask_ref[...] * (gate * (1.0 + pre * (1.0 - gate)))
        grad_ref[...] = grad
        stat_ref[...] = jnp.concatenate([column_sum(grad * normed), column_sum(grad)], 0)
        flat_ref[...] = pre * gate
        for level, row, col, at in cell_rows(images, sides):
            y_refs[level][row, col] = flat_ref[at : at + images].astype(BF16)

    return body


def input_grad_kernel(images, sides):
    def body(dz_ref, w_ref, side_ref, w_side_ref, *rest):
        out_refs, flat_ref = rest[:3], rest[3]
        for kind in range(4):
            value = dot_nt(dz_ref[kind], w_ref[...])
            if kind == 0:
                value += dot_nt(side_ref[...], w_side_ref[...])
            flat_ref[...] = value
            for level, row, col, at in cell_rows(images, sides):
                out_refs[level][2 * row + kind // 2, 2 * col + kind % 2] = flat_ref[
                    at : at + images
                ]

    return body


def norm_back(grad, normed, sums, recip, mask, scale):
    return scale * (grad - mask * (sums[1:2] * recip + normed * (sums[0:1] * recip)))


def back_linear_kernel(count):
    def body(*refs):
        grad_ref, z_ref = refs[:2]
        parts = refs[2 : 2 + count]
        sums = refs[2 + count : 2 + 2 * count]
        affine_ref, recip_ref, mask_ref, w_ref, below_ref = refs[2 + 2 * count : 7 + 2 * count]
        below_parts = refs[7 + 2 * count : 7 + 3 * count]
        below_affine_ref, dz_ref, out_ref, stat_ref = refs[7 + 3 * count :]
        recip = recip_ref[...]
        mean, inv = moments(parts, recip)
        total = tree_sum([part[...] for part in sums])
        normed = (z_ref[...] - mean) * inv
        dz = norm_back(grad_ref[...], normed, total, recip, mask_ref[...], affine_ref[0:1] * inv)
        dz = dz.astype(BF16)
        dz_ref[...] = dz
        term = dot_nt(dz, w_ref[...])

        @pl.when(pl.program_id(0) == 0)
        def _():
            out_ref[...] = term

        @pl.when(pl.program_id(0) > 0)
        def _():
            out_ref[...] += term

        @pl.when(pl.program_id(0) == pl.num_programs(0) - 1)
        def _():
            finish_below(out_ref, below_ref, below_parts, below_affine_ref, recip, stat_ref)

    return body


def finish_below(out_ref, below_ref, below_parts, below_affine_ref, recip, stat_ref):
    mean, inv = moments(below_parts, recip)
    normed = (below_ref[...] - mean) * inv
    pre = below_affine_ref[0:1] * normed + below_affine_ref[1:2]
    grad = out_ref[...] * slope(pre)
    out_ref[...] = grad
    stat_ref[...] = jnp.concatenate([column_sum(grad * normed), column_sum(grad)], 0)


def back_conv_kernel(count, kinds, stride):
    def body(*refs):
        grad_ref, z_ref = refs[:2]
        parts = refs[2 : 2 + count]
        sums = refs[2 + count : 2 + 2 * count]
        affine_ref, recip_ref, mask_ref, shift_ref, w_ref, below_ref = refs[
            2 + 2 * count : 8 + 2 * count
        ]
        below_parts = refs[8 + 2 * count : 8 + 3 * count]
        below_affine_ref, below_recip_ref, dz_ref, out_ref, stat_ref = refs[8 + 3 * count :]
        tap = pl.program_id(0)

        @pl.when(tap == 0)
        def _():
            recip = recip_ref[...]
            mean, inv = moments(parts, recip)
            total = tree_sum([part[...] for part in sums])
            normed = (z_ref[...] - mean) * inv
            dz = norm_back(
                grad_ref[...], normed, total, recip, mask_ref[...], affine_ref[0:1] * inv
            )
            dz_ref[...] = dz.astype(BF16)
            out_ref[...] = jnp.zeros_like(out_ref)

        kind, shift = tap_backward(tap, stride)
        patch = dot_nn(shift_ref[shift], dz_ref[...]).astype(BF16)
        out_ref[kind] += dot_nt(patch, w_ref[...])

        @pl.when(tap == 8)
        def _():
            mean, inv = moments(below_parts, below_recip_ref[...])
            rows = None
            for which in range(kinds):
                normed = (below_ref[which] - mean) * inv
                pre = below_affine_ref[0:1] * normed + below_affine_ref[1:2]
                grad = out_ref[which] * slope(pre)
                out_ref[which] = grad
                part = jnp.concatenate([column_sum(grad * normed), column_sum(grad)], 0)
                rows = part if rows is None else rows + part
            stat_ref[...] = rows

    return body


def back_mix_kernel(count):
    def body(*refs):
        grad_ref, z_ref = refs[:2]
        parts = refs[2 : 2 + count]
        sums = refs[2 + count : 2 + 2 * count]
        affine_ref, recip_ref, mask_ref, w_ref, above_ref, mid_ref, side_ref = refs[
            2 + 2 * count : 9 + 2 * count
        ]
        pair_parts = refs[9 + 2 * count : 9 + 3 * count]
        affine_mid_ref, affine_side_ref, dz_ref, out_ref, stat_ref = refs[9 + 3 * count :]
        recip = recip_ref[...]

        @pl.when(pl.program_id(0) == 0)
        def _():
            mean, inv = moments(parts, recip)
            total = tree_sum([part[...] for part in sums])
            normed = (z_ref[...] - mean) * inv
            dz = norm_back(
                grad_ref[...], normed, total, recip, mask_ref[...], affine_ref[0:1] * inv
            )
            dz_ref[...] = dz.astype(BF16)

        mean, inv, mean_side, inv_side = pair_moments(pair_parts, recip)
        normed = (mid_ref[...] - mean) * inv
        normed_side = (side_ref[...] - mean_side) * inv_side
        pre = (
            affine_mid_ref[0:1] * normed
            + affine_mid_ref[1:2]
            + affine_side_ref[0:1] * normed_side
            + affine_side_ref[1:2]
        )
        grad = (above_ref[...] + dot_nt(dz_ref[...], w_ref[...])) * slope(pre)
        out_ref[...] = grad
        stat_ref[...] = jnp.concatenate(
            [column_sum(grad * normed), column_sum(grad), column_sum(grad * normed_side)], 0
        )

    return body


def back_pair_kernel(count):
    def body(*refs):
        grad_ref, mid_ref, side_ref = refs[:3]
        pair_parts = refs[3 : 3 + count]
        sums = refs[3 + count : 3 + 2 * count]
        affine_mid_ref, affine_side_ref, recip_ref, mask_ref, w_ref, below_ref = refs[
            3 + 2 * count : 9 + 2 * count
        ]
        below_parts = refs[9 + 2 * count : 9 + 3 * count]
        below_affine_ref, dz_ref, dz_side_ref, out_ref, stat_ref = refs[9 + 3 * count :]
        recip = recip_ref[...]
        mean, inv, mean_side, inv_side = pair_moments(pair_parts, recip)
        total = tree_sum([part[...] for part in sums])
        normed = (mid_ref[...] - mean) * inv
        normed_side = (side_ref[...] - mean_side) * inv_side
        grad = grad_ref[...]
        mask = mask_ref[...]
        dz = norm_back(grad, normed, total[0:2], recip, mask, affine_mid_ref[0:1] * inv)
        dz = dz.astype(BF16)
        dz_ref[...] = dz
        total_side = jnp.concatenate([total[2:3], total[1:2]], 0)
        dz_side_ref[...] = norm_back(
            grad, normed_side, total_side, recip, mask, affine_side_ref[0:1] * inv_side
        ).astype(BF16)
        term = dot_nt(dz, w_ref[...])

        @pl.when(pl.program_id(0) == 0)
        def _():
            out_ref[...] = term

        @pl.when(pl.program_id(0) > 0)
        def _():
            out_ref[...] += term

        @pl.when(pl.program_id(0) == pl.num_programs(0) - 1)
        def _():
            finish_below(out_ref, below_ref, below_parts, below_affine_ref, recip, stat_ref)

    return body


def back_first_kernel(count):
    def body(*refs):
        grad_ref, z_ref = refs[:2]
        parts = refs[2 : 2 + count]
        sums = refs[2 + count : 2 + 2 * count]
        affine_ref, recip_ref, mask_ref, x_ref, _, dz_ref, grad_w_ref, total_ref = refs[
            2 + 2 * count :
        ]
        recip = recip_ref[...]
        mean, inv = moments(parts, recip)
        total = tree_sum([part[...] for part in sums])
        normed = (z_ref[0] - mean) * inv
        dz = norm_back(grad_ref[0], normed, total, recip, mask_ref[...], affine_ref[0:1] * inv)
        dz = dz.astype(BF16)
        dz_ref[0] = dz
        term = dot_tn(x_ref[0], dz)

        @pl.when(pl.program_id(0) == 0)
        def _():
            total_ref[...] = term

        @pl.when(pl.program_id(0) > 0)
        def _():
            total_ref[...] += term

        @pl.when(pl.program_id(0) == pl.num_programs(0) - 1)
        def _():
            grad_w_ref[...] = total_ref[...].astype(BF16)

    return body


def weight_grad_kernel(act_ref, dz_ref, *rest):
    rest[-1][...] = dot_tn(act_ref[...], dz_ref[...]).astype(BF16)


def conv_grad_kernel(stride, first):
    def body(act_ref, shift_ref, dz_ref, *rest):
        kind, shift = tap_forward(pl.program_id(0) + first, stride)
        patch = dot_nn(shift_ref[shift], act_ref[kind]).astype(BF16)
        rest[-1][...] = dot_tn(patch, dz_ref[...]).astype(BF16)

    return body


def pack_kernel(count, spans, piece):
    def body(*refs):
        out_ref = refs[-1]
        columns = out_ref.shape[1]
        high = out_ref.shape[0] // 2
        for which, (start, width, rows) in enumerate(spans):
            parts = refs[which * count : (which + 1) * count]
            total = tree_sum([part[...] for part in parts])
            for offset in range(0, width, piece):
                line, at = (start + offset) // columns, (start + offset) % columns
                for slot, row in enumerate(rows):
                    here = slot * high + line
                    out_ref[here : here + 1, at : at + piece] = total[
                        row : row + 1, offset : offset + piece
                    ]

    return body


def merge_kernel(split, has_kept, last):
    def add(kept_ref, came_ref):
        total = kept_ref[...].astype(F32) + came_ref[...].astype(F32)
        return total if last else total.astype(BF16)

    def body(index_ref, *refs):
        if not has_kept:
            refs[1][...] = refs[0][...]
        elif split:
            refs[4][...] = add(refs[0], refs[1])
            refs[5][...] = add(refs[2], refs[3])
        else:
            refs[2][...] = add(refs[0], refs[1])

    return body


def level_masks(first_row, rows, bounds):
    index = first_row + lax.broadcasted_iota(jnp.int32, (rows, 1), 0)
    return [
        ((index >= bounds[level]) & (index < bounds[level + 1])).astype(F32)
        for level in range(len(bounds) - 1)
    ]


def tally_kernel(bounds, extra):
    levels = len(bounds) - 1

    def body(first_ref, grad_ref, master_ref, old_ref, *rest):
        rows_ref, sums_ref = rest[-2:]
        if extra:
            sums_ref[4 * levels :] = rest[0][...]
        grad = grad_ref[...]
        master = master_ref[...]
        square = grad * grad
        raised = square + EPS_ONE
        rows_new = DECAY * old_ref[...] + (1.0 - DECAY) * jnp.mean(raised, 1, keepdims=True)
        rows_ref[...] = rows_new
        ratio = square / rows_new
        weight = jnp.sum(master * master, 1, keepdims=True)
        masks = level_masks(first_ref[0], grad.shape[0], bounds)
        spread = jnp.zeros((1, grad.shape[1]), F32)
        for level in range(levels):
            mask = masks[level]
            sums_ref[level : level + 1] = column_sum(raised * mask)
            sums_ref[levels + level : levels + level + 1] = column_sum(ratio * mask)
            low = 2 * levels + level
            sums_ref[low : low + 1] = spread + column_sum(rows_new * mask)
            low = 3 * levels + level
            sums_ref[low : low + 1] = spread + column_sum(weight * mask)

    return body


def renew_kernel(bounds):
    levels = len(bounds) - 1

    def body(first_ref, grad_ref, master_ref, rows_ref, sums_ref, old_ref, cols_ref, new_ref, low_ref):
        grad = grad_ref[...]
        columns = grad.shape[1]
        masks = level_masks(first_ref[0], grad.shape[0], bounds)
        factor = None
        for level in range(levels):
            height = float(bounds[level + 1] - bounds[level])
            cells = height * columns
            col_sum = sums_ref[level : level + 1]
            ratio_sum = sums_ref[levels + level : levels + level + 1]
            row_mean = sums_ref[2 * levels + level : 2 * levels + level + 1] / height
            weight_sum = sums_ref[3 * levels + level : 3 * levels + level + 1]
            cols_new = DECAY * old_ref[level : level + 1] + (1.0 - DECAY) * (col_sum / height)
            cols_ref[level : level + 1] = cols_new
            relative = cols_new / row_mean
            update_sq = jnp.sum(ratio_sum / relative, axis=1, keepdims=True)
            update_rms = jnp.sqrt(update_sq / cells)
            weight_rms = jnp.sqrt(weight_sum / cells)
            step = STEP_RATE * jnp.maximum(EPS_TWO, weight_rms) / jnp.maximum(1.0, update_rms)
            part = masks[level] * (step * lax.rsqrt(relative))
            factor = part if factor is None else factor + part
        new = master_ref[...] - grad * lax.rsqrt(rows_ref[...]) * factor
        new_ref[...] = new
        low_ref[...] = new.astype(BF16)

    return body


class Exchange:
    def __init__(self, n_wide, n_narrow):
        self.n_narrow = n_narrow
        self.total = n_wide * n_narrow
        self.bits = self.total.bit_length() - 1
        self.narrow_bits = n_narrow.bit_length() - 1
        self.index = lax.axis_index(AXES)

    def bit(self, level):
        return (self.index >> level) & 1

    def swap(self, value, level):
        pairs = [(device, device ^ (1 << level)) for device in range(self.total)]
        return lax.ppermute(value, AXES, pairs)

    def group_parts(self, value):
        return [value] + [
            lax.ppermute(value, "narrow", [(i, i ^ k) for i in range(self.n_narrow)])
            for k in range(1, self.n_narrow)
        ]

    def total_sums(self, value, first=0):
        sums = []
        for level in range(first, self.bits):
            value = value + self.swap(value, level)
            sums.append(value)
        return sums


def move_kernel(moves, outs, bases):
    def body(index_ref, *refs):
        out_refs, sems = refs[-1 - outs : -1], refs[-1]
        copies = []
        for which, (operand, unit, out, rows, to, apart) in enumerate(moves):
            start = pl.multiple_of((index_ref[0] ^ to) * rows, rows) if apart else to * rows
            copies.append(
                pltpu.make_async_copy(
                    refs[operand].at[unit], out_refs[out].at[pl.ds(start, rows)], sems.at[which]
                )
            )
        for copy in copies:
            copy.start()
        for copy in copies:
            copy.wait()

    return body


class Gather:
    def __init__(self, link, kernels, shards, names, narrow_first):
        self.link = link
        self.kernels = kernels
        self.names = names
        self.rows = [shard.shape[0] for shard in shards]
        self.columns = [shard.shape[1] for shard in shards]
        inner = list(range(1, link.narrow_bits))
        outer = list(range(link.narrow_bits, link.bits - 2))
        self.levels = [
            (inner + outer if narrow else outer + inner) + [0] for narrow in narrow_first
        ]
        self.stages = len(self.levels[0])
        low, high = link.bits - 2, link.bits - 1
        self.slots = [[] for _ in range(4)]
        for shard, name in zip(shards, names):
            own = shard
            with jax.named_scope(name + "_down"):
                beside = link.swap(own, low)
                across = link.swap(own, high)
                both = link.swap(across, low)
            for slot, (units, apart) in enumerate(
                [
                    (own, 0),
                    (beside, 1 << low),
                    (across, 1 << high),
                    (both, (1 << low) | (1 << high)),
                ]
            ):
                self.slots[slot].append(
                    dict(units=units, pieces=[units], apart=[apart], came=None)
                )
        self.full = None

    def send(self, slot, stage):
        for which, state in enumerate(self.slots[slot]):
            level = self.levels[which][stage]
            with jax.named_scope(f"{self.names[which]}_{slot}_bit{level}"):
                state["came"] = self.link.swap(state["units"], level)

    def move(self, name, moves, args, shapes, aliases, after):
        any_spec = pl.BlockSpec(memory_space=pl.ANY)
        bases = len(aliases)
        return self.kernels(
            move_kernel(moves, len(shapes), bases),
            name,
            (1,),
            [whole(arg.shape) for arg in args[: len(args) - bases]] + [any_spec] * bases,
            [any_spec] * len(shapes),
            [shape_of(dims, BF16) for dims in shapes],
            1,
            scratch=[pltpu.SemaphoreType.DMA((len(moves),))],
            aliases=aliases,
            scalars=1,
            after=after,
        )(self.link.index.astype(jnp.int32).reshape(1), *args)

    def join(self, slot, stage):
        args, moves, shapes = [], [], []
        for which, state in enumerate(self.slots[slot]):
            rows, bit = self.rows[which], 1 << self.levels[which][stage]
            have = len(state["apart"])
            for place, value in enumerate((state["units"], state["came"])):
                moves.append((len(args), slice(None), which, have * rows, place, False))
                args.append(value)
            shapes.append((2 * have * rows, self.columns[which]))
            state["pieces"].append(state["came"])
            state["apart"] += [apart ^ bit for apart in state["apart"]]
        later = {(0, 0): (1, 2), (1, 0): (3,)}.get((slot, stage), ())
        waits = [state["pieces"][0] for ahead in later for state in self.slots[ahead]]
        joined = self.move(f"join_{slot}_{stage}", moves, args, shapes, {}, waits)
        for state, units in zip(self.slots[slot], joined):
            state["units"] = units
        self.send(slot, stage + 1)

    def place(self, slot, after):
        args, moves, shapes = [], [], []
        for which, state in enumerate(self.slots[slot]):
            rows, bit = self.rows[which], 1 << self.levels[which][-1]
            apart = state["apart"]
            for value, extra in ((state["units"], 0), (state["came"], bit)):
                for unit, bits in enumerate(apart):
                    part = slice(unit * rows, (unit + 1) * rows)
                    moves.append((len(args), part, which, rows, bits ^ extra, True))
                args.append(value)
            shapes.append((rows * self.link.total, self.columns[which]))
        aliases = {}
        if self.full is not None:
            aliases = {1 + len(args) + which: which for which in range(len(shapes))}
            args = args + list(self.full)
        self.full = self.move(f"place_{slot}", moves, args, shapes, aliases, after)
        return self.full

    def start(self):
        for slot in range(4):
            self.send(slot, 0)

    @property
    def length(self):
        return self.stages + 3

    def run(self, times, after):
        for time in times:
            for slot in reversed(range(4)):
                stage = time - slot
                if 0 <= stage < self.stages - 1:
                    self.join(slot, stage)
                elif stage == self.stages - 1:
                    self.place(slot, after if slot == 0 else [])


def insert_bit(unit, place, bit):
    return ((unit >> place) << (place + 1)) | (bit << place) | (unit & ((1 << place) - 1))


class Scatter:
    def __init__(self, link, kernels, part, name, prefix=(), first="narrow"):
        self.link = link
        self.kernels = kernels
        self.name = name
        self.prefix = prefix
        self.open_bits = link.bits - len(prefix)
        units = 1 << self.open_bits
        self.kept = part.reshape(units, part.shape[0] // units, part.shape[1])
        self.left = list(range(self.open_bits))
        inner = list(range(1, link.narrow_bits))
        outer = list(range(link.narrow_bits, link.bits))
        orders = {
            "narrow": inner + outer,
            "wide": outer[:1] + inner + outer[1:],
            "all_wide": outer + inner,
        }
        self.levels = [0] + orders[first]
        self.at = 0
        self.came = None
        self.chosen = None
        self.after = []
        self.send_half(None)

    def place(self, level):
        return self.left.index(level)

    def unit_spec(self, source):
        dims = (1,) + self.kept.shape[1:]
        return block(dims, lambda unit, index: (source(unit, index[0]), 0, 0))

    def kept_source(self, source):
        if self.chosen is None:
            return source
        place, level = self.chosen
        return lambda unit, index: insert_bit(
            source(unit, index), place, (index >> level) & 1
        )

    def run(self, body, specs, outs, number, args, dtype):
        spec = self.unit_spec(lambda unit, index: unit)
        shape = shape_of((number,) + self.kept.shape[1:], dtype)
        out = self.kernels(
            body,
            self.name + "_" + str(self.at),
            (number,),
            specs,
            [spec] * outs,
            [shape] * outs,
            4 * number * self.kept.shape[1] * self.kept.shape[2] * 200,
            scalars=1,
            after=self.after,
        )(self.link.index.astype(jnp.int32).reshape(1), *args)
        return out

    def send_half(self, came):
        level = self.levels[self.at] if self.at < len(self.levels) else None
        total_units = 1 << len(self.left)
        if level is not None and level < self.open_bits:
            place = self.place(level)

            def keep(unit, index):
                return insert_bit(unit, place, (index >> level) & 1)

            def send(unit, index):
                return insert_bit(unit, place, 1 - ((index >> level) & 1))

            half = total_units // 2
            if came is None:
                (sent,) = self.run(
                    merge_kernel(True, False, False),
                    [self.unit_spec(send)],
                    1,
                    half,
                    [self.kept],
                    BF16,
                )
                self.chosen = (place, level)
            else:
                kept_keep = self.unit_spec(self.kept_source(keep))
                kept_send = self.unit_spec(self.kept_source(send))
                kept, sent = self.run(
                    merge_kernel(True, True, False),
                    [kept_keep, self.unit_spec(keep), kept_send, self.unit_spec(send)],
                    2,
                    half,
                    [self.kept, came, self.kept, came],
                    BF16,
                )
                self.kept, self.chosen = kept, None
            self.left.remove(level)
            with jax.named_scope(self.name + "_bit" + str(level)):
                self.came = self.link.swap(sent, level)
        else:
            same = lambda unit, index: unit
            (self.kept,) = self.run(
                merge_kernel(False, True, level is None),
                [self.unit_spec(self.kept_source(same)), self.unit_spec(same)],
                1,
                total_units,
                [self.kept, came],
                F32 if level is None else BF16,
            )
            self.chosen = None
            if level is None:
                return
            pairs = []
            for device in range(self.link.total):
                settled = all(
                    (device >> other) & 1 == self.prefix[other - self.open_bits]
                    for other in range(self.open_bits, level)
                )
                if settled and (device >> level) & 1 != self.prefix[level - self.open_bits]:
                    pairs.append((device, device ^ (1 << level)))
            with jax.named_scope(self.name + "_bit" + str(level)):
                self.came = lax.ppermute(self.kept, AXES, pairs)

    def step(self, after=()):
        if self.at < len(self.levels):
            self.at += 1
            self.after = list(after)
            self.send_half(self.came)

    def finish(self):
        while self.at < len(self.levels):
            self.step()
        return self.kept.reshape(self.kept.shape[1:])


def make_body(mesh):
    n_wide, n_narrow = mesh.shape["wide"], mesh.shape["narrow"]

    def body(
        x_lo,
        x_mid,
        x_hi,
        cot_lo,
        cot_mid,
        cot_hi,
        live_counts,
        slim_master,
        broad_master,
        slim_rowstat,
        broad_rowstat,
        slim_colstat,
        broad_colstat,
        norm_params,
        norm_moments,
    ):
        link = Exchange(n_wide, n_narrow)
        kernel_call = Kernels()
        count = n_narrow
        images = x_lo.shape[0]
        sides = tuple(value.shape[1] // 2 for value in (x_lo, x_mid, x_hi))
        c_in, mid, c_out = x_lo.shape[3], slim_master.shape[1], broad_master.shape[1]
        cells = grid_rows(images, sides)
        cells_in = 4 * cells
        rows = -(-cells // 16) * 16
        chunks = c_out // mid
        bounds_slim = (0, c_in, c_in + 9 * mid, c_in + 9 * mid + c_out, c_in + 18 * mid + c_out)
        bounds_broad = (0, mid, mid + c_in, 2 * mid + c_in)
        at_two, at_four, at_five = (bounds_slim[level] // mid for level in (1, 2, 3))
        at_six = bounds_broad[2] // mid
        widths = (mid, mid, c_out, c_out, mid, mid, c_out)
        norm_at = [sum(widths[:level]) // mid for level in range(7)]

        kinds = class_table(images, sides, rows)
        shifts = one_hot(shift_table(images, sides, rows), rows)

        def by_cell(value):
            return jnp.transpose(value, (1, 2, 0, 3))

        x_flat = jnp.concatenate(
            [by_cell(value).reshape(-1, c_in) for value in (x_lo, x_mid, x_hi)], 0
        )
        x_kinds = jnp.dot(one_hot(kinds.reshape(-1), cells_in), x_flat, preferred_element_type=F32)
        x_kinds = x_kinds.astype(BF16).reshape(4, rows, c_in)
        alive = (
            jnp.arange(images, dtype=jnp.int32)[None] < live_counts[0][:, None]
        ).astype(F32)
        slots = np.zeros((rows, len(sides) * images), np.float32)
        base = 0
        for level, side in enumerate(sides):
            for at in range(images * side * side):
                slots[base + at, level * images + at % images] = 1.0
            base += images * side * side
        mask = jnp.sum(jnp.asarray(slots) * alive.reshape(1, -1), 1)
        cell_count = tree_sum(link.group_parts(jnp.sum(mask).reshape(1, 1)))
        mask = mask[:, None]
        recip = 1.0 / cell_count
        recip_in = 0.25 / cell_count

        slim = lax.all_gather(slim_master.astype(BF16), AXES, axis=0, tiled=True)
        gather = Gather(link, kernel_call, [broad_master.astype(BF16)], ["broad"], [False])
        gather.start()
        gather.run(range(gather.length - LATE_STEPS), [x_kinds, mask, shifts, recip])

        narrow_all = whole((rows, mid))
        kinds_all = whole((4, rows, mid))
        stat_all = whole((2, mid))
        mask_all = whole((rows, 1))
        one_all = whole((1, 1))
        shifts_all = whole((9, rows, rows))
        chunk = block((rows, mid), lambda j: (0, j))

        def stat_chunk(height):
            return block((height, mid), lambda j: (0, j))

        def affine(level):
            return block((2, mid), lambda j: (0, norm_at[level]))

        def affine_chunk(level):
            return block((2, mid), lambda j: (0, norm_at[level] + j))

        def slim_block(at):
            return block((mid, mid), lambda j: (at + j, 0))

        def broad_block(at):
            return block((mid, mid), lambda j: (at, j))

        narrow_f32 = shape_of((rows, mid), F32)
        wide_f32 = shape_of((rows, c_out), F32)
        narrow_low = shape_of((rows, mid), BF16)
        wide_low = shape_of((rows, c_out), BF16)
        stat_narrow = shape_of((2, mid), F32)
        stat_wide = shape_of((2, c_out), F32)
        flops_conv = 2 * rows * 9 * mid * (mid + rows)
        flops_wide = 2 * rows * mid * c_out

        z_one, stat = kernel_call(
            first_kernel,
            "first",
            (4,),
            [
                block((1, rows, c_in), lambda j: (j, 0, 0)),
                whole((c_in, mid)),
                mask_all,
            ],
            [block((1, rows, mid), lambda j: (j, 0, 0)), stat_all],
            [shape_of((4, rows, mid), F32), stat_narrow],
            2 * 4 * rows * c_in * mid,
            after=[recip],
        )(x_kinds, slim, mask)
        parts_one = link.group_parts(stat)
        act_one, z_two, stat = kernel_call(
            conv_kernel(count, 4, 2),
            "conv_two",
            (9,),
            [kinds_all]
            + [stat_all] * count
            + [affine(0), one_all, mask_all, shifts_all, slim_block(at_two)],
            [kinds_all, narrow_all, stat_all],
            [shape_of((4, rows, mid), BF16), narrow_f32, stat_narrow],
            flops_conv,
        )(z_one, *parts_one, norm_params, recip_in, mask, shifts, slim)
        parts_two = link.group_parts(stat)
        gather.run(range(gather.length - LATE_STEPS, gather.length), [])
        (broad,) = gather.full
        z_side, stat_side = kernel_call(
            side_kernel,
            "side",
            (chunks, c_in // mid),
            [
                block((1, rows, mid), lambda j, k: (0, 0, k)),
                block((mid, mid), lambda j, k: (1 + k, j)),
                whole((rows, 1)),
            ],
            [
                block((rows, mid), lambda j, k: (0, j)),
                block((2, mid), lambda j, k: (0, j)),
            ],
            [wide_f32, stat_wide],
            2 * rows * c_in * c_out,
        )(x_kinds, broad, mask)
        act_two, z_three, stat = kernel_call(
            widen_kernel(count, True),
            "widen_three",
            (chunks,),
            [narrow_all]
            + [stat_all] * count
            + [affine(1), one_all, mask_all, broad_block(0), stat_chunk(2)],
            [narrow_all, chunk, stat_chunk(4)],
            [narrow_low, wide_f32, shape_of((4, c_out), F32)],
            flops_wide,
        )(z_two, *parts_two, norm_params, recip, mask, broad, stat_side)
        parts_pair = link.group_parts(stat)
        hidden, hidden_low, z_four, stat = kernel_call(
            mix_kernel(count),
            "mix",
            (chunks,),
            [chunk, chunk]
            + [stat_chunk(4)] * count
            + [affine_chunk(2), affine_chunk(3), one_all, mask_all, slim_block(at_four)],
            [chunk, chunk, narrow_all, stat_all],
            [wide_f32, wide_low, narrow_f32, stat_narrow],
            flops_wide,
        )(z_three, z_side, *parts_pair, norm_params, norm_params, recip, mask, slim)
        parts_four = link.group_parts(stat)
        one_kind = whole((1, rows, mid))
        act_four, z_five, stat = kernel_call(
            conv_kernel(count, 1, 1),
            "conv_five",
            (9,),
            [one_kind]
            + [stat_all] * count
            + [affine(4), one_all, mask_all, shifts_all, slim_block(at_five)],
            [one_kind, narrow_all, stat_all],
            [shape_of((1, rows, mid), BF16), narrow_f32, stat_narrow],
            flops_conv,
        )(z_four[None], *parts_four, norm_params, recip, mask, shifts, slim)
        parts_five = link.group_parts(stat)
        act_five, z_six, stat = kernel_call(
            widen_kernel(count, False),
            "widen_six",
            (chunks,),
            [narrow_all]
            + [stat_all] * count
            + [affine(5), one_all, mask_all, broad_block(at_six)],
            [narrow_all, chunk, stat_chunk(2)],
            [narrow_low, wide_f32, stat_wide],
            flops_wide,
        )(z_five, *parts_five, norm_params, recip, mask, broad)
        parts_six = link.group_parts(stat)
        grids = [
            block((side, side, images, mid), lambda j: (0, 0, 0, j)) for side in sides
        ]
        *y_grids, grad_out, stat = kernel_call(
            output_kernel(count, images, sides),
            "output",
            (chunks,),
            [chunk]
            + [stat_chunk(2)] * count
            + [affine_chunk(6), one_all, mask_all, chunk]
            + grids,
            grids + [chunk, stat_chunk(2)],
            [shape_of((side, side, images, c_out), BF16) for side in sides]
            + [wide_f32, stat_wide],
            flops_wide // 8,
            scratch=[pltpu.VMEM((rows, mid), F32)],
        )(
            z_six,
            *parts_six,
            norm_params,
            recip,
            mask,
            hidden,
            *[by_cell(value) for value in (cot_lo, cot_mid, cot_hi)],
        )
        sums_six = link.group_parts(stat)

        dz_six, grad_five, stat = kernel_call(
            back_linear_kernel(count),
            "back_six",
            (chunks,),
            [chunk, chunk]
            + [stat_chunk(2)] * (2 * count)
            + [affine_chunk(6), one_all, mask_all, broad_block(at_six), narrow_all]
            + [stat_all] * count
            + [affine(5)],
            [chunk, narrow_all, stat_all],
            [wide_low, narrow_f32, stat_narrow],
            flops_wide,
        )(
            grad_out,
            z_six,
            *parts_six,
            *sums_six,
            norm_params,
            recip,
            mask,
            broad,
            z_five,
            *parts_five,
            norm_params,
        )
        sums_five = link.group_parts(stat)

        def weight_grad(act, dz, steps, act_at, out_shape, out_at, base, name):
            high, across = steps
            height = act.shape[0]
            specs = [
                block((height, mid), lambda i, j: (0, act_at + i)),
                block((height, mid), lambda i, j: (0, j)),
            ]
            args = [act, dz]
            if base is not None:
                specs.append(pl.BlockSpec(memory_space=pl.ANY))
                args.append(base)
            return kernel_call(
                weight_grad_kernel,
                name,
                (high, across),
                specs,
                block((mid, mid), lambda i, j: (out_at + i, j)),
                shape_of(out_shape, BF16),
                2 * height * mid * mid * high * across,
                aliases={2: 0} if base is not None else None,
            )(*args)

        def conv_grad(act, dz, stride, taps, out_shape, out_at, base, name):
            first, number = taps
            kinds_here = act.shape[0]
            specs = [whole((kinds_here, rows, mid)), shifts_all, narrow_all]
            args = [act, shifts, dz]
            if base is not None:
                specs.append(pl.BlockSpec(memory_space=pl.ANY))
                args.append(base)
            return kernel_call(
                conv_grad_kernel(stride, first),
                name,
                (number,),
                specs,
                block((mid, mid), lambda t: (out_at + t, 0)),
                shape_of(out_shape, BF16),
                flops_conv * number // 9,
                aliases={3: 0} if base is not None else None,
            )(*args)

        slim_part = (bounds_slim[-1] // 4, mid)
        broad_part = (bounds_broad[-1] // 4, c_out)
        per_part = slim_part[0] // mid
        term_six = weight_grad(act_five, dz_six, (1, chunks), 0, broad_part, 0, None, "grad_six")
        chain_six = Scatter(link, kernel_call, term_six, "sum_six", (1, 1), "all_wide")

        dz_five, grad_four, stat = kernel_call(
            back_conv_kernel(count, 1, 1),
            "back_five",
            (9,),
            [narrow_all, narrow_all]
            + [stat_all] * (2 * count)
            + [affine(5), one_all, mask_all, shifts_all, slim_block(at_five), one_kind]
            + [stat_all] * count
            + [affine(4), one_all],
            [narrow_all, one_kind, stat_all],
            [narrow_low, shape_of((1, rows, mid), F32), stat_narrow],
            flops_conv,
        )(
            grad_five,
            z_five,
            *parts_five,
            *sums_five,
            norm_params,
            recip,
            mask,
            shifts,
            slim,
            z_four[None],
            *parts_four,
            norm_params,
            recip,
        )
        grad_four = grad_four[0]
        sums_four = link.group_parts(stat)
        low_four = 2 * per_part - at_four
        low_five = 3 * per_part - at_five
        chain_six.step()
        term = conv_grad(
            act_four, dz_five, 1, (low_five, 9 - low_five), slim_part, 0, None, "grad_five_high"
        )
        chain_five = Scatter(link, kernel_call, term, "sum_five", (1, 1), "all_wide")
        term_four = conv_grad(
            act_four, dz_five, 1, (0, low_five), slim_part, chunks - low_four, None, "grad_five_low"
        )
        dz_four, grad_mid, stat = kernel_call(
            back_mix_kernel(count),
            "back_four",
            (chunks,),
            [narrow_all, narrow_all]
            + [stat_all] * (2 * count)
            + [affine(4), one_all, mask_all, slim_block(at_four), chunk, chunk, chunk]
            + [stat_chunk(4)] * count
            + [affine_chunk(2), affine_chunk(3)],
            [narrow_all, chunk, stat_chunk(3)],
            [narrow_low, wide_f32, shape_of((3, c_out), F32)],
            flops_wide,
        )(
            grad_four,
            z_four,
            *parts_four,
            *sums_four,
            norm_params,
            recip,
            mask,
            slim,
            grad_out,
            z_three,
            z_side,
            *parts_pair,
            norm_params,
            norm_params,
        )
        sums_pair = link.group_parts(stat)
        chain_five.step()
        chain_six.step()
        term_four = weight_grad(
            hidden_low,
            dz_four,
            (chunks - low_four, 1),
            low_four,
            slim_part,
            0,
            term_four,
            "grad_four",
        )
        chain_four = Scatter(link, kernel_call, term_four, "sum_four", (0, 1), "all_wide")
        dz_three, dz_side, grad_two, stat = kernel_call(
            back_pair_kernel(count),
            "back_three",
            (chunks,),
            [chunk, chunk, chunk]
            + [stat_chunk(4)] * count
            + [stat_chunk(3)] * count
            + [affine_chunk(2), affine_chunk(3), one_all, mask_all, broad_block(0), narrow_all]
            + [stat_all] * count
            + [affine(1)],
            [chunk, chunk, narrow_all, stat_all],
            [wide_low, wide_low, narrow_f32, stat_narrow],
            flops_wide,
        )(
            grad_mid,
            z_three,
            z_side,
            *parts_pair,
            *sums_pair,
            norm_params,
            norm_params,
            recip,
            mask,
            broad,
            z_two,
            *parts_two,
            norm_params,
        )
        sums_two = link.group_parts(stat)
        chain_four.step()
        x_sub = x_kinds[0]
        two_parts = (2 * broad_part[0], c_out)
        term_three = weight_grad(
            act_two, dz_three, (1, chunks), 0, two_parts, 0, None, "grad_three"
        )
        term = weight_grad(
            x_sub, dz_side, (1, chunks), 0, two_parts, 1, term_three, "grad_side_low"
        )
        chain_six.step()
        chain_three = Scatter(link, kernel_call, term, "sum_three", (0,), "all_wide")
        chain_five.step()
        term = weight_grad(
            x_sub, dz_side, (1, chunks), 1, broad_part, 0, None, "grad_side_high"
        )
        chain_side = Scatter(link, kernel_call, term, "sum_side", (0, 1), "narrow")

        dz_two, grad_one, stat = kernel_call(
            back_conv_kernel(count, 4, 2),
            "back_two",
            (9,),
            [narrow_all, narrow_all]
            + [stat_all] * (2 * count)
            + [affine(1), one_all, mask_all, shifts_all, slim_block(at_two), kinds_all]
            + [stat_all] * count
            + [affine(0), one_all],
            [narrow_all, kinds_all, stat_all],
            [narrow_low, shape_of((4, rows, mid), F32), stat_narrow],
            flops_conv,
        )(
            grad_two,
            z_two,
            *parts_two,
            *sums_two,
            norm_params,
            recip,
            mask,
            shifts,
            slim,
            z_one,
            *parts_one,
            norm_params,
            recip_in,
        )
        sums_one = link.group_parts(stat)
        chain_three.step()
        chain_four.step()
        chain_five.step()
        term = conv_grad(
            act_one, dz_two, 2, (per_part - at_two, 9 - per_part + at_two), slim_part, 0, None,
            "grad_two_high",
        )
        term = weight_grad(
            hidden_low, dz_four, (low_four, 1), 0, slim_part, per_part - low_four, term,
            "grad_four_low",
        )
        chain_two = Scatter(link, kernel_call, term, "sum_two", (1, 0), "narrow")
        slim_low = conv_grad(
            act_one, dz_two, 2, (0, per_part - at_two), slim_part, at_two, None, "grad_two_low"
        )
        dz_one, slim_low = kernel_call(
            back_first_kernel(count),
            "back_one",
            (4,),
            [block((1, rows, mid), lambda j: (j, 0, 0))] * 2
            + [stat_all] * (2 * count)
            + [
                affine(0),
                one_all,
                mask_all,
                block((1, rows, c_in), lambda j: (j, 0, 0)),
                pl.BlockSpec(memory_space=pl.ANY),
            ],
            [block((1, rows, mid), lambda j: (j, 0, 0)), whole((c_in, mid))],
            [shape_of((4, rows, mid), BF16), shape_of(slim_part, BF16)],
            2 * 4 * rows * c_in * mid,
            scratch=[pltpu.VMEM((c_in, mid), F32)],
            aliases={2 + 2 * count + 4: 1},
        )(grad_one, z_one, *parts_one, *sums_one, norm_params, recip_in, mask, x_kinds, slim_low)
        chain_one = Scatter(link, kernel_call, slim_low, "sum_one", (0, 0), "wide")
        chain_side.step()
        chain_two.step()
        chain_six.step()

        extents = tuple(2 * side for side in sides)
        dx_grids = kernel_call(
            input_grad_kernel(images, sides),
            "input_grad",
            (c_in // mid,),
            [
                kinds_all,
                slim_block(0),
                whole((rows, c_out)),
                block((mid, c_out), lambda j: (1 + j, 0)),
            ],
            [
                block((extent, extent, images, mid), lambda j: (0, 0, 0, j))
                for extent in extents
            ],
            [shape_of((extent, extent, images, c_in), F32) for extent in extents],
            2 * 4 * rows * c_in * mid + 2 * rows * c_in * c_out,
            scratch=[pltpu.VMEM((rows, mid), F32)],
        )(dz_one, slim, dz_side, broad)

        def by_image(value):
            return jnp.transpose(value, (2, 0, 1, 3))

        y_parts = [by_image(value) for value in y_grids]
        dx_parts = [by_image(value) for value in dx_grids]

        top = link.bit(link.bits - 1)
        second = link.bit(link.bits - 2)

        def choose(bit, upper, lower):
            return jnp.where(bit == 1, upper, lower)

        def tally(grad, master, rowstat, bounds, name, after, extra=None):
            height, columns = grad.shape
            levels = len(bounds) - 1
            first = (link.index * height).astype(jnp.int32).reshape(1)
            matrix, column = whole((height, columns)), whole((height, 1))
            extras = [] if extra is None else [extra]
            sum_dims = (4 * levels + sum(value.shape[0] for value in extras), columns)
            rows_new, sums = kernel_call(
                tally_kernel(bounds, bool(extras)),
                name,
                (1,),
                [pl.BlockSpec(memory_space=pltpu.SMEM), matrix, matrix, column]
                + [whole(value.shape) for value in extras],
                [column, whole(sum_dims)],
                [shape_of((height, 1), F32), shape_of(sum_dims, F32)],
                20 * height * columns,
                after=after,
            )(first, grad, master, rowstat.reshape(height, 1), *extras)
            return rows_new, link.total_sums(sums)

        def renew(grad, master, rows_new, sums, colstat, bounds, name):
            height, columns = grad.shape
            levels = len(bounds) - 1
            first = (link.index * height).astype(jnp.int32).reshape(1)
            matrix, column = whole((height, columns)), whole((height, 1))
            sums_all, cols_all = whole((4 * levels, columns)), whole((levels, columns))
            return kernel_call(
                renew_kernel(bounds),
                name,
                (1,),
                [
                    pl.BlockSpec(memory_space=pltpu.SMEM),
                    matrix,
                    matrix,
                    column,
                    sums_all,
                    cols_all,
                ],
                [cols_all, matrix, matrix],
                [
                    shape_of((levels, columns), F32),
                    shape_of((height, columns), F32),
                    shape_of((height, columns), BF16),
                ],
                20 * height * columns,
            )(first, grad, master, rows_new, sums, colstat)

        spans = [
            (mid * at, width, rows_of)
            for at, width, rows_of in zip(
                norm_at, widths, ((0, 1),) * 2 + ((0, 1), (2, 1)) + ((0, 1),) * 3
            )
        ]
        sum_sets = [sums_one, sums_two, sums_pair, sums_pair, sums_four, sums_five, sums_six]
        flat_sets = [part for parts in sum_sets for part in parts]
        norm_rows = norm_params.size // c_out
        norm_sums = kernel_call(
            pack_kernel(count, spans, mid),
            "pack",
            (1,),
            [whole(part.shape) for part in flat_sets],
            whole((norm_rows, c_out)),
            shape_of((norm_rows, c_out), F32),
            1000000,
        )(*flat_sets)

        chain_one.step()
        chain_three.step()
        chain_four.step()
        chain_five.step()
        chain_side.step()
        chain_two.step()
        chain_one.step()
        chain_three.step()
        chain_side.step()
        chain_four.step()
        broad_six = chain_six.finish()
        chain_two.step()
        chain_one.step()
        chain_side.step()
        slim_five = chain_five.finish()
        chain_three.step()
        chain_two.step()
        chain_one.step()
        broad_side = chain_side.finish()
        broad_three = chain_three.finish()
        broad_grad = choose(top, choose(second, broad_six, broad_side), broad_three)
        broad_rows_new, broad_sums = tally(
            broad_grad, broad_master, broad_rowstat, bounds_broad, "broad_tally", [], norm_sums
        )
        slim_four = chain_four.finish()
        slim_two = chain_two.finish()
        slim_one = chain_one.finish()
        slim_high = choose(second, slim_five, slim_four)
        slim_low = choose(second, slim_two, slim_one)
        slim_grad = choose(top, slim_high, slim_low)

        slim_rows_new, slim_sums = tally(
            slim_grad, slim_master, slim_rowstat, bounds_slim, "slim_tally", []
        )
        broad_cols_new, broad_new, broad_copy = renew(
            broad_grad,
            broad_master,
            broad_rows_new,
            broad_sums[-1][:-norm_rows],
            broad_colstat,
            bounds_broad,
            "broad_renew",
        )
        slim_cols_new, slim_new, slim_copy = renew(
            slim_grad,
            slim_master,
            slim_rows_new,
            slim_sums[-1],
            slim_colstat,
            bounds_slim,
            "slim_renew",
        )
        norm_grad = broad_sums[-1][-norm_rows:].reshape(norm_params.shape) * (1.0 / n_narrow)
        norm_moments_new = DECAY * norm_moments + (1.0 - DECAY) * (
            norm_grad * norm_grad + EPS_ONE
        )
        norm_update = norm_grad * lax.rsqrt(norm_moments_new)
        update_rms = jnp.sqrt(jnp.mean(norm_update * norm_update, 1))
        weight_rms = jnp.sqrt(jnp.mean(norm_params * norm_params, 1))
        step = STEP_RATE * jnp.maximum(EPS_TWO, weight_rms) / jnp.maximum(1.0, update_rms)
        norm_new = norm_params - step[:, None] * norm_update
        return (
            *y_parts,
            *dx_parts,
            slim_grad,
            broad_grad,
            slim_rows_new.reshape(-1),
            broad_rows_new.reshape(-1),
            slim_cols_new,
            broad_cols_new,
            slim_new,
            broad_new,
            slim_copy,
            broad_copy,
            norm_grad,
            norm_moments_new,
            norm_new,
        )

    return body


def solution(mesh):
    split = P(AXES)
    return jax.shard_map(
        make_body(mesh),
        mesh=mesh,
        in_specs=(split,) * 11 + (P(),) * 4,
        out_specs=(split,) * 10 + (P(),) * 2 + (split,) * 4 + (P(),) * 3,
        check_vma=False,
    )
```

```python
import jax
import jax.numpy as jnp
import numpy as np
from jax import lax
from jax.experimental import pallas as pl
from jax.experimental.pallas import tpu as pltpu
from jax.sharding import PartitionSpec as P

STEP = 10
EPS_NORM = 1e-05
EPS_ONE = 1e-30
EPS_TWO = 0.001
STEP_RATE = 0.3
DECAY = 1.0 - STEP ** (-0.8)
AXES = ("wide", "narrow")
BF16 = jnp.bfloat16
F32 = jnp.float32
LATE_STEPS = 2
VMEM_LIMIT = 48 * 1024 * 1024


def shape_of(dims, dtype):
    return jax.ShapeDtypeStruct(dims, dtype)


def far_shape(dims, dtype):
    return pltpu.HBM(dims, dtype)


def whole(dims):
    return pl.BlockSpec(dims, lambda *step: (0,) * len(dims))


def block(dims, place):
    return pl.BlockSpec(dims, place)


LENGTHS = dict(
    first=3.9,
    conv_two=10.8,
    side=7.2,
    widen_three=3.8,
    mix=5.3,
    conv_five=8.9,
    widen_six=3.9,
    output=6.8,
    back_six=5.1,
    grad_six=2.1,
    back_five=10,
    grad_five=8,
    back_four=6.5,
    grad_four=2.6,
    back_three=6,
    grad_three=3,
    grad_side_low=2.1,
    grad_side_high=2.1,
    back_two=13.7,
    grad_two_high=4.8,
    grad_four_low=0.5,
    grad_two_low=4.8,
    back_one=6.3,
    input_grad=6.7,
    sum_six_0=1,
    sum_five_0=1.8,
    sum_four_0=2.1,
    sum_three_0=4.5,
    sum_side_0=1.5,
    sum_two_0=2.2,
    sum_one_0=2,
    sum_five_1=2.2,
    sum_four_1=2.7,
    sum_three_1=3.6,
    sum_side_1=2,
    sum_two_1=2.2,
)


def length(name):
    return LENGTHS.get(name, 1)


class Kernels:
    def __init__(self):
        self.last = None

    def __call__(
        self,
        body,
        name,
        grid,
        in_specs,
        out_specs,
        out_shape,
        flops,
        scratch=(),
        aliases=None,
        after=(),
        scalars=0,
    ):
        taken = scalars + len(in_specs)

        def run(*args):
            waits = [
                value
                for value in (*after, self.last)
                if value is not None and not any(value is arg for arg in args)
            ]

            def trimmed(*refs):
                body(*refs[:taken], *refs[taken + len(waits) :])

            out = pl.pallas_call(
                trimmed,
                grid_spec=pltpu.PrefetchScalarGridSpec(
                    num_scalar_prefetch=scalars,
                    grid=grid,
                    in_specs=list(in_specs) + [pl.BlockSpec(memory_space=pl.ANY)] * len(waits),
                    out_specs=out_specs,
                    scratch_shapes=list(scratch),
                ),
                out_shape=out_shape,
                input_output_aliases=aliases or {},
                cost_estimate=pl.CostEstimate(
                    flops=int(length(name) * 1.15e8),
                    bytes_accessed=int(length(name) * 3.6e5),
                    transcendentals=0,
                ),
                compiler_params=pltpu.CompilerParams(vmem_limit_bytes=VMEM_LIMIT),
                name=name,
            )(*args, *waits)
            self.last = out[0] if isinstance(out, (list, tuple)) else out
            return out

        return run


def dot_nn(first, second):
    return jnp.dot(first, second, preferred_element_type=F32)


def dot_nt(first, second):
    return lax.dot_general(first, second, (((1,), (1,)), ((), ())), preferred_element_type=F32)


def dot_tn(first, second):
    return lax.dot_general(first, second, (((0,), (0,)), ((), ())), preferred_element_type=F32)


def sigmoid(value):
    return 1.0 / (1.0 + jnp.exp(-value))


def slope(value):
    gate = sigmoid(value)
    return gate * (1.0 + value * (1.0 - gate))


def tree_sum(values):
    values = list(values)
    while len(values) > 1:
        values = [values[i] + values[i + 1] for i in range(0, len(values), 2)]
    return values[0]


def moments(parts, recip):
    total = tree_sum([part[...] for part in parts]) * recip
    mean = total[0:1]
    return mean, lax.rsqrt(total[1:2] - mean * mean + EPS_NORM)


def column_sum(value):
    return jnp.sum(value, axis=0, keepdims=True)


def stat_rows(value, mask):
    kept = value * mask
    return jnp.concatenate([column_sum(kept), column_sum(kept * value)], 0)


def grid_rows(images, sides):
    return sum(images * side * side for side in sides)


def class_table(images, sides_out, padded):
    table = -np.ones((4, padded), np.int32)
    base_in, base_out = 0, 0
    for side in sides_out:
        extent = 2 * side
        for row in range(side):
            for col in range(side):
                for image in range(images):
                    for kind in range(4):
                        cell = (2 * row + kind // 2) * extent + 2 * col + kind % 2
                        table[kind, base_out + (row * side + col) * images + image] = (
                            base_in + cell * images + image
                        )
        base_in += images * extent * extent
        base_out += images * side * side
    return table


def shift_table(images, sides_out, padded):
    table = -np.ones((9, padded), np.int32)
    base = 0
    for side in sides_out:
        for row in range(side):
            for col in range(side):
                for which in range(9):
                    row_to, col_to = row + which // 3 - 1, col + which % 3 - 1
                    if 0 <= row_to < side and 0 <= col_to < side:
                        for image in range(images):
                            table[which, base + (row * side + col) * images + image] = (
                                base + (row_to * side + col_to) * images + image
                            )
        base += images * side * side
    return table


def one_hot(table, width):
    return (jnp.asarray(table)[..., None] == jnp.arange(width, dtype=jnp.int32)).astype(BF16)


def first_kernel(x_ref, w_ref, mask_ref, z_ref, stat_ref):
    z = dot_nn(x_ref[0], w_ref[...])
    z_ref[0] = z
    rows = stat_rows(z, mask_ref[...])

    @pl.when(pl.program_id(0) == 0)
    def _():
        stat_ref[...] = rows

    @pl.when(pl.program_id(0) > 0)
    def _():
        stat_ref[...] += rows


def side_kernel(x_ref, w_ref, mask_ref, z_ref, stat_ref):
    term = dot_nn(x_ref[0], w_ref[...])

    @pl.when(pl.program_id(1) == 0)
    def _():
        z_ref[...] = term

    @pl.when(pl.program_id(1) > 0)
    def _():
        z_ref[...] += term

    @pl.when(pl.program_id(1) == pl.num_programs(1) - 1)
    def _():
        stat_ref[...] = stat_rows(z_ref[...], mask_ref[...])


def tap_forward(tap, stride):
    if stride == 1:
        return 0, tap
    row_tap, col_tap = tap // 3, tap % 3
    kind = jnp.where(row_tap == 1, 0, 2) + jnp.where(col_tap == 1, 0, 1)
    shift = jnp.where(row_tap == 0, 0, 3) + jnp.where(col_tap == 0, 0, 1)
    return kind, shift


def tap_backward(tap, stride):
    if stride == 1:
        return 0, 8 - tap
    row_tap, col_tap = tap // 3, tap % 3
    kind = jnp.where(row_tap == 1, 0, 2) + jnp.where(col_tap == 1, 0, 1)
    shift = jnp.where(row_tap == 0, 6, 3) + jnp.where(col_tap == 0, 2, 1)
    return kind, shift


def conv_kernel(count, kinds, stride):
    def body(*refs):
        z_ref = refs[0]
        parts = refs[1 : 1 + count]
        affine_ref, recip_ref, mask_ref, shift_ref = refs[1 + count : 5 + count]
        w_refs = refs[5 + count : 8 + count]
        act_ref, out_ref, stat_ref = refs[8 + count :]
        tap = pl.program_id(0)

        @pl.when(tap == 0)
        def _():
            mean, inv = moments(parts, recip_ref[...])
            for kind in range(kinds):
                pre = affine_ref[0:1] * ((z_ref[kind] - mean) * inv) + affine_ref[1:2]
                act_ref[kind] = (pre * sigmoid(pre)).astype(BF16)

        patches = []
        for offset in range(3):
            kind, shift = tap_forward(3 * tap + offset, stride)
            patches.append(dot_nn(shift_ref[shift], act_ref[kind]).astype(BF16))
        term = None
        for patch, w_ref in zip(patches, w_refs):
            part = dot_nn(patch, w_ref[...])
            term = part if term is None else term + part

        @pl.when(tap == 0)
        def _():
            out_ref[...] = term

        @pl.when(tap > 0)
        def _():
            out_ref[...] += term

        @pl.when(tap == 2)
        def _():
            stat_ref[...] = stat_rows(out_ref[...], mask_ref[...])

    return body


def widen_kernel(count, carry):
    def body(*refs):
        z_ref = refs[0]
        parts = refs[1 : 1 + count]
        rest = refs[1 + count :]
        if carry:
            affine_ref, recip_ref, mask_ref, w_ref, side_ref, act_ref, out_ref, stat_ref = rest
        else:
            affine_ref, recip_ref, mask_ref, w_ref, act_ref, out_ref, stat_ref = rest

        @pl.when(pl.program_id(0) == 0)
        def _():
            mean, inv = moments(parts, recip_ref[...])
            pre = affine_ref[0:1] * ((z_ref[...] - mean) * inv) + affine_ref[1:2]
            act_ref[...] = (pre * sigmoid(pre)).astype(BF16)

        z = dot_nn(act_ref[...], w_ref[...])
        out_ref[...] = z
        if carry:
            stat_ref[...] = jnp.concatenate([stat_rows(z, mask_ref[...]), side_ref[...]], 0)
        else:
            stat_ref[...] = stat_rows(z, mask_ref[...])

    return body


def pair_moments(parts, recip):
    total = tree_sum([part[...] for part in parts]) * recip
    mean, mean_side = total[0:1], total[2:3]
    inv = lax.rsqrt(total[1:2] - mean * mean + EPS_NORM)
    inv_side = lax.rsqrt(total[3:4] - mean_side * mean_side + EPS_NORM)
    return mean, inv, mean_side, inv_side


def mix_kernel(count):
    def body(*refs):
        z_ref, side_ref = refs[:2]
        parts = refs[2 : 2 + count]
        (affine_ref, affine_side_ref, recip_ref, mask_ref, w_ref) = refs[2 + count : 7 + count]
        hidden_ref, low_ref, out_ref, stat_ref = refs[7 + count :]
        mean, inv, mean_side, inv_side = pair_moments(parts, recip_ref[...])
        pre = (
            affine_ref[0:1] * ((z_ref[...] - mean) * inv)
            + affine_ref[1:2]
            + affine_side_ref[0:1] * ((side_ref[...] - mean_side) * inv_side)
            + affine_side_ref[1:2]
        )
        hidden = pre * sigmoid(pre)
        hidden_ref[...] = hidden
        low = hidden.astype(BF16)
        low_ref[...] = low
        term = dot_nn(low, w_ref[...])

        @pl.when(pl.program_id(0) == 0)
        def _():
            out_ref[...] = term

        @pl.when(pl.program_id(0) > 0)
        def _():
            out_ref[...] += term

        @pl.when(pl.program_id(0) == pl.num_programs(0) - 1)
        def _():
            stat_ref[...] = stat_rows(out_ref[...], mask_ref[...])

    return body


def cell_rows(images, sides):
    base = 0
    for level, side in enumerate(sides):
        for row in range(side):
            for col in range(side):
                yield level, row, col, base + (row * side + col) * images
        base += images * side * side


def output_kernel(count, images, sides):
    def body(*refs):
        z_ref = refs[0]
        parts = refs[1 : 1 + count]
        affine_ref, recip_ref, mask_ref, hidden_ref = refs[1 + count : 5 + count]
        cot_refs = refs[5 + count : 8 + count]
        y_refs = refs[8 + count : 11 + count]
        grad_ref, stat_ref, flat_ref = refs[11 + count :]
        used = grid_rows(images, sides)
        if flat_ref.shape[0] > used:
            flat_ref[used:] = jnp.zeros((flat_ref.shape[0] - used, flat_ref.shape[1]), F32)
        for level, row, col, at in cell_rows(images, sides):
            flat_ref[at : at + images] = cot_refs[level][row, col].astype(F32)
        mean, inv = moments(parts, recip_ref[...])
        normed = (z_ref[...] - mean) * inv
        pre = affine_ref[0:1] * normed + affine_ref[1:2] + hidden_ref[...]
        gate = sigmoid(pre)
        grad = flat_ref[...] * mask_ref[...] * (gate * (1.0 + pre * (1.0 - gate)))
        grad_ref[...] = grad
        stat_ref[...] = jnp.concatenate([column_sum(grad * normed), column_sum(grad)], 0)
        flat_ref[...] = pre * gate
        for level, row, col, at in cell_rows(images, sides):
            y_refs[level][row, col] = flat_ref[at : at + images].astype(BF16)

    return body


def input_grad_kernel(images, sides):
    def body(dz_ref, w_ref, side_ref, w_side_ref, *rest):
        out_refs, flat_ref = rest[:3], rest[3]
        for kind in range(4):
            value = dot_nt(dz_ref[kind], w_ref[...])
            if kind == 0:
                value += dot_nt(side_ref[...], w_side_ref[...])
            flat_ref[...] = value
            for level, row, col, at in cell_rows(images, sides):
                out_refs[level][2 * row + kind // 2, 2 * col + kind % 2] = flat_ref[
                    at : at + images
                ]

    return body


def norm_back(grad, normed, sums, recip, mask, scale):
    return scale * (grad - mask * (sums[1:2] * recip + normed * (sums[0:1] * recip)))


def back_linear_kernel(count):
    def body(*refs):
        grad_ref, z_ref = refs[:2]
        parts = refs[2 : 2 + count]
        sums = refs[2 + count : 2 + 2 * count]
        affine_ref, recip_ref, mask_ref, w_ref, below_ref = refs[2 + 2 * count : 7 + 2 * count]
        below_parts = refs[7 + 2 * count : 7 + 3 * count]
        below_affine_ref, dz_ref, out_ref, stat_ref = refs[7 + 3 * count :]
        recip = recip_ref[...]
        mean, inv = moments(parts, recip)
        total = tree_sum([part[...] for part in sums])
        normed = (z_ref[...] - mean) * inv
        dz = norm_back(grad_ref[...], normed, total, recip, mask_ref[...], affine_ref[0:1] * inv)
        dz = dz.astype(BF16)
        dz_ref[...] = dz
        term = dot_nt(dz, w_ref[...])

        @pl.when(pl.program_id(0) == 0)
        def _():
            out_ref[...] = term

        @pl.when(pl.program_id(0) > 0)
        def _():
            out_ref[...] += term

        @pl.when(pl.program_id(0) == pl.num_programs(0) - 1)
        def _():
            finish_below(out_ref, below_ref, below_parts, below_affine_ref, recip, stat_ref)

    return body


def finish_below(out_ref, below_ref, below_parts, below_affine_ref, recip, stat_ref):
    mean, inv = moments(below_parts, recip)
    normed = (below_ref[...] - mean) * inv
    pre = below_affine_ref[0:1] * normed + below_affine_ref[1:2]
    grad = out_ref[...] * slope(pre)
    out_ref[...] = grad
    stat_ref[...] = jnp.concatenate([column_sum(grad * normed), column_sum(grad)], 0)


def back_conv_kernel(count, kinds, stride):
    def body(*refs):
        grad_ref, z_ref = refs[:2]
        parts = refs[2 : 2 + count]
        sums = refs[2 + count : 2 + 2 * count]
        affine_ref, recip_ref, mask_ref, shift_ref = refs[2 + 2 * count : 6 + 2 * count]
        w_refs = refs[6 + 2 * count : 9 + 2 * count]
        below_ref = refs[9 + 2 * count]
        below_parts = refs[10 + 2 * count : 10 + 3 * count]
        below_affine_ref, below_recip_ref, dz_ref, out_ref, stat_ref = refs[10 + 3 * count :]
        tap = pl.program_id(0)

        @pl.when(tap == 0)
        def _():
            recip = recip_ref[...]
            mean, inv = moments(parts, recip)
            total = tree_sum([part[...] for part in sums])
            normed = (z_ref[...] - mean) * inv
            dz = norm_back(
                grad_ref[...], normed, total, recip, mask_ref[...], affine_ref[0:1] * inv
            )
            dz_ref[...] = dz.astype(BF16)
            out_ref[...] = jnp.zeros_like(out_ref)

        if stride == 1:
            term = None
            for offset in range(3):
                _, shift = tap_backward(3 * tap + offset, stride)
                patch = dot_nn(shift_ref[shift], dz_ref[...]).astype(BF16)
                part = dot_nt(patch, w_refs[offset][...])
                term = part if term is None else term + part
            out_ref[0] += term
        else:
            for offset in range(3):
                kind, shift = tap_backward(3 * tap + offset, stride)
                patch = dot_nn(shift_ref[shift], dz_ref[...]).astype(BF16)
                out_ref[kind] += dot_nt(patch, w_refs[offset][...])

        @pl.when(tap == 2)
        def _():
            mean, inv = moments(below_parts, below_recip_ref[...])
            rows = None
            for which in range(kinds):
                normed = (below_ref[which] - mean) * inv
                pre = below_affine_ref[0:1] * normed + below_affine_ref[1:2]
                grad = out_ref[which] * slope(pre)
                out_ref[which] = grad
                part = jnp.concatenate([column_sum(grad * normed), column_sum(grad)], 0)
                rows = part if rows is None else rows + part
            stat_ref[...] = rows

    return body


def back_mix_kernel(count):
    def body(*refs):
        grad_ref, z_ref = refs[:2]
        parts = refs[2 : 2 + count]
        sums = refs[2 + count : 2 + 2 * count]
        affine_ref, recip_ref, mask_ref, w_ref, above_ref, mid_ref, side_ref = refs[
            2 + 2 * count : 9 + 2 * count
        ]
        pair_parts = refs[9 + 2 * count : 9 + 3 * count]
        affine_mid_ref, affine_side_ref, dz_ref, out_ref, stat_ref = refs[9 + 3 * count :]
        recip = recip_ref[...]

        @pl.when(pl.program_id(0) == 0)
        def _():
            mean, inv = moments(parts, recip)
            total = tree_sum([part[...] for part in sums])
            normed = (z_ref[...] - mean) * inv
            dz = norm_back(
                grad_ref[...], normed, total, recip, mask_ref[...], affine_ref[0:1] * inv
            )
            dz_ref[...] = dz.astype(BF16)

        mean, inv, mean_side, inv_side = pair_moments(pair_parts, recip)
        normed = (mid_ref[...] - mean) * inv
        normed_side = (side_ref[...] - mean_side) * inv_side
        pre = (
            affine_mid_ref[0:1] * normed
            + affine_mid_ref[1:2]
            + affine_side_ref[0:1] * normed_side
            + affine_side_ref[1:2]
        )
        grad = (above_ref[...] + dot_nt(dz_ref[...], w_ref[...])) * slope(pre)
        out_ref[...] = grad
        stat_ref[...] = jnp.concatenate(
            [column_sum(grad * normed), column_sum(grad), column_sum(grad * normed_side)], 0
        )

    return body


def back_pair_kernel(count):
    def body(*refs):
        grad_ref, mid_ref, side_ref = refs[:3]
        pair_parts = refs[3 : 3 + count]
        sums = refs[3 + count : 3 + 2 * count]
        affine_mid_ref, affine_side_ref, recip_ref, mask_ref, w_ref, below_ref = refs[
            3 + 2 * count : 9 + 2 * count
        ]
        below_parts = refs[9 + 2 * count : 9 + 3 * count]
        below_affine_ref, dz_ref, dz_side_ref, out_ref, stat_ref = refs[9 + 3 * count :]
        recip = recip_ref[...]
        mean, inv, mean_side, inv_side = pair_moments(pair_parts, recip)
        total = tree_sum([part[...] for part in sums])
        normed = (mid_ref[...] - mean) * inv
        normed_side = (side_ref[...] - mean_side) * inv_side
        grad = grad_ref[...]
        mask = mask_ref[...]
        dz = norm_back(grad, normed, total[0:2], recip, mask, affine_mid_ref[0:1] * inv)
        dz = dz.astype(BF16)
        dz_ref[...] = dz
        total_side = jnp.concatenate([total[2:3], total[1:2]], 0)
        dz_side_ref[...] = norm_back(
            grad, normed_side, total_side, recip, mask, affine_side_ref[0:1] * inv_side
        ).astype(BF16)
        term = dot_nt(dz, w_ref[...])

        @pl.when(pl.program_id(0) == 0)
        def _():
            out_ref[...] = term

        @pl.when(pl.program_id(0) > 0)
        def _():
            out_ref[...] += term

        @pl.when(pl.program_id(0) == pl.num_programs(0) - 1)
        def _():
            finish_below(out_ref, below_ref, below_parts, below_affine_ref, recip, stat_ref)

    return body


def back_first_kernel(count):
    def body(*refs):
        grad_ref, z_ref = refs[:2]
        parts = refs[2 : 2 + count]
        sums = refs[2 + count : 2 + 2 * count]
        affine_ref, recip_ref, mask_ref, x_ref, _, dz_ref, grad_w_ref, total_ref = refs[
            2 + 2 * count :
        ]
        recip = recip_ref[...]
        mean, inv = moments(parts, recip)
        total = tree_sum([part[...] for part in sums])
        normed = (z_ref[0] - mean) * inv
        dz = norm_back(grad_ref[0], normed, total, recip, mask_ref[...], affine_ref[0:1] * inv)
        dz = dz.astype(BF16)
        dz_ref[0] = dz
        term = dot_tn(x_ref[0], dz)

        @pl.when(pl.program_id(0) == 0)
        def _():
            total_ref[...] = term

        @pl.when(pl.program_id(0) > 0)
        def _():
            total_ref[...] += term

        @pl.when(pl.program_id(0) == pl.num_programs(0) - 1)
        def _():
            grad_w_ref[...] = total_ref[...].astype(BF16)

    return body


def weight_grad_kernel(act_ref, dz_ref, *rest):
    rest[-1][...] = dot_tn(act_ref[...], dz_ref[...]).astype(BF16)


def conv_grad_kernel(stride, first, per):
    def body(act_ref, shift_ref, dz_ref, *rest):
        out_ref = rest[-1]
        width = dz_ref.shape[1]
        for offset in range(per):
            kind, shift = tap_forward(per * pl.program_id(0) + first + offset, stride)
            patch = dot_nn(shift_ref[shift], act_ref[kind]).astype(BF16)
            out_ref[offset * width : (offset + 1) * width] = dot_tn(patch, dz_ref[...]).astype(
                BF16
            )

    return body


def pack_kernel(count, spans, piece):
    def body(*refs):
        out_ref = refs[-1]
        columns = out_ref.shape[1]
        high = out_ref.shape[0] // 2
        for which, (start, width, rows) in enumerate(spans):
            parts = refs[which * count : (which + 1) * count]
            total = tree_sum([part[...] for part in parts])
            for offset in range(0, width, piece):
                line, at = (start + offset) // columns, (start + offset) % columns
                for slot, row in enumerate(rows):
                    here = slot * high + line
                    out_ref[here : here + 1, at : at + piece] = total[
                        row : row + 1, offset : offset + piece
                    ]

    return body


def merge_kernel(split, has_kept, last):
    def add(kept_ref, came_ref):
        total = kept_ref[...].astype(F32) + came_ref[...].astype(F32)
        return total if last else total.astype(BF16)

    def body(index_ref, *refs):
        if not has_kept:
            refs[1][...] = refs[0][...]
        elif split:
            refs[4][...] = add(refs[0], refs[1])
            refs[5][...] = add(refs[2], refs[3])
        else:
            refs[2][...] = add(refs[0], refs[1])

    return body


def level_masks(first_row, rows, bounds):
    index = first_row + lax.broadcasted_iota(jnp.int32, (rows, 1), 0)
    return [
        ((index >= bounds[level]) & (index < bounds[level + 1])).astype(F32)
        for level in range(len(bounds) - 1)
    ]


LANES = 128


def tally_kernel(bounds_slim, bounds_broad):
    wide = len(bounds_broad) - 1

    def body(first_ref, *refs):
        inputs, (slim_rows_ref, broad_rows_ref, sums_ref) = refs[:6], refs[6:]
        sums_ref[...] = jnp.zeros_like(sums_ref)
        scalar = 0
        last = sums_ref.shape[0] - 1
        for which, (bounds, rows_ref) in enumerate(
            ((bounds_broad, broad_rows_ref), (bounds_slim, slim_rows_ref))
        ):
            grad_ref, master_ref, old_ref = inputs[3 * which : 3 * which + 3]
            grad = grad_ref[...]
            master = master_ref[...]
            columns = grad.shape[1]
            square = grad * grad
            raised = square + EPS_ONE
            rows_new = DECAY * old_ref[...] + (1.0 - DECAY) * jnp.mean(raised, 1, keepdims=True)
            rows_ref[...] = rows_new
            ratio = square / rows_new
            weight = jnp.sum(master * master, 1, keepdims=True)
            masks = level_masks(first_ref[which], grad.shape[0], bounds)
            for level, mask in enumerate(masks):
                col_sum, ratio_sum = column_sum(raised * mask), column_sum(ratio * mask)
                if which == 0:
                    sums_ref[level : level + 1] = col_sum
                    sums_ref[wide + level : wide + level + 1] = ratio_sum
                else:
                    here = slice(level * columns, (level + 1) * columns)
                    sums_ref[2 * wide : 2 * wide + 1, here] = col_sum
                    sums_ref[2 * wide + 1 : 2 * wide + 2, here] = ratio_sum
                for value in (rows_new, weight):
                    here = slice(scalar * LANES, (scalar + 1) * LANES)
                    sums_ref[last : last + 1, here] = jnp.zeros((1, LANES), F32) + column_sum(
                        value * mask
                    )
                    scalar += 1

    return body


def renew_kernel(bounds, which, bounds_broad):
    wide = len(bounds_broad) - 1

    def body(first_ref, grad_ref, master_ref, rows_ref, sums_ref, old_ref, cols_ref, new_ref, low_ref):
        grad = grad_ref[...]
        columns = grad.shape[1]
        last = sums_ref.shape[0] - 1
        masks = level_masks(first_ref[which], grad.shape[0], bounds)
        factor = None
        for level, mask in enumerate(masks):
            height = float(bounds[level + 1] - bounds[level])
            cells = height * columns
            if which == 0:
                col_sum = sums_ref[level : level + 1]
                ratio_sum = sums_ref[wide + level : wide + level + 1]
            else:
                here = slice(level * columns, (level + 1) * columns)
                col_sum = sums_ref[2 * wide : 2 * wide + 1, here]
                ratio_sum = sums_ref[2 * wide + 1 : 2 * wide + 2, here]
            scalar = (2 * wide if which else 0) + 2 * level
            row_mean = sums_ref[last : last + 1, scalar * LANES : scalar * LANES + 1] / height
            scalar += 1
            weight_sum = sums_ref[last : last + 1, scalar * LANES : scalar * LANES + 1]
            cols_new = DECAY * old_ref[level : level + 1] + (1.0 - DECAY) * (col_sum / height)
            cols_ref[level : level + 1] = cols_new
            relative = cols_new / row_mean
            update_sq = jnp.sum(ratio_sum / relative, axis=1, keepdims=True)
            update_rms = jnp.sqrt(update_sq / cells)
            weight_rms = jnp.sqrt(weight_sum / cells)
            step = STEP_RATE * jnp.maximum(EPS_TWO, weight_rms) / jnp.maximum(1.0, update_rms)
            part = mask * (step * lax.rsqrt(relative))
            factor = part if factor is None else factor + part
        new = master_ref[...] - grad * lax.rsqrt(rows_ref[...]) * factor
        new_ref[...] = new
        low_ref[...] = new.astype(BF16)

    return body


class Exchange:
    def __init__(self, n_wide, n_narrow):
        self.n_narrow = n_narrow
        self.total = n_wide * n_narrow
        self.bits = self.total.bit_length() - 1
        self.narrow_bits = n_narrow.bit_length() - 1
        self.index = lax.axis_index(AXES)

    def bit(self, level):
        return (self.index >> level) & 1

    def swap(self, value, level):
        pairs = [(device, device ^ (1 << level)) for device in range(self.total)]
        return lax.ppermute(value, AXES, pairs)

    def scatter_upper(self, part):
        half = lax.psum_scatter(part, AXES, scatter_dimension=0, tiled=True)
        firsts = self.total // 2
        halves = [
            lax.ppermute(half, AXES, [(2 * k + side, firsts + k) for k in range(firsts)])
            for side in range(2)
        ]
        return jnp.concatenate(halves, 0)

    def group_parts(self, value):
        return [value] + [
            lax.ppermute(value, "narrow", [(i, i ^ k) for i in range(self.n_narrow)])
            for k in range(1, self.n_narrow)
        ]

    def total_sums(self, value, first=0):
        sums = []
        for level in range(first, self.bits):
            value = value + self.swap(value, level)
            sums.append(value)
        return sums


def move_kernel(moves, outs, bases):
    def body(index_ref, *refs):
        out_refs, sems = refs[-1 - outs : -1], refs[-1]
        copies = []
        for which, (operand, unit, out, rows, to, apart) in enumerate(moves):
            start = pl.multiple_of((index_ref[0] ^ to) * rows, rows) if apart else to * rows
            copies.append(
                pltpu.make_async_copy(
                    refs[operand].at[unit], out_refs[out].at[pl.ds(start, rows)], sems.at[which]
                )
            )
        for copy in copies:
            copy.start()
        for copy in copies:
            copy.wait()

    return body


class Gather:
    def __init__(self, link, kernels, shards, names, narrow_first):
        self.link = link
        self.kernels = kernels
        self.names = names
        self.rows = [shard.shape[0] for shard in shards]
        self.columns = [shard.shape[1] for shard in shards]
        inner = list(range(1, link.narrow_bits))
        outer = list(range(link.narrow_bits, link.bits - 2))
        self.levels = [
            (inner + outer if narrow else outer + inner) + [0] for narrow in narrow_first
        ]
        self.stages = len(self.levels[0])
        low, high = link.bits - 2, link.bits - 1
        self.slots = [[] for _ in range(4)]
        for shard, name in zip(shards, names):
            own = shard
            with jax.named_scope(name + "_down"):
                beside = link.swap(own, low)
                across = link.swap(own, high)
                both = link.swap(across, low)
            for slot, (units, apart) in enumerate(
                [
                    (own, 0),
                    (beside, 1 << low),
                    (across, 1 << high),
                    (both, (1 << low) | (1 << high)),
                ]
            ):
                self.slots[slot].append(
                    dict(units=units, pieces=[units], apart=[apart], came=None)
                )
        self.full = None

    def send(self, slot, stage):
        for which, state in enumerate(self.slots[slot]):
            level = self.levels[which][stage]
            with jax.named_scope(f"{self.names[which]}_{slot}_bit{level}"):
                state["came"] = self.link.swap(state["units"], level)

    def move(self, name, moves, args, shapes, aliases, after):
        any_spec = pl.BlockSpec(memory_space=pl.ANY)
        bases = len(aliases)
        return self.kernels(
            move_kernel(moves, len(shapes), bases),
            name,
            (1,),
            [whole(arg.shape) for arg in args[: len(args) - bases]] + [any_spec] * bases,
            [any_spec] * len(shapes),
            [shape_of(dims, BF16) for dims in shapes],
            1,
            scratch=[pltpu.SemaphoreType.DMA((len(moves),))],
            aliases=aliases,
            scalars=1,
            after=after,
        )(self.link.index.astype(jnp.int32).reshape(1), *args)

    def join(self, slot, stage):
        args, moves, shapes = [], [], []
        for which, state in enumerate(self.slots[slot]):
            rows, bit = self.rows[which], 1 << self.levels[which][stage]
            have = len(state["apart"])
            for place, value in enumerate((state["units"], state["came"])):
                moves.append((len(args), slice(None), which, have * rows, place, False))
                args.append(value)
            shapes.append((2 * have * rows, self.columns[which]))
            state["pieces"].append(state["came"])
            state["apart"] += [apart ^ bit for apart in state["apart"]]
        later = {(0, 0): (1, 2), (1, 0): (3,)}.get((slot, stage), ())
        waits = [state["pieces"][0] for ahead in later for state in self.slots[ahead]]
        joined = self.move(f"join_{slot}_{stage}", moves, args, shapes, {}, waits)
        for state, units in zip(self.slots[slot], joined):
            state["units"] = units
        self.send(slot, stage + 1)

    def place(self, slot, after):
        args, moves, shapes = [], [], []
        for which, state in enumerate(self.slots[slot]):
            rows, bit = self.rows[which], 1 << self.levels[which][-1]
            apart = state["apart"]
            for value, extra in ((state["units"], 0), (state["came"], bit)):
                for unit, bits in enumerate(apart):
                    part = slice(unit * rows, (unit + 1) * rows)
                    moves.append((len(args), part, which, rows, bits ^ extra, True))
                args.append(value)
            shapes.append((rows * self.link.total, self.columns[which]))
        aliases = {}
        if self.full is not None:
            aliases = {1 + len(args) + which: which for which in range(len(shapes))}
            args = args + list(self.full)
        self.full = self.move(f"place_{slot}", moves, args, shapes, aliases, after)
        return self.full

    def start(self):
        for slot in range(4):
            self.send(slot, 0)

    @property
    def length(self):
        return self.stages + 3

    def run(self, times, after):
        for time in times:
            for slot in reversed(range(4)):
                stage = time - slot
                if 0 <= stage < self.stages - 1:
                    self.join(slot, stage)
                elif stage == self.stages - 1:
                    self.place(slot, after if slot == 0 else [])


def insert_bit(unit, place, bit):
    return ((unit >> place) << (place + 1)) | (bit << place) | (unit & ((1 << place) - 1))


class Scatter:
    def __init__(self, link, kernels, part, name, prefix=(), first="narrow"):
        self.link = link
        self.kernels = kernels
        self.name = name
        self.prefix = prefix
        self.open_bits = link.bits - len(prefix)
        units = 1 << self.open_bits
        self.kept = part.reshape(units, part.shape[0] // units, part.shape[1])
        self.left = list(range(self.open_bits))
        inner = list(range(1, link.narrow_bits))
        outer = list(range(link.narrow_bits, link.bits))
        orders = {
            "narrow": inner + outer,
            "wide": outer[:1] + inner + outer[1:],
            "all_wide": outer + inner,
        }
        self.levels = [0] + orders[first]
        self.at = 0
        self.came = None
        self.chosen = None
        self.after = []
        self.send_half(None)

    def place(self, level):
        return self.left.index(level)

    def unit_spec(self, source):
        dims = (1,) + self.kept.shape[1:]
        return block(dims, lambda unit, index: (source(unit, index[0]), 0, 0))

    def kept_source(self, source):
        if self.chosen is None:
            return source
        place, level = self.chosen
        return lambda unit, index: insert_bit(
            source(unit, index), place, (index >> level) & 1
        )

    def run(self, body, specs, outs, number, args, dtype):
        spec = self.unit_spec(lambda unit, index: unit)
        shape = shape_of((number,) + self.kept.shape[1:], dtype)
        out = self.kernels(
            body,
            self.name + "_" + str(self.at),
            (number,),
            specs,
            [spec] * outs,
            [shape] * outs,
            4 * number * self.kept.shape[1] * self.kept.shape[2] * 200,
            scalars=1,
            after=self.after,
        )(self.link.index.astype(jnp.int32).reshape(1), *args)
        return out

    def send_half(self, came):
        level = self.levels[self.at] if self.at < len(self.levels) else None
        total_units = 1 << len(self.left)
        if level is not None and level < self.open_bits:
            place = self.place(level)

            def keep(unit, index):
                return insert_bit(unit, place, (index >> level) & 1)

            def send(unit, index):
                return insert_bit(unit, place, 1 - ((index >> level) & 1))

            half = total_units // 2
            if came is None:
                (sent,) = self.run(
                    merge_kernel(True, False, False),
                    [self.unit_spec(send)],
                    1,
                    half,
                    [self.kept],
                    BF16,
                )
                self.chosen = (place, level)
            else:
                kept_keep = self.unit_spec(self.kept_source(keep))
                kept_send = self.unit_spec(self.kept_source(send))
                kept, sent = self.run(
                    merge_kernel(True, True, False),
                    [kept_keep, self.unit_spec(keep), kept_send, self.unit_spec(send)],
                    2,
                    half,
                    [self.kept, came, self.kept, came],
                    BF16,
                )
                self.kept, self.chosen = kept, None
            self.left.remove(level)
            with jax.named_scope(self.name + "_bit" + str(level)):
                self.came = self.link.swap(sent, level)
        else:
            same = lambda unit, index: unit
            (self.kept,) = self.run(
                merge_kernel(False, True, level is None),
                [self.unit_spec(self.kept_source(same)), self.unit_spec(same)],
                1,
                total_units,
                [self.kept, came],
                F32 if level is None else BF16,
            )
            self.chosen = None
            if level is None:
                return
            pairs = []
            for device in range(self.link.total):
                settled = all(
                    (device >> other) & 1 == self.prefix[other - self.open_bits]
                    for other in range(self.open_bits, level)
                )
                if settled and (device >> level) & 1 != self.prefix[level - self.open_bits]:
                    pairs.append((device, device ^ (1 << level)))
            with jax.named_scope(self.name + "_bit" + str(level)):
                self.came = lax.ppermute(self.kept, AXES, pairs)

    def step(self, after=()):
        if self.at < len(self.levels):
            self.at += 1
            self.after = list(after)
            self.send_half(self.came)

    def finish(self):
        while self.at < len(self.levels):
            self.step()
        return self.kept.reshape(self.kept.shape[1:])


def make_body(mesh):
    n_wide, n_narrow = mesh.shape["wide"], mesh.shape["narrow"]

    def body(
        x_lo,
        x_mid,
        x_hi,
        cot_lo,
        cot_mid,
        cot_hi,
        live_counts,
        slim_master,
        broad_master,
        slim_rowstat,
        broad_rowstat,
        slim_colstat,
        broad_colstat,
        norm_params,
        norm_moments,
    ):
        link = Exchange(n_wide, n_narrow)
        kernel_call = Kernels()
        count = n_narrow
        images = x_lo.shape[0]
        sides = tuple(value.shape[1] // 2 for value in (x_lo, x_mid, x_hi))
        c_in, mid, c_out = x_lo.shape[3], slim_master.shape[1], broad_master.shape[1]
        cells = grid_rows(images, sides)
        cells_in = 4 * cells
        rows = -(-cells // 16) * 16
        chunks = c_out // mid
        bounds_slim = (0, c_in, c_in + 9 * mid, c_in + 9 * mid + c_out, c_in + 18 * mid + c_out)
        bounds_broad = (0, mid, mid + c_in, 2 * mid + c_in)
        at_two, at_four, at_five = (bounds_slim[level] // mid for level in (1, 2, 3))
        at_six = bounds_broad[2] // mid
        widths = (mid, mid, c_out, c_out, mid, mid, c_out)
        norm_at = [sum(widths[:level]) // mid for level in range(7)]

        kinds = class_table(images, sides, rows)
        shifts = one_hot(shift_table(images, sides, rows), rows)

        def by_cell(value):
            return jnp.transpose(value, (1, 2, 0, 3))

        x_flat = jnp.concatenate(
            [by_cell(value).reshape(-1, c_in) for value in (x_lo, x_mid, x_hi)], 0
        )
        x_kinds = jnp.dot(one_hot(kinds.reshape(-1), cells_in), x_flat, preferred_element_type=F32)
        x_kinds = x_kinds.astype(BF16).reshape(4, rows, c_in)
        alive = (
            jnp.arange(images, dtype=jnp.int32)[None] < live_counts[0][:, None]
        ).astype(F32)
        slots = np.zeros((rows, len(sides) * images), np.float32)
        base = 0
        for level, side in enumerate(sides):
            for at in range(images * side * side):
                slots[base + at, level * images + at % images] = 1.0
            base += images * side * side
        mask = jnp.sum(jnp.asarray(slots) * alive.reshape(1, -1), 1)
        cell_count = tree_sum(link.group_parts(jnp.sum(mask).reshape(1, 1)))
        mask = mask[:, None]
        recip = 1.0 / cell_count
        recip_in = 0.25 / cell_count

        slim = lax.all_gather(slim_master.astype(BF16), AXES, axis=0, tiled=True)
        gather = Gather(link, kernel_call, [broad_master.astype(BF16)], ["broad"], [False])
        gather.start()
        gather.run(range(gather.length - LATE_STEPS), [x_kinds, mask, shifts, recip])

        narrow_all = whole((rows, mid))
        kinds_all = whole((4, rows, mid))
        stat_all = whole((2, mid))
        mask_all = whole((rows, 1))
        one_all = whole((1, 1))
        shifts_all = whole((9, rows, rows))
        chunk = block((rows, mid), lambda j: (0, j))

        def stat_chunk(height):
            return block((height, mid), lambda j: (0, j))

        def affine(level):
            return block((2, mid), lambda j: (0, norm_at[level]))

        def affine_chunk(level):
            return block((2, mid), lambda j: (0, norm_at[level] + j))

        def slim_block(at):
            return block((mid, mid), lambda j: (at + j, 0))

        def slim_taps(at):
            return [
                block((mid, mid), lambda j, offset=offset: (at + 3 * j + offset, 0))
                for offset in range(3)
            ]

        def broad_block(at):
            return block((mid, mid), lambda j: (at, j))

        narrow_f32 = shape_of((rows, mid), F32)
        wide_f32 = shape_of((rows, c_out), F32)
        narrow_low = shape_of((rows, mid), BF16)
        wide_low = shape_of((rows, c_out), BF16)
        stat_narrow = shape_of((2, mid), F32)
        stat_wide = shape_of((2, c_out), F32)
        flops_conv = 2 * rows * 9 * mid * (mid + rows)
        flops_wide = 2 * rows * mid * c_out

        def part_of(which):
            return pl.BlockSpec((None, 2, mid), lambda *step: (which, 0, 0))

        stat_gathered = [part_of(which) for which in range(count)]

        z_one, stat = kernel_call(
            first_kernel,
            "first",
            (4,),
            [
                block((1, rows, c_in), lambda j: (j, 0, 0)),
                whole((c_in, mid)),
                mask_all,
            ],
            [block((1, rows, mid), lambda j: (j, 0, 0)), stat_all],
            [shape_of((4, rows, mid), F32), stat_narrow],
            2 * 4 * rows * c_in * mid,
            after=[recip],
        )(x_kinds, slim, mask)
        parts_one = link.group_parts(stat)
        act_one, z_two, stat = kernel_call(
            conv_kernel(count, 4, 2),
            "conv_two",
            (3,),
            [kinds_all]
            + [stat_all] * count
            + [affine(0), one_all, mask_all, shifts_all, *slim_taps(at_two)],
            [kinds_all, narrow_all, stat_all],
            [shape_of((4, rows, mid), BF16), narrow_f32, stat_narrow],
            flops_conv,
        )(z_one, *parts_one, norm_params, recip_in, mask, shifts, slim, slim, slim)
        parts_two = link.group_parts(stat)
        gather.run(range(gather.length - LATE_STEPS, gather.length), [])
        (broad,) = gather.full
        z_side, stat_side = kernel_call(
            side_kernel,
            "side",
            (chunks, c_in // mid),
            [
                block((1, rows, mid), lambda j, k: (0, 0, k)),
                block((mid, mid), lambda j, k: (1 + k, j)),
                whole((rows, 1)),
            ],
            [
                block((rows, mid), lambda j, k: (0, j)),
                block((2, mid), lambda j, k: (0, j)),
            ],
            [wide_f32, stat_wide],
            2 * rows * c_in * c_out,
        )(x_kinds, broad, mask)
        act_two, z_three, stat = kernel_call(
            widen_kernel(count, True),
            "widen_three",
            (chunks,),
            [narrow_all]
            + [stat_all] * count
            + [affine(1), one_all, mask_all, broad_block(0), stat_chunk(2)],
            [narrow_all, chunk, stat_chunk(4)],
            [narrow_low, wide_f32, shape_of((4, c_out), F32)],
            flops_wide,
        )(z_two, *parts_two, norm_params, recip, mask, broad, stat_side)
        parts_pair = link.group_parts(stat)
        hidden, hidden_low, z_four, stat = kernel_call(
            mix_kernel(count),
            "mix",
            (chunks,),
            [chunk, chunk]
            + [stat_chunk(4)] * count
            + [affine_chunk(2), affine_chunk(3), one_all, mask_all, slim_block(at_four)],
            [chunk, chunk, narrow_all, stat_all],
            [wide_f32, wide_low, narrow_f32, stat_narrow],
            flops_wide,
        )(z_three, z_side, *parts_pair, norm_params, norm_params, recip, mask, slim)
        parts_four = link.group_parts(stat)
        one_kind = whole((1, rows, mid))
        act_four, z_five, stat = kernel_call(
            conv_kernel(count, 1, 1),
            "conv_five",
            (3,),
            [one_kind]
            + [stat_all] * count
            + [affine(4), one_all, mask_all, shifts_all, *slim_taps(at_five)],
            [one_kind, narrow_all, stat_all],
            [shape_of((1, rows, mid), BF16), narrow_f32, stat_narrow],
            flops_conv,
        )(z_four[None], *parts_four, norm_params, recip, mask, shifts, slim, slim, slim)
        parts_five = link.group_parts(stat)
        act_five, z_six, stat = kernel_call(
            widen_kernel(count, False),
            "widen_six",
            (chunks,),
            [narrow_all]
            + [stat_all] * count
            + [affine(5), one_all, mask_all, broad_block(at_six)],
            [narrow_all, chunk, stat_chunk(2)],
            [narrow_low, wide_f32, stat_wide],
            flops_wide,
        )(z_five, *parts_five, norm_params, recip, mask, broad)
        parts_six = link.group_parts(stat)
        grids = [
            block((side, side, images, mid), lambda j: (0, 0, 0, j)) for side in sides
        ]
        *y_grids, grad_out, stat = kernel_call(
            output_kernel(count, images, sides),
            "output",
            (chunks,),
            [chunk]
            + [stat_chunk(2)] * count
            + [affine_chunk(6), one_all, mask_all, chunk]
            + grids,
            grids + [chunk, stat_chunk(2)],
            [shape_of((side, side, images, c_out), BF16) for side in sides]
            + [wide_f32, stat_wide],
            flops_wide // 8,
            scratch=[pltpu.VMEM((rows, mid), F32)],
        )(
            z_six,
            *parts_six,
            norm_params,
            recip,
            mask,
            hidden,
            *[by_cell(value) for value in (cot_lo, cot_mid, cot_hi)],
        )
        sums_six = link.group_parts(stat)

        dz_six, grad_five, stat = kernel_call(
            back_linear_kernel(count),
            "back_six",
            (chunks,),
            [chunk, chunk]
            + [stat_chunk(2)] * (2 * count)
            + [affine_chunk(6), one_all, mask_all, broad_block(at_six), narrow_all]
            + [stat_all] * count
            + [affine(5)],
            [chunk, narrow_all, stat_all],
            [wide_low, narrow_f32, stat_narrow],
            flops_wide,
        )(
            grad_out,
            z_six,
            *parts_six,
            *sums_six,
            norm_params,
            recip,
            mask,
            broad,
            z_five,
            *parts_five,
            norm_params,
        )
        sums_five = link.group_parts(stat)

        def weight_grad(act, dz, steps, act_at, out_shape, out_at, base, name):
            high, across = steps
            height = act.shape[0]
            specs = [
                block((height, mid), lambda i, j: (0, act_at + i)),
                block((height, mid), lambda i, j: (0, j)),
            ]
            args = [act, dz]
            if base is not None:
                specs.append(pl.BlockSpec(memory_space=pl.ANY))
                args.append(base)
            return kernel_call(
                weight_grad_kernel,
                name,
                (high, across),
                specs,
                block((mid, mid), lambda i, j: (out_at + i, j)),
                far_shape(out_shape, BF16),
                2 * height * mid * mid * high * across,
                aliases={2: 0} if base is not None else None,
            )(*args)

        def conv_grad(act, dz, stride, taps, out_shape, out_at, base, name):
            first, number, per = taps
            kinds_here = act.shape[0]
            specs = [whole((kinds_here, rows, mid)), shifts_all, narrow_all]
            args = [act, shifts, dz]
            if base is not None:
                specs.append(pl.BlockSpec(memory_space=pl.ANY))
                args.append(base)
            return kernel_call(
                conv_grad_kernel(stride, first, per),
                name,
                (number // per,),
                specs,
                block((per * mid, mid), lambda t: (out_at // per + t, 0)),
                far_shape(out_shape, BF16),
                flops_conv * number // 9,
                aliases={3: 0} if base is not None else None,
            )(*args)

        slim_part = (bounds_slim[-1] // 4, mid)
        broad_part = (bounds_broad[-1] // 4, c_out)
        per_part = slim_part[0] // mid
        term_six = weight_grad(act_five, dz_six, (1, chunks), 0, broad_part, 0, None, "grad_six")
        chain_six = Scatter(link, kernel_call, term_six, "sum_six", (1, 1), "all_wide")

        dz_five, grad_four, stat = kernel_call(
            back_conv_kernel(count, 1, 1),
            "back_five",
            (3,),
            [narrow_all, narrow_all]
            + [stat_all] * (2 * count)
            + [affine(5), one_all, mask_all, shifts_all, *slim_taps(at_five), one_kind]
            + [stat_all] * count
            + [affine(4), one_all],
            [narrow_all, one_kind, stat_all],
            [narrow_low, shape_of((1, rows, mid), F32), stat_narrow],
            flops_conv,
        )(
            grad_five,
            z_five,
            *parts_five,
            *sums_five,
            norm_params,
            recip,
            mask,
            shifts,
            slim,
            slim,
            slim,
            z_four[None],
            *parts_four,
            norm_params,
            recip,
        )
        grad_four = grad_four[0]
        sums_four = link.group_parts(stat)
        low_four = 2 * per_part - at_four
        chain_six.step()
        upper_part = (2 * slim_part[0], mid)
        term_upper = conv_grad(
            act_four, dz_five, 1, (0, 9, 3), upper_part, chunks - low_four, None, "grad_five"
        )
        dz_four, grad_mid, stat = kernel_call(
            back_mix_kernel(count),
            "back_four",
            (chunks,),
            [narrow_all, narrow_all]
            + [stat_all] * (2 * count)
            + [affine(4), one_all, mask_all, slim_block(at_four), chunk, chunk, chunk]
            + [stat_chunk(4)] * count
            + [affine_chunk(2), affine_chunk(3)],
            [narrow_all, chunk, stat_chunk(3)],
            [narrow_low, wide_f32, shape_of((3, c_out), F32)],
            flops_wide,
        )(
            grad_four,
            z_four,
            *parts_four,
            *sums_four,
            norm_params,
            recip,
            mask,
            slim,
            grad_out,
            z_three,
            z_side,
            *parts_pair,
            norm_params,
            norm_params,
        )
        sums_pair = link.group_parts(stat)
        chain_six.step()
        term_upper = weight_grad(
            hidden_low,
            dz_four,
            (chunks - low_four, 1),
            low_four,
            upper_part,
            0,
            term_upper,
            "grad_four",
        )
        slim_upper = link.scatter_upper(term_upper)
        dz_three, dz_side, grad_two, stat = kernel_call(
            back_pair_kernel(count),
            "back_three",
            (chunks,),
            [chunk, chunk, chunk]
            + [stat_chunk(4)] * count
            + [stat_chunk(3)] * count
            + [affine_chunk(2), affine_chunk(3), one_all, mask_all, broad_block(0), narrow_all]
            + [stat_all] * count
            + [affine(1)],
            [chunk, chunk, narrow_all, stat_all],
            [wide_low, wide_low, narrow_f32, stat_narrow],
            flops_wide,
        )(
            grad_mid,
            z_three,
            z_side,
            *parts_pair,
            *sums_pair,
            norm_params,
            norm_params,
            recip,
            mask,
            broad,
            z_two,
            *parts_two,
            norm_params,
        )
        sums_two = [lax.all_gather(stat, "narrow")] * count
        x_sub = x_kinds[0]
        two_parts = (2 * broad_part[0], c_out)
        term_three = weight_grad(
            act_two, dz_three, (1, chunks), 0, two_parts, 0, None, "grad_three"
        )
        term = weight_grad(
            x_sub, dz_side, (1, chunks), 0, two_parts, 1, term_three, "grad_side_low"
        )
        chain_six.step()
        chain_three = Scatter(link, kernel_call, term, "sum_three", (0,), "all_wide")
        term = weight_grad(
            x_sub, dz_side, (1, chunks), 1, broad_part, 0, None, "grad_side_high"
        )
        chain_side = Scatter(link, kernel_call, term, "sum_side", (0, 1), "narrow")

        dz_two, grad_one, stat = kernel_call(
            back_conv_kernel(count, 4, 2),
            "back_two",
            (3,),
            [narrow_all, narrow_all]
            + [stat_all] * count
            + stat_gathered
            + [affine(1), one_all, mask_all, shifts_all, *slim_taps(at_two), kinds_all]
            + [stat_all] * count
            + [affine(0), one_all],
            [narrow_all, kinds_all, stat_all],
            [narrow_low, shape_of((4, rows, mid), F32), stat_narrow],
            flops_conv,
        )(
            grad_two,
            z_two,
            *parts_two,
            *sums_two,
            norm_params,
            recip,
            mask,
            shifts,
            slim,
            slim,
            slim,
            z_one,
            *parts_one,
            norm_params,
            recip_in,
        )
        sums_one = [lax.all_gather(stat, "narrow")] * count
        chain_six.step()
        chain_three.step()
        term = conv_grad(
            act_one, dz_two, 2, (per_part - at_two, 9 - per_part + at_two, 9 - per_part + at_two), slim_part, 0, None,
            "grad_two_high",
        )
        term = weight_grad(
            hidden_low, dz_four, (low_four, 1), 0, slim_part, per_part - low_four, term,
            "grad_four_low",
        )
        chain_two = Scatter(link, kernel_call, term, "sum_two", (1, 0), "narrow")
        slim_low = conv_grad(
            act_one, dz_two, 2, (0, per_part - at_two, at_two), slim_part, at_two, None, "grad_two_low"
        )
        chain_side.step()
        dz_one, slim_low = kernel_call(
            back_first_kernel(count),
            "back_one",
            (4,),
            [block((1, rows, mid), lambda j: (j, 0, 0))] * 2
            + [stat_all] * count
            + stat_gathered
            + [
                affine(0),
                one_all,
                mask_all,
                block((1, rows, c_in), lambda j: (j, 0, 0)),
                pl.BlockSpec(memory_space=pl.ANY),
            ],
            [block((1, rows, mid), lambda j: (j, 0, 0)), whole((c_in, mid))],
            [shape_of((4, rows, mid), BF16), far_shape(slim_part, BF16)],
            2 * 4 * rows * c_in * mid,
            scratch=[pltpu.VMEM((c_in, mid), F32)],
            aliases={2 + 2 * count + 4: 1},
        )(grad_one, z_one, *parts_one, *sums_one, norm_params, recip_in, mask, x_kinds, slim_low)
        chain_one = Scatter(link, kernel_call, slim_low, "sum_one", (0, 0), "wide")
        chain_three.step()
        chain_one.step()
        chain_two.step()

        extents = tuple(2 * side for side in sides)
        dx_grids = kernel_call(
            input_grad_kernel(images, sides),
            "input_grad",
            (c_in // mid,),
            [
                kinds_all,
                slim_block(0),
                whole((rows, c_out)),
                block((mid, c_out), lambda j: (1 + j, 0)),
            ],
            [
                block((extent, extent, images, mid), lambda j: (0, 0, 0, j))
                for extent in extents
            ],
            [shape_of((extent, extent, images, c_in), F32) for extent in extents],
            2 * 4 * rows * c_in * mid + 2 * rows * c_in * c_out,
            scratch=[pltpu.VMEM((rows, mid), F32)],
        )(dz_one, slim, dz_side, broad)

        def by_image(value):
            return jnp.transpose(value, (2, 0, 1, 3))

        y_parts = [by_image(value) for value in y_grids]
        dx_parts = [by_image(value) for value in dx_grids]

        top = link.bit(link.bits - 1)
        second = link.bit(link.bits - 2)

        def choose(bit, upper, lower):
            return jnp.where(bit == 1, upper, lower)

        place = link.index.astype(jnp.int32)
        firsts = jnp.stack([place * broad_master.shape[0], place * slim_master.shape[0]])
        scalars = pl.BlockSpec(memory_space=pltpu.SMEM)

        def tally(name):
            values, specs = [], []
            for grad, master, rowstat in (
                (broad_grad, broad_master, broad_rowstat),
                (slim_grad, slim_master, slim_rowstat),
            ):
                column = whole((grad.shape[0], 1))
                specs += [whole(grad.shape), whole(grad.shape), column]
                values += [grad, master, rowstat.reshape(-1, 1)]
            sums_dims = (2 * (len(bounds_broad) - 1) + 3, c_out)
            columns = [(value.shape[0], 1) for value in (slim_master, broad_master)]
            return kernel_call(
                tally_kernel(bounds_slim, bounds_broad),
                name,
                (1,),
                [scalars] + specs,
                [whole(dims) for dims in columns] + [whole(sums_dims)],
                [shape_of(dims, F32) for dims in columns] + [shape_of(sums_dims, F32)],
                1,
            )(firsts, *values)

        def renew(grad, master, rows_new, sums, colstat, bounds, which, name):
            matrix, column = whole(grad.shape), whole((grad.shape[0], 1))
            cols_all = whole(colstat.shape)
            return kernel_call(
                renew_kernel(bounds, which, bounds_broad),
                name,
                (1,),
                [scalars, matrix, matrix, column, whole(sums.shape), cols_all],
                [cols_all, matrix, matrix],
                [
                    shape_of(colstat.shape, F32),
                    shape_of(grad.shape, F32),
                    shape_of(grad.shape, BF16),
                ],
                1,
            )(firsts, grad, master, rows_new, sums, colstat)

        spans = [
            (mid * at, width, rows_of)
            for at, width, rows_of in zip(
                norm_at, widths, ((0, 1),) * 2 + ((0, 1), (2, 1)) + ((0, 1),) * 3
            )
        ]
        sum_sets = [sums_one, sums_two, sums_pair, sums_pair, sums_four, sums_five, sums_six]
        flat_sets = [part for parts in sum_sets for part in parts]
        norm_rows = norm_params.size // c_out
        norm_sums = kernel_call(
            pack_kernel(count, spans, mid),
            "pack",
            (1,),
            stat_gathered * 2 + [whole(part.shape) for part in flat_sets[2 * count :]],
            whole((norm_rows, c_out)),
            shape_of((norm_rows, c_out), F32),
            1000000,
        )(*flat_sets)
        norm_totals = link.total_sums(norm_sums, link.narrow_bits)

        chain_one.step()
        chain_side.step()
        chain_three.step()
        chain_two.step(after=norm_totals[:1])
        chain_one.step()
        chain_six.step()
        chain_side.step()
        chain_two.step(after=norm_totals[1:2])
        chain_three.step()
        chain_one.step()
        chain_side.step()
        chain_two.step(after=norm_totals[2:])
        broad_six = chain_six.finish()
        chain_three.step(after=[slim_upper])
        broad_three = chain_three.finish()
        slim_one = chain_one.finish()
        broad_side = chain_side.finish()
        slim_two = chain_two.finish()
        broad_grad = choose(top, choose(second, broad_six, broad_side), broad_three)
        slim_low = choose(second, slim_two, slim_one)
        slim_grad = choose(top, slim_upper.astype(F32), slim_low)

        slim_rows_new, broad_rows_new, sums = tally("tally")
        sums = link.total_sums(sums)[-1]
        broad_cols_new, broad_new, broad_copy = renew(
            broad_grad, broad_master, broad_rows_new, sums, broad_colstat, bounds_broad, 0,
            "broad_renew",
        )
        slim_cols_new, slim_new, slim_copy = renew(
            slim_grad, slim_master, slim_rows_new, sums, slim_colstat, bounds_slim, 1,
            "slim_renew",
        )
        norm_grad = norm_totals[-1].reshape(norm_params.shape)
        norm_moments_new = DECAY * norm_moments + (1.0 - DECAY) * (
            norm_grad * norm_grad + EPS_ONE
        )
        norm_update = norm_grad * lax.rsqrt(norm_moments_new)
        update_rms = jnp.sqrt(jnp.mean(norm_update * norm_update, 1))
        weight_rms = jnp.sqrt(jnp.mean(norm_params * norm_params, 1))
        step = STEP_RATE * jnp.maximum(EPS_TWO, weight_rms) / jnp.maximum(1.0, update_rms)
        norm_new = norm_params - step[:, None] * norm_update
        return (
            *y_parts,
            *dx_parts,
            slim_grad,
            broad_grad,
            slim_rows_new.reshape(-1),
            broad_rows_new.reshape(-1),
            slim_cols_new,
            broad_cols_new,
            slim_new,
            broad_new,
            slim_copy,
            broad_copy,
            norm_grad,
            norm_moments_new,
            norm_new,
        )

    return body


def solution(mesh):
    split = P(AXES)
    return jax.shard_map(
        make_body(mesh),
        mesh=mesh,
        in_specs=(split,) * 11 + (P(),) * 4,
        out_specs=(split,) * 10 + (P(),) * 2 + (split,) * 4 + (P(),) * 3,
        check_vma=False,
    )
```

```python
import jax
import jax.numpy as jnp
import numpy as np
from jax import lax
from jax.experimental import pallas as pl
from jax.experimental.pallas import tpu as pltpu
from jax.sharding import PartitionSpec as P

STEP = 10
EPS_NORM = 1e-05
EPS_ONE = 1e-30
EPS_TWO = 0.001
STEP_RATE = 0.3
DECAY = 1.0 - STEP ** (-0.8)
AXES = ("wide", "narrow")
BF16 = jnp.bfloat16
F32 = jnp.float32
LATE_STEPS = 1
VMEM_LIMIT = 48 * 1024 * 1024


def shape_of(dims, dtype):
    return jax.ShapeDtypeStruct(dims, dtype)


def far_shape(dims, dtype):
    return pltpu.HBM(dims, dtype)


def whole(dims):
    return pl.BlockSpec(dims, lambda *step: (0,) * len(dims))


def block(dims, place):
    return pl.BlockSpec(dims, place)


LENGTHS = dict(
    first=3.9,
    conv_two=10.8,
    side=7.2,
    widen_three=3.8,
    mix=5.3,
    conv_five=8.9,
    widen_six=3.9,
    output=6.8,
    back_six=5.1,
    grad_six=2.1,
    back_five=10,
    grad_five=8,
    back_four=6.5,
    grad_four=2.6,
    back_three=6,
    grad_three=3,
    grad_side_low=2.1,
    grad_side_high=2.1,
    back_two=13.7,
    grad_two_high=4.8,
    grad_four_low=0.5,
    grad_two_low=4.8,
    back_one=6.3,
    input_grad=6.7,
    sum_six_0=1,
    sum_five_0=1.8,
    sum_four_0=2.1,
    sum_three_0=4.5,
    sum_side_0=1.5,
    sum_two_0=2.2,
    sum_one_0=2,
    sum_five_1=2.2,
    sum_four_1=2.7,
    sum_three_1=3.6,
    sum_side_1=2,
    sum_two_1=2.2,
)


def length(name):
    return LENGTHS.get(name, 1)


class Kernels:
    def __init__(self):
        self.last = None

    def __call__(
        self,
        body,
        name,
        grid,
        in_specs,
        out_specs,
        out_shape,
        flops,
        scratch=(),
        aliases=None,
        after=(),
        scalars=0,
    ):
        taken = scalars + len(in_specs)

        def run(*args):
            waits = [
                value
                for value in (*after, self.last)
                if value is not None and not any(value is arg for arg in args)
            ]

            def trimmed(*refs):
                body(*refs[:taken], *refs[taken + len(waits) :])

            out = pl.pallas_call(
                trimmed,
                grid_spec=pltpu.PrefetchScalarGridSpec(
                    num_scalar_prefetch=scalars,
                    grid=grid,
                    in_specs=list(in_specs) + [pl.BlockSpec(memory_space=pl.ANY)] * len(waits),
                    out_specs=out_specs,
                    scratch_shapes=list(scratch),
                ),
                out_shape=out_shape,
                input_output_aliases=aliases or {},
                cost_estimate=pl.CostEstimate(
                    flops=int(length(name) * 1.15e8),
                    bytes_accessed=int(length(name) * 3.6e5),
                    transcendentals=0,
                ),
                compiler_params=pltpu.CompilerParams(vmem_limit_bytes=VMEM_LIMIT),
                name=name,
            )(*args, *waits)
            self.last = out[0] if isinstance(out, (list, tuple)) else out
            return out

        return run


def dot_nn(first, second):
    return jnp.dot(first, second, preferred_element_type=F32)


def dot_nt(first, second):
    return lax.dot_general(first, second, (((1,), (1,)), ((), ())), preferred_element_type=F32)


def dot_tn(first, second):
    return lax.dot_general(first, second, (((0,), (0,)), ((), ())), preferred_element_type=F32)


def sigmoid(value):
    return 1.0 / (1.0 + jnp.exp(-value))


def slope(value):
    gate = sigmoid(value)
    return gate * (1.0 + value * (1.0 - gate))


def tree_sum(values):
    values = list(values)
    while len(values) > 1:
        values = [values[i] + values[i + 1] for i in range(0, len(values), 2)]
    return values[0]


def moments(parts, recip):
    total = tree_sum([part[...] for part in parts]) * recip
    mean = total[0:1]
    return mean, lax.rsqrt(total[1:2] - mean * mean + EPS_NORM)


def column_sum(value):
    return jnp.sum(value, axis=0, keepdims=True)


def stat_rows(value, mask):
    kept = value * mask
    return jnp.concatenate([column_sum(kept), column_sum(kept * value)], 0)


def grid_rows(images, sides):
    return sum(images * side * side for side in sides)


def class_table(images, sides_out, padded):
    table = -np.ones((4, padded), np.int32)
    base_in, base_out = 0, 0
    for side in sides_out:
        extent = 2 * side
        for row in range(side):
            for col in range(side):
                for image in range(images):
                    for kind in range(4):
                        cell = (2 * row + kind // 2) * extent + 2 * col + kind % 2
                        table[kind, base_out + (row * side + col) * images + image] = (
                            base_in + cell * images + image
                        )
        base_in += images * extent * extent
        base_out += images * side * side
    return table


def shift_table(images, sides_out, padded):
    table = -np.ones((9, padded), np.int32)
    base = 0
    for side in sides_out:
        for row in range(side):
            for col in range(side):
                for which in range(9):
                    row_to, col_to = row + which // 3 - 1, col + which % 3 - 1
                    if 0 <= row_to < side and 0 <= col_to < side:
                        for image in range(images):
                            table[which, base + (row * side + col) * images + image] = (
                                base + (row_to * side + col_to) * images + image
                            )
        base += images * side * side
    return table


def one_hot(table, width):
    return (jnp.asarray(table)[..., None] == jnp.arange(width, dtype=jnp.int32)).astype(BF16)


def first_kernel(x_ref, w_ref, mask_ref, z_ref, stat_ref):
    z = dot_nn(x_ref[0], w_ref[...])
    z_ref[0] = z
    rows = stat_rows(z, mask_ref[...])

    @pl.when(pl.program_id(0) == 0)
    def _():
        stat_ref[...] = rows

    @pl.when(pl.program_id(0) > 0)
    def _():
        stat_ref[...] += rows


def side_kernel(x_ref, w_ref, mask_ref, z_ref, stat_ref):
    term = dot_nn(x_ref[0], w_ref[...])

    @pl.when(pl.program_id(1) == 0)
    def _():
        z_ref[...] = term

    @pl.when(pl.program_id(1) > 0)
    def _():
        z_ref[...] += term

    @pl.when(pl.program_id(1) == pl.num_programs(1) - 1)
    def _():
        stat_ref[...] = stat_rows(z_ref[...], mask_ref[...])


def tap_forward(tap, stride):
    if stride == 1:
        return 0, tap
    row_tap, col_tap = tap // 3, tap % 3
    kind = jnp.where(row_tap == 1, 0, 2) + jnp.where(col_tap == 1, 0, 1)
    shift = jnp.where(row_tap == 0, 0, 3) + jnp.where(col_tap == 0, 0, 1)
    return kind, shift


def tap_backward(tap, stride):
    if stride == 1:
        return 0, 8 - tap
    row_tap, col_tap = tap // 3, tap % 3
    kind = jnp.where(row_tap == 1, 0, 2) + jnp.where(col_tap == 1, 0, 1)
    shift = jnp.where(row_tap == 0, 6, 3) + jnp.where(col_tap == 0, 2, 1)
    return kind, shift


def conv_kernel(count, kinds, stride):
    def body(*refs):
        z_ref = refs[0]
        parts = refs[1 : 1 + count]
        affine_ref, recip_ref, mask_ref, shift_ref = refs[1 + count : 5 + count]
        w_refs = refs[5 + count : 8 + count]
        act_ref, out_ref, stat_ref = refs[8 + count :]
        tap = pl.program_id(0)

        @pl.when(tap == 0)
        def _():
            mean, inv = moments(parts, recip_ref[...])
            for kind in range(kinds):
                pre = affine_ref[0:1] * ((z_ref[kind] - mean) * inv) + affine_ref[1:2]
                act_ref[kind] = (pre * sigmoid(pre)).astype(BF16)

        patches = []
        for offset in range(3):
            kind, shift = tap_forward(3 * tap + offset, stride)
            patches.append(dot_nn(shift_ref[shift], act_ref[kind]).astype(BF16))
        term = None
        for patch, w_ref in zip(patches, w_refs):
            part = dot_nn(patch, w_ref[...])
            term = part if term is None else term + part

        @pl.when(tap == 0)
        def _():
            out_ref[...] = term

        @pl.when(tap > 0)
        def _():
            out_ref[...] += term

        @pl.when(tap == 2)
        def _():
            stat_ref[...] = stat_rows(out_ref[...], mask_ref[...])

    return body


def widen_kernel(count, carry):
    def body(*refs):
        z_ref = refs[0]
        parts = refs[1 : 1 + count]
        rest = refs[1 + count :]
        if carry:
            affine_ref, recip_ref, mask_ref, w_ref, side_ref, act_ref, out_ref, stat_ref = rest
        else:
            affine_ref, recip_ref, mask_ref, w_ref, act_ref, out_ref, stat_ref = rest

        @pl.when(pl.program_id(0) == 0)
        def _():
            mean, inv = moments(parts, recip_ref[...])
            pre = affine_ref[0:1] * ((z_ref[...] - mean) * inv) + affine_ref[1:2]
            act_ref[...] = (pre * sigmoid(pre)).astype(BF16)

        z = dot_nn(act_ref[...], w_ref[...])
        out_ref[...] = z
        if carry:
            stat_ref[...] = jnp.concatenate([stat_rows(z, mask_ref[...]), side_ref[...]], 0)
        else:
            stat_ref[...] = stat_rows(z, mask_ref[...])

    return body


def pair_moments(parts, recip):
    total = tree_sum([part[...] for part in parts]) * recip
    mean, mean_side = total[0:1], total[2:3]
    inv = lax.rsqrt(total[1:2] - mean * mean + EPS_NORM)
    inv_side = lax.rsqrt(total[3:4] - mean_side * mean_side + EPS_NORM)
    return mean, inv, mean_side, inv_side


def mix_kernel(count):
    def body(*refs):
        z_ref, side_ref = refs[:2]
        parts = refs[2 : 2 + count]
        (affine_ref, affine_side_ref, recip_ref, mask_ref, w_ref) = refs[2 + count : 7 + count]
        hidden_ref, low_ref, out_ref, stat_ref = refs[7 + count :]
        mean, inv, mean_side, inv_side = pair_moments(parts, recip_ref[...])
        pre = (
            affine_ref[0:1] * ((z_ref[...] - mean) * inv)
            + affine_ref[1:2]
            + affine_side_ref[0:1] * ((side_ref[...] - mean_side) * inv_side)
            + affine_side_ref[1:2]
        )
        hidden = pre * sigmoid(pre)
        hidden_ref[...] = hidden
        low = hidden.astype(BF16)
        low_ref[...] = low
        term = dot_nn(low, w_ref[...])

        @pl.when(pl.program_id(0) == 0)
        def _():
            out_ref[...] = term

        @pl.when(pl.program_id(0) > 0)
        def _():
            out_ref[...] += term

        @pl.when(pl.program_id(0) == pl.num_programs(0) - 1)
        def _():
            stat_ref[...] = stat_rows(out_ref[...], mask_ref[...])

    return body


def cell_rows(images, sides):
    base = 0
    for level, side in enumerate(sides):
        for row in range(side):
            for col in range(side):
                yield level, row, col, base + (row * side + col) * images
        base += images * side * side


def output_kernel(count, images, sides):
    def body(*refs):
        z_ref = refs[0]
        parts = refs[1 : 1 + count]
        affine_ref, recip_ref, mask_ref, hidden_ref = refs[1 + count : 5 + count]
        cot_refs = refs[5 + count : 8 + count]
        y_refs = refs[8 + count : 11 + count]
        grad_ref, stat_ref, flat_ref = refs[11 + count :]
        used = grid_rows(images, sides)
        if flat_ref.shape[0] > used:
            flat_ref[used:] = jnp.zeros((flat_ref.shape[0] - used, flat_ref.shape[1]), F32)
        for level, row, col, at in cell_rows(images, sides):
            flat_ref[at : at + images] = cot_refs[level][row, col].astype(F32)
        mean, inv = moments(parts, recip_ref[...])
        normed = (z_ref[...] - mean) * inv
        pre = affine_ref[0:1] * normed + affine_ref[1:2] + hidden_ref[...]
        gate = sigmoid(pre)
        grad = flat_ref[...] * mask_ref[...] * (gate * (1.0 + pre * (1.0 - gate)))
        grad_ref[...] = grad
        stat_ref[...] = jnp.concatenate([column_sum(grad * normed), column_sum(grad)], 0)
        flat_ref[...] = pre * gate
        for level, row, col, at in cell_rows(images, sides):
            y_refs[level][row, col] = flat_ref[at : at + images].astype(BF16)

    return body


def input_grad_kernel(images, sides):
    def body(dz_ref, w_ref, side_ref, w_side_ref, *rest):
        out_refs, flat_ref = rest[:3], rest[3]
        for kind in range(4):
            value = dot_nt(dz_ref[kind], w_ref[...])
            if kind == 0:
                value += dot_nt(side_ref[...], w_side_ref[...])
            flat_ref[...] = value
            for level, row, col, at in cell_rows(images, sides):
                out_refs[level][2 * row + kind // 2, 2 * col + kind % 2] = flat_ref[
                    at : at + images
                ]

    return body


def norm_back(grad, normed, sums, recip, mask, scale):
    return scale * (grad - mask * (sums[1:2] * recip + normed * (sums[0:1] * recip)))


def back_linear_kernel(count):
    def body(*refs):
        grad_ref, z_ref = refs[:2]
        parts = refs[2 : 2 + count]
        sums = refs[2 + count : 2 + 2 * count]
        affine_ref, recip_ref, mask_ref, w_ref, below_ref = refs[2 + 2 * count : 7 + 2 * count]
        below_parts = refs[7 + 2 * count : 7 + 3 * count]
        below_affine_ref, dz_ref, out_ref, stat_ref = refs[7 + 3 * count :]
        recip = recip_ref[...]
        mean, inv = moments(parts, recip)
        total = tree_sum([part[...] for part in sums])
        normed = (z_ref[...] - mean) * inv
        dz = norm_back(grad_ref[...], normed, total, recip, mask_ref[...], affine_ref[0:1] * inv)
        dz = dz.astype(BF16)
        dz_ref[...] = dz
        term = dot_nt(dz, w_ref[...])

        @pl.when(pl.program_id(0) == 0)
        def _():
            out_ref[...] = term

        @pl.when(pl.program_id(0) > 0)
        def _():
            out_ref[...] += term

        @pl.when(pl.program_id(0) == pl.num_programs(0) - 1)
        def _():
            finish_below(out_ref, below_ref, below_parts, below_affine_ref, recip, stat_ref)

    return body


def finish_below(out_ref, below_ref, below_parts, below_affine_ref, recip, stat_ref):
    mean, inv = moments(below_parts, recip)
    normed = (below_ref[...] - mean) * inv
    pre = below_affine_ref[0:1] * normed + below_affine_ref[1:2]
    grad = out_ref[...] * slope(pre)
    out_ref[...] = grad
    stat_ref[...] = jnp.concatenate([column_sum(grad * normed), column_sum(grad)], 0)


def back_conv_kernel(count, kinds, stride):
    def body(*refs):
        grad_ref, z_ref = refs[:2]
        parts = refs[2 : 2 + count]
        sums = refs[2 + count : 2 + 2 * count]
        affine_ref, recip_ref, mask_ref, shift_ref = refs[2 + 2 * count : 6 + 2 * count]
        w_refs = refs[6 + 2 * count : 9 + 2 * count]
        below_ref = refs[9 + 2 * count]
        below_parts = refs[10 + 2 * count : 10 + 3 * count]
        below_affine_ref, below_recip_ref, dz_ref, out_ref, stat_ref = refs[10 + 3 * count :]
        tap = pl.program_id(0)

        @pl.when(tap == 0)
        def _():
            recip = recip_ref[...]
            mean, inv = moments(parts, recip)
            total = tree_sum([part[...] for part in sums])
            normed = (z_ref[...] - mean) * inv
            dz = norm_back(
                grad_ref[...], normed, total, recip, mask_ref[...], affine_ref[0:1] * inv
            )
            dz_ref[...] = dz.astype(BF16)
            out_ref[...] = jnp.zeros_like(out_ref)

        if stride == 1:
            term = None
            for offset in range(3):
                _, shift = tap_backward(3 * tap + offset, stride)
                patch = dot_nn(shift_ref[shift], dz_ref[...]).astype(BF16)
                part = dot_nt(patch, w_refs[offset][...])
                term = part if term is None else term + part
            out_ref[0] += term
        else:
            for offset in range(3):
                kind, shift = tap_backward(3 * tap + offset, stride)
                patch = dot_nn(shift_ref[shift], dz_ref[...]).astype(BF16)
                out_ref[kind] += dot_nt(patch, w_refs[offset][...])

        @pl.when(tap == 2)
        def _():
            mean, inv = moments(below_parts, below_recip_ref[...])
            rows = None
            for which in range(kinds):
                normed = (below_ref[which] - mean) * inv
                pre = below_affine_ref[0:1] * normed + below_affine_ref[1:2]
                grad = out_ref[which] * slope(pre)
                out_ref[which] = grad
                part = jnp.concatenate([column_sum(grad * normed), column_sum(grad)], 0)
                rows = part if rows is None else rows + part
            stat_ref[...] = rows

    return body


def back_mix_kernel(count):
    def body(*refs):
        grad_ref, z_ref = refs[:2]
        parts = refs[2 : 2 + count]
        sums = refs[2 + count : 2 + 2 * count]
        affine_ref, recip_ref, mask_ref, w_ref, above_ref, mid_ref, side_ref = refs[
            2 + 2 * count : 9 + 2 * count
        ]
        pair_parts = refs[9 + 2 * count : 9 + 3 * count]
        affine_mid_ref, affine_side_ref, dz_ref, out_ref, stat_ref = refs[9 + 3 * count :]
        recip = recip_ref[...]

        @pl.when(pl.program_id(0) == 0)
        def _():
            mean, inv = moments(parts, recip)
            total = tree_sum([part[...] for part in sums])
            normed = (z_ref[...] - mean) * inv
            dz = norm_back(
                grad_ref[...], normed, total, recip, mask_ref[...], affine_ref[0:1] * inv
            )
            dz_ref[...] = dz.astype(BF16)

        mean, inv, mean_side, inv_side = pair_moments(pair_parts, recip)
        normed = (mid_ref[...] - mean) * inv
        normed_side = (side_ref[...] - mean_side) * inv_side
        pre = (
            affine_mid_ref[0:1] * normed
            + affine_mid_ref[1:2]
            + affine_side_ref[0:1] * normed_side
            + affine_side_ref[1:2]
        )
        grad = (above_ref[...] + dot_nt(dz_ref[...], w_ref[...])) * slope(pre)
        out_ref[...] = grad
        stat_ref[...] = jnp.concatenate(
            [column_sum(grad * normed), column_sum(grad), column_sum(grad * normed_side)], 0
        )

    return body


def back_pair_kernel(count):
    def body(*refs):
        grad_ref, mid_ref, side_ref = refs[:3]
        pair_parts = refs[3 : 3 + count]
        sums = refs[3 + count : 3 + 2 * count]
        affine_mid_ref, affine_side_ref, recip_ref, mask_ref, w_ref, below_ref = refs[
            3 + 2 * count : 9 + 2 * count
        ]
        below_parts = refs[9 + 2 * count : 9 + 3 * count]
        below_affine_ref, dz_ref, dz_side_ref, out_ref, stat_ref = refs[9 + 3 * count :]
        recip = recip_ref[...]
        mean, inv, mean_side, inv_side = pair_moments(pair_parts, recip)
        total = tree_sum([part[...] for part in sums])
        normed = (mid_ref[...] - mean) * inv
        normed_side = (side_ref[...] - mean_side) * inv_side
        grad = grad_ref[...]
        mask = mask_ref[...]
        dz = norm_back(grad, normed, total[0:2], recip, mask, affine_mid_ref[0:1] * inv)
        dz = dz.astype(BF16)
        dz_ref[...] = dz
        total_side = jnp.concatenate([total[2:3], total[1:2]], 0)
        dz_side_ref[...] = norm_back(
            grad, normed_side, total_side, recip, mask, affine_side_ref[0:1] * inv_side
        ).astype(BF16)
        term = dot_nt(dz, w_ref[...])

        @pl.when(pl.program_id(0) == 0)
        def _():
            out_ref[...] = term

        @pl.when(pl.program_id(0) > 0)
        def _():
            out_ref[...] += term

        @pl.when(pl.program_id(0) == pl.num_programs(0) - 1)
        def _():
            finish_below(out_ref, below_ref, below_parts, below_affine_ref, recip, stat_ref)

    return body


def back_first_kernel(count):
    def body(*refs):
        grad_ref, z_ref = refs[:2]
        parts = refs[2 : 2 + count]
        sums = refs[2 + count : 2 + 2 * count]
        affine_ref, recip_ref, mask_ref, x_ref, _, dz_ref, grad_w_ref, total_ref = refs[
            2 + 2 * count :
        ]
        recip = recip_ref[...]
        mean, inv = moments(parts, recip)
        total = tree_sum([part[...] for part in sums])
        normed = (z_ref[0] - mean) * inv
        dz = norm_back(grad_ref[0], normed, total, recip, mask_ref[...], affine_ref[0:1] * inv)
        dz = dz.astype(BF16)
        dz_ref[0] = dz
        term = dot_tn(x_ref[0], dz)

        @pl.when(pl.program_id(0) == 0)
        def _():
            total_ref[...] = term

        @pl.when(pl.program_id(0) > 0)
        def _():
            total_ref[...] += term

        @pl.when(pl.program_id(0) == pl.num_programs(0) - 1)
        def _():
            grad_w_ref[...] = total_ref[...].astype(BF16)

    return body


def weight_grad_kernel(act_ref, dz_ref, *rest):
    rest[-1][...] = dot_tn(act_ref[...], dz_ref[...]).astype(BF16)


def conv_grad_kernel(stride, first, per):
    def body(act_ref, shift_ref, dz_ref, *rest):
        out_ref = rest[-1]
        width = dz_ref.shape[1]
        for offset in range(per):
            kind, shift = tap_forward(per * pl.program_id(0) + first + offset, stride)
            patch = dot_nn(shift_ref[shift], act_ref[kind]).astype(BF16)
            out_ref[offset * width : (offset + 1) * width] = dot_tn(patch, dz_ref[...]).astype(
                BF16
            )

    return body


def pack_kernel(count, spans, piece):
    def body(*refs):
        out_ref = refs[-1]
        columns = out_ref.shape[1]
        high = out_ref.shape[0] // 2
        for which, (start, width, rows) in enumerate(spans):
            parts = refs[which * count : (which + 1) * count]
            total = tree_sum([part[...] for part in parts])
            for offset in range(0, width, piece):
                line, at = (start + offset) // columns, (start + offset) % columns
                for slot, row in enumerate(rows):
                    here = slot * high + line
                    out_ref[here : here + 1, at : at + piece] = total[
                        row : row + 1, offset : offset + piece
                    ]

    return body


def merge_kernel(split, has_kept, last):
    def add(kept_ref, came_ref):
        total = kept_ref[...].astype(F32) + came_ref[...].astype(F32)
        return total if last else total.astype(BF16)

    def body(index_ref, *refs):
        if not has_kept:
            refs[1][...] = refs[0][...]
        elif split:
            refs[4][...] = add(refs[0], refs[1])
            refs[5][...] = add(refs[2], refs[3])
        else:
            refs[2][...] = add(refs[0], refs[1])

    return body


def level_masks(first_row, rows, bounds):
    index = first_row + lax.broadcasted_iota(jnp.int32, (rows, 1), 0)
    return [
        ((index >= bounds[level]) & (index < bounds[level + 1])).astype(F32)
        for level in range(len(bounds) - 1)
    ]


LANES = 128


def tally_kernel(bounds_slim, bounds_broad):
    wide = len(bounds_broad) - 1

    def body(first_ref, *refs):
        inputs, (slim_rows_ref, broad_rows_ref, sums_ref) = refs[:6], refs[6:]
        sums_ref[...] = jnp.zeros_like(sums_ref)
        scalar = 0
        last = sums_ref.shape[0] - 1
        for which, (bounds, rows_ref) in enumerate(
            ((bounds_broad, broad_rows_ref), (bounds_slim, slim_rows_ref))
        ):
            grad_ref, master_ref, old_ref = inputs[3 * which : 3 * which + 3]
            grad = grad_ref[...]
            master = master_ref[...]
            columns = grad.shape[1]
            square = grad * grad
            raised = square + EPS_ONE
            rows_new = DECAY * old_ref[...] + (1.0 - DECAY) * jnp.mean(raised, 1, keepdims=True)
            rows_ref[...] = rows_new
            ratio = square / rows_new
            weight = jnp.sum(master * master, 1, keepdims=True)
            masks = level_masks(first_ref[which], grad.shape[0], bounds)
            for level, mask in enumerate(masks):
                col_sum, ratio_sum = column_sum(raised * mask), column_sum(ratio * mask)
                if which == 0:
                    sums_ref[level : level + 1] = col_sum
                    sums_ref[wide + level : wide + level + 1] = ratio_sum
                else:
                    here = slice(level * columns, (level + 1) * columns)
                    sums_ref[2 * wide : 2 * wide + 1, here] = col_sum
                    sums_ref[2 * wide + 1 : 2 * wide + 2, here] = ratio_sum
                for value in (rows_new, weight):
                    here = slice(scalar * LANES, (scalar + 1) * LANES)
                    sums_ref[last : last + 1, here] = jnp.zeros((1, LANES), F32) + column_sum(
                        value * mask
                    )
                    scalar += 1

    return body


def renew_kernel(bounds, which, bounds_broad):
    wide = len(bounds_broad) - 1

    def body(first_ref, grad_ref, master_ref, rows_ref, sums_ref, old_ref, cols_ref, new_ref, low_ref):
        grad = grad_ref[...]
        columns = grad.shape[1]
        last = sums_ref.shape[0] - 1
        masks = level_masks(first_ref[which], grad.shape[0], bounds)
        factor = None
        for level, mask in enumerate(masks):
            height = float(bounds[level + 1] - bounds[level])
            cells = height * columns
            if which == 0:
                col_sum = sums_ref[level : level + 1]
                ratio_sum = sums_ref[wide + level : wide + level + 1]
            else:
                here = slice(level * columns, (level + 1) * columns)
                col_sum = sums_ref[2 * wide : 2 * wide + 1, here]
                ratio_sum = sums_ref[2 * wide + 1 : 2 * wide + 2, here]
            scalar = (2 * wide if which else 0) + 2 * level
            row_mean = sums_ref[last : last + 1, scalar * LANES : scalar * LANES + 1] / height
            scalar += 1
            weight_sum = sums_ref[last : last + 1, scalar * LANES : scalar * LANES + 1]
            cols_new = DECAY * old_ref[level : level + 1] + (1.0 - DECAY) * (col_sum / height)
            cols_ref[level : level + 1] = cols_new
            relative = cols_new / row_mean
            update_sq = jnp.sum(ratio_sum / relative, axis=1, keepdims=True)
            update_rms = jnp.sqrt(update_sq / cells)
            weight_rms = jnp.sqrt(weight_sum / cells)
            step = STEP_RATE * jnp.maximum(EPS_TWO, weight_rms) / jnp.maximum(1.0, update_rms)
            part = mask * (step * lax.rsqrt(relative))
            factor = part if factor is None else factor + part
        new = master_ref[...] - grad * lax.rsqrt(rows_ref[...]) * factor
        new_ref[...] = new
        low_ref[...] = new.astype(BF16)

    return body


class Exchange:
    def __init__(self, n_wide, n_narrow):
        self.n_narrow = n_narrow
        self.total = n_wide * n_narrow
        self.bits = self.total.bit_length() - 1
        self.narrow_bits = n_narrow.bit_length() - 1
        self.index = lax.axis_index(AXES)

    def bit(self, level):
        return (self.index >> level) & 1

    def swap(self, value, level):
        pairs = [(device, device ^ (1 << level)) for device in range(self.total)]
        return lax.ppermute(value, AXES, pairs)

    def scatter_upper(self, part):
        half = lax.psum_scatter(part, AXES, scatter_dimension=0, tiled=True)
        firsts = self.total // 2
        halves = [
            lax.ppermute(half, AXES, [(2 * k + side, firsts + k) for k in range(firsts)])
            for side in range(2)
        ]
        return jnp.concatenate(halves, 0)

    def group_parts(self, value):
        return [value] + [
            lax.ppermute(value, "narrow", [(i, i ^ k) for i in range(self.n_narrow)])
            for k in range(1, self.n_narrow)
        ]

    def total_sums(self, value, first=0):
        sums = []
        for level in range(first, self.bits):
            value = value + self.swap(value, level)
            sums.append(value)
        return sums


def move_kernel(moves, outs, bases):
    def body(index_ref, *refs):
        out_refs, sems = refs[-1 - outs : -1], refs[-1]
        copies = []
        for which, (operand, unit, out, rows, to, apart) in enumerate(moves):
            start = pl.multiple_of((index_ref[0] ^ to) * rows, rows) if apart else to * rows
            copies.append(
                pltpu.make_async_copy(
                    refs[operand].at[unit], out_refs[out].at[pl.ds(start, rows)], sems.at[which]
                )
            )
        for copy in copies:
            copy.start()
        for copy in copies:
            copy.wait()

    return body


class Gather:
    def __init__(self, link, kernels, shards, names, narrow_first):
        self.link = link
        self.kernels = kernels
        self.names = names
        self.rows = [shard.shape[0] for shard in shards]
        self.columns = [shard.shape[1] for shard in shards]
        inner = list(range(1, link.narrow_bits))
        outer = list(range(link.narrow_bits, link.bits - 2))
        self.levels = [
            (inner + outer if narrow else outer + inner) + [0] for narrow in narrow_first
        ]
        self.stages = len(self.levels[0])
        low, high = link.bits - 2, link.bits - 1
        self.slots = [[] for _ in range(4)]
        for shard, name in zip(shards, names):
            own = shard
            with jax.named_scope(name + "_down"):
                beside = link.swap(own, low)
                across = link.swap(own, high)
                both = link.swap(across, low)
            for slot, (units, apart) in enumerate(
                [
                    (own, 0),
                    (beside, 1 << low),
                    (across, 1 << high),
                    (both, (1 << low) | (1 << high)),
                ]
            ):
                self.slots[slot].append(
                    dict(units=units, pieces=[units], apart=[apart], came=None)
                )
        self.full = None

    def send(self, slot, stage):
        for which, state in enumerate(self.slots[slot]):
            level = self.levels[which][stage]
            with jax.named_scope(f"{self.names[which]}_{slot}_bit{level}"):
                state["came"] = self.link.swap(state["units"], level)

    def move(self, name, moves, args, shapes, aliases, after):
        any_spec = pl.BlockSpec(memory_space=pl.ANY)
        bases = len(aliases)
        return self.kernels(
            move_kernel(moves, len(shapes), bases),
            name,
            (1,),
            [whole(arg.shape) for arg in args[: len(args) - bases]] + [any_spec] * bases,
            [any_spec] * len(shapes),
            [shape_of(dims, BF16) for dims in shapes],
            1,
            scratch=[pltpu.SemaphoreType.DMA((len(moves),))],
            aliases=aliases,
            scalars=1,
            after=after,
        )(self.link.index.astype(jnp.int32).reshape(1), *args)

    def join(self, slot, stage):
        args, moves, shapes = [], [], []
        for which, state in enumerate(self.slots[slot]):
            rows, bit = self.rows[which], 1 << self.levels[which][stage]
            have = len(state["apart"])
            for place, value in enumerate((state["units"], state["came"])):
                moves.append((len(args), slice(None), which, have * rows, place, False))
                args.append(value)
            shapes.append((2 * have * rows, self.columns[which]))
            state["pieces"].append(state["came"])
            state["apart"] += [apart ^ bit for apart in state["apart"]]
        later = {(0, 0): (1, 2), (1, 0): (3,)}.get((slot, stage), ())
        waits = [state["pieces"][0] for ahead in later for state in self.slots[ahead]]
        joined = self.move(f"join_{slot}_{stage}", moves, args, shapes, {}, waits)
        for state, units in zip(self.slots[slot], joined):
            state["units"] = units
        self.send(slot, stage + 1)

    def place(self, slot, after):
        args, moves, shapes = [], [], []
        for which, state in enumerate(self.slots[slot]):
            rows, bit = self.rows[which], 1 << self.levels[which][-1]
            apart = state["apart"]
            for value, extra in ((state["units"], 0), (state["came"], bit)):
                for unit, bits in enumerate(apart):
                    part = slice(unit * rows, (unit + 1) * rows)
                    moves.append((len(args), part, which, rows, bits ^ extra, True))
                args.append(value)
            shapes.append((rows * self.link.total, self.columns[which]))
        aliases = {}
        if self.full is not None:
            aliases = {1 + len(args) + which: which for which in range(len(shapes))}
            args = args + list(self.full)
        self.full = self.move(f"place_{slot}", moves, args, shapes, aliases, after)
        return self.full

    def start(self):
        for slot in range(4):
            self.send(slot, 0)

    @property
    def length(self):
        return self.stages + 3

    def run(self, times, after):
        for time in times:
            for slot in reversed(range(4)):
                stage = time - slot
                if 0 <= stage < self.stages - 1:
                    self.join(slot, stage)
                elif stage == self.stages - 1:
                    self.place(slot, after if slot == 0 else [])


def insert_bit(unit, place, bit):
    return ((unit >> place) << (place + 1)) | (bit << place) | (unit & ((1 << place) - 1))


class Scatter:
    def __init__(self, link, kernels, part, name, prefix=(), first="narrow"):
        self.link = link
        self.kernels = kernels
        self.name = name
        self.prefix = prefix
        self.open_bits = link.bits - len(prefix)
        units = 1 << self.open_bits
        self.kept = part.reshape(units, part.shape[0] // units, part.shape[1])
        self.left = list(range(self.open_bits))
        inner = list(range(1, link.narrow_bits))
        outer = list(range(link.narrow_bits, link.bits))
        orders = {
            "narrow": inner + outer,
            "wide": outer[:1] + inner + outer[1:],
            "all_wide": outer + inner,
            "most_wide": outer[:-1] + inner + outer[-1:],
        }
        self.levels = [0] + orders[first]
        self.at = 0
        self.came = None
        self.chosen = None
        self.after = []
        self.send_half(None)

    def place(self, level):
        return self.left.index(level)

    def unit_spec(self, source):
        dims = (1,) + self.kept.shape[1:]
        return block(dims, lambda unit, index: (source(unit, index[0]), 0, 0))

    def kept_source(self, source):
        if self.chosen is None:
            return source
        place, level = self.chosen
        return lambda unit, index: insert_bit(
            source(unit, index), place, (index >> level) & 1
        )

    def run(self, body, specs, outs, number, args, dtype):
        spec = self.unit_spec(lambda unit, index: unit)
        shape = shape_of((number,) + self.kept.shape[1:], dtype)
        out = self.kernels(
            body,
            self.name + "_" + str(self.at),
            (number,),
            specs,
            [spec] * outs,
            [shape] * outs,
            4 * number * self.kept.shape[1] * self.kept.shape[2] * 200,
            scalars=1,
            after=self.after,
        )(self.link.index.astype(jnp.int32).reshape(1), *args)
        return out

    def send_half(self, came):
        level = self.levels[self.at] if self.at < len(self.levels) else None
        total_units = 1 << len(self.left)
        if level is not None and level < self.open_bits:
            place = self.place(level)

            def keep(unit, index):
                return insert_bit(unit, place, (index >> level) & 1)

            def send(unit, index):
                return insert_bit(unit, place, 1 - ((index >> level) & 1))

            half = total_units // 2
            if came is None:
                (sent,) = self.run(
                    merge_kernel(True, False, False),
                    [self.unit_spec(send)],
                    1,
                    half,
                    [self.kept],
                    BF16,
                )
                self.chosen = (place, level)
            else:
                kept_keep = self.unit_spec(self.kept_source(keep))
                kept_send = self.unit_spec(self.kept_source(send))
                kept, sent = self.run(
                    merge_kernel(True, True, False),
                    [kept_keep, self.unit_spec(keep), kept_send, self.unit_spec(send)],
                    2,
                    half,
                    [self.kept, came, self.kept, came],
                    BF16,
                )
                self.kept, self.chosen = kept, None
            self.left.remove(level)
            with jax.named_scope(self.name + "_bit" + str(level)):
                self.came = self.link.swap(sent, level)
        else:
            same = lambda unit, index: unit
            (self.kept,) = self.run(
                merge_kernel(False, True, level is None),
                [self.unit_spec(self.kept_source(same)), self.unit_spec(same)],
                1,
                total_units,
                [self.kept, came],
                F32 if level is None else BF16,
            )
            self.chosen = None
            if level is None:
                return
            pairs = []
            for device in range(self.link.total):
                settled = all(
                    (device >> other) & 1 == self.prefix[other - self.open_bits]
                    for other in range(self.open_bits, level)
                )
                if settled and (device >> level) & 1 != self.prefix[level - self.open_bits]:
                    pairs.append((device, device ^ (1 << level)))
            with jax.named_scope(self.name + "_bit" + str(level)):
                self.came = lax.ppermute(self.kept, AXES, pairs)

    def step(self, after=()):
        if self.at < len(self.levels):
            self.at += 1
            self.after = list(after)
            self.send_half(self.came)

    def finish(self):
        while self.at < len(self.levels):
            self.step()
        return self.kept.reshape(self.kept.shape[1:])


def make_body(mesh):
    n_wide, n_narrow = mesh.shape["wide"], mesh.shape["narrow"]

    def body(
        x_lo,
        x_mid,
        x_hi,
        cot_lo,
        cot_mid,
        cot_hi,
        live_counts,
        slim_master,
        broad_master,
        slim_rowstat,
        broad_rowstat,
        slim_colstat,
        broad_colstat,
        norm_params,
        norm_moments,
    ):
        link = Exchange(n_wide, n_narrow)
        kernel_call = Kernels()
        count = n_narrow
        images = x_lo.shape[0]
        sides = tuple(value.shape[1] // 2 for value in (x_lo, x_mid, x_hi))
        c_in, mid, c_out = x_lo.shape[3], slim_master.shape[1], broad_master.shape[1]
        cells = grid_rows(images, sides)
        cells_in = 4 * cells
        rows = -(-cells // 16) * 16
        chunks = c_out // mid
        bounds_slim = (0, c_in, c_in + 9 * mid, c_in + 9 * mid + c_out, c_in + 18 * mid + c_out)
        bounds_broad = (0, mid, mid + c_in, 2 * mid + c_in)
        at_two, at_four, at_five = (bounds_slim[level] // mid for level in (1, 2, 3))
        at_six = bounds_broad[2] // mid
        widths = (mid, mid, c_out, c_out, mid, mid, c_out)
        norm_at = [sum(widths[:level]) // mid for level in range(7)]

        kinds = class_table(images, sides, rows)
        shifts = one_hot(shift_table(images, sides, rows), rows)

        def by_cell(value):
            return jnp.transpose(value, (1, 2, 0, 3))

        x_flat = jnp.concatenate(
            [by_cell(value).reshape(-1, c_in) for value in (x_lo, x_mid, x_hi)], 0
        )
        x_kinds = jnp.dot(one_hot(kinds.reshape(-1), cells_in), x_flat, preferred_element_type=F32)
        x_kinds = x_kinds.astype(BF16).reshape(4, rows, c_in)
        alive = (
            jnp.arange(images, dtype=jnp.int32)[None] < live_counts[0][:, None]
        ).astype(F32)
        slots = np.zeros((rows, len(sides) * images), np.float32)
        base = 0
        for level, side in enumerate(sides):
            for at in range(images * side * side):
                slots[base + at, level * images + at % images] = 1.0
            base += images * side * side
        mask = jnp.sum(jnp.asarray(slots) * alive.reshape(1, -1), 1)
        cell_count = tree_sum(link.group_parts(jnp.sum(mask).reshape(1, 1)))
        mask = mask[:, None]
        recip = 1.0 / cell_count
        recip_in = 0.25 / cell_count

        slim = lax.all_gather(slim_master.astype(BF16), AXES, axis=0, tiled=True)
        gather = Gather(link, kernel_call, [broad_master.astype(BF16)], ["broad"], [False])
        gather.start()
        gather.run(range(gather.length - LATE_STEPS), [x_kinds, mask, shifts, recip])

        narrow_all = whole((rows, mid))
        kinds_all = whole((4, rows, mid))
        stat_all = whole((2, mid))
        mask_all = whole((rows, 1))
        one_all = whole((1, 1))
        shifts_all = whole((9, rows, rows))
        chunk = block((rows, mid), lambda j: (0, j))

        def stat_chunk(height):
            return block((height, mid), lambda j: (0, j))

        def affine(level):
            return block((2, mid), lambda j: (0, norm_at[level]))

        def affine_chunk(level):
            return block((2, mid), lambda j: (0, norm_at[level] + j))

        def slim_block(at):
            return block((mid, mid), lambda j: (at + j, 0))

        def slim_taps(at):
            return [
                block((mid, mid), lambda j, offset=offset: (at + 3 * j + offset, 0))
                for offset in range(3)
            ]

        def broad_block(at):
            return block((mid, mid), lambda j: (at, j))

        narrow_f32 = shape_of((rows, mid), F32)
        wide_f32 = shape_of((rows, c_out), F32)
        narrow_low = shape_of((rows, mid), BF16)
        wide_low = shape_of((rows, c_out), BF16)
        stat_narrow = shape_of((2, mid), F32)
        stat_wide = shape_of((2, c_out), F32)
        flops_conv = 2 * rows * 9 * mid * (mid + rows)
        flops_wide = 2 * rows * mid * c_out

        def part_of(which):
            return pl.BlockSpec((None, 2, mid), lambda *step: (which, 0, 0))

        stat_gathered = [part_of(which) for which in range(count)]

        z_one, stat = kernel_call(
            first_kernel,
            "first",
            (4,),
            [
                block((1, rows, c_in), lambda j: (j, 0, 0)),
                whole((c_in, mid)),
                mask_all,
            ],
            [block((1, rows, mid), lambda j: (j, 0, 0)), stat_all],
            [shape_of((4, rows, mid), F32), stat_narrow],
            2 * 4 * rows * c_in * mid,
            after=[recip],
        )(x_kinds, slim, mask)
        parts_one = link.group_parts(stat)
        act_one, z_two, stat = kernel_call(
            conv_kernel(count, 4, 2),
            "conv_two",
            (3,),
            [kinds_all]
            + [stat_all] * count
            + [affine(0), one_all, mask_all, shifts_all, *slim_taps(at_two)],
            [kinds_all, narrow_all, stat_all],
            [shape_of((4, rows, mid), BF16), narrow_f32, stat_narrow],
            flops_conv,
        )(z_one, *parts_one, norm_params, recip_in, mask, shifts, slim, slim, slim)
        parts_two = link.group_parts(stat)
        gather.run(range(gather.length - LATE_STEPS, gather.length), [])
        (broad,) = gather.full
        z_side, stat_side = kernel_call(
            side_kernel,
            "side",
            (chunks, c_in // mid),
            [
                block((1, rows, mid), lambda j, k: (0, 0, k)),
                block((mid, mid), lambda j, k: (1 + k, j)),
                whole((rows, 1)),
            ],
            [
                block((rows, mid), lambda j, k: (0, j)),
                block((2, mid), lambda j, k: (0, j)),
            ],
            [wide_f32, stat_wide],
            2 * rows * c_in * c_out,
        )(x_kinds, broad, mask)
        act_two, z_three, stat = kernel_call(
            widen_kernel(count, True),
            "widen_three",
            (chunks,),
            [narrow_all]
            + [stat_all] * count
            + [affine(1), one_all, mask_all, broad_block(0), stat_chunk(2)],
            [narrow_all, chunk, stat_chunk(4)],
            [narrow_low, wide_f32, shape_of((4, c_out), F32)],
            flops_wide,
        )(z_two, *parts_two, norm_params, recip, mask, broad, stat_side)
        parts_pair = link.group_parts(stat)
        hidden, hidden_low, z_four, stat = kernel_call(
            mix_kernel(count),
            "mix",
            (chunks,),
            [chunk, chunk]
            + [stat_chunk(4)] * count
            + [affine_chunk(2), affine_chunk(3), one_all, mask_all, slim_block(at_four)],
            [chunk, chunk, narrow_all, stat_all],
            [wide_f32, wide_low, narrow_f32, stat_narrow],
            flops_wide,
        )(z_three, z_side, *parts_pair, norm_params, norm_params, recip, mask, slim)
        parts_four = link.group_parts(stat)
        one_kind = whole((1, rows, mid))
        act_four, z_five, stat = kernel_call(
            conv_kernel(count, 1, 1),
            "conv_five",
            (3,),
            [one_kind]
            + [stat_all] * count
            + [affine(4), one_all, mask_all, shifts_all, *slim_taps(at_five)],
            [one_kind, narrow_all, stat_all],
            [shape_of((1, rows, mid), BF16), narrow_f32, stat_narrow],
            flops_conv,
        )(z_four[None], *parts_four, norm_params, recip, mask, shifts, slim, slim, slim)
        parts_five = link.group_parts(stat)
        act_five, z_six, stat = kernel_call(
            widen_kernel(count, False),
            "widen_six",
            (chunks,),
            [narrow_all]
            + [stat_all] * count
            + [affine(5), one_all, mask_all, broad_block(at_six)],
            [narrow_all, chunk, stat_chunk(2)],
            [narrow_low, wide_f32, stat_wide],
            flops_wide,
        )(z_five, *parts_five, norm_params, recip, mask, broad)
        parts_six = link.group_parts(stat)
        grids = [
            block((side, side, images, mid), lambda j: (0, 0, 0, j)) for side in sides
        ]
        *y_grids, grad_out, stat = kernel_call(
            output_kernel(count, images, sides),
            "output",
            (chunks,),
            [chunk]
            + [stat_chunk(2)] * count
            + [affine_chunk(6), one_all, mask_all, chunk]
            + grids,
            grids + [chunk, stat_chunk(2)],
            [shape_of((side, side, images, c_out), BF16) for side in sides]
            + [wide_f32, stat_wide],
            flops_wide // 8,
            scratch=[pltpu.VMEM((rows, mid), F32)],
        )(
            z_six,
            *parts_six,
            norm_params,
            recip,
            mask,
            hidden,
            *[by_cell(value) for value in (cot_lo, cot_mid, cot_hi)],
        )
        sums_six = link.group_parts(stat)

        dz_six, grad_five, stat = kernel_call(
            back_linear_kernel(count),
            "back_six",
            (chunks,),
            [chunk, chunk]
            + [stat_chunk(2)] * (2 * count)
            + [affine_chunk(6), one_all, mask_all, broad_block(at_six), narrow_all]
            + [stat_all] * count
            + [affine(5)],
            [chunk, narrow_all, stat_all],
            [wide_low, narrow_f32, stat_narrow],
            flops_wide,
        )(
            grad_out,
            z_six,
            *parts_six,
            *sums_six,
            norm_params,
            recip,
            mask,
            broad,
            z_five,
            *parts_five,
            norm_params,
        )
        sums_five = link.group_parts(stat)

        def weight_grad(act, dz, steps, act_at, out_shape, out_at, base, name):
            high, across = steps
            height = act.shape[0]
            specs = [
                block((height, mid), lambda i, j: (0, act_at + i)),
                block((height, mid), lambda i, j: (0, j)),
            ]
            args = [act, dz]
            if base is not None:
                specs.append(pl.BlockSpec(memory_space=pl.ANY))
                args.append(base)
            return kernel_call(
                weight_grad_kernel,
                name,
                (high, across),
                specs,
                block((mid, mid), lambda i, j: (out_at + i, j)),
                far_shape(out_shape, BF16),
                2 * height * mid * mid * high * across,
                aliases={2: 0} if base is not None else None,
            )(*args)

        def conv_grad(act, dz, stride, taps, out_shape, out_at, base, name):
            first, number, per = taps
            kinds_here = act.shape[0]
            specs = [whole((kinds_here, rows, mid)), shifts_all, narrow_all]
            args = [act, shifts, dz]
            if base is not None:
                specs.append(pl.BlockSpec(memory_space=pl.ANY))
                args.append(base)
            return kernel_call(
                conv_grad_kernel(stride, first, per),
                name,
                (number // per,),
                specs,
                block((per * mid, mid), lambda t: (out_at // per + t, 0)),
                far_shape(out_shape, BF16),
                flops_conv * number // 9,
                aliases={3: 0} if base is not None else None,
            )(*args)

        slim_part = (bounds_slim[-1] // 4, mid)
        broad_part = (bounds_broad[-1] // 4, c_out)
        per_part = slim_part[0] // mid
        term_six = weight_grad(act_five, dz_six, (1, chunks), 0, broad_part, 0, None, "grad_six")
        chain_six = Scatter(link, kernel_call, term_six, "sum_six", (1, 1), "all_wide")

        dz_five, grad_four, stat = kernel_call(
            back_conv_kernel(count, 1, 1),
            "back_five",
            (3,),
            [narrow_all, narrow_all]
            + [stat_all] * (2 * count)
            + [affine(5), one_all, mask_all, shifts_all, *slim_taps(at_five), one_kind]
            + [stat_all] * count
            + [affine(4), one_all],
            [narrow_all, one_kind, stat_all],
            [narrow_low, shape_of((1, rows, mid), F32), stat_narrow],
            flops_conv,
        )(
            grad_five,
            z_five,
            *parts_five,
            *sums_five,
            norm_params,
            recip,
            mask,
            shifts,
            slim,
            slim,
            slim,
            z_four[None],
            *parts_four,
            norm_params,
            recip,
        )
        grad_four = grad_four[0]
        sums_four = link.group_parts(stat)
        low_four = 2 * per_part - at_four
        chain_six.step()
        upper_part = (2 * slim_part[0], mid)
        term_upper = conv_grad(
            act_four, dz_five, 1, (0, 9, 3), upper_part, chunks - low_four, None, "grad_five"
        )
        dz_four, grad_mid, stat = kernel_call(
            back_mix_kernel(count),
            "back_four",
            (chunks,),
            [narrow_all, narrow_all]
            + [stat_all] * (2 * count)
            + [affine(4), one_all, mask_all, slim_block(at_four), chunk, chunk, chunk]
            + [stat_chunk(4)] * count
            + [affine_chunk(2), affine_chunk(3)],
            [narrow_all, chunk, stat_chunk(3)],
            [narrow_low, wide_f32, shape_of((3, c_out), F32)],
            flops_wide,
        )(
            grad_four,
            z_four,
            *parts_four,
            *sums_four,
            norm_params,
            recip,
            mask,
            slim,
            grad_out,
            z_three,
            z_side,
            *parts_pair,
            norm_params,
            norm_params,
        )
        sums_pair = link.group_parts(stat)
        chain_six.step()
        term_upper = weight_grad(
            hidden_low,
            dz_four,
            (chunks - low_four, 1),
            low_four,
            upper_part,
            0,
            term_upper,
            "grad_four",
        )
        slim_upper = link.scatter_upper(term_upper)
        dz_three, dz_side, grad_two, stat = kernel_call(
            back_pair_kernel(count),
            "back_three",
            (chunks,),
            [chunk, chunk, chunk]
            + [stat_chunk(4)] * count
            + [stat_chunk(3)] * count
            + [affine_chunk(2), affine_chunk(3), one_all, mask_all, broad_block(0), narrow_all]
            + [stat_all] * count
            + [affine(1)],
            [chunk, chunk, narrow_all, stat_all],
            [wide_low, wide_low, narrow_f32, stat_narrow],
            flops_wide,
        )(
            grad_mid,
            z_three,
            z_side,
            *parts_pair,
            *sums_pair,
            norm_params,
            norm_params,
            recip,
            mask,
            broad,
            z_two,
            *parts_two,
            norm_params,
        )
        sums_two = [lax.all_gather(stat, "narrow")] * count
        x_sub = x_kinds[0]
        two_parts = (2 * broad_part[0], c_out)
        term_three = weight_grad(
            act_two, dz_three, (1, chunks), 0, two_parts, 0, None, "grad_three"
        )
        term = weight_grad(
            x_sub, dz_side, (1, chunks), 0, two_parts, 1, term_three, "grad_side_low"
        )
        chain_six.step()
        chain_three = Scatter(link, kernel_call, term, "sum_three", (0,), "most_wide")
        term = weight_grad(
            x_sub, dz_side, (1, chunks), 1, broad_part, 0, None, "grad_side_high"
        )
        chain_side = Scatter(link, kernel_call, term, "sum_side", (0, 1), "narrow")

        dz_two, grad_one, stat = kernel_call(
            back_conv_kernel(count, 4, 2),
            "back_two",
            (3,),
            [narrow_all, narrow_all]
            + [stat_all] * count
            + stat_gathered
            + [affine(1), one_all, mask_all, shifts_all, *slim_taps(at_two), kinds_all]
            + [stat_all] * count
            + [affine(0), one_all],
            [narrow_all, kinds_all, stat_all],
            [narrow_low, shape_of((4, rows, mid), F32), stat_narrow],
            flops_conv,
        )(
            grad_two,
            z_two,
            *parts_two,
            *sums_two,
            norm_params,
            recip,
            mask,
            shifts,
            slim,
            slim,
            slim,
            z_one,
            *parts_one,
            norm_params,
            recip_in,
        )
        sums_one = [lax.all_gather(stat, "narrow")] * count
        chain_six.step()
        chain_three.step()
        term = conv_grad(
            act_one, dz_two, 2, (per_part - at_two, 9 - per_part + at_two, 9 - per_part + at_two), slim_part, 0, None,
            "grad_two_high",
        )
        term = weight_grad(
            hidden_low, dz_four, (low_four, 1), 0, slim_part, per_part - low_four, term,
            "grad_four_low",
        )
        chain_two = Scatter(link, kernel_call, term, "sum_two", (1, 0), "narrow")
        slim_low = conv_grad(
            act_one, dz_two, 2, (0, per_part - at_two, at_two), slim_part, at_two, None, "grad_two_low"
        )
        chain_side.step()
        chain_two.step()
        dz_one, slim_low = kernel_call(
            back_first_kernel(count),
            "back_one",
            (4,),
            [block((1, rows, mid), lambda j: (j, 0, 0))] * 2
            + [stat_all] * count
            + stat_gathered
            + [
                affine(0),
                one_all,
                mask_all,
                block((1, rows, c_in), lambda j: (j, 0, 0)),
                pl.BlockSpec(memory_space=pl.ANY),
            ],
            [block((1, rows, mid), lambda j: (j, 0, 0)), whole((c_in, mid))],
            [shape_of((4, rows, mid), BF16), far_shape(slim_part, BF16)],
            2 * 4 * rows * c_in * mid,
            scratch=[pltpu.VMEM((c_in, mid), F32)],
            aliases={2 + 2 * count + 4: 1},
        )(grad_one, z_one, *parts_one, *sums_one, norm_params, recip_in, mask, x_kinds, slim_low)
        chain_three.step()
        chain_one = Scatter(link, kernel_call, slim_low, "sum_one", (0, 0), "wide")
        chain_one.step()

        extents = tuple(2 * side for side in sides)
        dx_grids = kernel_call(
            input_grad_kernel(images, sides),
            "input_grad",
            (c_in // mid,),
            [
                kinds_all,
                slim_block(0),
                whole((rows, c_out)),
                block((mid, c_out), lambda j: (1 + j, 0)),
            ],
            [
                block((extent, extent, images, mid), lambda j: (0, 0, 0, j))
                for extent in extents
            ],
            [shape_of((extent, extent, images, c_in), F32) for extent in extents],
            2 * 4 * rows * c_in * mid + 2 * rows * c_in * c_out,
            scratch=[pltpu.VMEM((rows, mid), F32)],
        )(dz_one, slim, dz_side, broad)

        def by_image(value):
            return jnp.transpose(value, (2, 0, 1, 3))

        y_parts = [by_image(value) for value in y_grids]
        dx_parts = [by_image(value) for value in dx_grids]

        top = link.bit(link.bits - 1)
        second = link.bit(link.bits - 2)

        def choose(bit, upper, lower):
            return jnp.where(bit == 1, upper, lower)

        place = link.index.astype(jnp.int32)
        firsts = jnp.stack([place * broad_master.shape[0], place * slim_master.shape[0]])
        scalars = pl.BlockSpec(memory_space=pltpu.SMEM)

        def tally(name):
            values, specs = [], []
            for grad, master, rowstat in (
                (broad_grad, broad_master, broad_rowstat),
                (slim_grad, slim_master, slim_rowstat),
            ):
                column = whole((grad.shape[0], 1))
                specs += [whole(grad.shape), whole(grad.shape), column]
                values += [grad, master, rowstat.reshape(-1, 1)]
            sums_dims = (2 * (len(bounds_broad) - 1) + 3, c_out)
            columns = [(value.shape[0], 1) for value in (slim_master, broad_master)]
            return kernel_call(
                tally_kernel(bounds_slim, bounds_broad),
                name,
                (1,),
                [scalars] + specs,
                [whole(dims) for dims in columns] + [whole(sums_dims)],
                [shape_of(dims, F32) for dims in columns] + [shape_of(sums_dims, F32)],
                1,
            )(firsts, *values)

        def renew(grad, master, rows_new, sums, colstat, bounds, which, name):
            matrix, column = whole(grad.shape), whole((grad.shape[0], 1))
            cols_all = whole(colstat.shape)
            return kernel_call(
                renew_kernel(bounds, which, bounds_broad),
                name,
                (1,),
                [scalars, matrix, matrix, column, whole(sums.shape), cols_all],
                [cols_all, matrix, matrix],
                [
                    shape_of(colstat.shape, F32),
                    shape_of(grad.shape, F32),
                    shape_of(grad.shape, BF16),
                ],
                1,
            )(firsts, grad, master, rows_new, sums, colstat)

        spans = [
            (mid * at, width, rows_of)
            for at, width, rows_of in zip(
                norm_at, widths, ((0, 1),) * 2 + ((0, 1), (2, 1)) + ((0, 1),) * 3
            )
        ]
        sum_sets = [sums_one, sums_two, sums_pair, sums_pair, sums_four, sums_five, sums_six]
        flat_sets = [part for parts in sum_sets for part in parts]
        norm_rows = norm_params.size // c_out
        norm_sums = kernel_call(
            pack_kernel(count, spans, mid),
            "pack",
            (1,),
            stat_gathered * 2 + [whole(part.shape) for part in flat_sets[2 * count :]],
            whole((norm_rows, c_out)),
            shape_of((norm_rows, c_out), F32),
            1000000,
        )(*flat_sets)
        norm_totals = link.total_sums(norm_sums, link.narrow_bits)

        chain_two.step()
        chain_three.step(after=norm_totals[:1])
        chain_one.step()
        chain_side.step()
        chain_one.step()
        chain_two.step(after=norm_totals[1:2])
        chain_three.step()
        chain_six.step()
        chain_side.step()
        chain_one.step()
        chain_side.step(after=norm_totals[2:])
        chain_two.step()
        broad_six = chain_six.finish()
        chain_three.step(after=[slim_upper])
        broad_three = chain_three.finish()
        slim_one = chain_one.finish()
        broad_side = chain_side.finish()
        slim_two = chain_two.finish()
        broad_grad = choose(top, choose(second, broad_six, broad_side), broad_three)
        slim_low = choose(second, slim_two, slim_one)
        slim_grad = choose(top, slim_upper.astype(F32), slim_low)

        slim_rows_new, broad_rows_new, sums = tally("tally")
        sums = link.total_sums(sums)[-1]
        broad_cols_new, broad_new, broad_copy = renew(
            broad_grad, broad_master, broad_rows_new, sums, broad_colstat, bounds_broad, 0,
            "broad_renew",
        )
        slim_cols_new, slim_new, slim_copy = renew(
            slim_grad, slim_master, slim_rows_new, sums, slim_colstat, bounds_slim, 1,
            "slim_renew",
        )
        norm_grad = norm_totals[-1].reshape(norm_params.shape)
        norm_moments_new = DECAY * norm_moments + (1.0 - DECAY) * (
            norm_grad * norm_grad + EPS_ONE
        )
        norm_update = norm_grad * lax.rsqrt(norm_moments_new)
        update_rms = jnp.sqrt(jnp.mean(norm_update * norm_update, 1))
        weight_rms = jnp.sqrt(jnp.mean(norm_params * norm_params, 1))
        step = STEP_RATE * jnp.maximum(EPS_TWO, weight_rms) / jnp.maximum(1.0, update_rms)
        norm_new = norm_params - step[:, None] * norm_update
        return (
            *y_parts,
            *dx_parts,
            slim_grad,
            broad_grad,
            slim_rows_new.reshape(-1),
            broad_rows_new.reshape(-1),
            slim_cols_new,
            broad_cols_new,
            slim_new,
            broad_new,
            slim_copy,
            broad_copy,
            norm_grad,
            norm_moments_new,
            norm_new,
        )

    return body


def solution(mesh):
    split = P(AXES)
    return jax.shard_map(
        make_body(mesh),
        mesh=mesh,
        in_specs=(split,) * 11 + (P(),) * 4,
        out_specs=(split,) * 10 + (P(),) * 2 + (split,) * 4 + (P(),) * 3,
        check_vma=False,
    )
```

```python
import jax
import jax.numpy as jnp
import numpy as np
from jax import lax
from jax.experimental import pallas as pl
from jax.experimental.pallas import tpu as pltpu
from jax.sharding import PartitionSpec as P

STEP = 10
EPS_NORM = 1e-05
EPS_ONE = 1e-30
EPS_TWO = 0.001
STEP_RATE = 0.3
DECAY = 1.0 - STEP ** (-0.8)
AXES = ("wide", "narrow")
BF16 = jnp.bfloat16
F32 = jnp.float32
LATE_STEPS = 1
VMEM_LIMIT = 48 * 1024 * 1024


def shape_of(dims, dtype):
    return jax.ShapeDtypeStruct(dims, dtype)


def far_shape(dims, dtype):
    return pltpu.HBM(dims, dtype)


def whole(dims):
    return pl.BlockSpec(dims, lambda *step: (0,) * len(dims))


def block(dims, place):
    return pl.BlockSpec(dims, place)


LENGTHS = dict(
    first=3.9,
    conv_two=10.8,
    side=7.2,
    widen_three=3.8,
    mix=5.3,
    conv_five=8.9,
    widen_six=3.9,
    output=6.8,
    back_six=5.1,
    grad_six=2.1,
    back_five=10,
    grad_five=8,
    back_four=6.5,
    grad_four=2.6,
    back_three=6,
    grad_three=3,
    grad_side_low=2.1,
    grad_side_high=2.1,
    back_two=13.7,
    grad_two_high=4.8,
    grad_four_low=0.5,
    grad_two_low=4.8,
    back_one=6.3,
    input_grad=6.7,
    sum_six_0=1,
    sum_five_0=1.8,
    sum_four_0=2.1,
    sum_three_0=4.5,
    sum_side_0=1.5,
    sum_two_0=2.2,
    sum_one_0=2,
    sum_five_1=2.2,
    sum_four_1=2.7,
    sum_three_1=3.6,
    sum_side_1=2,
    sum_two_1=2.2,
)


def length(name):
    return LENGTHS.get(name, 1)


class Kernels:
    def __init__(self):
        self.last = None

    def __call__(
        self,
        body,
        name,
        grid,
        in_specs,
        out_specs,
        out_shape,
        flops,
        scratch=(),
        aliases=None,
        after=(),
        scalars=0,
    ):
        taken = scalars + len(in_specs)

        def run(*args):
            waits = [
                value
                for value in (*after, self.last)
                if value is not None and not any(value is arg for arg in args)
            ]

            def trimmed(*refs):
                body(*refs[:taken], *refs[taken + len(waits) :])

            out = pl.pallas_call(
                trimmed,
                grid_spec=pltpu.PrefetchScalarGridSpec(
                    num_scalar_prefetch=scalars,
                    grid=grid,
                    in_specs=list(in_specs) + [pl.BlockSpec(memory_space=pl.ANY)] * len(waits),
                    out_specs=out_specs,
                    scratch_shapes=list(scratch),
                ),
                out_shape=out_shape,
                input_output_aliases=aliases or {},
                cost_estimate=pl.CostEstimate(
                    flops=int(length(name) * 1.15e8),
                    bytes_accessed=int(length(name) * 3.6e5),
                    transcendentals=0,
                ),
                compiler_params=pltpu.CompilerParams(vmem_limit_bytes=VMEM_LIMIT),
                name=name,
            )(*args, *waits)
            self.last = out[0] if isinstance(out, (list, tuple)) else out
            return out

        return run


def dot_nn(first, second):
    return jnp.dot(first, second, preferred_element_type=F32)


def dot_nt(first, second):
    return lax.dot_general(first, second, (((1,), (1,)), ((), ())), preferred_element_type=F32)


def dot_tn(first, second):
    return lax.dot_general(first, second, (((0,), (0,)), ((), ())), preferred_element_type=F32)


def sigmoid(value):
    return 1.0 / (1.0 + jnp.exp(-value))


def slope(value):
    gate = sigmoid(value)
    return gate * (1.0 + value * (1.0 - gate))


def tree_sum(values):
    values = list(values)
    while len(values) > 1:
        values = [values[i] + values[i + 1] for i in range(0, len(values), 2)]
    return values[0]


def moments(parts, recip):
    total = tree_sum([part[...] for part in parts]) * recip
    mean = total[0:1]
    return mean, lax.rsqrt(total[1:2] - mean * mean + EPS_NORM)


def column_sum(value):
    return jnp.sum(value, axis=0, keepdims=True)


def stat_rows(value, mask):
    kept = value * mask
    return jnp.concatenate([column_sum(kept), column_sum(kept * value)], 0)


def grid_rows(images, sides):
    return sum(images * side * side for side in sides)


def class_table(images, sides_out, padded):
    table = -np.ones((4, padded), np.int32)
    base_in, base_out = 0, 0
    for side in sides_out:
        extent = 2 * side
        for row in range(side):
            for col in range(side):
                for image in range(images):
                    for kind in range(4):
                        cell = (2 * row + kind // 2) * extent + 2 * col + kind % 2
                        table[kind, base_out + (row * side + col) * images + image] = (
                            base_in + cell * images + image
                        )
        base_in += images * extent * extent
        base_out += images * side * side
    return table


def shift_table(images, sides_out, padded):
    table = -np.ones((9, padded), np.int32)
    base = 0
    for side in sides_out:
        for row in range(side):
            for col in range(side):
                for which in range(9):
                    row_to, col_to = row + which // 3 - 1, col + which % 3 - 1
                    if 0 <= row_to < side and 0 <= col_to < side:
                        for image in range(images):
                            table[which, base + (row * side + col) * images + image] = (
                                base + (row_to * side + col_to) * images + image
                            )
        base += images * side * side
    return table


def one_hot(table, width):
    return (jnp.asarray(table)[..., None] == jnp.arange(width, dtype=jnp.int32)).astype(BF16)


def first_kernel(x_ref, w_ref, mask_ref, z_ref, stat_ref):
    z = dot_nn(x_ref[0], w_ref[...])
    z_ref[0] = z
    rows = stat_rows(z, mask_ref[...])

    @pl.when(pl.program_id(0) == 0)
    def _():
        stat_ref[...] = rows

    @pl.when(pl.program_id(0) > 0)
    def _():
        stat_ref[...] += rows


def side_kernel(pieces):
    def body(x_ref, *refs):
        mask_ref, z_ref, stat_ref = refs[pieces:]
        depth = refs[0].shape[0]
        z = None
        for piece in range(pieces):
            part = dot_nn(x_ref[0, :, piece * depth : (piece + 1) * depth], refs[piece][...])
            z = part if z is None else z + part
        z_ref[...] = z
        stat_ref[...] = stat_rows(z, mask_ref[...])

    return body


def tap_forward(tap, stride):
    if stride == 1:
        return 0, tap
    row_tap, col_tap = tap // 3, tap % 3
    kind = jnp.where(row_tap == 1, 0, 2) + jnp.where(col_tap == 1, 0, 1)
    shift = jnp.where(row_tap == 0, 0, 3) + jnp.where(col_tap == 0, 0, 1)
    return kind, shift


def tap_backward(tap, stride):
    if stride == 1:
        return 0, 8 - tap
    row_tap, col_tap = tap // 3, tap % 3
    kind = jnp.where(row_tap == 1, 0, 2) + jnp.where(col_tap == 1, 0, 1)
    shift = jnp.where(row_tap == 0, 6, 3) + jnp.where(col_tap == 0, 2, 1)
    return kind, shift


def conv_kernel(count, kinds, stride):
    def body(*refs):
        z_ref = refs[0]
        parts = refs[1 : 1 + count]
        affine_ref, recip_ref, mask_ref, shift_ref = refs[1 + count : 5 + count]
        w_refs = refs[5 + count : 8 + count]
        act_ref, out_ref, stat_ref = refs[8 + count :]
        tap = pl.program_id(0)

        @pl.when(tap == 0)
        def _():
            mean, inv = moments(parts, recip_ref[...])
            for kind in range(kinds):
                pre = affine_ref[0:1] * ((z_ref[kind] - mean) * inv) + affine_ref[1:2]
                act_ref[kind] = (pre * sigmoid(pre)).astype(BF16)

        patches = []
        for offset in range(3):
            kind, shift = tap_forward(3 * tap + offset, stride)
            patches.append(dot_nn(shift_ref[shift], act_ref[kind]).astype(BF16))
        term = None
        for patch, w_ref in zip(patches, w_refs):
            part = dot_nn(patch, w_ref[...])
            term = part if term is None else term + part

        @pl.when(tap == 0)
        def _():
            out_ref[...] = term

        @pl.when(tap > 0)
        def _():
            out_ref[...] += term

        @pl.when(tap == 2)
        def _():
            stat_ref[...] = stat_rows(out_ref[...], mask_ref[...])

    return body


def widen_kernel(count, carry):
    def body(*refs):
        z_ref = refs[0]
        parts = refs[1 : 1 + count]
        rest = refs[1 + count :]
        if carry:
            affine_ref, recip_ref, mask_ref, w_ref, side_ref, act_ref, out_ref, stat_ref = rest
        else:
            affine_ref, recip_ref, mask_ref, w_ref, act_ref, out_ref, stat_ref = rest

        @pl.when(pl.program_id(0) == 0)
        def _():
            mean, inv = moments(parts, recip_ref[...])
            pre = affine_ref[0:1] * ((z_ref[...] - mean) * inv) + affine_ref[1:2]
            act_ref[...] = (pre * sigmoid(pre)).astype(BF16)

        z = dot_nn(act_ref[...], w_ref[...])
        out_ref[...] = z
        if carry:
            stat_ref[...] = jnp.concatenate([stat_rows(z, mask_ref[...]), side_ref[...]], 0)
        else:
            stat_ref[...] = stat_rows(z, mask_ref[...])

    return body


def pair_moments(parts, recip):
    total = tree_sum([part[...] for part in parts]) * recip
    mean, mean_side = total[0:1], total[2:3]
    inv = lax.rsqrt(total[1:2] - mean * mean + EPS_NORM)
    inv_side = lax.rsqrt(total[3:4] - mean_side * mean_side + EPS_NORM)
    return mean, inv, mean_side, inv_side


def mix_kernel(count):
    def body(*refs):
        z_ref, side_ref = refs[:2]
        parts = refs[2 : 2 + count]
        (affine_ref, affine_side_ref, recip_ref, mask_ref, w_ref) = refs[2 + count : 7 + count]
        hidden_ref, low_ref, out_ref, stat_ref = refs[7 + count :]
        mean, inv, mean_side, inv_side = pair_moments(parts, recip_ref[...])
        pre = (
            affine_ref[0:1] * ((z_ref[...] - mean) * inv)
            + affine_ref[1:2]
            + affine_side_ref[0:1] * ((side_ref[...] - mean_side) * inv_side)
            + affine_side_ref[1:2]
        )
        hidden = pre * sigmoid(pre)
        hidden_ref[...] = hidden
        low = hidden.astype(BF16)
        low_ref[...] = low
        term = dot_nn(low, w_ref[...])

        @pl.when(pl.program_id(0) == 0)
        def _():
            out_ref[...] = term

        @pl.when(pl.program_id(0) > 0)
        def _():
            out_ref[...] += term

        @pl.when(pl.program_id(0) == pl.num_programs(0) - 1)
        def _():
            stat_ref[...] = stat_rows(out_ref[...], mask_ref[...])

    return body


def cell_rows(images, sides):
    base = 0
    for level, side in enumerate(sides):
        for row in range(side):
            for col in range(side):
                yield level, row, col, base + (row * side + col) * images
        base += images * side * side


def output_kernel(count, images, sides):
    def body(*refs):
        z_ref = refs[0]
        parts = refs[1 : 1 + count]
        affine_ref, recip_ref, mask_ref, hidden_ref = refs[1 + count : 5 + count]
        cot_refs = refs[5 + count : 8 + count]
        y_refs = refs[8 + count : 11 + count]
        grad_ref, stat_ref, flat_ref = refs[11 + count :]
        used = grid_rows(images, sides)
        if flat_ref.shape[0] > used:
            flat_ref[used:] = jnp.zeros((flat_ref.shape[0] - used, flat_ref.shape[1]), F32)
        for level, row, col, at in cell_rows(images, sides):
            flat_ref[at : at + images] = cot_refs[level][row, col].astype(F32)
        mean, inv = moments(parts, recip_ref[...])
        normed = (z_ref[...] - mean) * inv
        pre = affine_ref[0:1] * normed + affine_ref[1:2] + hidden_ref[...]
        gate = sigmoid(pre)
        grad = flat_ref[...] * mask_ref[...] * (gate * (1.0 + pre * (1.0 - gate)))
        grad_ref[...] = grad
        stat_ref[...] = jnp.concatenate([column_sum(grad * normed), column_sum(grad)], 0)
        flat_ref[...] = pre * gate
        for level, row, col, at in cell_rows(images, sides):
            y_refs[level][row, col] = flat_ref[at : at + images].astype(BF16)

    return body


def input_grad_kernel(images, sides):
    def body(dz_ref, w_ref, side_ref, w_side_ref, *rest):
        out_refs, flat_ref = rest[:3], rest[3]
        for kind in range(4):
            value = dot_nt(dz_ref[kind], w_ref[...])
            if kind == 0:
                value += dot_nt(side_ref[...], w_side_ref[...])
            flat_ref[...] = value
            for level, row, col, at in cell_rows(images, sides):
                out_refs[level][2 * row + kind // 2, 2 * col + kind % 2] = flat_ref[
                    at : at + images
                ]

    return body


def norm_back(grad, normed, sums, recip, mask, scale):
    return scale * (grad - mask * (sums[1:2] * recip + normed * (sums[0:1] * recip)))


def back_linear_kernel(count):
    def body(*refs):
        grad_ref, z_ref = refs[:2]
        parts = refs[2 : 2 + count]
        sums = refs[2 + count : 2 + 2 * count]
        affine_ref, recip_ref, mask_ref, w_ref, below_ref = refs[2 + 2 * count : 7 + 2 * count]
        below_parts = refs[7 + 2 * count : 7 + 3 * count]
        below_affine_ref, dz_ref, out_ref, stat_ref = refs[7 + 3 * count :]
        recip = recip_ref[...]
        mean, inv = moments(parts, recip)
        total = tree_sum([part[...] for part in sums])
        normed = (z_ref[...] - mean) * inv
        dz = norm_back(grad_ref[...], normed, total, recip, mask_ref[...], affine_ref[0:1] * inv)
        dz = dz.astype(BF16)
        dz_ref[...] = dz
        term = dot_nt(dz, w_ref[...])

        @pl.when(pl.program_id(0) == 0)
        def _():
            out_ref[...] = term

        @pl.when(pl.program_id(0) > 0)
        def _():
            out_ref[...] += term

        @pl.when(pl.program_id(0) == pl.num_programs(0) - 1)
        def _():
            finish_below(out_ref, below_ref, below_parts, below_affine_ref, recip, stat_ref)

    return body


def finish_below(out_ref, below_ref, below_parts, below_affine_ref, recip, stat_ref):
    mean, inv = moments(below_parts, recip)
    normed = (below_ref[...] - mean) * inv
    pre = below_affine_ref[0:1] * normed + below_affine_ref[1:2]
    grad = out_ref[...] * slope(pre)
    out_ref[...] = grad
    stat_ref[...] = jnp.concatenate([column_sum(grad * normed), column_sum(grad)], 0)


def back_conv_kernel(count, kinds, stride):
    def body(*refs):
        grad_ref, z_ref = refs[:2]
        parts = refs[2 : 2 + count]
        sums = refs[2 + count : 2 + 2 * count]
        affine_ref, recip_ref, mask_ref, shift_ref = refs[2 + 2 * count : 6 + 2 * count]
        w_refs = refs[6 + 2 * count : 9 + 2 * count]
        below_ref = refs[9 + 2 * count]
        below_parts = refs[10 + 2 * count : 10 + 3 * count]
        below_affine_ref, below_recip_ref, dz_ref, out_ref, stat_ref = refs[10 + 3 * count :]
        tap = pl.program_id(0)

        @pl.when(tap == 0)
        def _():
            recip = recip_ref[...]
            mean, inv = moments(parts, recip)
            total = tree_sum([part[...] for part in sums])
            normed = (z_ref[...] - mean) * inv
            dz = norm_back(
                grad_ref[...], normed, total, recip, mask_ref[...], affine_ref[0:1] * inv
            )
            dz_ref[...] = dz.astype(BF16)
            out_ref[...] = jnp.zeros_like(out_ref)

        if stride == 1:
            term = None
            for offset in range(3):
                _, shift = tap_backward(3 * tap + offset, stride)
                patch = dot_nn(shift_ref[shift], dz_ref[...]).astype(BF16)
                part = dot_nt(patch, w_refs[offset][...])
                term = part if term is None else term + part
            out_ref[0] += term
        else:
            for offset in range(3):
                kind, shift = tap_backward(3 * tap + offset, stride)
                patch = dot_nn(shift_ref[shift], dz_ref[...]).astype(BF16)
                out_ref[kind] += dot_nt(patch, w_refs[offset][...])

        @pl.when(tap == 2)
        def _():
            mean, inv = moments(below_parts, below_recip_ref[...])
            rows = None
            for which in range(kinds):
                normed = (below_ref[which] - mean) * inv
                pre = below_affine_ref[0:1] * normed + below_affine_ref[1:2]
                grad = out_ref[which] * slope(pre)
                out_ref[which] = grad
                part = jnp.concatenate([column_sum(grad * normed), column_sum(grad)], 0)
                rows = part if rows is None else rows + part
            stat_ref[...] = rows

    return body


def back_mix_kernel(count):
    def body(*refs):
        grad_ref, z_ref = refs[:2]
        parts = refs[2 : 2 + count]
        sums = refs[2 + count : 2 + 2 * count]
        affine_ref, recip_ref, mask_ref, w_ref, above_ref, mid_ref, side_ref = refs[
            2 + 2 * count : 9 + 2 * count
        ]
        pair_parts = refs[9 + 2 * count : 9 + 3 * count]
        affine_mid_ref, affine_side_ref, dz_ref, out_ref, stat_ref = refs[9 + 3 * count :]
        recip = recip_ref[...]

        @pl.when(pl.program_id(0) == 0)
        def _():
            mean, inv = moments(parts, recip)
            total = tree_sum([part[...] for part in sums])
            normed = (z_ref[...] - mean) * inv
            dz = norm_back(
                grad_ref[...], normed, total, recip, mask_ref[...], affine_ref[0:1] * inv
            )
            dz_ref[...] = dz.astype(BF16)

        mean, inv, mean_side, inv_side = pair_moments(pair_parts, recip)
        normed = (mid_ref[...] - mean) * inv
        normed_side = (side_ref[...] - mean_side) * inv_side
        pre = (
            affine_mid_ref[0:1] * normed
            + affine_mid_ref[1:2]
            + affine_side_ref[0:1] * normed_side
            + affine_side_ref[1:2]
        )
        grad = (above_ref[...] + dot_nt(dz_ref[...], w_ref[...])) * slope(pre)
        out_ref[...] = grad
        stat_ref[...] = jnp.concatenate(
            [column_sum(grad * normed), column_sum(grad), column_sum(grad * normed_side)], 0
        )

    return body


def back_pair_kernel(count):
    def body(*refs):
        grad_ref, mid_ref, side_ref = refs[:3]
        pair_parts = refs[3 : 3 + count]
        sums = refs[3 + count : 3 + 2 * count]
        affine_mid_ref, affine_side_ref, recip_ref, mask_ref, w_ref, below_ref = refs[
            3 + 2 * count : 9 + 2 * count
        ]
        below_parts = refs[9 + 2 * count : 9 + 3 * count]
        below_affine_ref, dz_ref, dz_side_ref, out_ref, stat_ref = refs[9 + 3 * count :]
        recip = recip_ref[...]
        mean, inv, mean_side, inv_side = pair_moments(pair_parts, recip)
        total = tree_sum([part[...] for part in sums])
        normed = (mid_ref[...] - mean) * inv
        normed_side = (side_ref[...] - mean_side) * inv_side
        grad = grad_ref[...]
        mask = mask_ref[...]
        dz = norm_back(grad, normed, total[0:2], recip, mask, affine_mid_ref[0:1] * inv)
        dz = dz.astype(BF16)
        dz_ref[...] = dz
        total_side = jnp.concatenate([total[2:3], total[1:2]], 0)
        dz_side_ref[...] = norm_back(
            grad, normed_side, total_side, recip, mask, affine_side_ref[0:1] * inv_side
        ).astype(BF16)
        term = dot_nt(dz, w_ref[...])

        @pl.when(pl.program_id(0) == 0)
        def _():
            out_ref[...] = term

        @pl.when(pl.program_id(0) > 0)
        def _():
            out_ref[...] += term

        @pl.when(pl.program_id(0) == pl.num_programs(0) - 1)
        def _():
            finish_below(out_ref, below_ref, below_parts, below_affine_ref, recip, stat_ref)

    return body


def back_first_kernel(count):
    def body(*refs):
        grad_ref, z_ref = refs[:2]
        parts = refs[2 : 2 + count]
        sums = refs[2 + count : 2 + 2 * count]
        affine_ref, recip_ref, mask_ref, x_ref, _, dz_ref, grad_w_ref, total_ref = refs[
            2 + 2 * count :
        ]
        recip = recip_ref[...]
        mean, inv = moments(parts, recip)
        total = tree_sum([part[...] for part in sums])
        normed = (z_ref[0] - mean) * inv
        dz = norm_back(grad_ref[0], normed, total, recip, mask_ref[...], affine_ref[0:1] * inv)
        dz = dz.astype(BF16)
        dz_ref[0] = dz
        term = dot_tn(x_ref[0], dz)

        @pl.when(pl.program_id(0) == 0)
        def _():
            total_ref[...] = term

        @pl.when(pl.program_id(0) > 0)
        def _():
            total_ref[...] += term

        @pl.when(pl.program_id(0) == pl.num_programs(0) - 1)
        def _():
            grad_w_ref[...] = total_ref[...].astype(BF16)

    return body


def weight_grad_kernel(act_ref, dz_ref, *rest):
    rest[-1][...] = dot_tn(act_ref[...], dz_ref[...]).astype(BF16)


def conv_grad_kernel(stride, first, per):
    def body(act_ref, shift_ref, dz_ref, *rest):
        out_ref = rest[-1]
        width = dz_ref.shape[1]
        for offset in range(per):
            kind, shift = tap_forward(per * pl.program_id(0) + first + offset, stride)
            patch = dot_nn(shift_ref[shift], act_ref[kind]).astype(BF16)
            out_ref[offset * width : (offset + 1) * width] = dot_tn(patch, dz_ref[...]).astype(
                BF16
            )

    return body


def pack_kernel(count, spans, piece):
    def body(*refs):
        out_ref = refs[-1]
        columns = out_ref.shape[1]
        high = out_ref.shape[0] // 2
        for which, (start, width, rows) in enumerate(spans):
            parts = refs[which * count : (which + 1) * count]
            total = tree_sum([part[...] for part in parts])
            for offset in range(0, width, piece):
                line, at = (start + offset) // columns, (start + offset) % columns
                for slot, row in enumerate(rows):
                    here = slot * high + line
                    out_ref[here : here + 1, at : at + piece] = total[
                        row : row + 1, offset : offset + piece
                    ]

    return body


def merge_kernel(split, has_kept, last):
    def add(kept_ref, came_ref):
        total = kept_ref[...].astype(F32) + came_ref[...].astype(F32)
        return total if last else total.astype(BF16)

    def body(index_ref, *refs):
        if not has_kept:
            refs[1][...] = refs[0][...]
        elif split:
            refs[4][...] = add(refs[0], refs[1])
            refs[5][...] = add(refs[2], refs[3])
        else:
            refs[2][...] = add(refs[0], refs[1])

    return body


def level_masks(first_row, rows, bounds):
    index = first_row + lax.broadcasted_iota(jnp.int32, (rows, 1), 0)
    return [
        ((index >= bounds[level]) & (index < bounds[level + 1])).astype(F32)
        for level in range(len(bounds) - 1)
    ]


LANES = 128


def tally_kernel(bounds_slim, bounds_broad):
    wide = len(bounds_broad) - 1

    def body(first_ref, *refs):
        inputs, (slim_rows_ref, broad_rows_ref, sums_ref) = refs[:6], refs[6:]
        sums_ref[...] = jnp.zeros_like(sums_ref)
        scalar = 0
        last = sums_ref.shape[0] - 1
        for which, (bounds, rows_ref) in enumerate(
            ((bounds_broad, broad_rows_ref), (bounds_slim, slim_rows_ref))
        ):
            grad_ref, master_ref, old_ref = inputs[3 * which : 3 * which + 3]
            grad = grad_ref[...]
            master = master_ref[...]
            columns = grad.shape[1]
            square = grad * grad
            raised = square + EPS_ONE
            rows_new = DECAY * old_ref[...] + (1.0 - DECAY) * jnp.mean(raised, 1, keepdims=True)
            rows_ref[...] = rows_new
            ratio = square / rows_new
            weight = jnp.sum(master * master, 1, keepdims=True)
            masks = level_masks(first_ref[which], grad.shape[0], bounds)
            for level, mask in enumerate(masks):
                col_sum, ratio_sum = column_sum(raised * mask), column_sum(ratio * mask)
                if which == 0:
                    sums_ref[level : level + 1] = col_sum
                    sums_ref[wide + level : wide + level + 1] = ratio_sum
                else:
                    here = slice(level * columns, (level + 1) * columns)
                    sums_ref[2 * wide : 2 * wide + 1, here] = col_sum
                    sums_ref[2 * wide + 1 : 2 * wide + 2, here] = ratio_sum
                for value in (rows_new, weight):
                    here = slice(scalar * LANES, (scalar + 1) * LANES)
                    sums_ref[last : last + 1, here] = jnp.zeros((1, LANES), F32) + column_sum(
                        value * mask
                    )
                    scalar += 1

    return body


def renew_kernel(bounds, which, bounds_broad):
    wide = len(bounds_broad) - 1

    def body(first_ref, grad_ref, master_ref, rows_ref, sums_ref, old_ref, cols_ref, new_ref, low_ref):
        grad = grad_ref[...]
        columns = grad.shape[1]
        last = sums_ref.shape[0] - 1
        masks = level_masks(first_ref[which], grad.shape[0], bounds)
        factor = None
        for level, mask in enumerate(masks):
            height = float(bounds[level + 1] - bounds[level])
            cells = height * columns
            if which == 0:
                col_sum = sums_ref[level : level + 1]
                ratio_sum = sums_ref[wide + level : wide + level + 1]
            else:
                here = slice(level * columns, (level + 1) * columns)
                col_sum = sums_ref[2 * wide : 2 * wide + 1, here]
                ratio_sum = sums_ref[2 * wide + 1 : 2 * wide + 2, here]
            scalar = (2 * wide if which else 0) + 2 * level
            row_mean = sums_ref[last : last + 1, scalar * LANES : scalar * LANES + 1] / height
            scalar += 1
            weight_sum = sums_ref[last : last + 1, scalar * LANES : scalar * LANES + 1]
            cols_new = DECAY * old_ref[level : level + 1] + (1.0 - DECAY) * (col_sum / height)
            cols_ref[level : level + 1] = cols_new
            relative = cols_new / row_mean
            update_sq = jnp.sum(ratio_sum / relative, axis=1, keepdims=True)
            update_rms = jnp.sqrt(update_sq / cells)
            weight_rms = jnp.sqrt(weight_sum / cells)
            step = STEP_RATE * jnp.maximum(EPS_TWO, weight_rms) / jnp.maximum(1.0, update_rms)
            part = mask * (step * lax.rsqrt(relative))
            factor = part if factor is None else factor + part
        new = master_ref[...] - grad * lax.rsqrt(rows_ref[...]) * factor
        new_ref[...] = new
        low_ref[...] = new.astype(BF16)

    return body


class Exchange:
    def __init__(self, n_wide, n_narrow):
        self.n_narrow = n_narrow
        self.total = n_wide * n_narrow
        self.bits = self.total.bit_length() - 1
        self.narrow_bits = n_narrow.bit_length() - 1
        self.index = lax.axis_index(AXES)

    def bit(self, level):
        return (self.index >> level) & 1

    def swap(self, value, level):
        pairs = [(device, device ^ (1 << level)) for device in range(self.total)]
        return lax.ppermute(value, AXES, pairs)

    def scatter_upper(self, part):
        half = lax.psum_scatter(part, AXES, scatter_dimension=0, tiled=True)
        firsts = self.total // 2
        halves = [
            lax.ppermute(half, AXES, [(2 * k + side, firsts + k) for k in range(firsts)])
            for side in range(2)
        ]
        return jnp.concatenate(halves, 0)

    def group_parts(self, value):
        return [value] + [
            lax.ppermute(value, "narrow", [(i, i ^ k) for i in range(self.n_narrow)])
            for k in range(1, self.n_narrow)
        ]

    def total_sums(self, value, first=0):
        sums = []
        for level in range(first, self.bits):
            value = value + self.swap(value, level)
            sums.append(value)
        return sums


def move_kernel(moves, outs, bases):
    def body(index_ref, *refs):
        out_refs, sems = refs[-1 - outs : -1], refs[-1]
        copies = []
        for which, (operand, unit, out, rows, to, apart) in enumerate(moves):
            start = pl.multiple_of((index_ref[0] ^ to) * rows, rows) if apart else to * rows
            copies.append(
                pltpu.make_async_copy(
                    refs[operand].at[unit], out_refs[out].at[pl.ds(start, rows)], sems.at[which]
                )
            )
        for copy in copies:
            copy.start()
        for copy in copies:
            copy.wait()

    return body


class Gather:
    def __init__(self, link, kernels, shards, names, narrow_first):
        self.link = link
        self.kernels = kernels
        self.names = names
        self.rows = [shard.shape[0] for shard in shards]
        self.columns = [shard.shape[1] for shard in shards]
        inner = list(range(1, link.narrow_bits))
        outer = list(range(link.narrow_bits, link.bits - 2))
        self.levels = [
            (inner + outer if narrow else outer + inner) + [0] for narrow in narrow_first
        ]
        self.stages = len(self.levels[0])
        low, high = link.bits - 2, link.bits - 1
        self.slots = [[] for _ in range(4)]
        for shard, name in zip(shards, names):
            own = shard
            with jax.named_scope(name + "_down"):
                beside = link.swap(own, low)
                across = link.swap(own, high)
                both = link.swap(across, low)
            for slot, (units, apart) in enumerate(
                [
                    (own, 0),
                    (beside, 1 << low),
                    (across, 1 << high),
                    (both, (1 << low) | (1 << high)),
                ]
            ):
                self.slots[slot].append(
                    dict(units=units, pieces=[units], apart=[apart], came=None)
                )
        self.full = None

    def send(self, slot, stage):
        for which, state in enumerate(self.slots[slot]):
            level = self.levels[which][stage]
            with jax.named_scope(f"{self.names[which]}_{slot}_bit{level}"):
                state["came"] = self.link.swap(state["units"], level)

    def move(self, name, moves, args, shapes, aliases, after):
        any_spec = pl.BlockSpec(memory_space=pl.ANY)
        bases = len(aliases)
        return self.kernels(
            move_kernel(moves, len(shapes), bases),
            name,
            (1,),
            [whole(arg.shape) for arg in args[: len(args) - bases]] + [any_spec] * bases,
            [any_spec] * len(shapes),
            [shape_of(dims, BF16) for dims in shapes],
            1,
            scratch=[pltpu.SemaphoreType.DMA((len(moves),))],
            aliases=aliases,
            scalars=1,
            after=after,
        )(self.link.index.astype(jnp.int32).reshape(1), *args)

    def join(self, slot, stage):
        args, moves, shapes = [], [], []
        for which, state in enumerate(self.slots[slot]):
            rows, bit = self.rows[which], 1 << self.levels[which][stage]
            have = len(state["apart"])
            for place, value in enumerate((state["units"], state["came"])):
                moves.append((len(args), slice(None), which, have * rows, place, False))
                args.append(value)
            shapes.append((2 * have * rows, self.columns[which]))
            state["pieces"].append(state["came"])
            state["apart"] += [apart ^ bit for apart in state["apart"]]
        later = {(0, 0): (1, 2), (1, 0): (3,)}.get((slot, stage), ())
        waits = [state["pieces"][0] for ahead in later for state in self.slots[ahead]]
        joined = self.move(f"join_{slot}_{stage}", moves, args, shapes, {}, waits)
        for state, units in zip(self.slots[slot], joined):
            state["units"] = units
        self.send(slot, stage + 1)

    def place(self, slot, after):
        args, moves, shapes = [], [], []
        for which, state in enumerate(self.slots[slot]):
            rows, bit = self.rows[which], 1 << self.levels[which][-1]
            apart = state["apart"]
            for value, extra in ((state["units"], 0), (state["came"], bit)):
                for unit, bits in enumerate(apart):
                    part = slice(unit * rows, (unit + 1) * rows)
                    moves.append((len(args), part, which, rows, bits ^ extra, True))
                args.append(value)
            shapes.append((rows * self.link.total, self.columns[which]))
        aliases = {}
        if self.full is not None:
            aliases = {1 + len(args) + which: which for which in range(len(shapes))}
            args = args + list(self.full)
        self.full = self.move(f"place_{slot}", moves, args, shapes, aliases, after)
        return self.full

    def start(self):
        for slot in range(4):
            self.send(slot, 0)

    @property
    def length(self):
        return self.stages + 3

    def run(self, times, after):
        for time in times:
            for slot in reversed(range(4)):
                stage = time - slot
                if 0 <= stage < self.stages - 1:
                    self.join(slot, stage)
                elif stage == self.stages - 1:
                    self.place(slot, after if slot == 0 else [])


def insert_bit(unit, place, bit):
    return ((unit >> place) << (place + 1)) | (bit << place) | (unit & ((1 << place) - 1))


class Scatter:
    def __init__(self, link, kernels, part, name, prefix=(), first="narrow"):
        self.link = link
        self.kernels = kernels
        self.name = name
        self.prefix = prefix
        self.open_bits = link.bits - len(prefix)
        units = 1 << self.open_bits
        self.kept = part.reshape(units, part.shape[0] // units, part.shape[1])
        self.left = list(range(self.open_bits))
        inner = list(range(1, link.narrow_bits))
        outer = list(range(link.narrow_bits, link.bits))
        orders = {
            "narrow": inner + outer,
            "wide": outer[:1] + inner + outer[1:],
            "all_wide": outer + inner,
            "most_wide": outer[:-1] + inner + outer[-1:],
        }
        self.levels = [0] + orders[first]
        self.at = 0
        self.came = None
        self.chosen = None
        self.after = []
        self.send_half(None)

    def place(self, level):
        return self.left.index(level)

    def unit_spec(self, source):
        dims = (1,) + self.kept.shape[1:]
        return block(dims, lambda unit, index: (source(unit, index[0]), 0, 0))

    def kept_source(self, source):
        if self.chosen is None:
            return source
        place, level = self.chosen
        return lambda unit, index: insert_bit(
            source(unit, index), place, (index >> level) & 1
        )

    def run(self, body, specs, outs, number, args, dtype):
        spec = self.unit_spec(lambda unit, index: unit)
        shape = shape_of((number,) + self.kept.shape[1:], dtype)
        out = self.kernels(
            body,
            self.name + "_" + str(self.at),
            (number,),
            specs,
            [spec] * outs,
            [shape] * outs,
            4 * number * self.kept.shape[1] * self.kept.shape[2] * 200,
            scalars=1,
            after=self.after,
        )(self.link.index.astype(jnp.int32).reshape(1), *args)
        return out

    def send_half(self, came):
        level = self.levels[self.at] if self.at < len(self.levels) else None
        total_units = 1 << len(self.left)
        if level is not None and level < self.open_bits:
            place = self.place(level)

            def keep(unit, index):
                return insert_bit(unit, place, (index >> level) & 1)

            def send(unit, index):
                return insert_bit(unit, place, 1 - ((index >> level) & 1))

            half = total_units // 2
            if came is None:
                (sent,) = self.run(
                    merge_kernel(True, False, False),
                    [self.unit_spec(send)],
                    1,
                    half,
                    [self.kept],
                    BF16,
                )
                self.chosen = (place, level)
            else:
                kept_keep = self.unit_spec(self.kept_source(keep))
                kept_send = self.unit_spec(self.kept_source(send))
                kept, sent = self.run(
                    merge_kernel(True, True, False),
                    [kept_keep, self.unit_spec(keep), kept_send, self.unit_spec(send)],
                    2,
                    half,
                    [self.kept, came, self.kept, came],
                    BF16,
                )
                self.kept, self.chosen = kept, None
            self.left.remove(level)
            with jax.named_scope(self.name + "_bit" + str(level)):
                self.came = self.link.swap(sent, level)
        else:
            same = lambda unit, index: unit
            (self.kept,) = self.run(
                merge_kernel(False, True, level is None),
                [self.unit_spec(self.kept_source(same)), self.unit_spec(same)],
                1,
                total_units,
                [self.kept, came],
                F32 if level is None else BF16,
            )
            self.chosen = None
            if level is None:
                return
            pairs = []
            for device in range(self.link.total):
                settled = all(
                    (device >> other) & 1 == self.prefix[other - self.open_bits]
                    for other in range(self.open_bits, level)
                )
                if settled and (device >> level) & 1 != self.prefix[level - self.open_bits]:
                    pairs.append((device, device ^ (1 << level)))
            with jax.named_scope(self.name + "_bit" + str(level)):
                self.came = lax.ppermute(self.kept, AXES, pairs)

    def step(self, after=()):
        if self.at < len(self.levels):
            self.at += 1
            self.after = list(after)
            self.send_half(self.came)

    def finish(self):
        while self.at < len(self.levels):
            self.step()
        return self.kept.reshape(self.kept.shape[1:])


def make_body(mesh):
    n_wide, n_narrow = mesh.shape["wide"], mesh.shape["narrow"]

    def body(
        x_lo,
        x_mid,
        x_hi,
        cot_lo,
        cot_mid,
        cot_hi,
        live_counts,
        slim_master,
        broad_master,
        slim_rowstat,
        broad_rowstat,
        slim_colstat,
        broad_colstat,
        norm_params,
        norm_moments,
    ):
        link = Exchange(n_wide, n_narrow)
        kernel_call = Kernels()
        count = n_narrow
        images = x_lo.shape[0]
        sides = tuple(value.shape[1] // 2 for value in (x_lo, x_mid, x_hi))
        c_in, mid, c_out = x_lo.shape[3], slim_master.shape[1], broad_master.shape[1]
        cells = grid_rows(images, sides)
        cells_in = 4 * cells
        rows = -(-cells // 16) * 16
        chunks = c_out // mid
        bounds_slim = (0, c_in, c_in + 9 * mid, c_in + 9 * mid + c_out, c_in + 18 * mid + c_out)
        bounds_broad = (0, mid, mid + c_in, 2 * mid + c_in)
        at_two, at_four, at_five = (bounds_slim[level] // mid for level in (1, 2, 3))
        at_six = bounds_broad[2] // mid
        widths = (mid, mid, c_out, c_out, mid, mid, c_out)
        norm_at = [sum(widths[:level]) // mid for level in range(7)]

        kinds = class_table(images, sides, rows)
        shifts = one_hot(shift_table(images, sides, rows), rows)

        def by_cell(value):
            return jnp.transpose(value, (1, 2, 0, 3))

        x_flat = jnp.concatenate(
            [by_cell(value).reshape(-1, c_in) for value in (x_lo, x_mid, x_hi)], 0
        )
        x_kinds = jnp.dot(one_hot(kinds.reshape(-1), cells_in), x_flat, preferred_element_type=F32)
        x_kinds = x_kinds.astype(BF16).reshape(4, rows, c_in)
        alive = (
            jnp.arange(images, dtype=jnp.int32)[None] < live_counts[0][:, None]
        ).astype(F32)
        slots = np.zeros((rows, len(sides) * images), np.float32)
        base = 0
        for level, side in enumerate(sides):
            for at in range(images * side * side):
                slots[base + at, level * images + at % images] = 1.0
            base += images * side * side
        mask = jnp.sum(jnp.asarray(slots) * alive.reshape(1, -1), 1)
        cell_count = tree_sum(link.group_parts(jnp.sum(mask).reshape(1, 1)))
        mask = mask[:, None]
        recip = 1.0 / cell_count
        recip_in = 0.25 / cell_count

        slim = lax.all_gather(slim_master.astype(BF16), AXES, axis=0, tiled=True)
        gather = Gather(link, kernel_call, [broad_master.astype(BF16)], ["broad"], [False])
        gather.start()
        gather.run(range(gather.length - LATE_STEPS), [x_kinds, mask, shifts, recip])

        narrow_all = whole((rows, mid))
        kinds_all = whole((4, rows, mid))
        stat_all = whole((2, mid))
        mask_all = whole((rows, 1))
        one_all = whole((1, 1))
        shifts_all = whole((9, rows, rows))
        chunk = block((rows, mid), lambda j: (0, j))

        def stat_chunk(height):
            return block((height, mid), lambda j: (0, j))

        def affine(level):
            return block((2, mid), lambda j: (0, norm_at[level]))

        def affine_chunk(level):
            return block((2, mid), lambda j: (0, norm_at[level] + j))

        def slim_block(at):
            return block((mid, mid), lambda j: (at + j, 0))

        def slim_taps(at):
            return [
                block((mid, mid), lambda j, offset=offset: (at + 3 * j + offset, 0))
                for offset in range(3)
            ]

        def broad_block(at):
            return block((mid, mid), lambda j: (at, j))

        narrow_f32 = shape_of((rows, mid), F32)
        wide_f32 = shape_of((rows, c_out), F32)
        narrow_low = shape_of((rows, mid), BF16)
        wide_low = shape_of((rows, c_out), BF16)
        stat_narrow = shape_of((2, mid), F32)
        stat_wide = shape_of((2, c_out), F32)
        flops_conv = 2 * rows * 9 * mid * (mid + rows)
        flops_wide = 2 * rows * mid * c_out

        def part_of(which):
            return pl.BlockSpec((None, 2, mid), lambda *step: (which, 0, 0))

        stat_gathered = [part_of(which) for which in range(count)]

        z_one, stat = kernel_call(
            first_kernel,
            "first",
            (4,),
            [
                block((1, rows, c_in), lambda j: (j, 0, 0)),
                whole((c_in, mid)),
                mask_all,
            ],
            [block((1, rows, mid), lambda j: (j, 0, 0)), stat_all],
            [shape_of((4, rows, mid), F32), stat_narrow],
            2 * 4 * rows * c_in * mid,
            after=[recip],
        )(x_kinds, slim, mask)
        parts_one = link.group_parts(stat)
        act_one, z_two, stat = kernel_call(
            conv_kernel(count, 4, 2),
            "conv_two",
            (3,),
            [kinds_all]
            + [stat_all] * count
            + [affine(0), one_all, mask_all, shifts_all, *slim_taps(at_two)],
            [kinds_all, narrow_all, stat_all],
            [shape_of((4, rows, mid), BF16), narrow_f32, stat_narrow],
            flops_conv,
        )(z_one, *parts_one, norm_params, recip_in, mask, shifts, slim, slim, slim)
        parts_two = link.group_parts(stat)
        gather.run(range(gather.length - LATE_STEPS, gather.length), [])
        (broad,) = gather.full
        pieces = c_in // mid
        z_side, stat_side = kernel_call(
            side_kernel(pieces),
            "side",
            (chunks,),
            [block((1, rows, c_in), lambda j: (0, 0, 0))]
            + [broad_block(1 + piece) for piece in range(pieces)]
            + [mask_all],
            [chunk, stat_chunk(2)],
            [wide_f32, stat_wide],
            2 * rows * c_in * c_out,
        )(x_kinds, *[broad] * pieces, mask)
        act_two, z_three, stat = kernel_call(
            widen_kernel(count, True),
            "widen_three",
            (chunks,),
            [narrow_all]
            + [stat_all] * count
            + [affine(1), one_all, mask_all, broad_block(0), stat_chunk(2)],
            [narrow_all, chunk, stat_chunk(4)],
            [narrow_low, wide_f32, shape_of((4, c_out), F32)],
            flops_wide,
        )(z_two, *parts_two, norm_params, recip, mask, broad, stat_side)
        parts_pair = link.group_parts(stat)
        hidden, hidden_low, z_four, stat = kernel_call(
            mix_kernel(count),
            "mix",
            (chunks,),
            [chunk, chunk]
            + [stat_chunk(4)] * count
            + [affine_chunk(2), affine_chunk(3), one_all, mask_all, slim_block(at_four)],
            [chunk, chunk, narrow_all, stat_all],
            [wide_f32, wide_low, narrow_f32, stat_narrow],
            flops_wide,
        )(z_three, z_side, *parts_pair, norm_params, norm_params, recip, mask, slim)
        parts_four = link.group_parts(stat)
        one_kind = whole((1, rows, mid))
        act_four, z_five, stat = kernel_call(
            conv_kernel(count, 1, 1),
            "conv_five",
            (3,),
            [one_kind]
            + [stat_all] * count
            + [affine(4), one_all, mask_all, shifts_all, *slim_taps(at_five)],
            [one_kind, narrow_all, stat_all],
            [shape_of((1, rows, mid), BF16), narrow_f32, stat_narrow],
            flops_conv,
        )(z_four[None], *parts_four, norm_params, recip, mask, shifts, slim, slim, slim)
        parts_five = link.group_parts(stat)
        act_five, z_six, stat = kernel_call(
            widen_kernel(count, False),
            "widen_six",
            (chunks,),
            [narrow_all]
            + [stat_all] * count
            + [affine(5), one_all, mask_all, broad_block(at_six)],
            [narrow_all, chunk, stat_chunk(2)],
            [narrow_low, wide_f32, stat_wide],
            flops_wide,
        )(z_five, *parts_five, norm_params, recip, mask, broad)
        parts_six = link.group_parts(stat)
        grids = [
            block((side, side, images, mid), lambda j: (0, 0, 0, j)) for side in sides
        ]
        *y_grids, grad_out, stat = kernel_call(
            output_kernel(count, images, sides),
            "output",
            (chunks,),
            [chunk]
            + [stat_chunk(2)] * count
            + [affine_chunk(6), one_all, mask_all, chunk]
            + grids,
            grids + [chunk, stat_chunk(2)],
            [shape_of((side, side, images, c_out), BF16) for side in sides]
            + [wide_f32, stat_wide],
            flops_wide // 8,
            scratch=[pltpu.VMEM((rows, mid), F32)],
        )(
            z_six,
            *parts_six,
            norm_params,
            recip,
            mask,
            hidden,
            *[by_cell(value) for value in (cot_lo, cot_mid, cot_hi)],
        )
        sums_six = link.group_parts(stat)

        dz_six, grad_five, stat = kernel_call(
            back_linear_kernel(count),
            "back_six",
            (chunks,),
            [chunk, chunk]
            + [stat_chunk(2)] * (2 * count)
            + [affine_chunk(6), one_all, mask_all, broad_block(at_six), narrow_all]
            + [stat_all] * count
            + [affine(5)],
            [chunk, narrow_all, stat_all],
            [wide_low, narrow_f32, stat_narrow],
            flops_wide,
        )(
            grad_out,
            z_six,
            *parts_six,
            *sums_six,
            norm_params,
            recip,
            mask,
            broad,
            z_five,
            *parts_five,
            norm_params,
        )
        sums_five = link.group_parts(stat)

        def weight_grad(act, dz, steps, act_at, out_shape, out_at, base, name):
            high, across = steps
            height = act.shape[0]
            specs = [
                block((height, mid), lambda i, j: (0, act_at + i)),
                block((height, mid), lambda i, j: (0, j)),
            ]
            args = [act, dz]
            if base is not None:
                specs.append(pl.BlockSpec(memory_space=pl.ANY))
                args.append(base)
            return kernel_call(
                weight_grad_kernel,
                name,
                (high, across),
                specs,
                block((mid, mid), lambda i, j: (out_at + i, j)),
                far_shape(out_shape, BF16),
                2 * height * mid * mid * high * across,
                aliases={2: 0} if base is not None else None,
            )(*args)

        def conv_grad(act, dz, stride, taps, out_shape, out_at, base, name):
            first, number, per = taps
            kinds_here = act.shape[0]
            specs = [whole((kinds_here, rows, mid)), shifts_all, narrow_all]
            args = [act, shifts, dz]
            if base is not None:
                specs.append(pl.BlockSpec(memory_space=pl.ANY))
                args.append(base)
            return kernel_call(
                conv_grad_kernel(stride, first, per),
                name,
                (number // per,),
                specs,
                block((per * mid, mid), lambda t: (out_at // per + t, 0)),
                far_shape(out_shape, BF16),
                flops_conv * number // 9,
                aliases={3: 0} if base is not None else None,
            )(*args)

        slim_part = (bounds_slim[-1] // 4, mid)
        broad_part = (bounds_broad[-1] // 4, c_out)
        per_part = slim_part[0] // mid
        term_six = weight_grad(act_five, dz_six, (1, chunks), 0, broad_part, 0, None, "grad_six")
        chain_six = Scatter(link, kernel_call, term_six, "sum_six", (1, 1), "all_wide")

        dz_five, grad_four, stat = kernel_call(
            back_conv_kernel(count, 1, 1),
            "back_five",
            (3,),
            [narrow_all, narrow_all]
            + [stat_all] * (2 * count)
            + [affine(5), one_all, mask_all, shifts_all, *slim_taps(at_five), one_kind]
            + [stat_all] * count
            + [affine(4), one_all],
            [narrow_all, one_kind, stat_all],
            [narrow_low, shape_of((1, rows, mid), F32), stat_narrow],
            flops_conv,
        )(
            grad_five,
            z_five,
            *parts_five,
            *sums_five,
            norm_params,
            recip,
            mask,
            shifts,
            slim,
            slim,
            slim,
            z_four[None],
            *parts_four,
            norm_params,
            recip,
        )
        grad_four = grad_four[0]
        sums_four = link.group_parts(stat)
        low_four = 2 * per_part - at_four
        chain_six.step()
        upper_part = (2 * slim_part[0], mid)
        term_upper = conv_grad(
            act_four, dz_five, 1, (0, 9, 3), upper_part, chunks - low_four, None, "grad_five"
        )
        dz_four, grad_mid, stat = kernel_call(
            back_mix_kernel(count),
            "back_four",
            (chunks,),
            [narrow_all, narrow_all]
            + [stat_all] * (2 * count)
            + [affine(4), one_all, mask_all, slim_block(at_four), chunk, chunk, chunk]
            + [stat_chunk(4)] * count
            + [affine_chunk(2), affine_chunk(3)],
            [narrow_all, chunk, stat_chunk(3)],
            [narrow_low, wide_f32, shape_of((3, c_out), F32)],
            flops_wide,
        )(
            grad_four,
            z_four,
            *parts_four,
            *sums_four,
            norm_params,
            recip,
            mask,
            slim,
            grad_out,
            z_three,
            z_side,
            *parts_pair,
            norm_params,
            norm_params,
        )
        sums_pair = link.group_parts(stat)
        chain_six.step()
        term_upper = weight_grad(
            hidden_low,
            dz_four,
            (chunks - low_four, 1),
            low_four,
            upper_part,
            0,
            term_upper,
            "grad_four",
        )
        slim_upper = link.scatter_upper(term_upper)
        dz_three, dz_side, grad_two, stat = kernel_call(
            back_pair_kernel(count),
            "back_three",
            (chunks,),
            [chunk, chunk, chunk]
            + [stat_chunk(4)] * count
            + [stat_chunk(3)] * count
            + [affine_chunk(2), affine_chunk(3), one_all, mask_all, broad_block(0), narrow_all]
            + [stat_all] * count
            + [affine(1)],
            [chunk, chunk, narrow_all, stat_all],
            [wide_low, wide_low, narrow_f32, stat_narrow],
            flops_wide,
        )(
            grad_mid,
            z_three,
            z_side,
            *parts_pair,
            *sums_pair,
            norm_params,
            norm_params,
            recip,
            mask,
            broad,
            z_two,
            *parts_two,
            norm_params,
        )
        sums_two = [lax.all_gather(stat, "narrow")] * count
        x_sub = x_kinds[0]
        two_parts = (2 * broad_part[0], c_out)
        term_three = weight_grad(
            act_two, dz_three, (1, chunks), 0, two_parts, 0, None, "grad_three"
        )
        term = weight_grad(
            x_sub, dz_side, (1, chunks), 0, two_parts, 1, term_three, "grad_side_low"
        )
        chain_six.step()
        chain_three = Scatter(link, kernel_call, term, "sum_three", (0,), "most_wide")
        term = weight_grad(
            x_sub, dz_side, (1, chunks), 1, broad_part, 0, None, "grad_side_high"
        )
        chain_side = Scatter(link, kernel_call, term, "sum_side", (0, 1), "narrow")

        dz_two, grad_one, stat = kernel_call(
            back_conv_kernel(count, 4, 2),
            "back_two",
            (3,),
            [narrow_all, narrow_all]
            + [stat_all] * count
            + stat_gathered
            + [affine(1), one_all, mask_all, shifts_all, *slim_taps(at_two), kinds_all]
            + [stat_all] * count
            + [affine(0), one_all],
            [narrow_all, kinds_all, stat_all],
            [narrow_low, shape_of((4, rows, mid), F32), stat_narrow],
            flops_conv,
        )(
            grad_two,
            z_two,
            *parts_two,
            *sums_two,
            norm_params,
            recip,
            mask,
            shifts,
            slim,
            slim,
            slim,
            z_one,
            *parts_one,
            norm_params,
            recip_in,
        )
        sums_one = [lax.all_gather(stat, "narrow")] * count
        chain_six.step()
        chain_three.step()
        term = conv_grad(
            act_one, dz_two, 2, (per_part - at_two, 9 - per_part + at_two, 9 - per_part + at_two), slim_part, 0, None,
            "grad_two_high",
        )
        term = weight_grad(
            hidden_low, dz_four, (low_four, 1), 0, slim_part, per_part - low_four, term,
            "grad_four_low",
        )
        chain_two = Scatter(link, kernel_call, term, "sum_two", (1, 0), "narrow")
        slim_low = conv_grad(
            act_one, dz_two, 2, (0, per_part - at_two, at_two), slim_part, at_two, None, "grad_two_low"
        )
        chain_side.step()
        chain_two.step()
        dz_one, slim_low = kernel_call(
            back_first_kernel(count),
            "back_one",
            (4,),
            [block((1, rows, mid), lambda j: (j, 0, 0))] * 2
            + [stat_all] * count
            + stat_gathered
            + [
                affine(0),
                one_all,
                mask_all,
                block((1, rows, c_in), lambda j: (j, 0, 0)),
                pl.BlockSpec(memory_space=pl.ANY),
            ],
            [block((1, rows, mid), lambda j: (j, 0, 0)), whole((c_in, mid))],
            [shape_of((4, rows, mid), BF16), far_shape(slim_part, BF16)],
            2 * 4 * rows * c_in * mid,
            scratch=[pltpu.VMEM((c_in, mid), F32)],
            aliases={2 + 2 * count + 4: 1},
        )(grad_one, z_one, *parts_one, *sums_one, norm_params, recip_in, mask, x_kinds, slim_low)
        chain_three.step()
        chain_one = Scatter(link, kernel_call, slim_low, "sum_one", (0, 0), "wide")
        chain_one.step()

        extents = tuple(2 * side for side in sides)
        dx_grids = kernel_call(
            input_grad_kernel(images, sides),
            "input_grad",
            (c_in // mid,),
            [
                kinds_all,
                slim_block(0),
                whole((rows, c_out)),
                block((mid, c_out), lambda j: (1 + j, 0)),
            ],
            [
                block((extent, extent, images, mid), lambda j: (0, 0, 0, j))
                for extent in extents
            ],
            [shape_of((extent, extent, images, c_in), F32) for extent in extents],
            2 * 4 * rows * c_in * mid + 2 * rows * c_in * c_out,
            scratch=[pltpu.VMEM((rows, mid), F32)],
        )(dz_one, slim, dz_side, broad)

        def by_image(value):
            return jnp.transpose(value, (2, 0, 1, 3))

        y_parts = [by_image(value) for value in y_grids]
        dx_parts = [by_image(value) for value in dx_grids]

        top = link.bit(link.bits - 1)
        second = link.bit(link.bits - 2)

        def choose(bit, upper, lower):
            return jnp.where(bit == 1, upper, lower)

        place = link.index.astype(jnp.int32)
        firsts = jnp.stack([place * broad_master.shape[0], place * slim_master.shape[0]])
        scalars = pl.BlockSpec(memory_space=pltpu.SMEM)

        def tally(name):
            values, specs = [], []
            for grad, master, rowstat in (
                (broad_grad, broad_master, broad_rowstat),
                (slim_grad, slim_master, slim_rowstat),
            ):
                column = whole((grad.shape[0], 1))
                specs += [whole(grad.shape), whole(grad.shape), column]
                values += [grad, master, rowstat.reshape(-1, 1)]
            sums_dims = (2 * (len(bounds_broad) - 1) + 3, c_out)
            columns = [(value.shape[0], 1) for value in (slim_master, broad_master)]
            return kernel_call(
                tally_kernel(bounds_slim, bounds_broad),
                name,
                (1,),
                [scalars] + specs,
                [whole(dims) for dims in columns] + [whole(sums_dims)],
                [shape_of(dims, F32) for dims in columns] + [shape_of(sums_dims, F32)],
                1,
            )(firsts, *values)

        def renew(grad, master, rows_new, sums, colstat, bounds, which, name):
            matrix, column = whole(grad.shape), whole((grad.shape[0], 1))
            cols_all = whole(colstat.shape)
            return kernel_call(
                renew_kernel(bounds, which, bounds_broad),
                name,
                (1,),
                [scalars, matrix, matrix, column, whole(sums.shape), cols_all],
                [cols_all, matrix, matrix],
                [
                    shape_of(colstat.shape, F32),
                    shape_of(grad.shape, F32),
                    shape_of(grad.shape, BF16),
                ],
                1,
            )(firsts, grad, master, rows_new, sums, colstat)

        spans = [
            (mid * at, width, rows_of)
            for at, width, rows_of in zip(
                norm_at, widths, ((0, 1),) * 2 + ((0, 1), (2, 1)) + ((0, 1),) * 3
            )
        ]
        sum_sets = [sums_one, sums_two, sums_pair, sums_pair, sums_four, sums_five, sums_six]
        flat_sets = [part for parts in sum_sets for part in parts]
        norm_rows = norm_params.size // c_out
        norm_sums = kernel_call(
            pack_kernel(count, spans, mid),
            "pack",
            (1,),
            stat_gathered * 2 + [whole(part.shape) for part in flat_sets[2 * count :]],
            whole((norm_rows, c_out)),
            shape_of((norm_rows, c_out), F32),
            1000000,
        )(*flat_sets)
        norm_totals = link.total_sums(norm_sums, link.narrow_bits)

        chain_two.step()
        chain_three.step(after=norm_totals[:1])
        chain_one.step()
        chain_side.step()
        chain_one.step()
        chain_two.step(after=norm_totals[1:2])
        chain_three.step()
        chain_six.step()
        chain_side.step()
        chain_one.step()
        chain_side.step(after=norm_totals[2:])
        chain_two.step()
        broad_six = chain_six.finish()
        chain_three.step(after=[slim_upper])
        broad_three = chain_three.finish()
        slim_one = chain_one.finish()
        broad_side = chain_side.finish()
        slim_two = chain_two.finish()
        broad_grad = choose(top, choose(second, broad_six, broad_side), broad_three)
        slim_low = choose(second, slim_two, slim_one)
        slim_grad = choose(top, slim_upper.astype(F32), slim_low)

        slim_rows_new, broad_rows_new, sums = tally("tally")
        sums = link.total_sums(sums)[-1]
        broad_cols_new, broad_new, broad_copy = renew(
            broad_grad, broad_master, broad_rows_new, sums, broad_colstat, bounds_broad, 0,
            "broad_renew",
        )
        slim_cols_new, slim_new, slim_copy = renew(
            slim_grad, slim_master, slim_rows_new, sums, slim_colstat, bounds_slim, 1,
            "slim_renew",
        )
        norm_grad = norm_totals[-1].reshape(norm_params.shape)
        norm_moments_new = DECAY * norm_moments + (1.0 - DECAY) * (
            norm_grad * norm_grad + EPS_ONE
        )
        norm_update = norm_grad * lax.rsqrt(norm_moments_new)
        update_rms = jnp.sqrt(jnp.mean(norm_update * norm_update, 1))
        weight_rms = jnp.sqrt(jnp.mean(norm_params * norm_params, 1))
        step = STEP_RATE * jnp.maximum(EPS_TWO, weight_rms) / jnp.maximum(1.0, update_rms)
        norm_new = norm_params - step[:, None] * norm_update
        return (
            *y_parts,
            *dx_parts,
            slim_grad,
            broad_grad,
            slim_rows_new.reshape(-1),
            broad_rows_new.reshape(-1),
            slim_cols_new,
            broad_cols_new,
            slim_new,
            broad_new,
            slim_copy,
            broad_copy,
            norm_grad,
            norm_moments_new,
            norm_new,
        )

    return body


def solution(mesh):
    split = P(AXES)
    return jax.shard_map(
        make_body(mesh),
        mesh=mesh,
        in_specs=(split,) * 11 + (P(),) * 4,
        out_specs=(split,) * 10 + (P(),) * 2 + (split,) * 4 + (P(),) * 3,
        check_vma=False,
    )
```
